32 devices in a mesh: dp: 8 (over z, y), tensor: 4 (over x, core).
Axes of the slice: x: 2, y: 2, z: 4, core: 2. Of those that a mesh axis runs over, the one named last changes fastest.
Arguments:
- hidden: bfloat16 [16, 1024, 2048], P('dp', 'tensor'), may hold values from -6 to 6
- pre_gain: float32 [2048], replicated, may hold values from 0.5 to 1.5
- w_zx: bfloat16 [2, 2048, 4096], P(None, 'dp', 'tensor'), may hold values from -0.125 to 0.125
- w_bcdt: bfloat16 [2048, 320], P('dp'), may hold values from -0.125 to 0.125
- conv_x: float32 [5, 4096], P(None, 'tensor'), may hold values from -0.5 to 0.5
- conv_bc: float32 [5, 256], replicated, may hold values from -0.5 to 0.5
- dt_bias: float32 [64], P('tensor'), may hold values from -6 to -2
- a_log: float32 [64], P('tensor'), may hold values from 0 to 2.5
- d_skip: float32 [64], P('tensor'), may hold values from 0.5 to 1.5
- gate_gain: float32 [4096], P('tensor'), may hold values from 0.5 to 1.5
- w_out: bfloat16 [4096, 2048], P('tensor', 'dp'), may hold values from -0.09375 to 0.09375
- cotangent: bfloat16 [16, 1024, 2048], P('dp', 'tensor'), may hold values from -6 to 6
- segments: int32 [16, 1024], P('dp'), may hold values from 0 to 1023, as said below
Outputs:
- out_hidden: bfloat16 [16, 1024, 2048], P('dp', 'tensor')
- d_hidden: float32 [16, 1024, 2048], P('dp', 'tensor')
- d_pre_gain: float32 [2048], replicated
- d_w_zx: float32 [2, 2048, 4096], P(None, 'dp', 'tensor')
- d_w_bcdt: float32 [2048, 320], P('dp')
- d_conv_x: float32 [5, 4096], P(None, 'tensor')
- d_conv_bc: float32 [5, 256], replicated
- d_dt_bias: float32 [64], P('tensor')
- d_a_log: float32 [64], P('tensor')
- d_d_skip: float32 [64], P('tensor')
- d_gate_gain: float32 [4096], P('tensor')
- d_w_out: float32 [4096, 2048], P('tensor', 'dp')
The draws below stay inside these ranges and needn't reach their ends.
Inputs may be any that keep to these rules, and one draw needn't show every extreme that they name: `segments`: within each sequence a document is numbered by the position of its first token, so numbers never fall along a sequence and the first token has 0; every sequence's last token begins a document of its own, and in every sequence one document covers the positions from 255 to 768.
All inputs are finite; a program needn't handle non-finite values.
Results may differ from the reference program's by a relative error of at most 0.009.
Values may be sent and summed in bfloat16 or wider, within the bound.
A program may use at most 320 MiB of HBM per device.

```python
import math
import jax
import jax.numpy as jnp
from jax import lax

D = 2048
H = 64
NSTATE = 128
KCONV = 4
BLOCK = 256
SEQ_LEN = 1024
DI = 4096
SEQS = 16


def draw_segments(key, part):
    key = jax.random.fold_in(key, 7)
    start_key, stop_key, rate_key, coin_key = jax.random.split(key, 4)
    quarter = SEQ_LEN // 4
    places = jnp.arange(SEQ_LEN)[None, :]
    long_start = jax.random.randint(start_key, (SEQS, 1), 1, quarter)
    long_stop = jax.random.randint(stop_key, (SEQS, 1), 3 * quarter + 1, SEQ_LEN)
    spacing = jax.random.randint(rate_key, (SEQS, 1), 2, 96)
    coins = jax.random.randint(coin_key, (SEQS, SEQ_LEN), 0, 6144)
    fresh_doc = coins < 6144 // spacing
    inside = (places > long_start) & (places < long_stop)
    fresh_doc = jnp.where(inside, False, fresh_doc)
    fresh_doc = fresh_doc | (places == long_start) | (places == long_stop) | (places == 0) | (places == SEQ_LEN - 1)
    starts = jnp.where(fresh_doc, places, 0).astype(jnp.int32)
    return lax.cummax(starts, axis=1).astype(jnp.int32)


def steps_of(key, shape, shards, low, top_value):
    loudness, own = 1.0, jax.random.fold_in(key, 6)
    for position, blocks in shards:
        draws = jnp.exp(jax.random.uniform(jax.random.fold_in(own, position), (blocks,), jnp.float32, low / len(shards), top_value / len(shards)))
        loudness = loudness * jnp.repeat(draws, shape[position] // blocks).reshape([-1 if axis == position else 1 for axis in range(len(shape))])
    return loudness


def scatter_about(own_key, dims, scale, bound, shards=(), dtype=jnp.bfloat16):
    values = scale * jax.random.normal(own_key, dims, jnp.float32)
    if shards:
        values = values * steps_of(own_key, dims, shards, -0.22, 0.18)
    return jnp.clip(values, -bound, bound).astype(dtype)


def setup_inputs(seed: int = 0) -> dict:
    key_list = jax.random.split(jax.random.key(seed), 14)
    hidden = scatter_about(key_list[0], (SEQS, SEQ_LEN, D), 1.0, 6.0, ((0, 8), (1, 4)))
    pre_gain = jnp.clip(1.0 + 0.1 * jax.random.normal(key_list[1], (D,), jnp.float32), 0.5, 1.5)
    w_zx = scatter_about(key_list[2], (2, D, DI), D ** -0.5, 0.125, ((1, 8), (2, 4)))
    w_bcdt = scatter_about(key_list[3], (D, 2 * NSTATE + H), D ** -0.5, 0.125, ((0, 8),))
    conv_x = jnp.clip(jax.random.uniform(key_list[4], (KCONV + 1, DI), jnp.float32, -0.5, 0.5) * steps_of(key_list[4], (KCONV + 1, DI), ((1, 4),), -0.4, 0.0), -0.5, 0.5)
    conv_bc = jnp.clip(jax.random.uniform(key_list[5], (KCONV + 1, 2 * NSTATE), jnp.float32, -0.5, 0.5), -0.5, 0.5)
    dt_bias = jnp.clip(-6.0 + 4.0 * jax.random.uniform(key_list[6], (H,), jnp.float32) ** steps_of(key_list[6], (H,), ((0, 4),), -0.2, 0.2), -6.0, -2.0)
    a_log = jnp.clip(2.5 * jax.random.uniform(key_list[7], (H,), jnp.float32) ** steps_of(key_list[7], (H,), ((0, 4),), -0.2, 0.2), 0.0, 2.5)
    d_skip = jnp.clip(0.5 + 1.0 * jax.random.uniform(key_list[8], (H,), jnp.float32) ** steps_of(key_list[8], (H,), ((0, 4),), -0.2, 0.2), 0.5, 1.5)
    gate_gain = jnp.clip(1.0 + 0.1 * jax.random.normal(key_list[9], (DI,), jnp.float32), 0.5, 1.5)
    w_out = scatter_about(key_list[10], (DI, D), DI ** -0.5, 0.09375, ((0, 4), (1, 8)))
    cotangent = scatter_about(key_list[11], (SEQS, SEQ_LEN, D), 1.0, 6.0, ((0, 8), (1, 4)))
    segments = draw_segments(jax.random.fold_in(key_list[13], 71), 0)
    return {"hidden": hidden, "pre_gain": pre_gain, "w_zx": w_zx, "w_bcdt": w_bcdt, "conv_x": conv_x, "conv_bc": conv_bc, "dt_bias": dt_bias, "a_log": a_log, "d_skip": d_skip, "gate_gain": gate_gain, "w_out": w_out, "cotangent": cotangent, "segments": segments}


EPS = 1e-05
EXACT = lax.Precision.HIGHEST

@jax.custom_vjp
def low(v):
    return lax.optimization_barrier(v.astype(jnp.bfloat16)).astype(jnp.float32)

@jax.custom_vjp
def low_back(v):
    return v

def low_keep(v):
    return (low(v), None)

def low_pass(kept, grad):
    return (grad,)

def back_keep(v):
    return (v, None)

def back_low(kept, grad):
    return (low(grad),)
low.defvjp(low_keep, low_pass)
low_back.defvjp(back_keep, back_low)

def rms_scale(values):
    return lax.rsqrt(lax.optimization_barrier(jnp.mean(values * values, axis=-1, keepdims=True)) + EPS)

def causal_conv(values, segment, conv_taps):
    tap_count = conv_taps.shape[0] - 1
    seq_length = values.shape[0]
    outcome = jnp.zeros_like(values) + conv_taps[tap_count]
    for tap_index in range(tap_count):
        lag_steps = tap_count - 1 - tap_index
        earlier_rows = jnp.pad(values, ((lag_steps, 0), (0, 0)))[:seq_length]
        earlier_doc = jnp.pad(segment, (lag_steps, 0), constant_values=-1)[:seq_length]
        outcome = outcome + jnp.where((earlier_doc == segment)[:, None], conv_taps[tap_index] * earlier_rows, 0.0)
    return outcome

def state_space(heads_x, step_size, a_log, b_mat, c_mat, segment):
    seq_length, heads, head_dim = heads_x.shape
    blocks = seq_length // BLOCK
    rate = (-jnp.exp(a_log) * step_size).reshape(blocks, BLOCK, heads)
    cumrate = jnp.cumsum(rate, axis=1)
    seg_block = segment.reshape(blocks, BLOCK)
    before = jnp.concatenate([jnp.full((1,), -1, jnp.int32), segment[:-1].astype(jnp.int32)]).reshape(blocks, BLOCK)[:, 0]
    places = jnp.arange(BLOCK)
    causal = places[:, None] >= places[None, :]
    same_doc = (seg_block[:, :, None] == seg_block[:, None, :]) & causal[None]
    head_cum = jnp.moveaxis(cumrate, 2, 1)
    gaps = head_cum[:, :, :, None] - head_cum[:, :, None, :]
    keeper = same_doc[:, None]
    decay = jnp.where(keeper, jnp.exp(jnp.where(keeper, gaps, 0.0)), 0.0)
    b_blocks = b_mat.reshape(blocks, BLOCK, -1)
    c_blocks = c_mat.reshape(blocks, BLOCK, -1)
    scores = jnp.einsum('cin,cjn->cij', c_blocks, b_blocks, precision=EXACT)
    weighted = heads_x.reshape(blocks, BLOCK, heads, head_dim) * step_size.reshape(blocks, BLOCK, heads)[..., None]
    inside = jnp.einsum('chij,cjhp->cihp', decay * scores[:, None], weighted, precision=EXACT)
    last_doc = seg_block == seg_block[:, -1:]
    to_end = jnp.where(last_doc[..., None], jnp.exp(cumrate[:, -1:, :] - cumrate), 0.0)
    block_states = jnp.einsum('cjh,cjhp,cjn->chpn', to_end, weighted, b_blocks, precision=EXACT)
    carry_on = jnp.where((seg_block[:, -1] == before)[:, None], jnp.exp(cumrate[:, -1, :]), 0.0)

    def advance(state, block_pair):
        new_states, factor = block_pair
        return (factor[:, None, None] * state + new_states, state)
    zero_state = jnp.zeros((heads, head_dim, b_mat.shape[1]), jnp.float32)
    _, earlier = lax.scan(advance, zero_state, (block_states, carry_on))
    reads = jnp.where((seg_block == before[:, None])[..., None], jnp.exp(cumrate), 0.0)
    outside = jnp.einsum('cih,cin,chpn->cihp', reads, c_blocks, earlier, precision=EXACT)
    return (inside + outside).reshape(seq_length, heads, head_dim)

def mixer(zx_proj, bc_dt, conv_x, conv_bc, dt_bias, a_log, d_skip, segment, head_first):
    heads = dt_bias.shape[0]
    states = conv_bc.shape[1] // 2
    seq_length = zx_proj.shape[1]
    x_part = jax.nn.silu(causal_conv(zx_proj[1], segment, conv_x))
    bc_part = jax.nn.silu(causal_conv(bc_dt[:, :2 * states], segment, conv_bc))
    raw_step = lax.dynamic_slice_in_dim(bc_dt, 2 * states + head_first, heads, 1)
    step_size = jax.nn.softplus(raw_step + dt_bias)
    heads_x = x_part.reshape(seq_length, heads, -1)
    mixed = state_space(heads_x, step_size, a_log, bc_part[:, :states], bc_part[:, states:], segment)
    mixed = mixed + d_skip[None, :, None] * heads_x
    return mixed.reshape(seq_length, -1) * jax.nn.silu(zx_proj[0])

def seq_forward(seq_rows, segment, weights_in):
    pre_gain, w_zx, w_bcdt, conv_x, conv_bc, dt_bias, a_log, d_skip, gate_gain, w_out = weights_in
    normed_in = low(seq_rows * rms_scale(seq_rows) * pre_gain)
    zx_proj = low_back(jnp.einsum('ld,kde->kle', normed_in, w_zx, precision=EXACT))
    bc_dt = low_back(jnp.dot(normed_in, w_bcdt, precision=EXACT))
    gated = mixer(zx_proj, bc_dt, conv_x, conv_bc, dt_bias, a_log, d_skip, segment, 0)
    normed_out = low(gated * rms_scale(gated) * gate_gain)
    return seq_rows + jnp.dot(normed_out, w_out, precision=EXACT)

def reference(hidden, pre_gain, w_zx, w_bcdt, conv_x, conv_bc, dt_bias, a_log, d_skip, gate_gain, w_out, cotangent, segments):
    group_size = math.gcd(SEQS, max(1, 4096 // SEQ_LEN))
    seg_groups = segments.reshape(SEQS // group_size, group_size, SEQ_LEN)

    def forward(tokens_in, *weights_in):

        def one_sequence(seq_rows, segment):
            return seq_forward(seq_rows, segment, weights_in)

        def one_group(group_pair):
            return jax.vmap(one_sequence)(group_pair[0], group_pair[1])
        grouped = tokens_in.reshape(SEQS // group_size, group_size, SEQ_LEN, D)
        mapped = lax.map(jax.checkpoint(one_group), (grouped, seg_groups))
        return mapped.reshape(SEQS, SEQ_LEN, D)
    float_args = [array_in.astype(jnp.float32) for array_in in (hidden, pre_gain, w_zx, w_bcdt, conv_x, conv_bc, dt_bias, a_log, d_skip, gate_gain, w_out)]
    outcome, pullback = jax.vjp(forward, *float_args)
    gradients = pullback(cotangent.astype(jnp.float32))
    return (outcome.astype(jnp.bfloat16), gradients[0], gradients[1], gradients[2], gradients[3], gradients[4], gradients[5], gradients[6], gradients[7], gradients[8], gradients[9], gradients[10])
```

```python
import functools

import jax
import jax.numpy as jnp
import numpy as np
from jax import lax
from jax.experimental import pallas as pl
from jax.experimental.pallas import tpu as pltpu
from jax.sharding import PartitionSpec as P

MESH = pl.DeviceIdType.MESH
EPS = 1e-05
BLOCK = 256
F32 = jnp.float32
BF16 = jnp.bfloat16
EXACT = lax.Precision.HIGHEST
LOG2E = 1.4426950408889634
NEG = -1e30


def sigmoid(v):
    return 0.5 * jnp.tanh(0.5 * v) + 0.5


def split3(v):
    hi = v.astype(BF16)
    rest = v - hi.astype(F32)
    mid = rest.astype(BF16)
    low = (rest - mid.astype(F32)).astype(BF16)
    return hi, mid, low


def dot(a, b):
    return jnp.dot(a, b, preferred_element_type=F32)


def dot_nt(a, b):
    return lax.dot_general(a, b, (((1,), (1,)), ((), ())), preferred_element_type=F32)


def dot_tn(a, b):
    return lax.dot_general(a, b, (((0,), (0,)), ((), ())), preferred_element_type=F32)


def softplus(v):
    return jnp.maximum(v, 0.0) + jnp.log1p(jnp.exp(-jnp.abs(v)))


def head_sizes(raw, dt_bias, a_log):
    q = raw.shape[0]
    tri = (
        lax.broadcasted_iota(jnp.int32, (q, q), 0) >= lax.broadcasted_iota(jnp.int32, (q, q), 1)
    ).astype(F32)
    biased = raw + dt_bias
    step = softplus(biased)
    rate = -jnp.exp(a_log) * step
    cum = jnp.dot(tri, rate, precision=EXACT, preferred_element_type=F32) * LOG2E
    return biased, step, rate, cum


def expand(values, spread):
    hi, mid, low = split3(values)
    return dot(hi, spread) + dot(mid, spread) + dot(low, spread)


def gather_heads(values, spread):
    hi, mid, _ = split3(values)
    return dot_nt(hi, spread) + dot_nt(mid, spread)


def exact_nt(a, b):
    a_hi, a_mid, _ = split3(a)
    b_hi, b_mid, _ = split3(b)
    return dot_nt(a_hi, b_hi) + dot_nt(a_hi, b_mid) + dot_nt(a_mid, b_hi)


def transpose_heads(values):
    pad = jnp.concatenate(
        [values, jnp.zeros((values.shape[0], 128 - values.shape[1]), F32)], axis=1
    )
    return pad.T


def forward_kernel(
    x_ref, bc_ref, dt_ref, cols_ref, segrow_ref, taps_x_ref, taps_bc_ref, bias_ref, alog_ref, skip_ref, spread_ref,
    y_ref, cx_ref, cbc_ref, states_ref,
    xs, bs, state, mask_bias,
):
    block = pl.program_id(1)
    q = BLOCK
    heads = dt_ref.shape[-1]
    channels = x_ref.shape[-1]
    width = channels // heads

    @pl.when(block == 0)
    def _():
        xs[0:8, :] = jnp.zeros((8, xs.shape[1]), F32)
        bs[0:8, :] = jnp.zeros((8, bs.shape[1]), F32)
        state[...] = jnp.zeros_like(state)

    cols = cols_ref[0]
    lag_masks = [cols[:, k : k + 1] for k in range(3)]
    reads, last, seg = cols[:, 3:4], cols[:, 4:5], cols[:, 5:6]

    def conv(value_ref, hold, taps_ref):
        hold[8 : 8 + q, :] = value_ref[0]
        out = taps_ref[4:5, :] + taps_ref[3:4, :] * hold[8 : 8 + q, :]
        for lag in (1, 2, 3):
            out = out + (lag_masks[lag - 1] * hold[8 - lag : 8 - lag + q, :]) * taps_ref[3 - lag : 4 - lag, :]
        hold[0:8, :] = hold[q : q + 8, :]
        return out

    cbc = conv(bc_ref, bs, taps_bc_ref)
    cbc_ref[0] = cbc
    bc = cbc * sigmoid(cbc)
    n = bc.shape[1] // 2
    scores = exact_nt(bc[:, n:], bc[:, :n])
    b_mat, c_mat = bc[:, :n].astype(BF16), bc[:, n:].astype(BF16)

    cx = conv(x_ref, xs, taps_x_ref)
    cx_ref[0] = cx
    xb = (cx * sigmoid(cx)).astype(BF16)

    biased, step, rate, cum = head_sizes(dt_ref[0], bias_ref[...], alog_ref[...])
    cum_end = cum[q - 1 : q, :]
    spread = spread_ref[...]
    reads_e = expand(reads * jnp.exp2(cum), spread)
    to_end_e = expand(last * jnp.exp2(cum_end - cum) * step, spread)
    carry = jnp.exp2(cum_end)
    carry_e = expand(jnp.broadcast_to(carry, (8, heads)), spread)[0:1]
    source = transpose_heads(cum - jnp.log(step) * LOG2E)

    rows = lax.broadcasted_iota(jnp.int32, (q, q), 0)
    places = lax.broadcasted_iota(jnp.int32, (q, q), 1)
    mask_bias[...] = jnp.where((seg == segrow_ref[0]) & (rows >= places), 0.0, NEG)

    st = state[...].astype(BF16)
    states_ref[0, 0] = st
    outside = dot(c_mat, st) * reads_e + skip_ref[...] * xb.astype(F32)

    half = q // 2
    lane = lax.broadcasted_iota(jnp.int32, (1, 2 * width), 1)
    for pair in range(heads // 2):
        at = slice(pair * 2 * width, (pair + 1) * 2 * width)
        xp = xb[:, at]
        both = []
        for h in (2 * pair, 2 * pair + 1):
            col = cum[:, h : h + 1]
            row = source[h : h + 1, :]
            top = (
                jnp.exp2((col[:half] - row[:, :half]) + mask_bias[:half, :half]) * scores[:half, :half]
            ).astype(BF16)
            low = (jnp.exp2((col[half:] - row) + mask_bias[half:, :]) * scores[half:, :]).astype(BF16)
            both.append(jnp.concatenate([dot(top, xp[:half]), dot(low, xp)], axis=0))
        y_ref[0, :, at] = outside[:, at] + jnp.where(lane < width, both[0], both[1])

    scaled = (xb.astype(F32) * to_end_e).astype(BF16)
    state[...] = carry_e * state[...] + dot_tn(b_mat, scaled)


def backward_kernel(
    dy_ref, x_ref, cx_ref, bc_ref, cbc_ref, dt_ref, cols_ref, segrow_ref, states_ref,
    taps_x_ref, taps_bc_ref, bias_ref, alog_ref, skip_ref, spread_ref,
    dx_ref, dbc_ref, ddt_ref, gx_ref, gbc_ref, gh_ref,
    ds_x, ds_bc, d_state, mask_bias, d_scores, d_in, row_sums,
):
    seq, step_id = pl.program_id(0), pl.program_id(1)
    q = BLOCK
    heads = dt_ref.shape[-1]
    channels = x_ref.shape[-1]
    width = channels // heads

    @pl.when(step_id == 0)
    def _():
        ds_x[:, q : q + 8, :] = jnp.zeros((4, 8, channels), F32)
        ds_bc[:, q : q + 8, :] = jnp.zeros((4, 8, ds_bc.shape[2]), F32)
        d_state[...] = jnp.zeros_like(d_state)

    @pl.when((step_id == 0) & (seq == 0))
    def _():
        gx_ref[...] = jnp.zeros_like(gx_ref)
        gbc_ref[...] = jnp.zeros_like(gbc_ref)
        gh_ref[...] = jnp.zeros_like(gh_ref)

    cols = cols_ref[0]
    lag_masks = [cols[:, k : k + 1] for k in range(3)]
    reads, last, seg = cols[:, 3:4], cols[:, 4:5], cols[:, 5:6]

    cbc = cbc_ref[0]
    sig_bc = sigmoid(cbc)
    bc = cbc * sig_bc
    n = bc.shape[1] // 2
    scores = exact_nt(bc[:, :n], bc[:, n:])
    b_mat, c_mat = bc[:, :n].astype(BF16), bc[:, n:].astype(BF16)
    cx = cx_ref[0]
    sig_x = sigmoid(cx)
    xc = cx * sig_x
    xb = xc.astype(BF16)
    xbf = xb.astype(F32)
    dyb = dy_ref[0]
    dyf = dyb.astype(F32)

    biased, step, rate, cum = head_sizes(dt_ref[0], bias_ref[...], alog_ref[...])
    cum_end = cum[q - 1 : q, :]
    spread = spread_ref[...]
    reads_e = expand(reads * jnp.exp2(cum), spread)
    to_end_e = expand(last * jnp.exp2(cum_end - cum) * step, spread)
    carry_e = expand(jnp.broadcast_to(jnp.exp2(cum_end), (8, heads)), spread)[0:1]
    source = cum - jnp.log(step) * LOG2E
    target = transpose_heads(cum)

    rows = lax.broadcasted_iota(jnp.int32, (q, q), 0)
    places = lax.broadcasted_iota(jnp.int32, (q, q), 1)
    mask_bias[...] = jnp.where((seg == segrow_ref[0]) & (rows <= places), 0.0, NEG)

    st = states_ref[0, 0]
    dst = d_state[...].astype(BF16)
    dye = (dyf * reads_e).astype(BF16)
    scaled = (xbf * to_end_e).astype(BF16)
    d_c = dot_nt(dye, st)
    d_b = dot_nt(scaled, dst)
    dx_st = dot(b_mat, dst) * to_end_e
    carried = carry_e * jnp.sum(d_state[...] * st.astype(F32), axis=0, keepdims=True)
    out_part = dyf * reads_e * dot(c_mat, st)
    d_state[...] = carry_e * d_state[...] + dot_tn(c_mat, dye)

    half = q // 2
    lane = lax.broadcasted_iota(jnp.int32, (1, 2 * width), 1)
    d_scores[...] = jnp.zeros_like(d_scores)
    head_lane = lax.broadcasted_iota(jnp.int32, (1, heads), 1)
    col_sums = jnp.zeros((q, heads), F32)
    for pair in range(heads // 2):
        at = slice(pair * 2 * width, (pair + 1) * 2 * width)
        xp, dyp = xb[:, at], dyb[:, at]
        both = []
        for which in (0, 1):
            h = 2 * pair + which
            mine = lane < width if which == 0 else lane >= width
            xm = jnp.where(mine, xp, jnp.zeros_like(xp))
            col = source[:, h : h + 1]
            row = target[h : h + 1, :]
            top = jnp.exp2((row - col[:half]) + mask_bias[:half, :])
            low = jnp.exp2((row[:, half:] - col[half:]) + mask_bias[half:, half:])
            d_top = top * dot_nt(xm[:half], dyp)
            d_low = low * dot_nt(xm[half:], dyp[half:])
            d_scores[:half, :] += d_top
            d_scores[half:, half:] += d_low
            m_top = d_top * scores[:half, :]
            m_low = d_low * scores[half:, half:]
            late = jnp.sum(m_top[:, half:], axis=0, keepdims=True) + jnp.sum(m_low, axis=0, keepdims=True)
            row_sums[h : h + 1, :half] = jnp.sum(m_top[:, :half], axis=0, keepdims=True)
            row_sums[h : h + 1, half:] = late
            here = jnp.concatenate(
                [
                    jnp.sum(m_top[:, :half] + m_top[:, half:], axis=1, keepdims=True),
                    jnp.sum(m_low, axis=1, keepdims=True),
                ],
                axis=0,
            )
            col_sums = jnp.where(head_lane == h, here, col_sums)
            top = (top * scores[:half, :]).astype(BF16)
            low = (low * scores[half:, half:]).astype(BF16)
            both.append(jnp.concatenate([dot(top, dyp), dot(low, dyp[half:])], axis=0))
        d_in[:, at] = jnp.where(lane < width, both[0], both[1])

    dsb = d_scores[...].astype(BF16)
    d_b = d_b + dot(dsb, c_mat)
    d_c = d_c + dot_tn(dsb, b_mat)

    dx = d_in[...] + dx_st
    skip = skip_ref[...]
    state_h = gather_heads(xbf * dx_st, spread)
    used_h = col_sums + state_h
    diff_h = row_sums[...].T[:, :heads] - col_sums + gather_heads(out_part, spread)
    from_here = (rows <= places).astype(F32)
    before = (rows > places).astype(F32)
    d_rate = (
        jnp.dot(from_here, diff_h, precision=EXACT, preferred_element_type=F32)
        + jnp.dot(before, state_h, precision=EXACT, preferred_element_type=F32)
        + gather_heads(jnp.broadcast_to(carried, (8, channels)), spread)[0:1]
    )
    sig_dt = sigmoid(biased)
    ratio = jnp.where(step < 1e-30, 1.0, sig_dt / jnp.maximum(step, 1e-30))
    d_raw = used_h * ratio - jnp.exp(alog_ref[...]) * sig_dt * d_rate
    ddt_ref[0] = d_raw
    gh_ref[0:1, :heads] += jnp.sum(d_raw, axis=0, keepdims=True)
    gh_ref[1:2, :heads] += jnp.sum(d_rate * rate, axis=0, keepdims=True)

    def conv_back(d_out, value_ref, hold, taps_ref, grad_ref):
        value = value_ref[0]
        d_value = d_out * taps_ref[3:4, :]
        grad_ref[3:4, :] += jnp.sum(value * d_out, axis=0, keepdims=True)
        grad_ref[4:5, :] += jnp.sum(d_out, axis=0, keepdims=True)
        for lag in (1, 2, 3):
            hold[lag, 0:q, :] = lag_masks[lag - 1] * d_out
            moved = hold[lag, lag : lag + q, :]
            d_value = d_value + moved * taps_ref[3 - lag : 4 - lag, :]
            grad_ref[3 - lag : 4 - lag, :] += jnp.sum(value * moved, axis=0, keepdims=True)
            hold[lag, q : q + 8, :] = hold[lag, 0:8, :]
        return d_value

    d_bc = jnp.concatenate([d_b, d_c], axis=1) * (sig_bc * (1.0 + cbc * (1.0 - sig_bc)))
    dbc_ref[0] = conv_back(d_bc, bc_ref, ds_bc, taps_bc_ref, gbc_ref)
    gx_ref[5:6, :] += jnp.sum(dyf * xbf, axis=0, keepdims=True)
    d_cx = (dx + skip * dyf) * (sig_x * (1.0 + cx * (1.0 - sig_x)))
    dx_ref[0] = conv_back(d_cx, x_ref, ds_x, taps_x_ref, gx_ref).astype(BF16)


def column_masks(segments):
    seqs, length = segments.shape
    blocks = length // BLOCK
    lags = []
    for lag in (1, 2, 3):
        earlier = jnp.pad(segments, ((0, 0), (lag, 0)), constant_values=-1)[:, :length]
        lags.append(earlier == segments)
    grouped = segments.reshape(seqs, blocks, BLOCK)
    before = jnp.pad(segments, ((0, 0), (1, 0)), constant_values=-1)[:, :length].reshape(seqs, blocks, BLOCK)
    reads = (grouped == before[:, :, :1]).reshape(seqs, length)
    last = (grouped == grouped[:, :, -1:]).reshape(seqs, length)
    stacked = [m.astype(F32) for m in (*lags, reads, last, segments)]
    stacked += [jnp.zeros_like(stacked[0])] * 2
    return jnp.stack(stacked, axis=-1)


def spread_matrix(heads, channels):
    width = channels // heads
    return (np.arange(heads)[:, None] == np.arange(channels)[None, :] // width).astype(np.float32)


def shared_specs(channels, n2, heads):
    full = lambda *shape: pl.BlockSpec(shape, lambda s, c: (0,) * len(shape))
    return [full(5, channels), full(5, n2), full(1, heads), full(1, heads), full(1, channels), full(heads, channels)]


def ssd_forward(x, bc, dt, cols, segrow, shared):
    seqs, length, channels = x.shape
    n2, heads = bc.shape[2], dt.shape[2]
    blocks = length // BLOCK
    tok = lambda w: pl.BlockSpec((1, BLOCK, w), lambda s, c: (s, c, 0))
    return pl.pallas_call(
        forward_kernel,
        grid=(seqs, blocks),
        in_specs=[tok(channels), tok(n2), tok(heads), tok(8), pl.BlockSpec((1, 1, BLOCK), lambda s, c: (s, 0, c))]
        + shared_specs(channels, n2, heads),
        out_specs=[tok(channels), tok(channels), tok(n2),
                   pl.BlockSpec((1, 1, n2 // 2, channels), lambda s, c: (s, c, 0, 0))],
        out_shape=[
            jax.ShapeDtypeStruct((seqs, length, channels), F32),
            jax.ShapeDtypeStruct((seqs, length, channels), F32),
            jax.ShapeDtypeStruct((seqs, length, n2), F32),
            jax.ShapeDtypeStruct((seqs, blocks, n2 // 2, channels), BF16),
        ],
        scratch_shapes=[
            pltpu.VMEM((BLOCK + 8, channels), F32),
            pltpu.VMEM((BLOCK + 8, n2), F32),
            pltpu.VMEM((n2 // 2, channels), F32),
            pltpu.VMEM((BLOCK, BLOCK), F32),
        ],
        compiler_params=pltpu.CompilerParams(vmem_limit_bytes=48 * 2**20),
        name="ssd_forward",
    )(x, bc, dt, cols, segrow, *shared)


def ssd_backward(dy, x, cx, bc, cbc, dt, cols, segrow, states, shared):
    seqs, length, channels = x.shape
    n2, heads = bc.shape[2], dt.shape[2]
    blocks = length // BLOCK
    tok = lambda w: pl.BlockSpec((1, BLOCK, w), lambda s, c: (s, blocks - 1 - c, 0))
    whole = lambda *shape: pl.BlockSpec(shape, lambda s, c: (0,) * len(shape))
    return pl.pallas_call(
        backward_kernel,
        grid=(seqs, blocks),
        in_specs=[tok(channels)] * 3 + [tok(n2)] * 2 + [tok(heads), tok(8),
                  pl.BlockSpec((1, 1, BLOCK), lambda s, c: (s, 0, blocks - 1 - c)),
                  pl.BlockSpec((1, 1, n2 // 2, channels), lambda s, c: (s, blocks - 1 - c, 0, 0))]
        + shared_specs(channels, n2, heads),
        out_specs=[tok(channels), tok(n2), tok(heads), whole(8, channels), whole(8, n2), whole(8, 128)],
        out_shape=[
            jax.ShapeDtypeStruct((seqs, length, channels), BF16),
            jax.ShapeDtypeStruct((seqs, length, n2), F32),
            jax.ShapeDtypeStruct((seqs, length, heads), F32),
            jax.ShapeDtypeStruct((8, channels), F32),
            jax.ShapeDtypeStruct((8, n2), F32),
            jax.ShapeDtypeStruct((8, 128), F32),
        ],
        scratch_shapes=[
            pltpu.VMEM((4, BLOCK + 8, channels), F32),
            pltpu.VMEM((4, BLOCK + 8, n2), F32),
            pltpu.VMEM((n2 // 2, channels), F32),
            pltpu.VMEM((BLOCK, BLOCK), F32),
            pltpu.VMEM((BLOCK, BLOCK), F32),
            pltpu.VMEM((BLOCK, channels), F32),
            pltpu.VMEM((128, BLOCK), F32),
        ],
        compiler_params=pltpu.CompilerParams(vmem_limit_bytes=56 * 2**20),
        name="ssd_backward",
    )(dy, x, cx, bc, cbc, dt, cols, segrow, states, *shared)


def ring_place(n):
    dp = lax.axis_index("dp")
    z, y = dp // 2, dp % 2

    def at(place):
        q = (place + 4 * n) % n
        return 2 * q + (q // (n // 2)) * (2 * n - 1 - 4 * q)

    return z + y * (n - 1 - 2 * z), at


def tensor_place():
    t = lax.axis_index("tensor")
    return t, t + 1 - 2 * (t % 2), (t + 2) % 4


def greet(n):
    place, at = ring_place(n)
    _, other, across = tensor_place()
    sem = pltpu.get_barrier_semaphore()
    for target in ({"dp": at(place + 1)}, {"dp": at(place - 1)}, {"tensor": other}, {"tensor": across}):
        pl.semaphore_signal(sem, inc=1, device_id=target, device_id_type=MESH)
    pl.semaphore_wait(sem, 4)


def remote(src, dst, send_sem, recv_sem, target):
    return pltpu.make_async_remote_copy(
        src_ref=src, dst_ref=dst, send_sem=send_sem, recv_sem=recv_sem, device_id=target, device_id_type=MESH
    )


def span(first, count, unit):
    return pl.ds(pl.multiple_of(first, unit), count)


class RingGather:
    def __init__(self, n, parts, keep, sems):
        self.n, self.parts, self.keep = n, parts, keep
        self.send_sem, self.recv_sem = sems
        self.place, self.at = ring_place(n)

    def copy(self, way, part, step):
        sign = 1 - 2 * way
        ref = self.keep(way, part, self.at(self.place - sign * step))
        return remote(
            ref,
            ref,
            self.send_sem.at[way, part, step],
            self.recv_sem.at[way, part, step],
            {"dp": self.at(self.place + sign)},
        )

    def step(self, k):
        for part in range(self.parts):
            for way in (0, 1):
                if k > 0:
                    self.copy(way, part, k - 1).wait_recv()
                if k < self.n - 1:
                    self.copy(way, part, k).start()

    def finish(self):
        for k in range(self.n - 1):
            for part in range(self.parts):
                for way in (0, 1):
                    self.copy(way, part, k).wait_send()


class RowGather:
    def __init__(self, keep, sems):
        self.keep = keep
        self.send_sem, self.recv_sem = sems
        self.me, self.other, self.across = tensor_place()

    def copy(self, kind, part):
        ref = self.keep(part, self.across if kind == 2 else self.me)
        target = self.across if kind == 0 else self.other
        return remote(
            ref, ref, self.send_sem.at[kind, part], self.recv_sem.at[kind, part], {"tensor": target}
        )

    def start(self, part):
        self.copy(0, part).start()
        self.copy(1, part).start()

    def forward(self, part):
        self.copy(0, part).wait_recv()
        self.copy(2, part).start()

    def finish(self, parts):
        for part in range(parts):
            self.copy(1, part).wait_recv()
            self.copy(2, part).wait_recv()
            for kind in range(3):
                self.copy(kind, part).wait_send()


def gather_kernel(
    n, u_ref, g_ref, wzx_ref, wbc_ref, wout_ref, uf_ref, gf_ref, wx_ref, wz_ref, wb_ref, wo_ref,
    u_hold, wzx_hold, wbc_hold, wout_hold, own_sem, *sems,
):
    rows, width = wzx_ref.shape[1:]
    out_rows, out_cols = wout_ref.shape
    seqs, piece, _ = u_ref.shape
    dp = lax.axis_index("dp")
    me, other, _ = tensor_place()
    core = me % 2

    def keep_wide(ref):
        def keep(way, part, d):
            return ref.at[span(d * rows, rows, 16), pl.ds(way * width // 2 + part * width // 4, width // 4)]

        return keep

    def keep_out(way, part, d):
        first = way * out_rows // 2 + part * out_rows // 4
        return wo_ref.at[pl.ds(first, out_rows // 4), span(d * out_cols, out_cols, 128)]

    def keep_small(way, part, d):
        return wb_ref.at[span(d * rows + core * rows // 2 + way * rows // 4, rows // 4, 16), :]

    def keep_rows(part, t):
        ref = uf_ref if part < seqs else gf_ref
        return ref.at[part % seqs, span(t * piece, piece, 16), :]

    moves = [
        (wzx_ref.at[1], wzx_hold.at[1], wx_ref.at[span(dp * rows, rows, 16), :]),
        (wbc_ref, wbc_hold, wb_ref.at[span(dp * rows, rows, 16), :]),
    ]
    moves += [(u_ref.at[s], u_hold.at[s], keep_rows(s, me)) for s in range(seqs)]
    moves += [
        (wzx_ref.at[0], wzx_hold.at[0], wz_ref.at[span(dp * rows, rows, 16), :]),
        (wout_ref, wout_hold, wo_ref.at[:, span(dp * out_cols, out_cols, 128)]),
    ]
    moves += [(g_ref.at[s], u_hold.at[seqs + s], keep_rows(seqs + s, me)) for s in range(seqs)]
    loads = [pltpu.make_async_copy(a, b, own_sem.at[0, i]) for i, (a, b, _) in enumerate(moves)]
    stores = [pltpu.make_async_copy(b, c, own_sem.at[1, i]) for i, (_, b, c) in enumerate(moves)]
    for load in loads:
        load.start()
    greet(n)

    def settle(first, last):
        for load, store in zip(loads[first:last], stores[first:last]):
            load.wait()
            store.start()
        for store in stores[first:last]:
            store.wait()

    x_ring = RingGather(n, 2, keep_wide(wx_ref), sems[0:2])
    small = RingGather(n, 1, keep_small, sems[2:4])
    z_ring = RingGather(n, 2, keep_wide(wz_ref), sems[4:6])
    out_ring = RingGather(n, 2, keep_out, sems[6:8])
    token_rows = RowGather(keep_rows, sems[8:10])
    halves_send, halves_recv = sems[10:12]

    def half(ahead, whose):
        d = (dp + ahead) % n
        ref = wb_ref.at[span(d * rows + whose * rows // 2, rows // 2, 16), :]
        return remote(ref, ref, halves_send.at[ahead], halves_recv.at[ahead], {"tensor": other})

    settle(0, 1)
    x_ring.step(0)
    settle(1, 4)
    small.step(0)
    token_rows.start(0)
    token_rows.start(1)
    settle(4, len(moves))
    for k in range(1, n):
        x_ring.step(k)
        small.step(k)
        if k == n - 1:
            z_ring.step(0)
        if k == 4:
            token_rows.forward(0)
            token_rows.start(2)
        if k == 7:
            token_rows.forward(1)
            token_rows.start(3)
    for ahead in range(1, n):
        half(ahead, core).start()
    for k in range(1, n):
        z_ring.step(k)
        if k == n - 1:
            out_ring.step(0)
        if k == 4:
            token_rows.forward(2)
        if k == 7:
            token_rows.forward(3)
    for k in range(1, n):
        out_ring.step(k)
    for ahead in range(1, n):
        half(ahead, 1 - core).wait_recv()
        half(ahead, core).wait_send()
    for ring in (x_ring, small, z_ring, out_ring):
        ring.finish()
    token_rows.finish(2 * seqs)


def gather_all(n, u, g, w_zx, w_bc, w_out):
    seqs, piece, model = u.shape
    rows, width = w_zx.shape[1:]
    out_rows, out_cols = w_out.shape
    sem = pltpu.SemaphoreType.DMA
    ring = [sem((2, 2, n - 1))] * 2
    anywhere = pl.BlockSpec(memory_space=pl.ANY)
    whole = [
        (seqs, 4 * piece, model),
        (seqs, 4 * piece, model),
        (rows * n, width),
        (rows * n, width),
        (rows * n, w_bc.shape[1]),
        (out_rows, out_cols * n),
    ]
    return pl.pallas_call(
        functools.partial(gather_kernel, n),
        in_specs=[anywhere] * 5,
        out_specs=[anywhere] * 6,
        out_shape=[jax.ShapeDtypeStruct(shape, BF16) for shape in whole],
        scratch_shapes=[
            pltpu.VMEM((2 * seqs, piece, model), BF16),
            pltpu.VMEM(w_zx.shape, BF16),
            pltpu.VMEM(w_bc.shape, BF16),
            pltpu.VMEM(w_out.shape, BF16),
            sem((2, 4 + 2 * seqs)),
        ]
        + ring + [sem((2, 1, n - 1))] * 2 + ring + ring
        + [sem((3, 2 * seqs))] * 2 + [sem((n,))] * 2,
        compiler_params=pltpu.CompilerParams(
            collective_id=0, has_side_effects=True, vmem_limit_bytes=32 * 2**20
        ),
        name="gather_all",
    )(u, g, w_zx, w_bc, w_out)


class RingScatter:
    def __init__(self, n, term, slots, sems):
        self.n, self.term, self.slots = n, term, slots
        self.send_sem, self.recv_sem = sems
        self.place, self.at = ring_place(n)

    def copy(self, way, k):
        sign = 1 - 2 * way
        return remote(
            self.slots.at[way, k],
            self.slots.at[way, k + 1],
            self.send_sem.at[way, k],
            self.recv_sem.at[way, k],
            {"dp": self.at(self.place + sign)},
        )

    def step(self, way, k):
        value = self.term(way, self.at(self.place - (1 - 2 * way) * (1 + k)))

        @pl.when(k == 0)
        def _():
            self.slots[way, 0] = value.astype(BF16)

        @pl.when(k > 0)
        def _():
            self.copy(way, k - 1).wait_recv()

            @pl.when(k < self.n - 1)
            def _():
                self.slots[way, k] = (value + self.slots[way, k].astype(F32)).astype(BF16)

        @pl.when(k < self.n - 1)
        def _():
            self.copy(way, k).start()

        return value

    def last(self, way, value):
        return value + self.slots[way, self.n - 1].astype(F32)

    def finish(self):
        for k in range(self.n - 1):
            for way in (0, 1):
                self.copy(way, k).wait_send()


class RowScatter:
    def __init__(self, parts, term, hold, sems):
        self.parts, self.term, self.hold = parts, term, hold
        self.send_sem, self.recv_sem = sems
        self.me, self.other, self.across = tensor_place()

    def copy(self, kind, part):
        return remote(
            self.hold.at[kind, 0, part],
            self.hold.at[kind, 1, part],
            self.send_sem.at[kind, part],
            self.recv_sem.at[kind, part],
            {"tensor": self.across if kind == 1 else self.other},
        )

    def step(self, j, store):
        stage, part = j // self.parts, j % self.parts
        x, core = self.me // 2, self.me % 2
        value = self.term(2 * ((x + 1 - stage // 2) % 2) + (core + 1 - stage % 2) % 2, part)

        @pl.when(stage == 0)
        def _():
            self.hold[0, 0, part] = value.astype(BF16)
            self.copy(0, part).start()

        @pl.when(stage == 1)
        def _():
            self.copy(0, part).wait_recv()
            self.hold[1, 0, part] = (value + self.hold[0, 1, part].astype(F32)).astype(BF16)
            self.copy(1, part).start()

        @pl.when(stage == 2)
        def _():
            self.hold[2, 0, part] = value.astype(BF16)
            self.copy(2, part).start()

        @pl.when(stage == 3)
        def _():
            self.copy(2, part).wait_recv()
            store(part, value + self.hold[2, 1, part].astype(F32))

    def finish(self, store):
        for part in range(self.parts):
            self.copy(1, part).wait_recv()
            store(part, self.hold[1, 1, part].astype(F32))
            for kind in range(3):
                self.copy(kind, part).wait_send()


def product_term(a_ref, b_ref, count):
    def term(way, d):
        half = b_ref.shape[1] // 2
        return dot_tn(a_ref[:, span(d * count, count, 128)], b_ref[:, pl.ds(way * half, half)])

    return term


def out_kernel(
    n, normed_ref, g_ref, u_ref, dz_ref, wo_ref, mixed_ref, gout_ref, gz_ref, out_slots, z_slots, hold, *sems
):
    seqs, length = mixed_ref.shape[0], normed_ref.shape[0] // mixed_ref.shape[0]
    piece = mixed_ref.shape[1]
    count = g_ref.shape[1] // n
    half = gz_ref.shape[1] // 2
    greet(n)

    def mixed_term(t, part):
        return dot(normed_ref[span(part * length + t * piece, piece, 16), :], wo_ref[...])

    rows = RowScatter(seqs, mixed_term, hold, sems[0:2])
    rings = [
        RingScatter(n, product_term(g_ref, normed_ref, count), out_slots, sems[2:4]),
        RingScatter(n, product_term(u_ref, dz_ref, count), z_slots, sems[4:6]),
    ]

    def store(part, value):
        mixed_ref[part] = value

    def out_step(k, _):
        for way in (0, 1):
            value = rings[0].step(way, k)

            @pl.when(k == n - 1)
            def _():
                gout_ref[pl.ds(way * half, half), :] = rings[0].last(way, value).T

        rows.step(k, store)
        return 0

    def z_step(k, _):
        for way in (0, 1):
            value = rings[1].step(way, k)

            @pl.when(k == n - 1)
            def _():
                gz_ref[:, pl.ds(way * half, half)] = rings[1].last(way, value)

        return 0

    lax.fori_loop(0, n, out_step, 0)
    lax.fori_loop(0, n, z_step, 0)

    def add(part, value):
        mixed_ref[part] += value

    rows.finish(add)
    for ring in rings:
        ring.finish()


def scatter_out(n, piece, normed, g, u, dz, w_out):
    tokens, width = normed.shape
    model = g.shape[1]
    seqs = tokens // (4 * piece)
    count = model // n
    sem = pltpu.SemaphoreType.DMA
    vmem = pl.BlockSpec(memory_space=pltpu.VMEM)
    return pl.pallas_call(
        functools.partial(out_kernel, n),
        in_specs=[vmem] * 5,
        out_specs=[vmem] * 3,
        out_shape=[
            jax.ShapeDtypeStruct((seqs, piece, model), F32),
            jax.ShapeDtypeStruct((width, count), F32),
            jax.ShapeDtypeStruct((count, width), F32),
        ],
        scratch_shapes=[
            pltpu.VMEM((2, n, count, width // 2), BF16),
            pltpu.VMEM((2, n, count, width // 2), BF16),
            pltpu.VMEM((3, 2, seqs, piece, model), BF16),
        ]
        + [sem((3, seqs))] * 2 + [sem((2, n - 1))] * 4,
        compiler_params=pltpu.CompilerParams(
            collective_id=1, has_side_effects=True, vmem_limit_bytes=60 * 2**20
        ),
        name="scatter_out",
    )(normed, g, u, dz, w_out)


def in_kernel(
    n, u_ref, dz_ref, dx_ref, wz_ref, wx_ref, wb_ref, dbc_ref,
    din_ref, gx_ref, gb_ref,
    x_slots, b_slots, hold, bc_hold, low, pair_hold, swap, *sems,
):
    seqs, piece = din_ref.shape[:2]
    tokens, model = u_ref.shape
    length = tokens // seqs
    count = model // n
    half = gx_ref.shape[1] // 2
    me, other, across = tensor_place()
    core = me % 2
    greet(n)

    def bc_term(t, part):
        return dbc_ref[span(part * length + t * piece, piece, 16), :].astype(F32)

    def in_term(t, part):
        at = span(part * length + t * piece, piece, 16)
        return dot_nt(dz_ref[at, :], wz_ref[...]) + dot_nt(dx_ref[at, :], wx_ref[...])

    def b_term(way, d):
        cols = u_ref.shape[1] // n // 4
        total = 0.0
        for t, which in ((me, 0), (other, 1)):
            for part in range(seqs):
                a = u_ref[span(part * length + t * piece, piece, 16), span(d * count + core * count // 2, count // 2, 128)]
                total = total + dot_tn(a, low[which, part])
        return total[way * cols : (way + 1) * cols]

    bc_rows = RowScatter(seqs, bc_term, bc_hold, sems[0:2])
    in_rows = RowScatter(seqs, in_term, hold, sems[2:4])
    x_ring = RingScatter(n, product_term(u_ref, dx_ref, count), x_slots, sems[4:6])
    b_ring = RingScatter(n, b_term, b_slots, sems[6:8])
    pair_send, pair_recv, swap_send, swap_recv = sems[8:12]

    def bc_store(part, value):
        pair_hold[part] = value

    def bc_step(j, _):
        bc_rows.step(j, bc_store)
        return 0

    lax.fori_loop(0, 4 * seqs, bc_step, 0)

    def store(part, value):
        din_ref[part] = value

    def step(k, _):
        for way in (0, 1):
            value = x_ring.step(way, k)

            @pl.when(k == n - 1)
            def _():
                gx_ref[:, pl.ds(way * half, half)] = x_ring.last(way, value)

        in_rows.step(k, store)
        return 0

    lax.fori_loop(0, n, step, 0)

    def bc_add(part, value):
        low[0, part] = (pair_hold[part] + value).astype(BF16)

    bc_rows.finish(bc_add)
    pair = remote(low.at[0], low.at[1], pair_send, pair_recv, {"tensor": other})
    pair.start()
    pair.wait_recv()

    def b_step(k, _):
        for way in (0, 1):
            value = b_ring.step(way, k)

            @pl.when(k == n - 1)
            def _():
                swap[0, pl.ds(way * count // 4, count // 4), :] = b_ring.last(way, value)

        return 0

    lax.fori_loop(0, n, b_step, 0)
    cross = remote(swap.at[0], swap.at[1], swap_send.at[0], swap_recv.at[0], {"tensor": across})
    cross.start()

    def add(part, value):
        din_ref[part] += value + dot_nt(low[0, part], wb_ref[...])

    in_rows.finish(add)
    cross.wait_recv()
    swap[2] = swap[0] + swap[1]
    fold = remote(swap.at[2], swap.at[3], swap_send.at[1], swap_recv.at[1], {"tensor": other})
    fold.start()
    gb_ref[span(core * count // 2, count // 2, 16), :] = swap[2]
    fold.wait_recv()
    gb_ref[span((1 - core) * count // 2, count // 2, 16), :] = swap[3]
    pair.wait_send()
    cross.wait_send()
    fold.wait_send()
    for ring in (x_ring, b_ring):
        ring.finish()


def scatter_in(n, piece, u, dz, dx, w_z, w_x, w_bc, dbc):
    tokens, model = u.shape
    width = dz.shape[1]
    small = dbc.shape[1]
    seqs = tokens // (4 * piece)
    count = model // n
    sem = pltpu.SemaphoreType.DMA
    vmem = pl.BlockSpec(memory_space=pltpu.VMEM)
    return pl.pallas_call(
        functools.partial(in_kernel, n),
        in_specs=[vmem] * 7,
        out_specs=[vmem] * 3,
        out_shape=[
            jax.ShapeDtypeStruct((seqs, piece, model), F32),
            jax.ShapeDtypeStruct((count, width), F32),
            jax.ShapeDtypeStruct((count, small), F32),
        ],
        scratch_shapes=[
            pltpu.VMEM((2, n, count, width // 2), BF16),
            pltpu.VMEM((2, n, count // 4, small), BF16),
            pltpu.VMEM((3, 2, seqs, piece, model), BF16),
            pltpu.VMEM((3, 2, seqs, piece, small), BF16),
            pltpu.VMEM((2, seqs, piece, small), BF16),
            pltpu.VMEM((seqs, piece, small), F32),
            pltpu.VMEM((4, count // 2, small), F32),
        ]
        + [sem((3, seqs))] * 4 + [sem((2, n - 1))] * 4 + [sem(())] * 2 + [sem((2,))] * 2,
        compiler_params=pltpu.CompilerParams(
            collective_id=2, has_side_effects=True, vmem_limit_bytes=62 * 2**20
        ),
        name="scatter_in",
    )(u, dz, dx, w_z, w_x, w_bc, dbc)


def rms_scale(values):
    return lax.rsqrt(jnp.mean(values * values, axis=-1, keepdims=True) + EPS)


def gather_plain(u, g, w_zx, w_bc, w_out):
    w_zx = lax.all_gather(w_zx, "dp", axis=1, tiled=True)
    return (
        lax.all_gather(u, "tensor", axis=1, tiled=True),
        lax.all_gather(g, "tensor", axis=1, tiled=True),
        w_zx[1],
        w_zx[0],
        lax.all_gather(w_bc, "dp", axis=0, tiled=True),
        lax.all_gather(w_out, "dp", axis=1, tiled=True),
    )


def rows_of(values, piece):
    by_seq = values.reshape(-1, 4 * piece, values.shape[-1])
    return lax.psum_scatter(by_seq, "tensor", scatter_dimension=1, tiled=True)


def scatter_out_plain(piece, normed, g, u, dz, w_out):
    return (
        rows_of(dot(normed, w_out), piece),
        lax.psum_scatter(dot_tn(normed, g), "dp", scatter_dimension=1, tiled=True),
        lax.psum_scatter(dot_tn(u, dz), "dp", scatter_dimension=0, tiled=True),
    )


def scatter_in_plain(piece, u, dz, dx, w_z, w_x, w_bc, dbc):
    low = lax.psum(dbc.astype(F32), "tensor").astype(BF16)
    d_in = rows_of(dot_nt(dz, w_z) + dot_nt(dx, w_x), piece)
    first = lax.axis_index("tensor") * piece
    own = lax.dynamic_slice_in_dim(low.reshape(-1, 4 * piece, low.shape[1]), first, piece, 1)
    d_in = d_in + jnp.einsum("slc,dc->sld", own, w_bc, preferred_element_type=F32)
    return (
        d_in,
        lax.psum_scatter(dot_tn(u, dx), "dp", scatter_dimension=0, tiled=True),
        lax.psum_scatter(dot_tn(u, low), "dp", scatter_dimension=0, tiled=True),
    )


def local(
    n_dp,
    n_tensor,
    hidden,
    pre_gain,
    w_zx,
    w_bcdt,
    conv_x,
    conv_bc,
    dt_bias,
    a_log,
    d_skip,
    gate_gain,
    w_out,
    cotangent,
    segments,
):
    seqs, piece, model = hidden.shape
    length = segments.shape[1]
    tokens = seqs * length
    heads = dt_bias.shape[0]
    channels = conv_x.shape[1]
    n2 = conv_bc.shape[1]
    columns = w_bcdt.shape[1]
    tensor = lax.axis_index("tensor")
    kernels = n_dp == 8 and n_tensor == 4

    x_piece = hidden.astype(F32)
    scale_in = rms_scale(x_piece)
    u_piece = (x_piece * scale_in * pre_gain).astype(BF16)
    w_bc_piece = jnp.pad(w_bcdt, ((0, 0), (0, -columns % 128)))
    gather = functools.partial(gather_all, n_dp) if kernels else gather_plain
    u, g, w_x, w_z, w_bc, w_o = gather(u_piece, cotangent, w_zx, w_bc_piece, w_out)
    u = u.reshape(tokens, model)
    g = g.reshape(tokens, model)

    x = dot(u, w_x).reshape(seqs, length, channels)
    z = dot(u, w_z)
    bc_dt = dot(u, w_bc).reshape(seqs, length, -1)
    bc = bc_dt[:, :, :n2]
    dt = lax.dynamic_slice_in_dim(bc_dt, n2 + tensor * heads, heads, 2)

    cols = column_masks(segments)
    segrow = segments.astype(F32)[:, None, :]
    spread = jnp.asarray(spread_matrix(heads, channels), BF16)
    skip = jnp.repeat(d_skip, channels // heads)[None]
    shared = (conv_x, conv_bc, dt_bias[None], a_log[None], skip, spread)
    y, cx, cbc, states = ssd_forward(x, bc, dt, cols, segrow, shared)

    d_normed = dot_nt(g, w_o)
    sig_z = sigmoid(z)
    silu_z = z * sig_z
    y_flat = y.reshape(tokens, channels)
    gated = y_flat * silu_z
    scaled = d_normed * gate_gain
    sums = jnp.stack([jnp.sum(gated * gated, axis=1), jnp.sum(scaled * gated, axis=1)])
    sums = lax.psum(sums, "tensor") / (channels * n_tensor)
    inverse = lax.rsqrt(sums[0] + EPS)[:, None]
    normed = (gated * inverse * gate_gain).astype(BF16)
    grad_gate = jnp.sum(d_normed * gated * inverse, axis=0)
    d_gated = inverse * scaled - gated * inverse**3 * sums[1][:, None]
    dy = (d_gated * silu_z).astype(BF16)
    dz = (d_gated * y_flat * (sig_z * (1.0 + z * (1.0 - sig_z)))).astype(BF16)

    scatter = functools.partial(scatter_out, n_dp) if kernels else scatter_out_plain
    mixed, grad_out, grad_z = scatter(piece, normed, g, u, dz, w_o)
    out_hidden = (x_piece + mixed).astype(BF16)

    dx, d_bc, d_dt, gx, gbc, gh = ssd_backward(
        dy.reshape(seqs, length, channels), x, cx, bc, cbc, dt, cols, segrow, states, shared
    )
    d_dt = lax.dynamic_update_slice_in_dim(
        jnp.zeros((seqs, length, w_bc.shape[1] - n2), F32), d_dt, tensor * heads, 2
    )
    dbc = jnp.concatenate([d_bc, d_dt], axis=2).astype(BF16).reshape(tokens, -1)

    scatter = functools.partial(scatter_in, n_dp) if kernels else scatter_in_plain
    d_in, grad_x, grad_bc = scatter(piece, u, dz, dx.reshape(tokens, channels), w_z, w_x, w_bc, dbc)

    grad_pre = jnp.sum(d_in * x_piece * scale_in, axis=(0, 1))
    gain_grad = d_in * pre_gain
    d_hidden = cotangent.astype(F32) + scale_in * gain_grad - x_piece * scale_in**3 * jnp.mean(
        gain_grad * x_piece, axis=-1, keepdims=True
    )
    grad_skip = gx[5].reshape(heads, -1).sum(axis=1)
    small_dp = lax.psum((gx[:5], gh[0, :heads], gh[1, :heads], grad_skip, grad_gate), "dp")
    small_all = lax.psum((gbc[:5], grad_pre), ("dp", "tensor"))
    return (
        out_hidden,
        d_hidden,
        small_all[1],
        jnp.stack([grad_z, grad_x]),
        grad_bc[:, :columns],
        small_dp[0],
        small_all[0],
        small_dp[1],
        small_dp[2],
        small_dp[3],
        small_dp[4],
        grad_out,
    )


def solution(mesh):
    placed = (
        P("dp", "tensor", None),
        P(),
        P(None, "dp", "tensor"),
        P("dp", None),
        P(None, "tensor"),
        P(),
        P("tensor"),
        P("tensor"),
        P("tensor"),
        P("tensor"),
        P("tensor", "dp"),
        P("dp", "tensor", None),
        P("dp", None),
    )
    return jax.shard_map(
        functools.partial(local, mesh.shape["dp"], mesh.shape["tensor"]),
        mesh=mesh,
        in_specs=placed,
        out_specs=(
            P("dp", "tensor", None),
            P("dp", "tensor", None),
            P(),
            P(None, "dp", "tensor"),
            P("dp", None),
            P(None, "tensor"),
            P(),
            P("tensor"),
            P("tensor"),
            P("tensor"),
            P("tensor"),
            P("tensor", "dp"),
        ),
        check_vma=False,
    )
```

```python
import functools

import jax
import jax.numpy as jnp
import numpy as np
from jax import lax
from jax.experimental import pallas as pl
from jax.experimental.pallas import tpu as pltpu
from jax.sharding import PartitionSpec as P

MESH = pl.DeviceIdType.MESH
EPS = 1e-05
BLOCK = 256
F32 = jnp.float32
BF16 = jnp.bfloat16
EXACT = lax.Precision.HIGHEST
LOG2E = 1.4426950408889634
NEG = -1e30


def sigmoid(v):
    return 0.5 * jnp.tanh(0.5 * v) + 0.5


def split3(v):
    hi = v.astype(BF16)
    rest = v - hi.astype(F32)
    mid = rest.astype(BF16)
    low = (rest - mid.astype(F32)).astype(BF16)
    return hi, mid, low


def dot(a, b):
    return jnp.dot(a, b, preferred_element_type=F32)


def dot_nt(a, b):
    return lax.dot_general(a, b, (((1,), (1,)), ((), ())), preferred_element_type=F32)


def dot_tn(a, b):
    return lax.dot_general(a, b, (((0,), (0,)), ((), ())), preferred_element_type=F32)


def softplus(v):
    return jnp.maximum(v, 0.0) + jnp.log1p(jnp.exp(-jnp.abs(v)))


def head_sizes(raw, dt_bias, a_log):
    q = raw.shape[0]
    tri = (
        lax.broadcasted_iota(jnp.int32, (q, q), 0) >= lax.broadcasted_iota(jnp.int32, (q, q), 1)
    ).astype(F32)
    biased = raw + dt_bias
    step = softplus(biased)
    rate = -jnp.exp(a_log) * step
    cum = jnp.dot(tri, rate, precision=EXACT, preferred_element_type=F32) * LOG2E
    return biased, step, rate, cum


def expand(values, spread):
    hi, mid, low = split3(values)
    return dot(hi, spread) + dot(mid, spread) + dot(low, spread)


def gather_heads(values, spread):
    hi, mid, _ = split3(values)
    return dot_nt(hi, spread) + dot_nt(mid, spread)


def exact_nt(a, b):
    a_hi, a_mid, _ = split3(a)
    b_hi, b_mid, _ = split3(b)
    return dot_nt(a_hi, b_hi) + dot_nt(a_hi, b_mid) + dot_nt(a_mid, b_hi)


def transpose_heads(values):
    pad = jnp.concatenate(
        [values, jnp.zeros((values.shape[0], 128 - values.shape[1]), F32)], axis=1
    )
    return pad.T


def forward_kernel(
    x_ref, bc_ref, dt_ref, cols_ref, segrow_ref, taps_x_ref, taps_bc_ref, bias_ref, alog_ref, skip_ref, spread_ref,
    y_ref, cx_ref, cbc_ref, states_ref,
    xs, bs, state, mask_bias,
):
    block = pl.program_id(1)
    q = BLOCK
    heads = dt_ref.shape[-1]
    channels = x_ref.shape[-1]
    width = channels // heads

    @pl.when(block == 0)
    def _():
        xs[0:8, :] = jnp.zeros((8, xs.shape[1]), F32)
        bs[0:8, :] = jnp.zeros((8, bs.shape[1]), F32)
        state[...] = jnp.zeros_like(state)

    cols = cols_ref[0]
    lag_masks = [cols[:, k : k + 1] for k in range(3)]
    reads, last, seg = cols[:, 3:4], cols[:, 4:5], cols[:, 5:6]

    def conv(value_ref, hold, taps_ref):
        hold[8 : 8 + q, :] = value_ref[0]
        out = taps_ref[4:5, :] + taps_ref[3:4, :] * hold[8 : 8 + q, :]
        for lag in (1, 2, 3):
            out = out + (lag_masks[lag - 1] * hold[8 - lag : 8 - lag + q, :]) * taps_ref[3 - lag : 4 - lag, :]
        hold[0:8, :] = hold[q : q + 8, :]
        return out

    cbc = conv(bc_ref, bs, taps_bc_ref)
    cbc_ref[0] = cbc
    bc = cbc * sigmoid(cbc)
    n = bc.shape[1] // 2
    scores = exact_nt(bc[:, n:], bc[:, :n])
    b_mat, c_mat = bc[:, :n].astype(BF16), bc[:, n:].astype(BF16)

    cx = conv(x_ref, xs, taps_x_ref)
    cx_ref[0] = cx
    xb = (cx * sigmoid(cx)).astype(BF16)

    biased, step, rate, cum = head_sizes(dt_ref[0], bias_ref[...], alog_ref[...])
    cum_end = cum[q - 1 : q, :]
    spread = spread_ref[...]
    reads_e = expand(reads * jnp.exp2(cum), spread)
    to_end_e = expand(last * jnp.exp2(cum_end - cum) * step, spread)
    carry = jnp.exp2(cum_end)
    carry_e = expand(jnp.broadcast_to(carry, (8, heads)), spread)[0:1]
    source = transpose_heads(cum - jnp.log(step) * LOG2E)

    rows = lax.broadcasted_iota(jnp.int32, (q, q), 0)
    places = lax.broadcasted_iota(jnp.int32, (q, q), 1)
    mask_bias[...] = jnp.where((seg == segrow_ref[0]) & (rows >= places), 0.0, NEG)

    st = state[...].astype(BF16)
    states_ref[0, 0] = st
    outside = dot(c_mat, st) * reads_e + skip_ref[...] * xb.astype(F32)

    half = q // 2
    lane = lax.broadcasted_iota(jnp.int32, (1, 2 * width), 1)
    for pair in range(heads // 2):
        at = slice(pair * 2 * width, (pair + 1) * 2 * width)
        xp = xb[:, at]
        both = []
        for h in (2 * pair, 2 * pair + 1):
            col = cum[:, h : h + 1]
            row = source[h : h + 1, :]
            top = (
                jnp.exp2((col[:half] - row[:, :half]) + mask_bias[:half, :half]) * scores[:half, :half]
            ).astype(BF16)
            low = (jnp.exp2((col[half:] - row) + mask_bias[half:, :]) * scores[half:, :]).astype(BF16)
            both.append(jnp.concatenate([dot(top, xp[:half]), dot(low, xp)], axis=0))
        y_ref[0, :, at] = outside[:, at] + jnp.where(lane < width, both[0], both[1])

    scaled = (xb.astype(F32) * to_end_e).astype(BF16)
    state[...] = carry_e * state[...] + dot_tn(b_mat, scaled)


def backward_block(
    seq, step_id, dy_ref, x_ref, cx_ref, bc_ref, cbc_ref, dt_ref, cols_ref, segrow_ref, states_ref,
    taps_x_ref, taps_bc_ref, bias_ref, alog_ref, skip_ref, spread_ref,
    dx_ref, dbc_ref, gx_ref, gbc_ref, gh_ref,
    ds_x, ds_bc, d_state, mask_bias, d_scores, d_in, row_sums,
):
    q = BLOCK
    heads = dt_ref.shape[-1]
    channels = x_ref.shape[-1]
    width = channels // heads

    @pl.when(step_id == 0)
    def _():
        ds_x[:, q : q + 8, :] = jnp.zeros((3, 8, channels), F32)
        ds_bc[:, q : q + 8, :] = jnp.zeros((3, 8, ds_bc.shape[2]), F32)
        d_state[...] = jnp.zeros_like(d_state)

    @pl.when((step_id == 0) & (seq == 0))
    def _():
        gx_ref[...] = jnp.zeros_like(gx_ref)
        gbc_ref[...] = jnp.zeros_like(gbc_ref)
        gh_ref[...] = jnp.zeros_like(gh_ref)

    cols = cols_ref[0]
    lag_masks = [cols[:, k : k + 1] for k in range(3)]
    reads, last, seg = cols[:, 3:4], cols[:, 4:5], cols[:, 5:6]

    cbc = cbc_ref[0]
    sig_bc = sigmoid(cbc)
    bc = cbc * sig_bc
    n = bc.shape[1] // 2
    scores = exact_nt(bc[:, :n], bc[:, n:])
    b_mat, c_mat = bc[:, :n].astype(BF16), bc[:, n:].astype(BF16)
    cx = cx_ref[0]
    xb = (cx * sigmoid(cx)).astype(BF16)
    dyb = dy_ref[0]

    biased, step, rate, cum = head_sizes(dt_ref[0], bias_ref[...], alog_ref[...])
    cum_end = cum[q - 1 : q, :]
    spread = spread_ref[...]
    carry_e = expand(jnp.broadcast_to(jnp.exp2(cum_end), (8, heads)), spread)[0:1]
    source = cum - jnp.log(step) * LOG2E
    target = transpose_heads(cum)

    rows = lax.broadcasted_iota(jnp.int32, (q, q), 0)
    places = lax.broadcasted_iota(jnp.int32, (q, q), 1)
    mask_bias[...] = jnp.where((seg == segrow_ref[0]) & (rows <= places), 0.0, NEG)

    st = states_ref[0, 0]
    dst = d_state[...].astype(BF16)
    dye = dyb.astype(F32) * expand(reads * jnp.exp2(cum), spread)
    out_h = gather_heads(dye * dot(c_mat, st), spread)
    dye = dye.astype(BF16)
    d_c = dot_nt(dye, st)
    carried = carry_e * jnp.sum(d_state[...] * st.astype(F32), axis=0, keepdims=True)
    d_state[...] = carry_e * d_state[...] + dot_tn(c_mat, dye)
    to_end_e = expand(last * jnp.exp2(cum_end - cum) * step, spread)
    d_b = dot_nt((xb.astype(F32) * to_end_e).astype(BF16), dst)
    dx_st = dot(b_mat, dst) * to_end_e
    state_h = gather_heads(xb.astype(F32) * dx_st, spread)
    d_in[...] = dx_st

    half = q // 2
    lane = lax.broadcasted_iota(jnp.int32, (1, 2 * width), 1)
    d_scores[...] = jnp.zeros_like(d_scores)
    head_lane = lax.broadcasted_iota(jnp.int32, (1, heads), 1)
    col_sums = jnp.zeros((q, heads), F32)
    for pair in range(heads // 2):
        at = slice(pair * 2 * width, (pair + 1) * 2 * width)
        xp, dyp = xb[:, at], dyb[:, at]
        both = []
        for which in (0, 1):
            h = 2 * pair + which
            mine = lane < width if which == 0 else lane >= width
            xm = jnp.where(mine, xp, jnp.zeros_like(xp))
            col = source[:, h : h + 1]
            row = target[h : h + 1, :]
            top = jnp.exp2((row - col[:half]) + mask_bias[:half, :])
            low = jnp.exp2((row[:, half:] - col[half:]) + mask_bias[half:, half:])
            d_top = top * dot_nt(xm[:half], dyp)
            d_low = low * dot_nt(xm[half:], dyp[half:])
            d_scores[:half, :] += d_top
            d_scores[half:, half:] += d_low
            m_top = d_top * scores[:half, :]
            m_low = d_low * scores[half:, half:]
            late = jnp.sum(m_top[:, half:], axis=0, keepdims=True) + jnp.sum(m_low, axis=0, keepdims=True)
            row_sums[h : h + 1, :half] = jnp.sum(m_top[:, :half], axis=0, keepdims=True)
            row_sums[h : h + 1, half:] = late
            here = jnp.concatenate(
                [
                    jnp.sum(m_top[:, :half] + m_top[:, half:], axis=1, keepdims=True),
                    jnp.sum(m_low, axis=1, keepdims=True),
                ],
                axis=0,
            )
            col_sums = jnp.where(head_lane == h, here, col_sums)
            top = (top * scores[:half, :]).astype(BF16)
            low = (low * scores[half:, half:]).astype(BF16)
            both.append(jnp.concatenate([dot(top, dyp), dot(low, dyp[half:])], axis=0))
        d_in[:, at] += jnp.where(lane < width, both[0], both[1])

    dsb = d_scores[...].astype(BF16)
    d_b = d_b + dot(dsb, c_mat)
    d_c = d_c + dot_tn(dsb, b_mat)

    used_h = col_sums + state_h
    diff_h = row_sums[...].T[:, :heads] - col_sums + out_h
    from_here = (rows <= places).astype(F32)
    before = (rows > places).astype(F32)
    d_rate = (
        jnp.dot(from_here, diff_h, precision=EXACT, preferred_element_type=F32)
        + jnp.dot(before, state_h, precision=EXACT, preferred_element_type=F32)
        + gather_heads(jnp.broadcast_to(carried, (8, channels)), spread)[0:1]
    )
    sig_dt = sigmoid(biased)
    ratio = jnp.where(step < 1e-30, 1.0, sig_dt / jnp.maximum(step, 1e-30))
    d_raw = used_h * ratio - jnp.exp(alog_ref[...]) * sig_dt * d_rate
    lanes = dbc_ref.shape[2] - 2 * n
    mine = lax.broadcasted_iota(jnp.int32, (heads, lanes), 0) + lax.axis_index("tensor") * heads
    own = (lax.broadcasted_iota(jnp.int32, (heads, lanes), 1) == mine).astype(BF16)
    dbc_ref[0, :, 2 * n :] = dot(d_raw.astype(BF16), own).astype(BF16)
    gh_ref[0:1, :heads] += jnp.sum(d_raw, axis=0, keepdims=True)
    gh_ref[1:2, :heads] += jnp.sum(d_rate * rate, axis=0, keepdims=True)

    def conv_back(d_out, value_ref, hold, taps_ref, grad_ref):
        value = value_ref[0].astype(F32)
        d_value = d_out * taps_ref[3:4, :]
        grad_ref[3:4, :] += jnp.sum(value * d_out, axis=0, keepdims=True)
        grad_ref[4:5, :] += jnp.sum(d_out, axis=0, keepdims=True)
        for lag in (1, 2, 3):
            hold[lag - 1, 0:q, :] = lag_masks[lag - 1] * d_out
            moved = hold[lag - 1, lag : lag + q, :]
            d_value = d_value + moved * taps_ref[3 - lag : 4 - lag, :]
            grad_ref[3 - lag : 4 - lag, :] += jnp.sum(value * moved, axis=0, keepdims=True)
            hold[lag - 1, q : q + 8, :] = hold[lag - 1, 0:8, :]
        return d_value

    d_bc = jnp.concatenate([d_b, d_c], axis=1) * (sig_bc * (1.0 + cbc * (1.0 - sig_bc)))
    dbc_ref[0, :, : 2 * n] = conv_back(d_bc, bc_ref, ds_bc, taps_bc_ref, gbc_ref).astype(BF16)
    dyf = dy_ref[0].astype(F32)
    cx = cx_ref[0]
    sig_x = sigmoid(cx)
    gx_ref[5:6, :] += jnp.sum(dyf * (cx * sig_x).astype(BF16).astype(F32), axis=0, keepdims=True)
    d_cx = (d_in[...] + skip_ref[...] * dyf) * (sig_x * (1.0 + cx * (1.0 - sig_x)))
    dx_ref[0] = conv_back(d_cx, x_ref, ds_x, taps_x_ref, gx_ref).astype(BF16)


def column_masks(segments):
    seqs, length = segments.shape
    blocks = length // BLOCK
    lags = []
    for lag in (1, 2, 3):
        earlier = jnp.pad(segments, ((0, 0), (lag, 0)), constant_values=-1)[:, :length]
        lags.append(earlier == segments)
    grouped = segments.reshape(seqs, blocks, BLOCK)
    before = jnp.pad(segments, ((0, 0), (1, 0)), constant_values=-1)[:, :length].reshape(seqs, blocks, BLOCK)
    reads = (grouped == before[:, :, :1]).reshape(seqs, length)
    last = (grouped == grouped[:, :, -1:]).reshape(seqs, length)
    stacked = [m.astype(F32) for m in (*lags, reads, last, segments)]
    stacked += [jnp.zeros_like(stacked[0])] * 2
    return jnp.stack(stacked, axis=-1)


def spread_matrix(heads, channels):
    width = channels // heads
    return (np.arange(heads)[:, None] == np.arange(channels)[None, :] // width).astype(np.float32)


def shared_specs(channels, n2, heads):
    full = lambda *shape: pl.BlockSpec(shape, lambda s, c: (0,) * len(shape))
    return [full(5, channels), full(5, n2), full(1, heads), full(1, heads), full(1, channels), full(heads, channels)]


def ssd_forward(x, bc, dt, cols, segrow, shared):
    seqs, length, channels = x.shape
    n2, heads = bc.shape[2], dt.shape[2]
    blocks = length // BLOCK
    tok = lambda w: pl.BlockSpec((1, BLOCK, w), lambda s, c: (s, c, 0))
    return pl.pallas_call(
        forward_kernel,
        grid=(seqs, blocks),
        in_specs=[tok(channels), tok(n2), tok(heads), tok(8), pl.BlockSpec((1, 1, BLOCK), lambda s, c: (s, 0, c))]
        + shared_specs(channels, n2, heads),
        out_specs=[tok(channels), tok(channels), tok(n2),
                   pl.BlockSpec((1, 1, n2 // 2, channels), lambda s, c: (s, c, 0, 0))],
        out_shape=[
            jax.ShapeDtypeStruct((seqs, length, channels), F32),
            jax.ShapeDtypeStruct((seqs, length, channels), F32),
            jax.ShapeDtypeStruct((seqs, length, n2), F32),
            jax.ShapeDtypeStruct((seqs, blocks, n2 // 2, channels), BF16),
        ],
        scratch_shapes=[
            pltpu.VMEM((BLOCK + 8, channels), F32),
            pltpu.VMEM((BLOCK + 8, n2), F32),
            pltpu.VMEM((n2 // 2, channels), F32),
            pltpu.VMEM((BLOCK, BLOCK), F32),
        ],
        compiler_params=pltpu.CompilerParams(vmem_limit_bytes=48 * 2**20),
        name="ssd_forward",
    )(x, bc, dt, cols, segrow, *shared)


def backward_kernel(*refs):
    backward_block(pl.program_id(0), pl.program_id(1), *refs)


def backward_scratch(channels, n2):
    return [
        pltpu.VMEM((3, BLOCK + 8, channels), F32),
        pltpu.VMEM((3, BLOCK + 8, n2), F32),
        pltpu.VMEM((n2 // 2, channels), F32),
        pltpu.VMEM((BLOCK, BLOCK), F32),
        pltpu.VMEM((BLOCK, BLOCK), F32),
        pltpu.VMEM((BLOCK, channels), F32),
        pltpu.VMEM((128, BLOCK), F32),
    ]


def backward_specs(channels, n2, heads, small, place):
    tok = lambda w: pl.BlockSpec((1, BLOCK, w), lambda *i: (*place(*i), 0))
    full = lambda *shape: pl.BlockSpec(shape, lambda *i: (0,) * len(shape))
    ins = [tok(channels)] * 3 + [tok(n2)] * 2 + [
        tok(heads),
        tok(8),
        pl.BlockSpec((1, 1, BLOCK), lambda *i: (place(*i)[0], 0, place(*i)[1])),
        pl.BlockSpec((1, 1, n2 // 2, channels), lambda *i: (*place(*i), 0, 0)),
        full(5, channels),
        full(5, n2),
        full(1, heads),
        full(1, heads),
        full(1, channels),
        full(heads, channels),
    ]
    return ins, [tok(channels), tok(small), full(8, channels), full(8, n2), full(8, 128)]


def backward_outs(seqs, length, channels, n2, small):
    return [
        jax.ShapeDtypeStruct((seqs, length, channels), BF16),
        jax.ShapeDtypeStruct((seqs, length, small), BF16),
        jax.ShapeDtypeStruct((8, channels), F32),
        jax.ShapeDtypeStruct((8, n2), F32),
        jax.ShapeDtypeStruct((8, 128), F32),
    ]


def ssd_backward(small, dy, x, cx, bc, cbc, dt, cols, segrow, states, shared):
    seqs, length, channels = x.shape
    n2, heads = bc.shape[2], dt.shape[2]
    blocks = length // BLOCK
    ins, outs = backward_specs(channels, n2, heads, small, lambda s, c: (s, blocks - 1 - c))
    return pl.pallas_call(
        backward_kernel,
        grid=(seqs, blocks),
        in_specs=ins,
        out_specs=outs,
        out_shape=backward_outs(seqs, length, channels, n2, small),
        scratch_shapes=backward_scratch(channels, n2),
        compiler_params=pltpu.CompilerParams(vmem_limit_bytes=56 * 2**20),
        name="ssd_backward",
    )(dy, x, cx, bc, cbc, dt, cols, segrow, states, *shared)


def ring_place(n):
    dp = lax.axis_index("dp")
    z, y = dp // 2, dp % 2

    def at(place):
        q = (place + 4 * n) % n
        return 2 * q + (q // (n // 2)) * (2 * n - 1 - 4 * q)

    return z + y * (n - 1 - 2 * z), at


def tensor_place():
    t = lax.axis_index("tensor")
    return t, t + 1 - 2 * (t % 2), (t + 2) % 4


def greet(n, more=()):
    place, at = ring_place(n)
    _, other, across = tensor_place()
    sem = pltpu.get_barrier_semaphore()
    targets = [{"dp": at(place + 1)}, {"dp": at(place - 1)}, {"tensor": other}, {"tensor": across}, *more]
    for target in targets:
        pl.semaphore_signal(sem, inc=1, device_id=target, device_id_type=MESH)
    pl.semaphore_wait(sem, len(targets))


def remote(src, dst, send_sem, recv_sem, target):
    return pltpu.make_async_remote_copy(
        src_ref=src, dst_ref=dst, send_sem=send_sem, recv_sem=recv_sem, device_id=target, device_id_type=MESH
    )


def span(first, count, unit):
    return pl.ds(pl.multiple_of(first, unit), count)


class RingGather:
    def __init__(self, n, parts, keep, sems):
        self.n, self.parts, self.keep = n, parts, keep
        self.send_sem, self.recv_sem = sems
        self.place, self.at = ring_place(n)

    def copy(self, way, part, step):
        sign = 1 - 2 * way
        ref = self.keep(way, part, self.at(self.place - sign * step))
        return remote(
            ref,
            ref,
            self.send_sem.at[way, part, step],
            self.recv_sem.at[way, part, step],
            {"dp": self.at(self.place + sign)},
        )

    def step(self, k):
        for part in range(self.parts):
            for way in (0, 1):
                if k > 0:
                    self.copy(way, part, k - 1).wait_recv()
                if k < self.n - 1:
                    self.copy(way, part, k).start()

    def finish(self):
        for k in range(self.n - 1):
            for part in range(self.parts):
                for way in (0, 1):
                    self.copy(way, part, k).wait_send()


class RowGather:
    def __init__(self, keep, sems):
        self.keep = keep
        self.send_sem, self.recv_sem = sems
        self.me, self.other, self.across = tensor_place()

    def copy(self, kind, part):
        ref = self.keep(part, self.across if kind == 2 else self.me)
        target = self.across if kind == 0 else self.other
        return remote(
            ref, ref, self.send_sem.at[kind, part], self.recv_sem.at[kind, part], {"tensor": target}
        )

    def start(self, part):
        self.copy(0, part).start()
        self.copy(1, part).start()

    def forward(self, part):
        self.copy(0, part).wait_recv()
        self.copy(2, part).start()

    def finish(self, parts):
        for part in range(parts):
            self.copy(1, part).wait_recv()
            self.copy(2, part).wait_recv()
            for kind in range(3):
                self.copy(kind, part).wait_send()


def gather_kernel(
    n, u_ref, g_ref, wzx_ref, wbc_ref, wout_ref, uf_ref, gf_ref, wx_ref, wz_ref, wb_ref, wo_ref,
    u_hold, wzx_hold, wbc_hold, wout_hold, own_sem, *sems,
):
    rows, width = wzx_ref.shape[1:]
    out_rows, out_cols = wout_ref.shape
    seqs, piece, _ = u_ref.shape
    dp = lax.axis_index("dp")
    me, other, _ = tensor_place()
    core = me % 2

    def keep_wide(ref):
        def keep(way, part, d):
            return ref.at[span(d * rows, rows, 16), pl.ds(way * width // 2 + part * width // 4, width // 4)]

        return keep

    def keep_out(way, part, d):
        first = way * out_rows // 2 + part * out_rows // 4
        return wo_ref.at[pl.ds(first, out_rows // 4), span(d * out_cols, out_cols, 128)]

    def keep_small(way, part, d):
        return wb_ref.at[span(d * rows + core * rows // 2 + way * rows // 4, rows // 4, 16), :]

    def keep_rows(part, t):
        ref = uf_ref if part < seqs else gf_ref
        return ref.at[part % seqs, span(t * piece, piece, 16), :]

    moves = [
        (wzx_ref.at[1], wzx_hold.at[1], wx_ref.at[span(dp * rows, rows, 16), :]),
        (wbc_ref, wbc_hold, wb_ref.at[span(dp * rows, rows, 16), :]),
    ]
    moves += [(u_ref.at[s], u_hold.at[s], keep_rows(s, me)) for s in range(seqs)]
    moves += [
        (wzx_ref.at[0], wzx_hold.at[0], wz_ref.at[span(dp * rows, rows, 16), :]),
        (wout_ref, wout_hold, wo_ref.at[:, span(dp * out_cols, out_cols, 128)]),
    ]
    moves += [(g_ref.at[s], u_hold.at[seqs + s], keep_rows(seqs + s, me)) for s in range(seqs)]
    loads = [pltpu.make_async_copy(a, b, own_sem.at[0, i]) for i, (a, b, _) in enumerate(moves)]
    stores = [pltpu.make_async_copy(b, c, own_sem.at[1, i]) for i, (_, b, c) in enumerate(moves)]
    for load in loads:
        load.start()
    greet(n)

    def settle(first, last):
        for load, store in zip(loads[first:last], stores[first:last]):
            load.wait()
            store.start()
        for store in stores[first:last]:
            store.wait()

    x_ring = RingGather(n, 2, keep_wide(wx_ref), sems[0:2])
    small = RingGather(n, 1, keep_small, sems[2:4])
    z_ring = RingGather(n, 2, keep_wide(wz_ref), sems[4:6])
    out_ring = RingGather(n, 2, keep_out, sems[6:8])
    token_rows = RowGather(keep_rows, sems[8:10])
    halves_send, halves_recv = sems[10:12]

    def half(ahead, whose):
        d = (dp + ahead) % n
        ref = wb_ref.at[span(d * rows + whose * rows // 2, rows // 2, 16), :]
        return remote(ref, ref, halves_send.at[ahead], halves_recv.at[ahead], {"tensor": other})

    settle(0, 1)
    x_ring.step(0)
    settle(1, 4)
    small.step(0)
    token_rows.start(0)
    token_rows.start(1)
    settle(4, len(moves))
    for k in range(1, n):
        x_ring.step(k)
        small.step(k)
        if k == n - 1:
            z_ring.step(0)
        if k == 4:
            token_rows.forward(0)
            token_rows.start(2)
        if k == 7:
            token_rows.forward(1)
            token_rows.start(3)
    for ahead in range(1, n):
        half(ahead, core).start()
    for k in range(1, n):
        z_ring.step(k)
        if k == n - 1:
            out_ring.step(0)
        if k == 4:
            token_rows.forward(2)
        if k == 7:
            token_rows.forward(3)
    for k in range(1, n):
        out_ring.step(k)
    for ahead in range(1, n):
        half(ahead, 1 - core).wait_recv()
        half(ahead, core).wait_send()
    for ring in (x_ring, small, z_ring, out_ring):
        ring.finish()
    token_rows.finish(2 * seqs)


def gather_all(n, u, g, w_zx, w_bc, w_out):
    seqs, piece, model = u.shape
    rows, width = w_zx.shape[1:]
    out_rows, out_cols = w_out.shape
    sem = pltpu.SemaphoreType.DMA
    ring = [sem((2, 2, n - 1))] * 2
    anywhere = pl.BlockSpec(memory_space=pl.ANY)
    whole = [
        (seqs, 4 * piece, model),
        (seqs, 4 * piece, model),
        (rows * n, width),
        (rows * n, width),
        (rows * n, w_bc.shape[1]),
        (out_rows, out_cols * n),
    ]
    return pl.pallas_call(
        functools.partial(gather_kernel, n),
        in_specs=[anywhere] * 5,
        out_specs=[anywhere] * 6,
        out_shape=[jax.ShapeDtypeStruct(shape, BF16) for shape in whole],
        scratch_shapes=[
            pltpu.VMEM((2 * seqs, piece, model), BF16),
            pltpu.VMEM(w_zx.shape, BF16),
            pltpu.VMEM(w_bc.shape, BF16),
            pltpu.VMEM(w_out.shape, BF16),
            sem((2, 4 + 2 * seqs)),
        ]
        + ring + [sem((2, 1, n - 1))] * 2 + ring + ring
        + [sem((3, 2 * seqs))] * 2 + [sem((n,))] * 2,
        compiler_params=pltpu.CompilerParams(
            collective_id=0, has_side_effects=True, vmem_limit_bytes=32 * 2**20
        ),
        name="gather_all",
    )(u, g, w_zx, w_bc, w_out)


class RingScatter:
    def __init__(self, n, term, slots, sems):
        self.n, self.term, self.slots = n, term, slots
        self.send_sem, self.recv_sem = sems
        self.place, self.at = ring_place(n)

    def copy(self, way, k):
        sign = 1 - 2 * way
        return remote(
            self.slots.at[way, k],
            self.slots.at[way, k + 1],
            self.send_sem.at[way, k],
            self.recv_sem.at[way, k],
            {"dp": self.at(self.place + sign)},
        )

    def step(self, way, k):
        value = self.term(way, self.at(self.place - (1 - 2 * way) * (1 + k)))

        @pl.when(k == 0)
        def _():
            self.slots[way, 0] = value.astype(BF16)

        @pl.when(k > 0)
        def _():
            self.copy(way, k - 1).wait_recv()

            @pl.when(k < self.n - 1)
            def _():
                self.slots[way, k] = (value + self.slots[way, k].astype(F32)).astype(BF16)

        @pl.when(k < self.n - 1)
        def _():
            self.copy(way, k).start()

        return value

    def last(self, way, value):
        return value + self.slots[way, self.n - 1].astype(F32)

    def finish(self):
        for k in range(self.n - 1):
            for way in (0, 1):
                self.copy(way, k).wait_send()


class RowScatter:
    def __init__(self, parts, term, hold, sems):
        self.parts, self.term, self.hold = parts, term, hold
        self.send_sem, self.recv_sem = sems
        self.me, self.other, self.across = tensor_place()

    def copy(self, kind, part):
        src, dst = ((0, 1), (1, 2), (0, 3))[kind]
        return remote(
            self.hold.at[src, part],
            self.hold.at[dst, part],
            self.send_sem.at[kind, part],
            self.recv_sem.at[kind, part],
            {"tensor": self.across if kind == 1 else self.other},
        )

    def step(self, j, store, wait=True):
        late = j // (2 * self.parts)
        near = j - 2 * self.parts
        stage = (1 - late) * (j % 2) + late * (2 + near // self.parts)
        part = (1 - late) * (j // 2) + late * (near % self.parts)
        x, core = self.me // 2, self.me % 2
        value = self.term(2 * ((x + 1 - stage // 2) % 2) + (core + 1 - stage % 2) % 2, part)

        @pl.when(stage == 0)
        def _():
            self.hold[0, part] = value.astype(BF16)
            self.copy(0, part).start()

        @pl.when(stage == 1)
        def _():
            self.copy(0, part).wait_recv()
            self.hold[1, part] = (value + self.hold[1, part].astype(F32)).astype(BF16)
            self.copy(1, part).start()

        @pl.when(stage == 2)
        def _():
            self.copy(0, part).wait_send()
            self.hold[0, part] = value.astype(BF16)
            self.copy(2, part).start()

        @pl.when(stage == 3)
        def _():
            store(part, value + self.arrived(part) if wait else value)

        return value, 2 * ((x + 1 - stage // 2) % 2) + (core + 1 - stage % 2) % 2, part

    def arrived(self, part):
        self.copy(2, part).wait_recv()
        self.copy(1, part).wait_recv()
        return self.hold[3, part].astype(F32) + self.hold[2, part].astype(F32)

    def finish(self):
        for part in range(self.parts):
            for kind in (1, 2):
                self.copy(kind, part).wait_send()


def product_term(a_ref, b_ref, count):
    def term(way, d):
        half = b_ref.shape[1] // 2
        return dot_tn(a_ref[:, span(d * count, count, 128)], b_ref[:, pl.ds(way * half, half)])

    return term


def back_kernel(n, *refs):
    (normed_ref, g_ref, u_ref, dz_ref, wo_ref, hidden_ref), refs = refs[:6], refs[6:]
    ins, refs = refs[:15], refs[15:]
    (out_ref, gout_ref, gz_ref), refs = refs[:3], refs[3:]
    outs, refs = refs[:5], refs[5:]
    scratch, refs = refs[:7], refs[7:]
    normed, dz, wo, g_cols, u_cols, out_slots, z_slots, hold, load_sem, stream_sem = refs[:10]
    sems = refs[10:]

    k = pl.program_id(0)
    blocks = 4
    piece = out_ref.shape[1]
    length = blocks * BLOCK
    count = g_ref.shape[1] // n
    half = gz_ref.shape[1] // 2
    place, at = ring_place(n)

    loads = [
        pltpu.make_async_copy(src, dst, load_sem.at[i])
        for i, (src, dst) in enumerate(((normed_ref, normed), (dz_ref, dz), (wo_ref, wo)))
    ]

    def streams(k):
        copies = []
        for way in (0, 1):
            d = at(place - (1 - 2 * way) * (1 + k))
            for i, (src, dst) in enumerate(((g_ref, g_cols), (u_ref, u_cols))):
                copies.append(
                    pltpu.make_async_copy(
                        src.at[:, span(d * count, count, 128)], dst.at[way], stream_sem.at[i, way]
                    )
                )
        return copies

    @pl.when(k == 0)
    def _():
        for copy in loads + streams(0):
            copy.start()
        greet(n)
        for copy in loads:
            copy.wait()

    for copy in streams(k):
        copy.wait()

    def half_product(a_ref, b_ref):
        def term(way, d):
            return dot_tn(a_ref[way], b_ref[:, pl.ds(way * half, half)])

        return term

    out_ring = RingScatter(n, half_product(g_cols, normed), out_slots, sems[0:2])
    z_ring = RingScatter(n, half_product(u_cols, dz), z_slots, sems[2:4])
    for way in (0, 1):
        value = out_ring.step(way, k)

        @pl.when(k == n - 1)
        def _():
            gout_ref[pl.ds(way * half, half), :] = out_ring.last(way, value).T

    for way in (0, 1):
        value = z_ring.step(way, k)

        @pl.when(k == n - 1)
        def _():
            gz_ref[:, pl.ds(way * half, half)] = z_ring.last(way, value)

    @pl.when(k < n - 1)
    def _():
        for copy in streams(k + 1):
            copy.start()

    def mixed_term(t, part):
        return dot(normed[span(part * length + t * piece, piece, 16), :], wo[...])

    def store(part, value):
        out_ref[0] = (hidden_ref[0].astype(F32) + value).astype(BF16)

    rows = RowScatter(2, mixed_term, hold, sems[4:6])
    rows.step(k, store)

    backward_block(k // blocks, k % blocks, *ins, *outs, *scratch)

    @pl.when(k == n - 1)
    def _():
        rows.finish()
        out_ring.finish()
        z_ring.finish()


def backward_all(n, small, hidden, normed, g, u, dz, w_out, dy, x, cx, bc, cbc, dt, cols, segrow, states, shared):
    seqs, length, channels = x.shape
    n2, heads = bc.shape[2], dt.shape[2]
    tokens, model = g.shape
    piece = hidden.shape[1]
    count = model // n
    blocks = length // BLOCK
    sem = pltpu.SemaphoreType.DMA
    anywhere = pl.BlockSpec(memory_space=pl.ANY)
    ins, outs = backward_specs(channels, n2, heads, small, lambda k: (k // blocks, blocks - 1 - k % blocks))
    late = lambda k: (jnp.maximum(k - (n - 2), 0), 0, 0)
    part = pl.BlockSpec((1, piece, model), late)
    single = pl.BlockSpec((1, piece, model), late, pipeline_mode=pl.Buffered(1))
    whole = lambda *shape: pl.BlockSpec(shape, lambda k: (0,) * len(shape))
    return pl.pallas_call(
        functools.partial(back_kernel, n),
        grid=(n,),
        in_specs=[anywhere] * 5 + [single] + ins,
        out_specs=[part, whole(channels, count), whole(count, channels)] + outs,
        out_shape=[
            jax.ShapeDtypeStruct(hidden.shape, BF16),
            jax.ShapeDtypeStruct((channels, count), F32),
            jax.ShapeDtypeStruct((count, channels), F32),
        ]
        + backward_outs(seqs, length, channels, n2, small),
        scratch_shapes=backward_scratch(channels, n2)
        + [
            pltpu.VMEM((tokens, channels), BF16),
            pltpu.VMEM((tokens, channels), BF16),
            pltpu.VMEM((channels, model), BF16),
            pltpu.VMEM((2, tokens, count), BF16),
            pltpu.VMEM((2, tokens, count), BF16),
            pltpu.VMEM((2, n, count, channels // 2), BF16),
            pltpu.VMEM((2, n, count, channels // 2), BF16),
            pltpu.VMEM((4, seqs, piece, model), BF16),
            sem((3,)),
            sem((2, 2)),
        ]
        + [sem((2, n - 1))] * 4
        + [sem((3, seqs))] * 2,
        compiler_params=pltpu.CompilerParams(
            collective_id=1, has_side_effects=True, vmem_limit_bytes=63 * 2**20
        ),
        name="backward_all",
    )(normed, g, u, dz, w_out, hidden, dy, x, cx, bc, cbc, dt, cols, segrow, states, *shared)


class Fold:
    def __init__(self, n, total, came, sems):
        self.total, self.came = total, came
        self.send_sem, self.recv_sem = sems
        dp = lax.axis_index("dp")
        _, other, across = tensor_place()
        partners, ahead = [], 1
        while ahead < n:
            partners.append({"dp": dp + ahead * (1 - 2 * ((dp // ahead) % 2))})
            ahead *= 2
        self.over_dp = partners
        self.partners = partners + [{"tensor": other}, {"tensor": across}]

    def copy(self, r):
        return remote(
            self.total.at[r], self.came.at[r], self.send_sem.at[r], self.recv_sem.at[r], self.partners[r]
        )

    def start(self, r):
        self.copy(r).start()

    def take(self, r):
        self.copy(r).wait_recv()
        self.total[r + 1] = self.total[r] + self.came[r]

    def finish(self):
        for r in range(len(self.partners)):
            self.copy(r).wait_send()


def in_kernel(
    n, u_hbm, dz_hbm, dx_hbm, wz_hbm, wx_hbm, wb_hbm, dbc_hbm, gx_in, gbc_in, gh_in, gate_in, gain_ref,
    din_ref, gx_ref, gb_ref, sums_ref,
    u_ref, dz_ref, dx_ref, wz_ref, wx_ref, wb_ref, dbc_ref,
    x_slots, b_slots, hold, bc_hold, low, swap, pre, total, came, load_sem, *sems,
):
    seqs, piece = din_ref.shape[:2]
    tokens, model = u_ref.shape
    length = tokens // seqs
    count = model // n
    half = gx_ref.shape[1] // 2
    me, other, across = tensor_place()
    core = me % 2

    moves = ((dx_hbm, dx_ref), (u_hbm, u_ref), (dbc_hbm, dbc_ref), (dz_hbm, dz_ref), (wz_hbm, wz_ref), (wx_hbm, wx_ref), (wb_hbm, wb_ref))
    loads = [pltpu.make_async_copy(src, dst, load_sem.at[i]) for i, (src, dst) in enumerate(moves)]
    for load in loads[:3]:
        load.start()

    def bc_term(t, part):
        return dbc_ref[span(part * length + t * piece, piece, 16), :].astype(F32)

    def in_term(t, part):
        at = span(part * length + t * piece, piece, 16)
        return dot_nt(dz_ref[at, :], wz_ref[...]) + dot_nt(dx_ref[at, :], wx_ref[...])

    def b_term(way, d):
        total_rows = 0.0
        for t, which in ((me, 0), (other, 1)):
            for part in range(seqs):
                rows = span(part * length + t * piece, piece, 16)
                cols = span(d * count + core * count // 2, count // 2, 128)
                total_rows = total_rows + dot_tn(u_ref[rows, cols], low[which, part])
        return total_rows[way * count // 4 : (way + 1) * count // 4]

    bc_rows = RowScatter(seqs, bc_term, bc_hold, sems[0:2])
    in_rows = RowScatter(seqs, in_term, hold, sems[2:4])
    x_ring = RingScatter(n, product_term(u_ref, dx_ref, count), x_slots, sems[4:6])
    b_ring = RingScatter(n, b_term, b_slots, sems[6:8])
    pair_send, pair_recv, swap_send, swap_recv = sems[8:12]
    fold = Fold(n, total, came, sems[12:14])
    rounds = len(fold.partners)
    pair = remote(low.at[0], low.at[1], pair_send, pair_recv, {"tensor": other})

    total[0] = jnp.zeros_like(total[0])
    total[0, 0:6, :] = gx_in[0:6, :]
    total[0, 6:7, :] = gate_in[...]
    total[0, 7:8, 0:128] = gh_in[0:1, :]
    total[0, 7:8, 128:256] = gh_in[1:2, :]
    total[0, 8:13, 0 : gbc_in.shape[1]] = gbc_in[0:5, :]
    pre[...] = jnp.zeros_like(pre)
    greet(n, fold.over_dp)
    for load in loads[:3]:
        load.wait()
    for load in loads[3:]:
        load.start()

    def bc_store(part, value):
        low[0, part] = value.astype(BF16)

    def store(part, value):
        value = value + dot_nt(low[0, part], wb_ref[...])
        din_ref[part] = value
        pre[...] += jnp.sum(
            value * u_ref[span(part * length + me * piece, piece, 16), :].astype(F32), axis=0, keepdims=True
        )

    def row_step(j):
        value, t, part = in_rows.step(j, store, wait=False)

        @pl.when(j < 3 * seqs)
        def _():
            pre[...] += jnp.sum(
                value * u_ref[span(part * length + t * piece, piece, 16), :].astype(F32), axis=0, keepdims=True
            )

    def ring_step(k):
        for way in (0, 1):
            value = x_ring.step(way, k)

            @pl.when(k == n - 1)
            def _():
                gx_ref[:, pl.ds(way * half, half)] = x_ring.last(way, value)

    def b_step(k):
        for way in (0, 1):
            value = b_ring.step(way, k)

            @pl.when(k == n - 1)
            def _():
                swap[0, pl.ds(way * count // 4, count // 4), :] = b_ring.last(way, value)

    ring_step(0)
    for load in loads[3:]:
        load.wait()
    for j in range(2 * seqs):
        bc_rows.step(j, bc_store)
    row_step(0)

    def step(k, _):
        row_step(k)
        ring_step(k)

        @pl.when(k == 1)
        def _():
            for j in range(2 * seqs, 4 * seqs):
                bc_rows.step(j, bc_store)
            pair.start()
            pair.wait_recv()

        @pl.when(k >= 2)
        def _():
            b_step(k - 2)

        return 0

    lax.fori_loop(1, n, step, 0)
    gain = gain_ref[...]
    width = total.shape[2]
    for i in range(model // width):
        at = slice(i * width, (i + 1) * width)
        total[0, 13 + i : 14 + i, :] = pre[:, at] / gain[:, at]
    fold.start(0)
    b_step(n - 2)
    fold.take(0)
    fold.start(1)
    b_step(n - 1)
    cross = remote(swap.at[0], swap.at[1], swap_send.at[0], swap_recv.at[0], {"tensor": across})
    cross.start()
    fold.take(1)
    fold.start(2)
    cross.wait_recv()
    swap[2] = swap[0] + swap[1]
    back = remote(swap.at[2], swap.at[3], swap_send.at[1], swap_recv.at[1], {"tensor": other})
    back.start()
    fold.take(2)
    fold.start(3)
    gb_ref[span(core * count // 2, count // 2, 16), :] = swap[2]
    din_ref[0] += in_rows.arrived(0)
    fold.take(3)
    fold.start(4)
    for part in range(1, seqs):
        din_ref[part] += in_rows.arrived(part)
    back.wait_recv()
    gb_ref[span((1 - core) * count // 2, count // 2, 16), :] = swap[3]
    fold.take(4)
    sums_ref[0:8, :] = total[rounds - 2, 0:8, :]
    sums_ref[8:16, :] = total[rounds, 8:16, :]
    for copy in (pair, cross, back):
        copy.wait_send()
    for part in (bc_rows, in_rows, x_ring, b_ring, fold):
        part.finish()


def scatter_in(n, piece, u, dz, dx, w_z, w_x, w_bc, dbc, gx, gbc, gh, grad_gate, gain):
    tokens, model = u.shape
    width = dz.shape[1]
    small = dbc.shape[1]
    seqs = tokens // (4 * piece)
    count = model // n
    rounds = 5
    sem = pltpu.SemaphoreType.DMA
    vmem = pl.BlockSpec(memory_space=pltpu.VMEM)
    anywhere = pl.BlockSpec(memory_space=pl.ANY)
    big = (u, dz, dx, w_z, w_x, w_bc, dbc)
    return pl.pallas_call(
        functools.partial(in_kernel, n),
        in_specs=[anywhere] * 7 + [vmem] * 5,
        out_specs=[vmem] * 4,
        out_shape=[
            jax.ShapeDtypeStruct((seqs, piece, model), F32),
            jax.ShapeDtypeStruct((count, width), F32),
            jax.ShapeDtypeStruct((count, small), F32),
            jax.ShapeDtypeStruct((16, width), F32),
        ],
        scratch_shapes=[pltpu.VMEM(a.shape, BF16) for a in big]
        + [
            pltpu.VMEM((2, n, count, width // 2), BF16),
            pltpu.VMEM((2, n, count // 4, small), BF16),
            pltpu.VMEM((4, seqs, piece, model), BF16),
            pltpu.VMEM((4, seqs, piece, small), BF16),
            pltpu.VMEM((2, seqs, piece, small), BF16),
            pltpu.VMEM((4, count // 2, small), F32),
            pltpu.VMEM((1, model), F32),
            pltpu.VMEM((rounds + 1, 16, width), F32),
            pltpu.VMEM((rounds, 16, width), F32),
            sem((len(big),)),
        ]
        + [sem((3, seqs))] * 4 + [sem((2, n - 1))] * 4 + [sem(())] * 2 + [sem((2,))] * 2 + [sem((rounds,))] * 2,
        compiler_params=pltpu.CompilerParams(
            collective_id=2, has_side_effects=True, vmem_limit_bytes=63 * 2**20
        ),
        name="scatter_in",
    )(*big, gx, gbc, gh, grad_gate, gain)


def rms_scale(values):
    return lax.rsqrt(jnp.mean(values * values, axis=-1, keepdims=True) + EPS)


def gather_plain(u, g, w_zx, w_bc, w_out):
    w_zx = lax.all_gather(w_zx, "dp", axis=1, tiled=True)
    return (
        lax.all_gather(u, "tensor", axis=1, tiled=True),
        lax.all_gather(g, "tensor", axis=1, tiled=True),
        w_zx[1],
        w_zx[0],
        lax.all_gather(w_bc, "dp", axis=0, tiled=True),
        lax.all_gather(w_out, "dp", axis=1, tiled=True),
    )


def rows_of(values, piece):
    by_seq = values.reshape(-1, 4 * piece, values.shape[-1])
    return lax.psum_scatter(by_seq, "tensor", scatter_dimension=1, tiled=True)


def scatter_out_plain(piece, normed, g, u, dz, w_out):
    return (
        rows_of(dot(normed, w_out), piece),
        lax.psum_scatter(dot_tn(normed, g), "dp", scatter_dimension=1, tiled=True),
        lax.psum_scatter(dot_tn(u, dz), "dp", scatter_dimension=0, tiled=True),
    )


def scatter_in_plain(piece, u, dz, dx, w_z, w_x, w_bc, dbc):
    low = lax.psum(dbc.astype(F32), "tensor").astype(BF16)
    d_in = rows_of(dot_nt(dz, w_z) + dot_nt(dx, w_x), piece)
    first = lax.axis_index("tensor") * piece
    own = lax.dynamic_slice_in_dim(low.reshape(-1, 4 * piece, low.shape[1]), first, piece, 1)
    d_in = d_in + jnp.einsum("slc,dc->sld", own, w_bc, preferred_element_type=F32)
    return (
        d_in,
        lax.psum_scatter(dot_tn(u, dx), "dp", scatter_dimension=0, tiled=True),
        lax.psum_scatter(dot_tn(u, low), "dp", scatter_dimension=0, tiled=True),
    )


def local(
    n_dp,
    n_tensor,
    hidden,
    pre_gain,
    w_zx,
    w_bcdt,
    conv_x,
    conv_bc,
    dt_bias,
    a_log,
    d_skip,
    gate_gain,
    w_out,
    cotangent,
    segments,
):
    seqs, piece, model = hidden.shape
    length = segments.shape[1]
    tokens = seqs * length
    heads = dt_bias.shape[0]
    channels = conv_x.shape[1]
    n2 = conv_bc.shape[1]
    columns = w_bcdt.shape[1]
    tensor = lax.axis_index("tensor")
    kernels = n_dp == 8 and n_tensor == 4 and seqs == 2 and length == 4 * BLOCK

    x_piece = hidden.astype(F32)
    scale_in = rms_scale(x_piece)
    u_piece = (x_piece * scale_in * pre_gain).astype(BF16)
    w_bc_piece = jnp.pad(w_bcdt, ((0, 0), (0, -columns % 128)))
    gather = functools.partial(gather_all, n_dp) if kernels else gather_plain
    u, g, w_x, w_z, w_bc, w_o = gather(u_piece, cotangent, w_zx, w_bc_piece, w_out)
    u = u.reshape(tokens, model)
    g = g.reshape(tokens, model)

    x = dot(u, w_x).reshape(seqs, length, channels)
    z = dot(u, w_z)
    bc_dt = dot(u, w_bc).reshape(seqs, length, -1)
    bc = bc_dt[:, :, :n2]
    dt = lax.dynamic_slice_in_dim(bc_dt, n2 + tensor * heads, heads, 2)

    cols = column_masks(segments)
    segrow = segments.astype(F32)[:, None, :]
    spread = jnp.asarray(spread_matrix(heads, channels), BF16)
    skip = jnp.repeat(d_skip, channels // heads)[None]
    shared = (conv_x, conv_bc, dt_bias[None], a_log[None], skip, spread)
    y, cx, cbc, states = ssd_forward(x, bc, dt, cols, segrow, shared)

    d_normed = dot_nt(g, w_o)
    sig_z = sigmoid(z)
    silu_z = z * sig_z
    y_flat = y.reshape(tokens, channels)
    gated = y_flat * silu_z
    scaled = d_normed * gate_gain
    sums = jnp.stack([jnp.sum(gated * gated, axis=1), jnp.sum(scaled * gated, axis=1)])
    sums = lax.psum(sums, "tensor") / (channels * n_tensor)
    inverse = lax.rsqrt(sums[0] + EPS)[:, None]
    normed = (gated * inverse * gate_gain).astype(BF16)
    grad_gate = jnp.sum(d_normed * gated * inverse, axis=0)
    d_gated = inverse * scaled - gated * inverse**3 * sums[1][:, None]
    dy = (d_gated * silu_z).astype(BF16)
    dz = (d_gated * y_flat * (sig_z * (1.0 + z * (1.0 - sig_z)))).astype(BF16)

    x, bc = x.astype(BF16), bc.astype(BF16)
    back_args = (dy.reshape(seqs, length, channels), x, cx, bc, cbc, dt, cols, segrow, states, shared)
    if kernels:
        out_hidden, grad_out, grad_z, *rest = backward_all(n_dp, w_bc.shape[1], hidden, normed, g, u, dz, w_o, *back_args)
    else:
        mixed, grad_out, grad_z = scatter_out_plain(piece, normed, g, u, dz, w_o)
        out_hidden = (x_piece + mixed).astype(BF16)
        rest = ssd_backward(w_bc.shape[1], *back_args)
    dx, dbc, gx, gbc, gh = rest
    in_args = (piece, u, dz, dx.reshape(tokens, channels), w_z, w_x, w_bc, dbc.reshape(tokens, -1))
    if kernels:
        d_in, grad_x, grad_bc, sums = scatter_in(n_dp, *in_args, gx, gbc, gh, grad_gate[None], pre_gain[None])
        grad_pre = sums[13:].reshape(-1)[:model]
        grad_conv_bc = sums[8:13, :n2]
    else:
        d_in, grad_x, grad_bc = scatter_in_plain(*in_args)
        grad_pre = jnp.sum(d_in * x_piece * scale_in, axis=(0, 1))
        steps = jnp.pad(gh[:2], ((0, 0), (0, channels - gh.shape[1])))
        sums = lax.psum(jnp.concatenate([gx[:6], grad_gate[None], steps]), "dp")
        sums = jnp.concatenate([sums[:7], jnp.concatenate([sums[7, :128], sums[8, : channels - 128]])[None]])
        grad_conv_bc, grad_pre = lax.psum((gbc[:5], grad_pre), ("dp", "tensor"))

    gain_grad = d_in * pre_gain
    d_hidden = cotangent.astype(F32) + scale_in * gain_grad - x_piece * scale_in**3 * jnp.mean(
        gain_grad * x_piece, axis=-1, keepdims=True
    )
    return (
        out_hidden,
        d_hidden,
        grad_pre,
        jnp.stack([grad_z, grad_x]),
        grad_bc[:, :columns],
        sums[:5],
        grad_conv_bc,
        sums[7, :heads],
        sums[7, 128 : 128 + heads],
        sums[5].reshape(heads, -1).sum(axis=1),
        sums[6],
        grad_out,
    )


def solution(mesh):
    placed = (
        P("dp", "tensor", None),
        P(),
        P(None, "dp", "tensor"),
        P("dp", None),
        P(None, "tensor"),
        P(),
        P("tensor"),
        P("tensor"),
        P("tensor"),
        P("tensor"),
        P("tensor", "dp"),
        P("dp", "tensor", None),
        P("dp", None),
    )
    return jax.shard_map(
        functools.partial(local, mesh.shape["dp"], mesh.shape["tensor"]),
        mesh=mesh,
        in_specs=placed,
        out_specs=(
            P("dp", "tensor", None),
            P("dp", "tensor", None),
            P(),
            P(None, "dp", "tensor"),
            P("dp", None),
            P(None, "tensor"),
            P(),
            P("tensor"),
            P("tensor"),
            P("tensor"),
            P("tensor"),
            P("tensor", "dp"),
        ),
        check_vma=False,
    )
```

```python
import functools

import jax
import jax.numpy as jnp
import numpy as np
from jax import lax
from jax.experimental import pallas as pl
from jax.experimental.pallas import tpu as pltpu
from jax.sharding import PartitionSpec as P

MESH = pl.DeviceIdType.MESH
EPS = 1e-05
BLOCK = 256
F32 = jnp.float32
BF16 = jnp.bfloat16
EXACT = lax.Precision.HIGHEST
LOG2E = 1.4426950408889634
NEG = -1e30


def sigmoid(v):
    return 0.5 * jnp.tanh(0.5 * v) + 0.5


def split3(v):
    hi = v.astype(BF16)
    rest = v - hi.astype(F32)
    mid = rest.astype(BF16)
    low = (rest - mid.astype(F32)).astype(BF16)
    return hi, mid, low


def dot(a, b):
    return jnp.dot(a, b, preferred_element_type=F32)


def dot_nt(a, b):
    return lax.dot_general(a, b, (((1,), (1,)), ((), ())), preferred_element_type=F32)


def dot_tn(a, b):
    return lax.dot_general(a, b, (((0,), (0,)), ((), ())), preferred_element_type=F32)


def softplus(v):
    return jnp.maximum(v, 0.0) + jnp.log1p(jnp.exp(-jnp.abs(v)))


def head_sizes(raw, dt_bias, a_log):
    q = raw.shape[0]
    tri = (
        lax.broadcasted_iota(jnp.int32, (q, q), 0) >= lax.broadcasted_iota(jnp.int32, (q, q), 1)
    ).astype(F32)
    biased = raw + dt_bias
    step = softplus(biased)
    rate = -jnp.exp(a_log) * step
    cum = jnp.dot(tri, rate, precision=EXACT, preferred_element_type=F32) * LOG2E
    return biased, step, rate, cum


def expand(values, spread):
    hi, mid, low = split3(values)
    return dot(hi, spread) + dot(mid, spread) + dot(low, spread)


def gather_heads(values, spread):
    hi, mid, _ = split3(values)
    return dot_nt(hi, spread) + dot_nt(mid, spread)


def exact_nt(a, b):
    a_hi, a_mid, _ = split3(a)
    b_hi, b_mid, _ = split3(b)
    return dot_nt(a_hi, b_hi) + dot_nt(a_hi, b_mid) + dot_nt(a_mid, b_hi)


def transpose_heads(values):
    pad = jnp.concatenate(
        [values, jnp.zeros((values.shape[0], 128 - values.shape[1]), F32)], axis=1
    )
    return pad.T


def mark_columns(marks_ref):
    marks = marks_ref[0]
    cols = jnp.concatenate([marks, jnp.zeros((128 - marks.shape[0], marks.shape[1]), F32)], axis=0).T
    return [cols[:, k : k + 1] for k in range(6)]


def forward_block(
    block, x, bc, dt, marks_ref, taps_x_ref, taps_bc_ref, bias_ref, alog_ref, skip_ref, spread_ref,
    y_ref, cx_ref, cbc_ref, states_ref,
    xs, bs, state, mask_bias,
):
    q = BLOCK
    heads = dt.shape[-1]
    channels = x.shape[-1]
    width = channels // heads

    @pl.when(block == 0)
    def _():
        xs[0:8, :] = jnp.zeros((8, xs.shape[1]), F32)
        bs[0:8, :] = jnp.zeros((8, bs.shape[1]), F32)
        state[...] = jnp.zeros_like(state)

    *lag_masks, reads, last, seg = mark_columns(marks_ref)

    def conv(value, hold, taps_ref):
        hold[8 : 8 + q, :] = value
        out = taps_ref[4:5, :] + taps_ref[3:4, :] * hold[8 : 8 + q, :]
        for lag in (1, 2, 3):
            out = out + (lag_masks[lag - 1] * hold[8 - lag : 8 - lag + q, :]) * taps_ref[3 - lag : 4 - lag, :]
        hold[0:8, :] = hold[q : q + 8, :]
        return out

    cbc = conv(bc, bs, taps_bc_ref)
    cbc_ref[0] = cbc
    bc = cbc * sigmoid(cbc)
    n = bc.shape[1] // 2
    scores = exact_nt(bc[:, n:], bc[:, :n])
    b_mat, c_mat = bc[:, :n].astype(BF16), bc[:, n:].astype(BF16)

    cx = conv(x, xs, taps_x_ref)
    cx_ref[0] = cx
    xb = (cx * sigmoid(cx)).astype(BF16)

    biased, step, rate, cum = head_sizes(dt, bias_ref[...], alog_ref[...])
    cum_end = cum[q - 1 : q, :]
    spread = spread_ref[...]
    reads_e = expand(reads * jnp.exp2(cum), spread)
    to_end_e = expand(last * jnp.exp2(cum_end - cum) * step, spread)
    carry = jnp.exp2(cum_end)
    carry_e = expand(jnp.broadcast_to(carry, (8, heads)), spread)[0:1]
    source = transpose_heads(cum - jnp.log(step) * LOG2E)

    rows = lax.broadcasted_iota(jnp.int32, (q, q), 0)
    places = lax.broadcasted_iota(jnp.int32, (q, q), 1)
    mask_bias[...] = jnp.where((seg == marks_ref[0, 5:6, :]) & (rows >= places), 0.0, NEG)

    st = state[...].astype(BF16)
    states_ref[0, 0] = st
    outside = dot(c_mat, st) * reads_e + skip_ref[...] * xb.astype(F32)

    half = q // 2
    lane = lax.broadcasted_iota(jnp.int32, (1, 2 * width), 1)
    for pair in range(heads // 2):
        at = slice(pair * 2 * width, (pair + 1) * 2 * width)
        xp = xb[:, at]
        both = []
        for h in (2 * pair, 2 * pair + 1):
            col = cum[:, h : h + 1]
            row = source[h : h + 1, :]
            top = (
                jnp.exp2((col[:half] - row[:, :half]) + mask_bias[:half, :half]) * scores[:half, :half]
            ).astype(BF16)
            low = (jnp.exp2((col[half:] - row) + mask_bias[half:, :]) * scores[half:, :]).astype(BF16)
            both.append(jnp.concatenate([dot(top, xp[:half]), dot(low, xp)], axis=0))
        y_ref[:, at] = outside[:, at] + jnp.where(lane < width, both[0], both[1])

    scaled = (xb.astype(F32) * to_end_e).astype(BF16)
    state[...] = carry_e * state[...] + dot_tn(b_mat, scaled)


def backward_block(
    seq, step_id, dy_ref, x_ref, cx_ref, bc_ref, cbc_ref, dt_ref, marks_ref, states_ref,
    taps_x_ref, taps_bc_ref, bias_ref, alog_ref, skip_ref, spread_ref,
    dx_ref, dbc_ref, gx_ref, gbc_ref, gh_ref,
    ds_x, ds_bc, d_state, mask_bias, d_scores, d_in, row_sums,
):
    q = BLOCK
    heads = dt_ref.shape[-1]
    channels = x_ref.shape[-1]
    width = channels // heads

    @pl.when(step_id == 0)
    def _():
        ds_x[:, q : q + 8, :] = jnp.zeros((3, 8, channels), F32)
        ds_bc[:, q : q + 8, :] = jnp.zeros((3, 8, ds_bc.shape[2]), F32)
        d_state[...] = jnp.zeros_like(d_state)

    @pl.when((step_id == 0) & (seq == 0))
    def _():
        gx_ref[...] = jnp.zeros_like(gx_ref)
        gbc_ref[...] = jnp.zeros_like(gbc_ref)
        gh_ref[...] = jnp.zeros_like(gh_ref)

    *lag_masks, reads, last, seg = mark_columns(marks_ref)

    cbc = cbc_ref[0]
    sig_bc = sigmoid(cbc)
    bc = cbc * sig_bc
    n = bc.shape[1] // 2
    scores = exact_nt(bc[:, :n], bc[:, n:])
    b_mat, c_mat = bc[:, :n].astype(BF16), bc[:, n:].astype(BF16)
    cx = cx_ref[0]
    xb = (cx * sigmoid(cx)).astype(BF16)
    dyb = dy_ref[0]

    biased, step, rate, cum = head_sizes(dt_ref[0], bias_ref[...], alog_ref[...])
    cum_end = cum[q - 1 : q, :]
    spread = spread_ref[...]
    carry_e = expand(jnp.broadcast_to(jnp.exp2(cum_end), (8, heads)), spread)[0:1]
    source = cum - jnp.log(step) * LOG2E
    target = transpose_heads(cum)

    rows = lax.broadcasted_iota(jnp.int32, (q, q), 0)
    places = lax.broadcasted_iota(jnp.int32, (q, q), 1)
    mask_bias[...] = jnp.where((seg == marks_ref[0, 5:6, :]) & (rows <= places), 0.0, NEG)

    st = states_ref[0, 0]
    dst = d_state[...].astype(BF16)
    dye = dyb.astype(F32) * expand(reads * jnp.exp2(cum), spread)
    out_h = gather_heads(dye * dot(c_mat, st), spread)
    dye = dye.astype(BF16)
    d_c = dot_nt(dye, st)
    carried = carry_e * jnp.sum(d_state[...] * st.astype(F32), axis=0, keepdims=True)
    d_state[...] = carry_e * d_state[...] + dot_tn(c_mat, dye)
    to_end_e = expand(last * jnp.exp2(cum_end - cum) * step, spread)
    d_b = dot_nt((xb.astype(F32) * to_end_e).astype(BF16), dst)
    dx_st = dot(b_mat, dst) * to_end_e
    state_h = gather_heads(xb.astype(F32) * dx_st, spread)
    d_in[...] = dx_st

    half = q // 2
    lane = lax.broadcasted_iota(jnp.int32, (1, 2 * width), 1)
    d_scores[...] = jnp.zeros_like(d_scores)
    head_lane = lax.broadcasted_iota(jnp.int32, (1, heads), 1)
    col_sums = jnp.zeros((q, heads), F32)
    for pair in range(heads // 2):
        at = slice(pair * 2 * width, (pair + 1) * 2 * width)
        xp, dyp = xb[:, at], dyb[:, at]
        both = []
        for which in (0, 1):
            h = 2 * pair + which
            mine = lane < width if which == 0 else lane >= width
            xm = jnp.where(mine, xp, jnp.zeros_like(xp))
            col = source[:, h : h + 1]
            row = target[h : h + 1, :]
            top = jnp.exp2((row - col[:half]) + mask_bias[:half, :])
            low = jnp.exp2((row[:, half:] - col[half:]) + mask_bias[half:, half:])
            d_top = top * dot_nt(xm[:half], dyp)
            d_low = low * dot_nt(xm[half:], dyp[half:])
            d_scores[:half, :] += d_top
            d_scores[half:, half:] += d_low
            m_top = d_top * scores[:half, :]
            m_low = d_low * scores[half:, half:]
            late = jnp.sum(m_top[:, half:], axis=0, keepdims=True) + jnp.sum(m_low, axis=0, keepdims=True)
            row_sums[h : h + 1, :half] = jnp.sum(m_top[:, :half], axis=0, keepdims=True)
            row_sums[h : h + 1, half:] = late
            here = jnp.concatenate(
                [
                    jnp.sum(m_top[:, :half] + m_top[:, half:], axis=1, keepdims=True),
                    jnp.sum(m_low, axis=1, keepdims=True),
                ],
                axis=0,
            )
            col_sums = jnp.where(head_lane == h, here, col_sums)
            top = (top * scores[:half, :]).astype(BF16)
            low = (low * scores[half:, half:]).astype(BF16)
            both.append(jnp.concatenate([dot(top, dyp), dot(low, dyp[half:])], axis=0))
        d_in[:, at] += jnp.where(lane < width, both[0], both[1])

    dsb = d_scores[...].astype(BF16)
    d_b = d_b + dot(dsb, c_mat)
    d_c = d_c + dot_tn(dsb, b_mat)

    used_h = col_sums + state_h
    diff_h = row_sums[...].T[:, :heads] - col_sums + out_h
    from_here = (rows <= places).astype(F32)
    before = (rows > places).astype(F32)
    d_rate = (
        jnp.dot(from_here, diff_h, precision=EXACT, preferred_element_type=F32)
        + jnp.dot(before, state_h, precision=EXACT, preferred_element_type=F32)
        + gather_heads(jnp.broadcast_to(carried, (8, channels)), spread)[0:1]
    )
    sig_dt = sigmoid(biased)
    ratio = jnp.where(step < 1e-30, 1.0, sig_dt / jnp.maximum(step, 1e-30))
    d_raw = used_h * ratio - jnp.exp(alog_ref[...]) * sig_dt * d_rate
    lanes = dbc_ref.shape[2] - 2 * n
    mine = lax.broadcasted_iota(jnp.int32, (heads, lanes), 0) + lax.axis_index("tensor") * heads
    own = (lax.broadcasted_iota(jnp.int32, (heads, lanes), 1) == mine).astype(BF16)
    dbc_ref[0, :, 2 * n :] = dot(d_raw.astype(BF16), own).astype(BF16)
    gh_ref[0:1, :heads] += jnp.sum(d_raw, axis=0, keepdims=True)
    gh_ref[1:2, :heads] += jnp.sum(d_rate * rate, axis=0, keepdims=True)

    def conv_back(d_out, value_ref, hold, taps_ref, grad_ref):
        value = value_ref[0].astype(F32)
        d_value = d_out * taps_ref[3:4, :]
        grad_ref[3:4, :] += jnp.sum(value * d_out, axis=0, keepdims=True)
        grad_ref[4:5, :] += jnp.sum(d_out, axis=0, keepdims=True)
        for lag in (1, 2, 3):
            hold[lag - 1, 0:q, :] = lag_masks[lag - 1] * d_out
            moved = hold[lag - 1, lag : lag + q, :]
            d_value = d_value + moved * taps_ref[3 - lag : 4 - lag, :]
            grad_ref[3 - lag : 4 - lag, :] += jnp.sum(value * moved, axis=0, keepdims=True)
            hold[lag - 1, q : q + 8, :] = hold[lag - 1, 0:8, :]
        return d_value

    d_bc = jnp.concatenate([d_b, d_c], axis=1) * (sig_bc * (1.0 + cbc * (1.0 - sig_bc)))
    dbc_ref[0, :, : 2 * n] = conv_back(d_bc, bc_ref, ds_bc, taps_bc_ref, gbc_ref).astype(BF16)
    dyf = dy_ref[0].astype(F32)
    cx = cx_ref[0]
    sig_x = sigmoid(cx)
    gx_ref[5:6, :] += jnp.sum(dyf * (cx * sig_x).astype(BF16).astype(F32), axis=0, keepdims=True)
    d_cx = (d_in[...] + skip_ref[...] * dyf) * (sig_x * (1.0 + cx * (1.0 - sig_x)))
    dx_ref[0] = conv_back(d_cx, x_ref, ds_x, taps_x_ref, gx_ref).astype(BF16)


def row_marks(segments):
    seqs, length = segments.shape
    blocks = length // BLOCK
    lags = []
    for lag in (1, 2, 3):
        earlier = jnp.pad(segments, ((0, 0), (lag, 0)), constant_values=-1)[:, :length]
        lags.append(earlier == segments)
    grouped = segments.reshape(seqs, blocks, BLOCK)
    before = jnp.pad(segments, ((0, 0), (1, 0)), constant_values=-1)[:, :length].reshape(seqs, blocks, BLOCK)
    reads = (grouped == before[:, :, :1]).reshape(seqs, length)
    last = (grouped == grouped[:, :, -1:]).reshape(seqs, length)
    rows = [m.astype(F32) for m in (*lags, reads, last, segments)]
    return jnp.stack(rows + [jnp.zeros_like(rows[0])] * 2, axis=1)


def spread_matrix(heads, channels):
    width = channels // heads
    return (np.arange(heads)[:, None] == np.arange(channels)[None, :] // width).astype(np.float32)


def shared_specs(channels, n2, heads):
    full = lambda *shape: pl.BlockSpec(shape, lambda *i: (0,) * len(shape))
    return [full(5, channels), full(5, n2), full(1, heads), full(1, heads), full(1, channels), full(heads, channels)]


def forward_scratch(channels, n2):
    return [
        pltpu.VMEM((BLOCK + 8, channels), F32),
        pltpu.VMEM((BLOCK + 8, n2), F32),
        pltpu.VMEM((n2 // 2, channels), F32),
        pltpu.VMEM((BLOCK, BLOCK), F32),
    ]


def forward_kernel(x_ref, bc_ref, dt_ref, *refs):
    y_ref = refs[7]
    forward_block(pl.program_id(1), x_ref[0], bc_ref[0], dt_ref[0], *refs[:7], y_ref.at[0], *refs[8:])


def ssd_forward(x, bc, dt, marks, shared):
    seqs, length, channels = x.shape
    n2, heads = bc.shape[2], dt.shape[2]
    blocks = length // BLOCK
    tok = lambda w: pl.BlockSpec((1, BLOCK, w), lambda s, c: (s, c, 0))
    return pl.pallas_call(
        forward_kernel,
        grid=(seqs, blocks),
        in_specs=[tok(channels), tok(n2), tok(heads), pl.BlockSpec((1, 8, BLOCK), lambda s, c: (s, 0, c))]
        + shared_specs(channels, n2, heads),
        out_specs=[
            tok(channels),
            tok(channels),
            tok(n2),
            pl.BlockSpec((1, 1, n2 // 2, channels), lambda s, c: (s, c, 0, 0)),
        ],
        out_shape=[
            jax.ShapeDtypeStruct((seqs, length, channels), F32),
            jax.ShapeDtypeStruct((seqs, length, channels), F32),
            jax.ShapeDtypeStruct((seqs, length, n2), F32),
            jax.ShapeDtypeStruct((seqs, blocks, n2 // 2, channels), BF16),
        ],
        scratch_shapes=forward_scratch(channels, n2),
        compiler_params=pltpu.CompilerParams(vmem_limit_bytes=48 * 2**20),
        name="ssd_forward",
    )(x, bc, dt, marks, *shared)


def backward_kernel(*refs):
    backward_block(pl.program_id(0), pl.program_id(1), *refs)


def backward_scratch(channels, n2):
    return [
        pltpu.VMEM((3, BLOCK + 8, channels), F32),
        pltpu.VMEM((3, BLOCK + 8, n2), F32),
        pltpu.VMEM((n2 // 2, channels), F32),
        pltpu.VMEM((BLOCK, BLOCK), F32),
        pltpu.VMEM((BLOCK, BLOCK), F32),
        pltpu.VMEM((BLOCK, channels), F32),
        pltpu.VMEM((128, BLOCK), F32),
    ]


def backward_specs(channels, n2, heads, small, place):
    tok = lambda w: pl.BlockSpec((1, BLOCK, w), lambda *i: (*place(*i), 0))
    full = lambda *shape: pl.BlockSpec(shape, lambda *i: (0,) * len(shape))
    ins = [tok(channels)] * 3 + [tok(n2)] * 2 + [
        tok(heads),
        pl.BlockSpec((1, 8, BLOCK), lambda *i: (place(*i)[0], 0, place(*i)[1])),
        pl.BlockSpec((1, 1, n2 // 2, channels), lambda *i: (*place(*i), 0, 0)),
    ]
    ins += shared_specs(channels, n2, heads)
    return ins, [tok(channels), tok(small), full(8, channels), full(8, n2), full(8, 128)]


def backward_outs(seqs, length, channels, n2, small):
    return [
        jax.ShapeDtypeStruct((seqs, length, channels), BF16),
        jax.ShapeDtypeStruct((seqs, length, small), BF16),
        jax.ShapeDtypeStruct((8, channels), F32),
        jax.ShapeDtypeStruct((8, n2), F32),
        jax.ShapeDtypeStruct((8, 128), F32),
    ]


def ssd_backward(small, dy, x, cx, bc, cbc, dt, marks, states, shared):
    seqs, length, channels = x.shape
    n2, heads = bc.shape[2], dt.shape[2]
    blocks = length // BLOCK
    ins, outs = backward_specs(channels, n2, heads, small, lambda s, c: (s, blocks - 1 - c))
    return pl.pallas_call(
        backward_kernel,
        grid=(seqs, blocks),
        in_specs=ins,
        out_specs=outs,
        out_shape=backward_outs(seqs, length, channels, n2, small),
        scratch_shapes=backward_scratch(channels, n2),
        compiler_params=pltpu.CompilerParams(vmem_limit_bytes=56 * 2**20),
        name="ssd_backward",
    )(dy, x, cx, bc, cbc, dt, marks, states, *shared)


def ring_place(n):
    dp = lax.axis_index("dp")
    z, y = dp // 2, dp % 2

    def at(place):
        q = (place + 4 * n) % n
        return 2 * q + (q // (n // 2)) * (2 * n - 1 - 4 * q)

    return z + y * (n - 1 - 2 * z), at


def tensor_place():
    t = lax.axis_index("tensor")
    return t, t + 1 - 2 * (t % 2), (t + 2) % 4


def greet(n, more=()):
    place, at = ring_place(n)
    _, other, across = tensor_place()
    sem = pltpu.get_barrier_semaphore()
    targets = [{"dp": at(place + 1)}, {"dp": at(place - 1)}, {"tensor": other}, {"tensor": across}, *more]
    for target in targets:
        pl.semaphore_signal(sem, inc=1, device_id=target, device_id_type=MESH)
    pl.semaphore_wait(sem, len(targets))


def remote(src, dst, send_sem, recv_sem, target):
    return pltpu.make_async_remote_copy(
        src_ref=src, dst_ref=dst, send_sem=send_sem, recv_sem=recv_sem, device_id=target, device_id_type=MESH
    )


def span(first, count, unit):
    return pl.ds(pl.multiple_of(first, unit), count)


class RingGather:
    def __init__(self, n, parts, keep, sems):
        self.n, self.parts, self.keep = n, parts, keep
        self.send_sem, self.recv_sem = sems
        self.place, self.at = ring_place(n)

    def copy(self, way, part, step):
        sign = 1 - 2 * way
        ref = self.keep(way, part, self.at(self.place - sign * step))
        return remote(
            ref,
            ref,
            self.send_sem.at[way, part, step],
            self.recv_sem.at[way, part, step],
            {"dp": self.at(self.place + sign)},
        )

    def step(self, k):
        for part in range(self.parts):
            for way in (0, 1):
                if k > 0:
                    self.copy(way, part, k - 1).wait_recv()
                if k < self.n - 1:
                    self.copy(way, part, k).start()

    def later(self, k):
        for part in range(self.parts):
            for way in (0, 1):
                self.copy(way, part, k - 1).wait_recv()

                @pl.when(k < self.n - 1)
                def _():
                    self.copy(way, part, k).start()

    def finish(self):
        for k in range(self.n - 1):
            for part in range(self.parts):
                for way in (0, 1):
                    self.copy(way, part, k).wait_send()


class RowGather:
    def __init__(self, keep, sems):
        self.keep = keep
        self.send_sem, self.recv_sem = sems
        self.me, self.other, self.across = tensor_place()

    def copy(self, kind, part):
        ref = self.keep(part, self.across if kind == 2 else self.me)
        target = self.across if kind == 0 else self.other
        return remote(
            ref, ref, self.send_sem.at[kind, part], self.recv_sem.at[kind, part], {"tensor": target}
        )

    def start(self, part):
        self.copy(0, part).start()
        self.copy(1, part).start()

    def forward(self, part):
        self.copy(0, part).wait_recv()
        self.copy(2, part).start()

    def wait(self, part):
        self.copy(1, part).wait_recv()
        self.copy(2, part).wait_recv()

    def finish(self, parts):
        for part in range(parts):
            for kind in range(3):
                self.copy(kind, part).wait_send()


def all_kernel(n, *refs):
    (hidden_ref, g_ref, wzx_ref, wbc_ref, wout_ref, gain_ref, gate_ref, marks_ref), refs = refs[:8], refs[8:]
    shared, refs = refs[:6], refs[6:]
    (u_out, gf_out, wx_out, wz_out, wb_out, wo_out), refs = refs[:6], refs[6:]
    (cx_ref, x_ref, cbc_ref, bc_ref, dt_ref, states_ref), refs = refs[:6], refs[6:]
    (normed_ref, dz_ref, dy_ref, grad_ref), refs = refs[:4], refs[4:]
    scratch, refs = refs[:4], refs[4:]
    (u, wx, wz, wo, wb, wdt, g_cols, y, z, dn, sums), refs = refs[:11], refs[11:]
    (load_sem, keep_sem, stream_sem), sems = refs[:3], refs[3:]

    i = pl.program_id(0)
    rows, width = wzx_ref.shape[1:]
    out_rows, out_cols = wout_ref.shape
    seqs, piece, model = hidden_ref.shape
    length = 4 * piece
    blocks = length // BLOCK
    heads = dt_ref.shape[2]
    n2 = bc_ref.shape[2]
    small_cols = wb.shape[1]
    dp = lax.axis_index("dp")
    place, at = ring_place(n)
    me, other, across = tensor_place()
    core = me % 2
    facing = (other + 2) % 4

    def keep_wide(ref):
        def keep(way, part, d):
            return ref.at[span(d * rows, rows, 16), pl.ds(way * width // 2 + part * width // 4, width // 4)]

        return keep

    def keep_out(way, part, d):
        first = way * out_rows // 2 + part * out_rows // 4
        return wo.at[pl.ds(first, out_rows // 4), span(d * out_cols, out_cols, 128)]

    def keep_small(way, part, d):
        return wb.at[span(d * rows + core * rows // 2 + way * rows // 4, rows // 4, 16), :]

    def keep_rows(part, t):
        if part < seqs:
            return u.at[span(part * length + t * piece, piece, 16), :]
        return gf_out.at[part - seqs, span(t * piece, piece, 16), :]

    x_ring = RingGather(n, 2, keep_wide(wx), sems[0:2])
    small = RingGather(n, 1, keep_small, sems[2:4])
    z_ring = RingGather(n, 2, keep_wide(wz), sems[4:6])
    out_ring = RingGather(n, 2, keep_out, sems[6:8])
    token_rows = RowGather(keep_rows, sems[8:10])
    halves_send, halves_recv, sums_send, sums_recv = sems[10:14]

    def half(ahead, whose):
        d = (dp + ahead) % n
        ref = wb.at[span(d * rows + whose * rows // 2, rows // 2, 16), :]
        return remote(ref, ref, halves_send.at[ahead], halves_recv.at[ahead], {"tensor": other})

    def sums_copy(kind):
        ref = sums.at[me]
        target = {"tensor": (other, across, facing)[kind]}
        return remote(ref, ref, sums_send.at[kind], sums_recv.at[kind], target)

    keeps = [
        pltpu.make_async_copy(src, dst, keep_sem.at[j])
        for j, (src, dst) in enumerate(((wx, wx_out), (wb, wb_out), (wz, wz_out), (u, u_out), (wo, wo_out)))
    ]

    def streams(k):
        return [
            pltpu.make_async_copy(
                gf_out.at[:, :, span(at(place - (1 - 2 * way) * k) * out_cols, out_cols, 128)],
                g_cols.at[way],
                stream_sem.at[way],
            )
            for way in (0, 1)
        ]

    def start(copies):
        for copy in copies:
            copy.start()

    def wait(copies):
        for copy in copies:
            copy.wait()

    @pl.when(i == 0)
    def _():
        def held(s, h):
            return z.at[pl.ds((2 * s + h) * piece, piece), :]

        halves = [(s, h) for s in range(seqs) for h in (0, 1)]
        cut = lambda h: pl.ds(h * (model // 2), model // 2)
        own = [
            (wzx_ref.at[1], wx.at[span(dp * rows, rows, 16), :]),
            (wbc_ref, wb.at[span(dp * rows, rows, 16), :]),
            (wzx_ref.at[0], wz.at[span(dp * rows, rows, 16), :]),
            (wout_ref, wo.at[:, span(dp * out_cols, out_cols, 128)]),
        ]
        own += [(hidden_ref.at[s, :, cut(h)], held(seqs + s, h)) for s, h in halves]
        own += [(g_ref.at[s, :, cut(h)], held(s, h)) for s, h in halves]
        loads = [pltpu.make_async_copy(a, b, load_sem.at[j]) for j, (a, b) in enumerate(own)]
        first = 4 + 2 * seqs
        stores = [
            pltpu.make_async_copy(
                held(s, h), gf_out.at[s, span(me * piece, piece, 16), cut(h)], load_sem.at[first + 2 * seqs + j]
            )
            for j, (s, h) in enumerate(halves)
        ]
        start(loads)
        greet(n, [{"tensor": facing}])
        loads[0].wait()
        x_ring.step(0)
        loads[1].wait()
        small.step(0)
        wait(loads[4:first])
        for s in range(seqs):
            left = z[pl.ds((2 * (seqs + s)) * piece, piece), :].astype(F32)
            right = z[pl.ds((2 * (seqs + s) + 1) * piece, piece), :].astype(F32)
            squares = jnp.sum(left * left + right * right, axis=1, keepdims=True)
            scale = lax.rsqrt(squares / model + EPS)
            to = span(s * length + me * piece, piece, 16)
            u[to, cut(0)] = (left * scale * gain_ref[:, cut(0)]).astype(BF16)
            u[to, cut(1)] = (right * scale * gain_ref[:, cut(1)]).astype(BF16)
            token_rows.start(s)
        wait(loads[first:])
        start(stores)
        wait(loads[2:4])
        wait(stores)
        for k in range(1, n):
            x_ring.step(k)
            small.step(k)
            if k == n - 1:
                z_ring.step(0)
            if k == n // 2:
                token_rows.forward(0)
                token_rows.start(seqs)
        for ahead in range(1, n):
            half(ahead, core).start()
        for ahead in range(1, n):
            half(ahead, 1 - core).wait_recv()
        token_rows.wait(0)
        start(keeps[:2])
        lanes = small_cols - n2
        pick = lax.broadcasted_iota(jnp.int32, (lanes, lanes), 0) == (
            lax.broadcasted_iota(jnp.int32, (lanes, lanes), 1) + me * heads
        )
        wdt[...] = dot(wb[:, n2:], pick.astype(BF16)).astype(BF16)

    b = i - 1

    @pl.when((b >= 0) & (b < n))
    def _():
        @pl.when(b < n - 1)
        def _():
            z_ring.later(b + 1)

        @pl.when(b == n - 2)
        def _():
            out_ring.step(0)

        @pl.when(b == n - 1)
        def _():
            keeps[2].start()
            out_ring.step(1)

        @pl.when(b == 0)
        def _():
            token_rows.forward(1)
            token_rows.start(seqs + 1)

        @pl.when(b == blocks)
        def _():
            token_rows.wait(1)
            keeps[3].start()

        at_block = span(b * BLOCK, BLOCK, BLOCK)
        tokens = u[at_block, :]
        x = dot(tokens, wx[...])
        bc = dot(tokens, wb[:, :n2])
        dt = dot(tokens, wdt[...])[:, :heads]
        x_ref[0] = x.astype(BF16)
        bc_ref[0] = bc.astype(BF16)
        dt_ref[0] = dt
        forward_block(
            b % blocks, x, bc, dt, marks_ref, *shared, y.at[at_block, :], cx_ref, cbc_ref, states_ref, *scratch
        )

    c = i - (n + 1)

    def add_shard(k):
        wait(streams(k))
        for way in (0, 1):
            e = pl.ds(way * (out_rows // 2), out_rows // 2)
            d = at(place - (1 - 2 * way) * k)
            cols = g_cols[way].reshape(seqs * length, out_cols)
            value = dot_nt(cols, wo[e, span(d * out_cols, out_cols, 128)])

            @pl.when(k == 0)
            def _():
                dn[:, e] = value

            @pl.when(k > 0)
            def _():
                dn[:, e] += value

    @pl.when((c >= 0) & (c < n - 2))
    def _():
        @pl.when(c == 0)
        def _():
            token_rows.forward(seqs)
            token_rows.forward(seqs + 1)
            token_rows.wait(seqs)
            token_rows.wait(seqs + 1)
            start(streams(0))
            add_shard(0)
            start(streams(1))

        @pl.when((c >= 1) & (c <= 4))
        def _():
            part = span((c - 1) * (seqs * length // 4), seqs * length // 4, 16)
            z[part, :] = dot(u[part, :], wz[...]).astype(BF16)

        add_shard(c + 1)
        start(streams(c + 2))
        out_ring.later(c + 2)

        @pl.when(c == n - 3)
        def _():
            add_shard(n - 1)
            keeps[4].start()

            def block_sums(e, _):
                part = span(e * BLOCK, BLOCK, BLOCK)
                zf = z[part, :].astype(F32)
                gated = y[part, :] * (zf * sigmoid(zf))
                squares = jnp.sum(gated * gated, axis=1, keepdims=True)
                inner = jnp.sum(gate_ref[...] * dn[part, :] * gated, axis=1, keepdims=True)
                lane = lax.broadcasted_iota(jnp.int32, (1, 128), 1)
                both = jnp.where(lane == 0, squares, jnp.where(lane == 1, inner, 0.0))
                sums[me, :, part] = both.T[0:8, :]
                return 0

            lax.fori_loop(0, n, block_sums, 0)
            for kind in range(3):
                sums_copy(kind).start()

    e = i - (2 * n - 1)

    @pl.when(e >= 0)
    def _():
        @pl.when(e == 0)
        def _():
            for kind in range(3):
                sums_copy(kind).wait_recv()
            grad_ref[...] = jnp.zeros_like(grad_ref)

        part = span(e * BLOCK, BLOCK, BLOCK)
        whole = (sums[0, :, part] + sums[1, :, part]) + (sums[2, :, part] + sums[3, :, part])
        cols = jnp.concatenate([whole, jnp.zeros((120, BLOCK), F32)], axis=0).T / (4 * width)
        inverse = lax.rsqrt(cols[:, 0:1] + EPS)
        zf = z[part, :].astype(F32)
        sig = sigmoid(zf)
        silu = zf * sig
        yf = y[part, :]
        dnf = dn[part, :]
        gain = gate_ref[...]
        gated = yf * silu
        scaled_gated = gated * inverse
        normed_ref[...] = (scaled_gated * gain).astype(BF16)
        grad_ref[...] += jnp.sum(dnf * scaled_gated, axis=0, keepdims=True)
        d_gated = inverse * (dnf * gain) - gated * (inverse * inverse * inverse * cols[:, 1:2])
        dy_ref[...] = (d_gated * silu).astype(BF16)
        dz_ref[...] = (d_gated * yf * (sig * (1.0 + zf * (1.0 - sig)))).astype(BF16)

        @pl.when(e == n - 1)
        def _():
            wait(keeps)
            for ring in (x_ring, small, z_ring, out_ring):
                ring.finish()
            token_rows.finish(2 * seqs)
            for ahead in range(1, n):
                half(ahead, core).wait_send()
            for kind in range(3):
                sums_copy(kind).wait_send()


def forward_all(n, hidden, g, w_zx, w_bc, w_out, pre_gain, gate_gain, marks, shared):
    seqs, piece, model = hidden.shape
    rows, width = w_zx.shape[1:]
    out_rows, out_cols = w_out.shape
    length = 4 * piece
    tokens = seqs * length
    blocks = length // BLOCK
    n2 = shared[1].shape[1]
    heads = shared[2].shape[1]
    small = w_bc.shape[1]
    sem = pltpu.SemaphoreType.DMA
    ring = [sem((2, 2, n - 1))] * 2
    anywhere = pl.BlockSpec(memory_space=pl.ANY)
    whole = lambda *shape: pl.BlockSpec(shape, lambda i: (0,) * len(shape))
    b = lambda i: jnp.minimum(jnp.maximum(i - 1, 0), n - 1)
    e = lambda i: jnp.maximum(i - (2 * n - 1), 0)
    tok = lambda w: pl.BlockSpec((1, BLOCK, w), lambda i: (b(i) // blocks, b(i) % blocks, 0))
    gate = pl.BlockSpec((BLOCK, width), lambda i: (e(i), 0))
    out_shape = [
        ((tokens, model), BF16),
        ((seqs, length, model), BF16),
        ((rows * n, width), BF16),
        ((rows * n, width), BF16),
        ((rows * n, small), BF16),
        ((out_rows, out_cols * n), BF16),
        ((seqs, length, width), F32),
        ((seqs, length, width), BF16),
        ((seqs, length, n2), F32),
        ((seqs, length, n2), BF16),
        ((seqs, length, heads), F32),
        ((seqs, blocks, n2 // 2, width), BF16),
        ((tokens, width), BF16),
        ((tokens, width), BF16),
        ((tokens, width), BF16),
        ((1, width), F32),
    ]
    return pl.pallas_call(
        functools.partial(all_kernel, n),
        grid=(3 * n - 1,),
        in_specs=[anywhere] * 5
        + [
            whole(1, model),
            whole(1, width),
            pl.BlockSpec((1, 8, BLOCK), lambda i: (b(i) // blocks, 0, b(i) % blocks)),
        ]
        + shared_specs(width, n2, heads),
        out_specs=[anywhere] * 6
        + [tok(width), tok(width), tok(n2), tok(n2), tok(heads)]
        + [pl.BlockSpec((1, 1, n2 // 2, width), lambda i: (b(i) // blocks, b(i) % blocks, 0, 0))]
        + [gate] * 3
        + [whole(1, width)],
        out_shape=[jax.ShapeDtypeStruct(*s) for s in out_shape],
        scratch_shapes=forward_scratch(width, n2)
        + [
            pltpu.VMEM((tokens, model), BF16),
            pltpu.VMEM((rows * n, width), BF16),
            pltpu.VMEM((rows * n, width), BF16),
            pltpu.VMEM((out_rows, out_cols * n), BF16),
            pltpu.VMEM((rows * n, small), BF16),
            pltpu.VMEM((rows * n, small - n2), BF16),
            pltpu.VMEM((2, seqs, length, out_cols), BF16),
            pltpu.VMEM((tokens, width), F32),
            pltpu.VMEM((tokens, width), BF16),
            pltpu.VMEM((tokens, width), F32),
            pltpu.VMEM((4, 8, tokens), F32),
            sem((4 + 6 * seqs,)),
            sem((5,)),
            sem((2,)),
        ]
        + ring + [sem((2, 1, n - 1))] * 2 + ring + ring
        + [sem((3, 2 * seqs))] * 2 + [sem((n,))] * 2 + [sem((3,))] * 2,
        compiler_params=pltpu.CompilerParams(
            collective_id=0, has_side_effects=True, vmem_limit_bytes=63 * 2**20
        ),
        name="forward_all",
    )(hidden, g, w_zx, w_bc, w_out, pre_gain, gate_gain, marks, *shared)


class RingScatter:
    def __init__(self, n, term, slots, sems):
        self.n, self.term, self.slots = n, term, slots
        self.send_sem, self.recv_sem = sems
        self.place, self.at = ring_place(n)

    def copy(self, way, k):
        sign = 1 - 2 * way
        return remote(
            self.slots.at[way, k],
            self.slots.at[way, k + 1],
            self.send_sem.at[way, k],
            self.recv_sem.at[way, k],
            {"dp": self.at(self.place + sign)},
        )

    def step(self, way, k):
        value = self.term(way, self.at(self.place - (1 - 2 * way) * (1 + k)))

        @pl.when(k == 0)
        def _():
            self.slots[way, 0] = value.astype(BF16)

        @pl.when(k > 0)
        def _():
            self.copy(way, k - 1).wait_recv()

            @pl.when(k < self.n - 1)
            def _():
                self.slots[way, k] = (value + self.slots[way, k].astype(F32)).astype(BF16)

        @pl.when(k < self.n - 1)
        def _():
            self.copy(way, k).start()

        return value

    def last(self, way, value):
        return value + self.slots[way, self.n - 1].astype(F32)

    def finish(self):
        for k in range(self.n - 1):
            for way in (0, 1):
                self.copy(way, k).wait_send()


class RowScatter:
    def __init__(self, parts, term, hold, sems):
        self.parts, self.term, self.hold = parts, term, hold
        self.send_sem, self.recv_sem = sems
        self.me, self.other, self.across = tensor_place()

    def copy(self, kind, part):
        src, dst = ((0, 1), (1, 2), (0, 3))[kind]
        return remote(
            self.hold.at[src, part],
            self.hold.at[dst, part],
            self.send_sem.at[kind, part],
            self.recv_sem.at[kind, part],
            {"tensor": self.across if kind == 1 else self.other},
        )

    def step(self, j, store, wait=True):
        late = j // (2 * self.parts)
        near = j - 2 * self.parts
        stage = (1 - late) * (j % 2) + late * (2 + near // self.parts)
        part = (1 - late) * (j // 2) + late * (near % self.parts)
        x, core = self.me // 2, self.me % 2
        value = self.term(2 * ((x + 1 - stage // 2) % 2) + (core + 1 - stage % 2) % 2, part)

        @pl.when(stage == 0)
        def _():
            self.hold[0, part] = value.astype(BF16)
            self.copy(0, part).start()

        @pl.when(stage == 1)
        def _():
            self.copy(0, part).wait_recv()
            self.hold[1, part] = (value + self.hold[1, part].astype(F32)).astype(BF16)
            self.copy(1, part).start()

        @pl.when(stage == 2)
        def _():
            self.copy(0, part).wait_send()
            self.hold[0, part] = value.astype(BF16)
            self.copy(2, part).start()

        @pl.when(stage == 3)
        def _():
            store(part, value + self.arrived(part) if wait else value)

        return value, 2 * ((x + 1 - stage // 2) % 2) + (core + 1 - stage % 2) % 2, part

    def arrived(self, part):
        self.copy(2, part).wait_recv()
        self.copy(1, part).wait_recv()
        return self.hold[3, part].astype(F32) + self.hold[2, part].astype(F32)

    def finish(self):
        for part in range(self.parts):
            for kind in (1, 2):
                self.copy(kind, part).wait_send()


def product_term(a_ref, b_ref, count):
    def term(way, d):
        half = b_ref.shape[1] // 2
        return dot_tn(a_ref[:, span(d * count, count, 128)], b_ref[:, pl.ds(way * half, half)])

    return term


def back_kernel(n, *refs):
    (normed_ref, g_ref, u_ref, dz_ref, wo_ref, hidden_ref), refs = refs[:6], refs[6:]
    ins, refs = refs[:14], refs[14:]
    (out_ref, gout_ref, gz_ref), refs = refs[:3], refs[3:]
    outs, refs = refs[:5], refs[5:]
    scratch, refs = refs[:7], refs[7:]
    normed, dz, wo, g_cols, u_cols, out_slots, z_slots, hold, load_sem, stream_sem = refs[:10]
    sems = refs[10:]

    k = pl.program_id(0)
    blocks = 4
    piece = out_ref.shape[1]
    length = blocks * BLOCK
    count = g_ref.shape[1] // n
    half = gz_ref.shape[1] // 2
    place, at = ring_place(n)

    loads = [
        pltpu.make_async_copy(src, dst, load_sem.at[i])
        for i, (src, dst) in enumerate(((normed_ref, normed), (dz_ref, dz), (wo_ref, wo)))
    ]

    def streams(k):
        copies = []
        for way in (0, 1):
            d = at(place - (1 - 2 * way) * (1 + k))
            for i, (src, dst) in enumerate(((g_ref, g_cols), (u_ref, u_cols))):
                copies.append(
                    pltpu.make_async_copy(
                        src.at[:, span(d * count, count, 128)], dst.at[way], stream_sem.at[i, way]
                    )
                )
        return copies

    @pl.when(k == 0)
    def _():
        for copy in loads + streams(0):
            copy.start()
        greet(n)
        for copy in loads:
            copy.wait()

    for copy in streams(k):
        copy.wait()

    def half_product(a_ref, b_ref):
        def term(way, d):
            return dot_tn(a_ref[way], b_ref[:, pl.ds(way * half, half)])

        return term

    out_ring = RingScatter(n, half_product(g_cols, normed), out_slots, sems[0:2])
    z_ring = RingScatter(n, half_product(u_cols, dz), z_slots, sems[2:4])
    for way in (0, 1):
        value = out_ring.step(way, k)

        @pl.when(k == n - 1)
        def _():
            gout_ref[pl.ds(way * half, half), :] = out_ring.last(way, value).T

    for way in (0, 1):
        value = z_ring.step(way, k)

        @pl.when(k == n - 1)
        def _():
            gz_ref[:, pl.ds(way * half, half)] = z_ring.last(way, value)

    @pl.when(k < n - 1)
    def _():
        for copy in streams(k + 1):
            copy.start()

    def mixed_term(t, part):
        return dot(normed[span(part * length + t * piece, piece, 16), :], wo[...])

    def store(part, value):
        out_ref[0] = (hidden_ref[0].astype(F32) + value).astype(BF16)

    rows = RowScatter(2, mixed_term, hold, sems[4:6])
    rows.step(k, store)

    backward_block(k // blocks, k % blocks, *ins, *outs, *scratch)

    @pl.when(k == n - 1)
    def _():
        rows.finish()
        out_ring.finish()
        z_ring.finish()


def backward_all(n, small, hidden, normed, g, u, dz, w_out, dy, x, cx, bc, cbc, dt, marks, states, shared):
    seqs, length, channels = x.shape
    n2, heads = bc.shape[2], dt.shape[2]
    tokens, model = g.shape
    piece = hidden.shape[1]
    count = model // n
    blocks = length // BLOCK
    sem = pltpu.SemaphoreType.DMA
    anywhere = pl.BlockSpec(memory_space=pl.ANY)
    ins, outs = backward_specs(channels, n2, heads, small, lambda k: (k // blocks, blocks - 1 - k % blocks))
    late = lambda k: (jnp.maximum(k - (n - 2), 0), 0, 0)
    part = pl.BlockSpec((1, piece, model), late)
    single = pl.BlockSpec((1, piece, model), late, pipeline_mode=pl.Buffered(1))
    whole = lambda *shape: pl.BlockSpec(shape, lambda k: (0,) * len(shape))
    return pl.pallas_call(
        functools.partial(back_kernel, n),
        grid=(n,),
        in_specs=[anywhere] * 5 + [single] + ins,
        out_specs=[part, whole(channels, count), whole(count, channels)] + outs,
        out_shape=[
            jax.ShapeDtypeStruct(hidden.shape, BF16),
            jax.ShapeDtypeStruct((channels, count), F32),
            jax.ShapeDtypeStruct((count, channels), F32),
        ]
        + backward_outs(seqs, length, channels, n2, small),
        scratch_shapes=backward_scratch(channels, n2)
        + [
            pltpu.VMEM((tokens, channels), BF16),
            pltpu.VMEM((tokens, channels), BF16),
            pltpu.VMEM((channels, model), BF16),
            pltpu.VMEM((2, tokens, count), BF16),
            pltpu.VMEM((2, tokens, count), BF16),
            pltpu.VMEM((2, n, count, channels // 2), BF16),
            pltpu.VMEM((2, n, count, channels // 2), BF16),
            pltpu.VMEM((4, seqs, piece, model), BF16),
            sem((3,)),
            sem((2, 2)),
        ]
        + [sem((2, n - 1))] * 4
        + [sem((3, seqs))] * 2,
        compiler_params=pltpu.CompilerParams(
            collective_id=1, has_side_effects=True, vmem_limit_bytes=63 * 2**20
        ),
        name="backward_all",
    )(normed, g, u, dz, w_out, hidden, dy, x, cx, bc, cbc, dt, marks, states, *shared)


class Fold:
    def __init__(self, n, total, came, sems):
        self.total, self.came = total, came
        self.send_sem, self.recv_sem = sems
        dp = lax.axis_index("dp")
        _, other, across = tensor_place()
        partners, ahead = [], 1
        while ahead < n:
            partners.append({"dp": dp + ahead * (1 - 2 * ((dp // ahead) % 2))})
            ahead *= 2
        self.over_dp = partners
        self.partners = partners + [{"tensor": other}, {"tensor": across}]

    def copy(self, r):
        return remote(
            self.total.at[r], self.came.at[r], self.send_sem.at[r], self.recv_sem.at[r], self.partners[r]
        )

    def start(self, r):
        self.copy(r).start()

    def take(self, r):
        self.copy(r).wait_recv()
        self.total[r + 1] = self.total[r] + self.came[r]

    def finish(self):
        for r in range(len(self.partners)):
            self.copy(r).wait_send()


def in_kernel(
    n, u_hbm, dz_hbm, dx_hbm, wz_hbm, wx_hbm, wb_hbm, dbc_hbm, gx_in, gbc_in, gh_in, gate_in, gain_ref,
    din_ref, gx_ref, gb_ref, sums_ref,
    u_ref, dz_ref, dx_ref, wz_ref, wx_ref, wb_ref, dbc_ref,
    x_slots, b_slots, hold, bc_hold, low, swap, pre, total, came, load_sem, *sems,
):
    seqs, piece = din_ref.shape[:2]
    tokens, model = u_ref.shape
    length = tokens // seqs
    count = model // n
    half = gx_ref.shape[1] // 2
    me, other, across = tensor_place()
    core = me % 2

    moves = ((dx_hbm, dx_ref), (u_hbm, u_ref), (dbc_hbm, dbc_ref), (dz_hbm, dz_ref), (wz_hbm, wz_ref), (wx_hbm, wx_ref), (wb_hbm, wb_ref))
    loads = [pltpu.make_async_copy(src, dst, load_sem.at[i]) for i, (src, dst) in enumerate(moves)]
    for load in loads[:3]:
        load.start()

    def bc_term(t, part):
        return dbc_ref[span(part * length + t * piece, piece, 16), :].astype(F32)

    def in_term(t, part):
        at = span(part * length + t * piece, piece, 16)
        return dot_nt(dz_ref[at, :], wz_ref[...]) + dot_nt(dx_ref[at, :], wx_ref[...])

    def b_term(way, d):
        total_rows = 0.0
        for t, which in ((me, 0), (other, 1)):
            for part in range(seqs):
                rows = span(part * length + t * piece, piece, 16)
                cols = span(d * count + core * count // 2, count // 2, 128)
                total_rows = total_rows + dot_tn(u_ref[rows, cols], low[which, part])
        return total_rows[way * count // 4 : (way + 1) * count // 4]

    bc_rows = RowScatter(seqs, bc_term, bc_hold, sems[0:2])
    in_rows = RowScatter(seqs, in_term, hold, sems[2:4])
    x_ring = RingScatter(n, product_term(u_ref, dx_ref, count), x_slots, sems[4:6])
    b_ring = RingScatter(n, b_term, b_slots, sems[6:8])
    pair_send, pair_recv, swap_send, swap_recv = sems[8:12]
    fold = Fold(n, total, came, sems[12:14])
    rounds = len(fold.partners)
    pair = remote(low.at[0], low.at[1], pair_send, pair_recv, {"tensor": other})

    total[0] = jnp.zeros_like(total[0])
    total[0, 0:6, :] = gx_in[0:6, :]
    total[0, 6:7, :] = gate_in[...]
    total[0, 7:8, 0:128] = gh_in[0:1, :]
    total[0, 7:8, 128:256] = gh_in[1:2, :]
    total[0, 8:13, 0 : gbc_in.shape[1]] = gbc_in[0:5, :]
    pre[...] = jnp.zeros_like(pre)
    greet(n, fold.over_dp)
    for load in loads[:3]:
        load.wait()
    for load in loads[3:]:
        load.start()

    def bc_store(part, value):
        low[0, part] = value.astype(BF16)

    def store(part, value):
        value = value + dot_nt(low[0, part], wb_ref[...])
        din_ref[part] = value
        pre[...] += jnp.sum(
            value * u_ref[span(part * length + me * piece, piece, 16), :].astype(F32), axis=0, keepdims=True
        )

    def row_step(j):
        value, t, part = in_rows.step(j, store, wait=False)

        @pl.when(j < 3 * seqs)
        def _():
            pre[...] += jnp.sum(
                value * u_ref[span(part * length + t * piece, piece, 16), :].astype(F32), axis=0, keepdims=True
            )

    def ring_step(k):
        for way in (0, 1):
            value = x_ring.step(way, k)

            @pl.when(k == n - 1)
            def _():
                gx_ref[:, pl.ds(way * half, half)] = x_ring.last(way, value)

    def b_step(k):
        for way in (0, 1):
            value = b_ring.step(way, k)

            @pl.when(k == n - 1)
            def _():
                swap[0, pl.ds(way * count // 4, count // 4), :] = b_ring.last(way, value)

    ring_step(0)
    for load in loads[3:]:
        load.wait()
    for j in range(2 * seqs):
        bc_rows.step(j, bc_store)
    row_step(0)

    def step(k, _):
        row_step(k)
        ring_step(k)

        @pl.when(k == 1)
        def _():
            for j in range(2 * seqs, 4 * seqs):
                bc_rows.step(j, bc_store)
            pair.start()
            pair.wait_recv()

        @pl.when(k >= 2)
        def _():
            b_step(k - 2)

        return 0

    lax.fori_loop(1, n, step, 0)
    gain = gain_ref[...]
    width = total.shape[2]
    for i in range(model // width):
        at = slice(i * width, (i + 1) * width)
        total[0, 13 + i : 14 + i, :] = pre[:, at] / gain[:, at]
    fold.start(0)
    b_step(n - 2)
    fold.take(0)
    fold.start(1)
    b_step(n - 1)
    cross = remote(swap.at[0], swap.at[1], swap_send.at[0], swap_recv.at[0], {"tensor": across})
    cross.start()
    fold.take(1)
    fold.start(2)
    cross.wait_recv()
    swap[2] = swap[0] + swap[1]
    back = remote(swap.at[2], swap.at[3], swap_send.at[1], swap_recv.at[1], {"tensor": other})
    back.start()
    fold.take(2)
    fold.start(3)
    gb_ref[span(core * count // 2, count // 2, 16), :] = swap[2]
    din_ref[0] += in_rows.arrived(0)
    fold.take(3)
    fold.start(4)
    for part in range(1, seqs):
        din_ref[part] += in_rows.arrived(part)
    back.wait_recv()
    gb_ref[span((1 - core) * count // 2, count // 2, 16), :] = swap[3]
    fold.take(4)
    sums_ref[0:8, :] = total[rounds - 2, 0:8, :]
    sums_ref[8:16, :] = total[rounds, 8:16, :]
    for copy in (pair, cross, back):
        copy.wait_send()
    for part in (bc_rows, in_rows, x_ring, b_ring, fold):
        part.finish()


def scatter_in(n, piece, u, dz, dx, w_z, w_x, w_bc, dbc, gx, gbc, gh, grad_gate, gain):
    tokens, model = u.shape
    width = dz.shape[1]
    small = dbc.shape[1]
    seqs = tokens // (4 * piece)
    count = model // n
    rounds = 5
    sem = pltpu.SemaphoreType.DMA
    vmem = pl.BlockSpec(memory_space=pltpu.VMEM)
    anywhere = pl.BlockSpec(memory_space=pl.ANY)
    big = (u, dz, dx, w_z, w_x, w_bc, dbc)
    return pl.pallas_call(
        functools.partial(in_kernel, n),
        in_specs=[anywhere] * 7 + [vmem] * 5,
        out_specs=[vmem] * 4,
        out_shape=[
            jax.ShapeDtypeStruct((seqs, piece, model), F32),
            jax.ShapeDtypeStruct((count, width), F32),
            jax.ShapeDtypeStruct((count, small), F32),
            jax.ShapeDtypeStruct((16, width), F32),
        ],
        scratch_shapes=[pltpu.VMEM(a.shape, BF16) for a in big]
        + [
            pltpu.VMEM((2, n, count, width // 2), BF16),
            pltpu.VMEM((2, n, count // 4, small), BF16),
            pltpu.VMEM((4, seqs, piece, model), BF16),
            pltpu.VMEM((4, seqs, piece, small), BF16),
            pltpu.VMEM((2, seqs, piece, small), BF16),
            pltpu.VMEM((4, count // 2, small), F32),
            pltpu.VMEM((1, model), F32),
            pltpu.VMEM((rounds + 1, 16, width), F32),
            pltpu.VMEM((rounds, 16, width), F32),
            sem((len(big),)),
        ]
        + [sem((3, seqs))] * 4 + [sem((2, n - 1))] * 4 + [sem(())] * 2 + [sem((2,))] * 2 + [sem((rounds,))] * 2,
        compiler_params=pltpu.CompilerParams(
            collective_id=2, has_side_effects=True, vmem_limit_bytes=63 * 2**20
        ),
        name="scatter_in",
    )(*big, gx, gbc, gh, grad_gate, gain)


def rms_scale(values):
    return lax.rsqrt(jnp.mean(values * values, axis=-1, keepdims=True) + EPS)


def gather_plain(u, g, w_zx, w_bc, w_out):
    w_zx = lax.all_gather(w_zx, "dp", axis=1, tiled=True)
    return (
        lax.all_gather(u, "tensor", axis=1, tiled=True),
        lax.all_gather(g, "tensor", axis=1, tiled=True),
        w_zx[1],
        w_zx[0],
        lax.all_gather(w_bc, "dp", axis=0, tiled=True),
        lax.all_gather(w_out, "dp", axis=1, tiled=True),
    )


def rows_of(values, piece):
    by_seq = values.reshape(-1, 4 * piece, values.shape[-1])
    return lax.psum_scatter(by_seq, "tensor", scatter_dimension=1, tiled=True)


def scatter_out_plain(piece, normed, g, u, dz, w_out):
    return (
        rows_of(dot(normed, w_out), piece),
        lax.psum_scatter(dot_tn(normed, g), "dp", scatter_dimension=1, tiled=True),
        lax.psum_scatter(dot_tn(u, dz), "dp", scatter_dimension=0, tiled=True),
    )


def scatter_in_plain(piece, u, dz, dx, w_z, w_x, w_bc, dbc):
    low = lax.psum(dbc.astype(F32), "tensor").astype(BF16)
    d_in = rows_of(dot_nt(dz, w_z) + dot_nt(dx, w_x), piece)
    first = lax.axis_index("tensor") * piece
    own = lax.dynamic_slice_in_dim(low.reshape(-1, 4 * piece, low.shape[1]), first, piece, 1)
    d_in = d_in + jnp.einsum("slc,dc->sld", own, w_bc, preferred_element_type=F32)
    return (
        d_in,
        lax.psum_scatter(dot_tn(u, dx), "dp", scatter_dimension=0, tiled=True),
        lax.psum_scatter(dot_tn(u, low), "dp", scatter_dimension=0, tiled=True),
    )


def local(
    n_dp,
    n_tensor,
    hidden,
    pre_gain,
    w_zx,
    w_bcdt,
    conv_x,
    conv_bc,
    dt_bias,
    a_log,
    d_skip,
    gate_gain,
    w_out,
    cotangent,
    segments,
):
    seqs, piece, model = hidden.shape
    length = segments.shape[1]
    tokens = seqs * length
    heads = dt_bias.shape[0]
    channels = conv_x.shape[1]
    n2 = conv_bc.shape[1]
    columns = w_bcdt.shape[1]
    tensor = lax.axis_index("tensor")
    kernels = n_dp == 8 and n_tensor == 4 and seqs == 2 and length == 4 * BLOCK

    x_piece = hidden.astype(F32)
    scale_in = rms_scale(x_piece)
    w_bc_piece = jnp.pad(w_bcdt, ((0, 0), (0, -columns % 128)))
    marks = row_marks(segments)
    spread = jnp.asarray(spread_matrix(heads, channels), BF16)
    skip = jnp.repeat(d_skip, channels // heads)[None]
    shared = (conv_x, conv_bc, dt_bias[None], a_log[None], skip, spread)
    if kernels:
        u, g, w_x, w_z, w_bc, w_o, cx, x, cbc, bc, dt, states, normed, dz, dy, grad_gate = forward_all(
            n_dp, hidden, cotangent, w_zx, w_bc_piece, w_out, pre_gain[None], gate_gain[None], marks, shared
        )
        g = g.reshape(tokens, model)
    else:
        u_piece = (x_piece * scale_in * pre_gain).astype(BF16)
        u, g, w_x, w_z, w_bc, w_o = gather_plain(u_piece, cotangent, w_zx, w_bc_piece, w_out)
        u = u.reshape(tokens, model)
        g = g.reshape(tokens, model)
        x = dot(u, w_x).reshape(seqs, length, channels)
        z = dot(u, w_z)
        bc_dt = dot(u, w_bc).reshape(seqs, length, -1)
        bc = bc_dt[:, :, :n2]
        dt = lax.dynamic_slice_in_dim(bc_dt, n2 + tensor * heads, heads, 2)
        y, cx, cbc, states = ssd_forward(x, bc, dt, marks, shared)
        d_normed = dot_nt(g, w_o)
        sig_z = sigmoid(z)
        silu_z = z * sig_z
        y_flat = y.reshape(tokens, channels)
        gated = y_flat * silu_z
        scaled = d_normed * gate_gain
        sums = jnp.stack([jnp.sum(gated * gated, axis=1), jnp.sum(scaled * gated, axis=1)])
        sums = lax.psum(sums, "tensor") / (channels * n_tensor)
        inverse = lax.rsqrt(sums[0] + EPS)[:, None]
        normed = (gated * inverse * gate_gain).astype(BF16)
        grad_gate = jnp.sum(d_normed * gated * inverse, axis=0)[None]
        d_gated = inverse * scaled - gated * inverse**3 * sums[1][:, None]
        dy = (d_gated * silu_z).astype(BF16)
        dz = (d_gated * y_flat * (sig_z * (1.0 + z * (1.0 - sig_z)))).astype(BF16)
        x, bc = x.astype(BF16), bc.astype(BF16)

    back_args = (dy.reshape(seqs, length, channels), x, cx, bc, cbc, dt, marks, states, shared)
    if kernels:
        out_hidden, grad_out, grad_z, *rest = backward_all(n_dp, w_bc.shape[1], hidden, normed, g, u, dz, w_o, *back_args)
    else:
        mixed, grad_out, grad_z = scatter_out_plain(piece, normed, g, u, dz, w_o)
        out_hidden = (x_piece + mixed).astype(BF16)
        rest = ssd_backward(w_bc.shape[1], *back_args)
    dx, dbc, gx, gbc, gh = rest
    in_args = (piece, u, dz, dx.reshape(tokens, channels), w_z, w_x, w_bc, dbc.reshape(tokens, -1))
    if kernels:
        d_in, grad_x, grad_bc, sums = scatter_in(n_dp, *in_args, gx, gbc, gh, grad_gate, pre_gain[None])
        grad_pre = sums[13:].reshape(-1)[:model]
        grad_conv_bc = sums[8:13, :n2]
    else:
        d_in, grad_x, grad_bc = scatter_in_plain(*in_args)
        grad_pre = jnp.sum(d_in * x_piece * scale_in, axis=(0, 1))
        steps = jnp.pad(gh[:2], ((0, 0), (0, channels - gh.shape[1])))
        sums = lax.psum(jnp.concatenate([gx[:6], grad_gate, steps]), "dp")
        sums = jnp.concatenate([sums[:7], jnp.concatenate([sums[7, :128], sums[8, : channels - 128]])[None]])
        grad_conv_bc, grad_pre = lax.psum((gbc[:5], grad_pre), ("dp", "tensor"))

    gain_grad = d_in * pre_gain
    d_hidden = cotangent.astype(F32) + scale_in * gain_grad - x_piece * scale_in**3 * jnp.mean(
        gain_grad * x_piece, axis=-1, keepdims=True
    )
    return (
        out_hidden,
        d_hidden,
        grad_pre,
        jnp.stack([grad_z, grad_x]),
        grad_bc[:, :columns],
        sums[:5],
        grad_conv_bc,
        sums[7, :heads],
        sums[7, 128 : 128 + heads],
        sums[5].reshape(heads, -1).sum(axis=1),
        sums[6],
        grad_out,
    )


def solution(mesh):
    placed = (
        P("dp", "tensor", None),
        P(),
        P(None, "dp", "tensor"),
        P("dp", None),
        P(None, "tensor"),
        P(),
        P("tensor"),
        P("tensor"),
        P("tensor"),
        P("tensor"),
        P("tensor", "dp"),
        P("dp", "tensor", None),
        P("dp", None),
    )
    return jax.shard_map(
        functools.partial(local, mesh.shape["dp"], mesh.shape["tensor"]),
        mesh=mesh,
        in_specs=placed,
        out_specs=(
            P("dp", "tensor", None),
            P("dp", "tensor", None),
            P(),
            P(None, "dp", "tensor"),
            P("dp", None),
            P(None, "tensor"),
            P(),
            P("tensor"),
            P("tensor"),
            P("tensor"),
            P("tensor"),
            P("tensor", "dp"),
        ),
        check_vma=False,
    )
```

```python
import functools

import jax
import jax.numpy as jnp
import numpy as np
from jax import lax
from jax.experimental import pallas as pl
from jax.experimental.pallas import tpu as pltpu
from jax.sharding import PartitionSpec as P

MESH = pl.DeviceIdType.MESH
EPS = 1e-05
BLOCK = 256
F32 = jnp.float32
BF16 = jnp.bfloat16
EXACT = lax.Precision.HIGHEST
LOG2E = 1.4426950408889634
NEG = -1e30


def sigmoid(v):
    return 0.5 * jnp.tanh(0.5 * v) + 0.5


def split3(v):
    hi = v.astype(BF16)
    rest = v - hi.astype(F32)
    mid = rest.astype(BF16)
    low = (rest - mid.astype(F32)).astype(BF16)
    return hi, mid, low


def dot(a, b):
    return jnp.dot(a, b, preferred_element_type=F32)


def dot_nt(a, b):
    return lax.dot_general(a, b, (((1,), (1,)), ((), ())), preferred_element_type=F32)


def dot_tn(a, b):
    return lax.dot_general(a, b, (((0,), (0,)), ((), ())), preferred_element_type=F32)


def softplus(v):
    return jnp.maximum(v, 0.0) + jnp.log1p(jnp.exp(-jnp.abs(v)))


def head_rows(raw, dt_bias, a_log):
    q = raw.shape[1]
    upto = (
        lax.broadcasted_iota(jnp.int32, (q, q), 0) <= lax.broadcasted_iota(jnp.int32, (q, q), 1)
    ).astype(F32)
    biased = raw + dt_bias
    step = softplus(biased)
    rate = -jnp.exp(a_log) * step
    cum = jnp.dot(rate, upto, precision=EXACT, preferred_element_type=F32) * LOG2E
    return biased, step, rate, cum


def exact_nt(a, b):
    a_hi, a_mid, _ = split3(a)
    b_hi, b_mid, _ = split3(b)
    return dot_nt(a_hi, b_hi) + dot_nt(a_hi, b_mid) + dot_nt(a_mid, b_hi)


def to_columns(rows):
    return jnp.concatenate([rows, jnp.zeros((128 - rows.shape[0], rows.shape[1]), F32)], axis=0).T


def head_columns(reads, last, step, cum, third):
    cum_end = cum[:, BLOCK - 1 : BLOCK]
    rows = []
    for factor in (reads * jnp.exp2(cum), last * jnp.exp2(cum_end - cum) * step):
        hi, mid, _ = split3(factor)
        rows += [hi.astype(F32), mid.astype(F32)]
    cols = to_columns(jnp.concatenate(rows + [third], axis=0))
    return cols[:, 4 * cum.shape[0] :], cols.astype(BF16), jnp.exp2(cum_end)


def log2_step(step):
    return jnp.log(jnp.maximum(step, 1e-37)) * LOG2E


def forward_block(
    block, x, bc, dt, marks_ref, taps_x_ref, taps_bc_ref, bias_ref, alog_ref, skip_ref, spread_ref, pick_ref,
    y_ref, cx_ref, cbc_ref, states_ref,
    xs, bs, state, mask_bias,
):
    q = BLOCK
    heads = dt.shape[0]
    channels = x.shape[-1]
    width = channels // heads

    @pl.when(block == 0)
    def _():
        xs[0:8, :] = jnp.zeros((8, xs.shape[1]), F32)
        bs[0:8, :] = jnp.zeros((8, bs.shape[1]), F32)
        state[...] = jnp.zeros_like(state)

    marks = to_columns(marks_ref[0])
    lag_masks = [marks[:, k : k + 1] for k in range(3)]

    def conv(hold, at, taps_ref):
        out = taps_ref[4:5, at] + taps_ref[3:4, at] * hold[8 : 8 + q, at]
        for lag in (1, 2, 3):
            out = out + (lag_masks[lag - 1] * hold[8 - lag : 8 - lag + q, at]) * taps_ref[3 - lag : 4 - lag, at]
        return out

    bs[8 : 8 + q, :] = bc
    xs[8 : 8 + q, :] = x
    cbc = conv(bs, slice(None), taps_bc_ref)
    cbc_ref[0] = cbc
    bc = cbc * sigmoid(cbc)
    n = bc.shape[1] // 2
    scores = exact_nt(bc[:, n:], bc[:, :n])
    b_mat, c_mat = bc[:, :n].astype(BF16), bc[:, n:].astype(BF16)
    b_turned = b_mat.T

    _, step, _, cum = head_rows(dt, bias_ref[...], alog_ref[...])
    cols, factors, carry = head_columns(marks_ref[0, 3:4, :], marks_ref[0, 4:5, :], step, cum, cum)
    source = cum - log2_step(step)
    carry_e = jnp.sum(carry * spread_ref[...].astype(F32), axis=0, keepdims=True)

    rows = lax.broadcasted_iota(jnp.int32, (q, q), 0)
    places = lax.broadcasted_iota(jnp.int32, (q, q), 1)
    mask_bias[...] = jnp.where((marks[:, 5:6] == marks_ref[0, 5:6, :]) & (rows >= places), 0.0, NEG)

    half = q // 2
    pair_width = 2 * width
    lane = lax.broadcasted_iota(jnp.int32, (1, pair_width), 1)
    every = slice(0, channels)
    cx = conv(xs, every, taps_x_ref)
    cx_ref[0] = cx
    xb = (cx * sigmoid(cx)).astype(BF16)
    xf = xb.astype(F32)
    stb = state[...].astype(BF16)
    states_ref[0, 0] = stb
    y_ref[...] = dot(c_mat, stb) * dot(factors, pick_ref[:, :channels]) + skip_ref[...] * xf
    scaled = (xf * dot(factors, pick_ref[:, channels:])).astype(BF16)
    state[...] = carry_e * state[...] + dot(b_turned, scaled)
    for pair in range(heads // 2):
        at = slice(pair * pair_width, (pair + 1) * pair_width)
        xp = xb[:, at]
        tops, lows = [], []
        for h in (2 * pair, 2 * pair + 1):
            col = cols[:, h : h + 1]
            row = source[h : h + 1, :]
            top = jnp.exp2((col[:half] - row[:, :half]) + mask_bias[:half, :half]) * scores[:half, :half]
            low = jnp.exp2((col[half:] - row) + mask_bias[half:, :]) * scores[half:, :]
            tops.append(top.astype(BF16))
            lows.append(low.astype(BF16))
        top = dot(jnp.concatenate(tops, axis=0), xp[:half])
        low = dot(jnp.concatenate(lows, axis=0), xp)
        first = lane < width
        y_ref[:half, at] += jnp.where(first, top[:half], top[half:])
        y_ref[half:, at] += jnp.where(first, low[:half], low[half:])

    xs[0:8, :] = xs[q : q + 8, :]
    bs[0:8, :] = bs[q : q + 8, :]


def backward_block(
    seq, step_id, dy_ref, x_ref, cx_ref, bc_ref, cbc_ref, dt_ref, marks_ref, states_ref,
    taps_x_ref, taps_bc_ref, bias_ref, alog_ref, skip_ref, spread_ref, pick_ref,
    dx_ref, dbc_ref, gx_ref, gbc_ref, gh_ref,
    ds_x, ds_bc, d_state, mask_bias, d_scores, d_in, row_sums,
):
    q = BLOCK
    heads = dt_ref.shape[1]
    channels = x_ref.shape[-1]
    width = channels // heads

    @pl.when(step_id == 0)
    def _():
        ds_x[:, q : q + 8, :] = jnp.zeros((3, 8, channels), F32)
        ds_bc[:, q : q + 8, :] = jnp.zeros((3, 8, ds_bc.shape[2]), F32)
        d_state[...] = jnp.zeros_like(d_state)

    @pl.when((step_id == 0) & (seq == 0))
    def _():
        gx_ref[...] = jnp.zeros_like(gx_ref)
        gbc_ref[...] = jnp.zeros_like(gbc_ref)
        gh_ref[...] = jnp.zeros_like(gh_ref)

    marks = to_columns(marks_ref[0])
    lag_masks = [marks[:, k : k + 1] for k in range(3)]

    def conv_back(d_out, value, hold, at, taps_ref, grad_ref):
        value = value.astype(F32)
        d_value = d_out * taps_ref[3:4, at]
        grad_ref[3:4, at] += jnp.sum(value * d_out, axis=0, keepdims=True)
        grad_ref[4:5, at] += jnp.sum(d_out, axis=0, keepdims=True)
        for lag in (1, 2, 3):
            hold[lag - 1, 0:q, at] = lag_masks[lag - 1] * d_out
            moved = hold[lag - 1, lag : lag + q, at]
            d_value = d_value + moved * taps_ref[3 - lag : 4 - lag, at]
            grad_ref[3 - lag : 4 - lag, at] += jnp.sum(value * moved, axis=0, keepdims=True)
            hold[lag - 1, q : q + 8, at] = hold[lag - 1, 0:8, at]
        return d_value

    cbc = cbc_ref[0]
    bc = cbc * sigmoid(cbc)
    n = bc.shape[1] // 2
    scores = exact_nt(bc[:, :n], bc[:, n:])
    b_mat, c_mat = bc[:, :n].astype(BF16), bc[:, n:].astype(BF16)
    c_turned = c_mat.T

    biased, step, rate, cum = head_rows(dt_ref[0], bias_ref[...], alog_ref[...])
    source = cum - log2_step(step)
    cols, factors, carry = head_columns(marks_ref[0, 3:4, :], marks_ref[0, 4:5, :], step, cum, source)
    carry_e = jnp.sum(carry * spread_ref[...].astype(F32), axis=0, keepdims=True)

    rows = lax.broadcasted_iota(jnp.int32, (q, q), 0)
    places = lax.broadcasted_iota(jnp.int32, (q, q), 1)
    mask_bias[...] = jnp.where((marks[:, 5:6] == marks_ref[0, 5:6, :]) & (rows <= places), 0.0, NEG)

    half = q // 2
    pair_width = 2 * width
    lane = lax.broadcasted_iota(jnp.int32, (1, pair_width), 1)
    first = lane < width
    d_scores[...] = jnp.zeros_like(d_scores)
    col_h = jnp.zeros((heads, q), F32)
    head_row = lax.broadcasted_iota(jnp.int32, (heads, 3 * half), 0)
    spread = spread_ref[...]
    cx = cx_ref[0]
    xb = (cx * sigmoid(cx)).astype(BF16)
    dyb = dy_ref[0]
    st = states_ref[0, 0]
    dye = dyb.astype(F32) * dot(factors, pick_ref[:, :channels])
    out_h = dot_nt(spread, (dye * dot(c_mat, st)).astype(BF16))
    dye = dye.astype(BF16)
    d_c = dot_nt(dye, st)
    dst = d_state[...].astype(BF16)
    kept = jnp.sum(d_state[...] * st.astype(F32), axis=0, keepdims=True) * carry_e
    carried = jnp.sum(spread.astype(F32) * kept, axis=1, keepdims=True)
    d_state[...] = carry_e * d_state[...] + dot(c_turned, dye)
    xf = xb.astype(F32)
    to_end = dot(factors, pick_ref[:, channels:])
    d_b = dot_nt((xf * to_end).astype(BF16), dst)
    dx_st = dot(b_mat, dst) * to_end
    state_h = dot_nt(spread, (xf * dx_st).astype(BF16))
    d_in[...] = dx_st
    for pair in range(heads // 2):
        at = slice(pair * pair_width, (pair + 1) * pair_width)
        xp, dyp = xb[:, at], dyb[:, at]
        none = jnp.zeros_like(xp)
        x_first, x_second = jnp.where(first, xp, none), jnp.where(first, none, xp)
        g_top = dot_nt(jnp.concatenate([x_first[:half], x_second[:half]], axis=0), dyp)
        g_low = dot_nt(jnp.concatenate([x_first[half:], x_second[half:]], axis=0), dyp[half:])
        tops, lows, d_top, d_low = [], [], 0.0, 0.0
        for which in (0, 1):
            h = 2 * pair + which
            own = slice(which * half, (which + 1) * half)
            col = cols[:, h : h + 1]
            row = cum[h : h + 1, :]
            top = jnp.exp2((row - col[:half]) + mask_bias[:half, :])
            low = jnp.exp2((row[:, half:] - col[half:]) + mask_bias[half:, half:])
            p_top = top * g_top[own]
            p_low = low * g_low[own]
            d_top = d_top + p_top
            d_low = d_low + p_low
            m_top = p_top * scores[:half, :]
            m_low = p_low * scores[half:, half:]
            late = jnp.sum(m_top[:, half:], axis=0, keepdims=True) + jnp.sum(m_low, axis=0, keepdims=True)
            row_sums[h : h + 1, :half] = jnp.sum(m_top[:, :half], axis=0, keepdims=True)
            row_sums[h : h + 1, half:] = late
            parts = split3(jnp.concatenate([m_top[:, :half] + m_top[:, half:], m_low], axis=0))
            col_h = col_h + dot_nt((head_row == h).astype(BF16), jnp.concatenate(parts, axis=1))
            tops.append((top * scores[:half, :]).astype(BF16))
            lows.append((low * scores[half:, half:]).astype(BF16))
        d_scores[:half, :] += d_top
        d_scores[half:, half:] += d_low
        top = dot(jnp.concatenate(tops, axis=0), dyp)
        low = dot(jnp.concatenate(lows, axis=0), dyp[half:])
        d_in[:half, at] += jnp.where(first, top[:half], top[half:])
        d_in[half:, at] += jnp.where(first, low[:half], low[half:])

    everywhere = slice(0, channels)
    dyf = dy_ref[0].astype(F32)
    cx = cx_ref[0]
    sig = sigmoid(cx)
    gx_ref[5:6, :] += jnp.sum(dyf * (cx * sig).astype(BF16).astype(F32), axis=0, keepdims=True)
    d_cx = (d_in[...] + skip_ref[...] * dyf) * (sig * (1.0 + cx * (1.0 - sig)))
    dx_ref[0] = conv_back(d_cx, x_ref[0], ds_x, everywhere, taps_x_ref, gx_ref).astype(BF16)

    dsb = d_scores[...].astype(BF16)
    d_b = d_b + dot(dsb, c_mat)
    d_c = d_c + dot_tn(dsb, b_mat)
    sig = sigmoid(cbc)
    d_cbc = jnp.concatenate([d_b, d_c], axis=1) * (sig * (1.0 + cbc * (1.0 - sig)))
    every = slice(0, 2 * n)
    dbc_ref[0, :, every] = conv_back(d_cbc, bc_ref[0], ds_bc, every, taps_bc_ref, gbc_ref).astype(BF16)

    used_h = col_h + state_h
    diff_h = row_sums[...] - col_h + out_h
    since = (rows >= places).astype(F32)
    before = (rows < places).astype(F32)
    d_rate = (
        jnp.dot(diff_h, since, precision=EXACT, preferred_element_type=F32)
        + jnp.dot(state_h, before, precision=EXACT, preferred_element_type=F32)
        + carried
    )
    sig_dt = sigmoid(biased)
    ratio = jnp.where(step < 1e-30, 1.0, sig_dt / jnp.maximum(step, 1e-30))
    d_raw = used_h * ratio - jnp.exp(alog_ref[...]) * sig_dt * d_rate
    lanes = dbc_ref.shape[2] - 2 * n
    mine = lax.broadcasted_iota(jnp.int32, (heads, lanes), 0) + lax.axis_index("tensor") * heads
    own = (lax.broadcasted_iota(jnp.int32, (heads, lanes), 1) == mine).astype(BF16)
    dbc_ref[0, :, 2 * n :] = dot_tn(d_raw.astype(BF16), own).astype(BF16)
    gh_ref[:, 0:1] += jnp.sum(d_raw, axis=1, keepdims=True)
    gh_ref[:, 1:2] += jnp.sum(d_rate * rate, axis=1, keepdims=True)


def row_marks(segments):
    seqs, length = segments.shape
    blocks = length // BLOCK
    lags = []
    for lag in (1, 2, 3):
        earlier = jnp.pad(segments, ((0, 0), (lag, 0)), constant_values=-1)[:, :length]
        lags.append(earlier == segments)
    grouped = segments.reshape(seqs, blocks, BLOCK)
    before = jnp.pad(segments, ((0, 0), (1, 0)), constant_values=-1)[:, :length].reshape(seqs, blocks, BLOCK)
    reads = (grouped == before[:, :, :1]).reshape(seqs, length)
    last = (grouped == grouped[:, :, -1:]).reshape(seqs, length)
    rows = [m.astype(F32) for m in (*lags, reads, last, segments)]
    return jnp.stack(rows + [jnp.zeros_like(rows[0])] * 2, axis=1)


def spread_matrix(heads, channels):
    width = channels // heads
    return (np.arange(heads)[:, None] == np.arange(channels)[None, :] // width).astype(np.float32)


def pick_matrix(heads, channels):
    spread = spread_matrix(heads, channels)
    out = np.zeros((128, 2 * channels), np.float32)
    for part in range(4):
        at = slice(part // 2 * channels, (part // 2 + 1) * channels)
        out[part * heads : (part + 1) * heads, at] = spread
    return out


def shared_specs(channels, n2, heads):
    full = lambda *shape: pl.BlockSpec(shape, lambda *i: (0,) * len(shape))
    return [
        full(5, channels),
        full(5, n2),
        full(heads, 1),
        full(heads, 1),
        full(1, channels),
        full(heads, channels),
        full(128, 2 * channels),
    ]


def forward_scratch(channels, n2):
    return [
        pltpu.VMEM((BLOCK + 8, channels), F32),
        pltpu.VMEM((BLOCK + 8, n2), F32),
        pltpu.VMEM((n2 // 2, channels), F32),
        pltpu.VMEM((BLOCK, BLOCK), F32),
    ]


def forward_kernel(x_ref, bc_ref, dt_ref, *refs):
    y_ref = refs[8]
    forward_block(pl.program_id(1), x_ref[0], bc_ref[0], dt_ref[0], *refs[:8], y_ref.at[0], *refs[9:])


def ssd_forward(x, bc, dt, marks, shared):
    seqs, length, channels = x.shape
    n2, heads = bc.shape[2], dt.shape[1]
    blocks = length // BLOCK
    tok = lambda w: pl.BlockSpec((1, BLOCK, w), lambda s, c: (s, c, 0))
    head = lambda w: pl.BlockSpec((1, w, BLOCK), lambda s, c: (s, 0, c))
    return pl.pallas_call(
        forward_kernel,
        grid=(seqs, blocks),
        in_specs=[tok(channels), tok(n2), head(heads), head(8)] + shared_specs(channels, n2, heads),
        out_specs=[
            tok(channels),
            tok(channels),
            tok(n2),
            pl.BlockSpec((1, 1, n2 // 2, channels), lambda s, c: (s, c, 0, 0)),
        ],
        out_shape=[
            jax.ShapeDtypeStruct((seqs, length, channels), F32),
            jax.ShapeDtypeStruct((seqs, length, channels), F32),
            jax.ShapeDtypeStruct((seqs, length, n2), F32),
            jax.ShapeDtypeStruct((seqs, blocks, n2 // 2, channels), BF16),
        ],
        scratch_shapes=forward_scratch(channels, n2),
        compiler_params=pltpu.CompilerParams(vmem_limit_bytes=48 * 2**20),
        name="ssd_forward",
    )(x, bc, dt, marks, *shared)


def backward_kernel(*refs):
    backward_block(pl.program_id(0), pl.program_id(1), *refs)


def backward_scratch(channels, n2, heads):
    return [
        pltpu.VMEM((3, BLOCK + 8, channels), F32),
        pltpu.VMEM((3, BLOCK + 8, n2), F32),
        pltpu.VMEM((n2 // 2, channels), F32),
        pltpu.VMEM((BLOCK, BLOCK), F32),
        pltpu.VMEM((BLOCK, BLOCK), F32),
        pltpu.VMEM((BLOCK, channels), F32),
        pltpu.VMEM((heads, BLOCK), F32),
    ]


def backward_specs(channels, n2, heads, small, place):
    tok = lambda w: pl.BlockSpec((1, BLOCK, w), lambda *i: (*place(*i), 0))
    full = lambda *shape: pl.BlockSpec(shape, lambda *i: (0,) * len(shape))
    ins = [tok(channels)] * 3 + [tok(n2)] * 2 + [
        pl.BlockSpec((1, heads, BLOCK), lambda *i: (place(*i)[0], 0, place(*i)[1])),
        pl.BlockSpec((1, 8, BLOCK), lambda *i: (place(*i)[0], 0, place(*i)[1])),
        pl.BlockSpec((1, 1, n2 // 2, channels), lambda *i: (*place(*i), 0, 0)),
    ]
    ins += shared_specs(channels, n2, heads)
    return ins, [tok(channels), tok(small), full(8, channels), full(8, n2), full(heads, 128)]


def backward_outs(seqs, length, channels, n2, heads, small):
    return [
        jax.ShapeDtypeStruct((seqs, length, channels), BF16),
        jax.ShapeDtypeStruct((seqs, length, small), BF16),
        jax.ShapeDtypeStruct((8, channels), F32),
        jax.ShapeDtypeStruct((8, n2), F32),
        jax.ShapeDtypeStruct((heads, 128), F32),
    ]


def ssd_backward(small, dy, x, cx, bc, cbc, dt, marks, states, shared):
    seqs, length, channels = x.shape
    n2, heads = bc.shape[2], dt.shape[1]
    blocks = length // BLOCK
    ins, outs = backward_specs(channels, n2, heads, small, lambda s, c: (s, blocks - 1 - c))
    return pl.pallas_call(
        backward_kernel,
        grid=(seqs, blocks),
        in_specs=ins,
        out_specs=outs,
        out_shape=backward_outs(seqs, length, channels, n2, heads, small),
        scratch_shapes=backward_scratch(channels, n2, heads),
        compiler_params=pltpu.CompilerParams(vmem_limit_bytes=56 * 2**20),
        name="ssd_backward",
    )(dy, x, cx, bc, cbc, dt, marks, states, *shared)


def ring_place(n):
    dp = lax.axis_index("dp")
    z, y = dp // 2, dp % 2

    def at(place):
        q = (place + 4 * n) % n
        return 2 * q + (q // (n // 2)) * (2 * n - 1 - 4 * q)

    return z + y * (n - 1 - 2 * z), at


def tensor_place():
    t = lax.axis_index("tensor")
    return t, t + 1 - 2 * (t % 2), (t + 2) % 4


def greet(n, more=()):
    place, at = ring_place(n)
    _, other, across = tensor_place()
    sem = pltpu.get_barrier_semaphore()
    targets = [{"dp": at(place + 1)}, {"dp": at(place - 1)}, {"tensor": other}, {"tensor": across}, *more]
    for target in targets:
        pl.semaphore_signal(sem, inc=1, device_id=target, device_id_type=MESH)
    pl.semaphore_wait(sem, len(targets))


def remote(src, dst, send_sem, recv_sem, target):
    return pltpu.make_async_remote_copy(
        src_ref=src, dst_ref=dst, send_sem=send_sem, recv_sem=recv_sem, device_id=target, device_id_type=MESH
    )


def span(first, count, unit):
    return pl.ds(pl.multiple_of(first, unit), count)


class RingGather:
    def __init__(self, n, parts, keep, sems):
        self.n, self.parts, self.keep = n, parts, keep
        self.send_sem, self.recv_sem = sems
        self.place, self.at = ring_place(n)

    def copy(self, way, part, step):
        sign = 1 - 2 * way
        ref = self.keep(way, part, self.at(self.place - sign * step))
        return remote(
            ref,
            ref,
            self.send_sem.at[way, part, step],
            self.recv_sem.at[way, part, step],
            {"dp": self.at(self.place + sign)},
        )

    def step(self, k):
        for part in range(self.parts):
            for way in (0, 1):
                if k > 0:
                    self.copy(way, part, k - 1).wait_recv()
                if k < self.n - 1:
                    self.copy(way, part, k).start()

    def later(self, k):
        for part in range(self.parts):
            for way in (0, 1):
                self.copy(way, part, k - 1).wait_recv()

                @pl.when(k < self.n - 1)
                def _():
                    self.copy(way, part, k).start()

    def finish(self):
        for k in range(self.n - 1):
            for part in range(self.parts):
                for way in (0, 1):
                    self.copy(way, part, k).wait_send()


class RowGather:
    def __init__(self, keep, sems):
        self.keep = keep
        self.send_sem, self.recv_sem = sems
        self.me, self.other, self.across = tensor_place()

    def copy(self, kind, part):
        ref = self.keep(part, self.across if kind == 2 else self.me)
        target = self.across if kind == 0 else self.other
        return remote(
            ref, ref, self.send_sem.at[kind, part], self.recv_sem.at[kind, part], {"tensor": target}
        )

    def start(self, part):
        self.copy(0, part).start()
        self.copy(1, part).start()

    def forward(self, part):
        self.copy(0, part).wait_recv()
        self.copy(2, part).start()

    def wait(self, part):
        self.copy(1, part).wait_recv()
        self.copy(2, part).wait_recv()

    def finish(self, parts):
        for part in range(parts):
            for kind in range(3):
                self.copy(kind, part).wait_send()


def all_kernel(n, *refs):
    (hidden_ref, g_ref, wzx_ref, wbc_ref, wout_ref, gain_ref, gate_ref, marks_ref), refs = refs[:8], refs[8:]
    shared, refs = refs[:7], refs[7:]
    (u_out, gf_out, wx_out, wz_out, wb_out, wo_out), refs = refs[:6], refs[6:]
    (cx_ref, x_ref, cbc_ref, bc_ref, dt_ref, states_ref), refs = refs[:6], refs[6:]
    (normed_ref, dz_ref, dy_ref, grad_ref, scale_ref), refs = refs[:5], refs[5:]
    scratch, refs = refs[:4], refs[4:]
    (u, wx, wz, wo, wb, wdt, g_cols, y, z, dn, sums), refs = refs[:11], refs[11:]
    (load_sem, keep_sem, stream_sem), sems = refs[:3], refs[3:]

    i = pl.program_id(0)
    rows, width = wzx_ref.shape[1:]
    out_rows, out_cols = wout_ref.shape
    seqs, piece, model = hidden_ref.shape
    length = 4 * piece
    blocks = length // BLOCK
    heads = dt_ref.shape[1]
    n2 = bc_ref.shape[2]
    small_cols = wb.shape[1]
    dp = lax.axis_index("dp")
    place, at = ring_place(n)
    me, other, across = tensor_place()
    core = me % 2
    facing = (other + 2) % 4

    def keep_wide(ref):
        def keep(way, part, d):
            return ref.at[span(d * rows, rows, 16), pl.ds(way * width // 2 + part * width // 4, width // 4)]

        return keep

    def keep_out(way, part, d):
        first = way * out_rows // 2 + part * out_rows // 4
        return wo.at[pl.ds(first, out_rows // 4), span(d * out_cols, out_cols, 128)]

    def keep_small(way, part, d):
        return wb.at[span(d * rows + core * rows // 2 + way * rows // 4, rows // 4, 16), :]

    def keep_rows(part, t):
        if part < seqs:
            return u.at[span(part * length + t * piece, piece, 16), :]
        return gf_out.at[part - seqs, span(t * piece, piece, 16), :]

    x_ring = RingGather(n, 2, keep_wide(wx), sems[0:2])
    small = RingGather(n, 1, keep_small, sems[2:4])
    z_ring = RingGather(n, 2, keep_wide(wz), sems[4:6])
    out_ring = RingGather(n, 2, keep_out, sems[6:8])
    token_rows = RowGather(keep_rows, sems[8:10])
    halves_send, halves_recv, sums_send, sums_recv = sems[10:14]

    def half(ahead, whose):
        d = (dp + ahead) % n
        ref = wb.at[span(d * rows + whose * rows // 2, rows // 2, 16), :]
        return remote(ref, ref, halves_send.at[ahead], halves_recv.at[ahead], {"tensor": other})

    def sums_copy(kind):
        ref = sums.at[me]
        target = {"tensor": (other, across, facing)[kind]}
        return remote(ref, ref, sums_send.at[kind], sums_recv.at[kind], target)

    keeps = [
        pltpu.make_async_copy(src, dst, keep_sem.at[j])
        for j, (src, dst) in enumerate(((wx, wx_out), (wb, wb_out), (wz, wz_out), (u, u_out), (wo, wo_out)))
    ]

    def streams(k):
        return [
            pltpu.make_async_copy(
                gf_out.at[:, :, span(at(place - (1 - 2 * way) * k) * out_cols, out_cols, 128)],
                g_cols.at[way],
                stream_sem.at[way],
            )
            for way in (0, 1)
        ]

    def start(copies):
        for copy in copies:
            copy.start()

    def wait(copies):
        for copy in copies:
            copy.wait()

    @pl.when(i == 0)
    def _():
        def held(s, h):
            return z.at[pl.ds((2 * s + h) * piece, piece), :]

        halves = [(s, h) for s in range(seqs) for h in (0, 1)]
        cut = lambda h: pl.ds(h * (model // 2), model // 2)
        own = [
            (wzx_ref.at[1], wx.at[span(dp * rows, rows, 16), :]),
            (wbc_ref, wb.at[span(dp * rows, rows, 16), :]),
            (wzx_ref.at[0], wz.at[span(dp * rows, rows, 16), :]),
            (wout_ref, wo.at[:, span(dp * out_cols, out_cols, 128)]),
        ]
        own += [(hidden_ref.at[s, :, cut(h)], held(seqs + s, h)) for s, h in halves]
        own += [(g_ref.at[s, :, cut(h)], held(s, h)) for s, h in halves]
        loads = [pltpu.make_async_copy(a, b, load_sem.at[j]) for j, (a, b) in enumerate(own)]
        first = 4 + 2 * seqs
        stores = [
            pltpu.make_async_copy(
                held(s, h), gf_out.at[s, span(me * piece, piece, 16), cut(h)], load_sem.at[first + 2 * seqs + j]
            )
            for j, (s, h) in enumerate(halves)
        ]
        start(loads)
        greet(n, [{"tensor": facing}])
        loads[0].wait()
        x_ring.step(0)
        loads[1].wait()
        small.step(0)
        wait(loads[4:first])
        for s in range(seqs):
            left = z[pl.ds((2 * (seqs + s)) * piece, piece), :].astype(F32)
            right = z[pl.ds((2 * (seqs + s) + 1) * piece, piece), :].astype(F32)
            squares = jnp.sum(left * left + right * right, axis=1, keepdims=True)
            scale = lax.rsqrt(squares / model + EPS)
            scale_ref[s] = jnp.broadcast_to(scale, (piece, 128))
            to = span(s * length + me * piece, piece, 16)
            u[to, cut(0)] = (left * scale * gain_ref[:, cut(0)]).astype(BF16)
            u[to, cut(1)] = (right * scale * gain_ref[:, cut(1)]).astype(BF16)
            token_rows.start(s)
        wait(loads[first:])
        start(stores)
        wait(loads[2:4])
        wait(stores)
        for k in range(1, n):
            x_ring.step(k)
            small.step(k)
            if k == n - 1:
                z_ring.step(0)
            if k == n // 2:
                token_rows.forward(0)
                token_rows.start(seqs)
        for ahead in range(1, n):
            half(ahead, core).start()
        for ahead in range(1, n):
            half(ahead, 1 - core).wait_recv()
        token_rows.wait(0)
        start(keeps[:2])
        lanes = small_cols - n2
        pick = lax.broadcasted_iota(jnp.int32, (heads, lanes), 1) == (
            lax.broadcasted_iota(jnp.int32, (heads, lanes), 0) + me * heads
        )
        wdt[...] = dot_nt(pick.astype(BF16), wb[:, n2:]).astype(BF16)

    b = i - 1

    @pl.when((b >= 0) & (b < n))
    def _():
        @pl.when(b < n - 1)
        def _():
            z_ring.later(b + 1)

        @pl.when(b == n - 2)
        def _():
            out_ring.step(0)

        @pl.when(b == n - 1)
        def _():
            keeps[2].start()
            out_ring.step(1)

        @pl.when(b == 0)
        def _():
            token_rows.forward(1)
            token_rows.start(seqs + 1)

        @pl.when(b == blocks)
        def _():
            token_rows.wait(1)
            keeps[3].start()

        at_block = span(b * BLOCK, BLOCK, BLOCK)
        tokens = u[at_block, :]
        x = dot(tokens, wx[...])
        bc = dot(tokens, wb[:, :n2])
        dt = dot_nt(wdt[...], tokens)
        x_ref[0] = x.astype(BF16)
        bc_ref[0] = bc.astype(BF16)
        dt_ref[0] = dt
        forward_block(
            b % blocks, x, bc, dt, marks_ref, *shared, y.at[at_block, :], cx_ref, cbc_ref, states_ref, *scratch
        )

    c = i - (n + 1)

    def add_shard(k):
        wait(streams(k))
        for way in (0, 1):
            e = pl.ds(way * (out_rows // 2), out_rows // 2)
            d = at(place - (1 - 2 * way) * k)
            cols = g_cols[way].reshape(seqs * length, out_cols)
            value = dot_nt(cols, wo[e, span(d * out_cols, out_cols, 128)])

            @pl.when(k == 0)
            def _():
                dn[:, e] = value

            @pl.when(k > 0)
            def _():
                dn[:, e] += value

    @pl.when((c >= 0) & (c < n - 2))
    def _():
        @pl.when(c == 0)
        def _():
            token_rows.forward(seqs)
            token_rows.forward(seqs + 1)
            token_rows.wait(seqs)
            token_rows.wait(seqs + 1)
            start(streams(0))
            add_shard(0)
            start(streams(1))

        @pl.when((c >= 1) & (c <= 4))
        def _():
            part = span((c - 1) * (seqs * length // 4), seqs * length // 4, 16)
            z[part, :] = dot(u[part, :], wz[...]).astype(BF16)

        add_shard(c + 1)
        start(streams(c + 2))
        out_ring.later(c + 2)

        @pl.when(c == n - 3)
        def _():
            add_shard(n - 1)
            keeps[4].start()

            def block_sums(e, _):
                part = span(e * BLOCK, BLOCK, BLOCK)
                zf = z[part, :].astype(F32)
                gated = y[part, :] * (zf * sigmoid(zf))
                squares = jnp.sum(gated * gated, axis=1, keepdims=True)
                inner = jnp.sum(gate_ref[...] * dn[part, :] * gated, axis=1, keepdims=True)
                lane = lax.broadcasted_iota(jnp.int32, (1, 128), 1)
                both = jnp.where(lane == 0, squares, jnp.where(lane == 1, inner, 0.0))
                sums[me, :, part] = both.T[0:8, :]
                return 0

            lax.fori_loop(0, n, block_sums, 0)
            for kind in range(3):
                sums_copy(kind).start()

    e = i - (2 * n - 1)

    @pl.when(e >= 0)
    def _():
        @pl.when(e == 0)
        def _():
            for kind in range(3):
                sums_copy(kind).wait_recv()
            grad_ref[...] = jnp.zeros_like(grad_ref)

        part = span(e * BLOCK, BLOCK, BLOCK)
        whole = (sums[0, :, part] + sums[1, :, part]) + (sums[2, :, part] + sums[3, :, part])
        cols = jnp.concatenate([whole, jnp.zeros((120, BLOCK), F32)], axis=0).T / (4 * width)
        inverse = lax.rsqrt(cols[:, 0:1] + EPS)
        zf = z[part, :].astype(F32)
        sig = sigmoid(zf)
        silu = zf * sig
        yf = y[part, :]
        dnf = dn[part, :]
        gain = gate_ref[...]
        gated = yf * silu
        scaled_gated = gated * inverse
        normed_ref[...] = (scaled_gated * gain).astype(BF16)
        grad_ref[...] += jnp.sum(dnf * scaled_gated, axis=0, keepdims=True)
        d_gated = inverse * (dnf * gain) - gated * (inverse * inverse * inverse * cols[:, 1:2])
        dy_ref[...] = (d_gated * silu).astype(BF16)
        dz_ref[...] = (d_gated * yf * (sig * (1.0 + zf * (1.0 - sig)))).astype(BF16)

        @pl.when(e == n - 1)
        def _():
            wait(keeps)
            for ring in (x_ring, small, z_ring, out_ring):
                ring.finish()
            token_rows.finish(2 * seqs)
            for ahead in range(1, n):
                half(ahead, core).wait_send()
            for kind in range(3):
                sums_copy(kind).wait_send()


def forward_all(n, hidden, g, w_zx, w_bc, w_out, pre_gain, gate_gain, marks, shared):
    seqs, piece, model = hidden.shape
    rows, width = w_zx.shape[1:]
    out_rows, out_cols = w_out.shape
    length = 4 * piece
    tokens = seqs * length
    blocks = length // BLOCK
    n2 = shared[1].shape[1]
    heads = shared[2].shape[0]
    small = w_bc.shape[1]
    sem = pltpu.SemaphoreType.DMA
    ring = [sem((2, 2, n - 1))] * 2
    anywhere = pl.BlockSpec(memory_space=pl.ANY)
    whole = lambda *shape: pl.BlockSpec(shape, lambda i: (0,) * len(shape))
    b = lambda i: jnp.minimum(jnp.maximum(i - 1, 0), n - 1)
    e = lambda i: jnp.maximum(i - (2 * n - 1), 0)
    tok = lambda w: pl.BlockSpec((1, BLOCK, w), lambda i: (b(i) // blocks, b(i) % blocks, 0))
    gate = pl.BlockSpec((BLOCK, width), lambda i: (e(i), 0))
    out_shape = [
        ((tokens, model), BF16),
        ((seqs, length, model), BF16),
        ((rows * n, width), BF16),
        ((rows * n, width), BF16),
        ((rows * n, small), BF16),
        ((out_rows, out_cols * n), BF16),
        ((seqs, length, width), F32),
        ((seqs, length, width), BF16),
        ((seqs, length, n2), F32),
        ((seqs, length, n2), BF16),
        ((seqs, heads, length), F32),
        ((seqs, blocks, n2 // 2, width), BF16),
        ((tokens, width), BF16),
        ((tokens, width), BF16),
        ((tokens, width), BF16),
        ((1, width), F32),
        ((seqs, piece, 128), F32),
    ]
    return pl.pallas_call(
        functools.partial(all_kernel, n),
        grid=(3 * n - 1,),
        in_specs=[anywhere] * 5
        + [
            whole(1, model),
            whole(1, width),
            pl.BlockSpec((1, 8, BLOCK), lambda i: (b(i) // blocks, 0, b(i) % blocks)),
        ]
        + shared_specs(width, n2, heads),
        out_specs=[anywhere] * 6
        + [tok(width), tok(width), tok(n2), tok(n2)]
        + [pl.BlockSpec((1, heads, BLOCK), lambda i: (b(i) // blocks, 0, b(i) % blocks))]
        + [pl.BlockSpec((1, 1, n2 // 2, width), lambda i: (b(i) // blocks, b(i) % blocks, 0, 0))]
        + [gate] * 3
        + [whole(1, width), whole(seqs, piece, 128)],
        out_shape=[jax.ShapeDtypeStruct(*s) for s in out_shape],
        scratch_shapes=forward_scratch(width, n2)
        + [
            pltpu.VMEM((tokens, model), BF16),
            pltpu.VMEM((rows * n, width), BF16),
            pltpu.VMEM((rows * n, width), BF16),
            pltpu.VMEM((out_rows, out_cols * n), BF16),
            pltpu.VMEM((rows * n, small), BF16),
            pltpu.VMEM((heads, rows * n), BF16),
            pltpu.VMEM((2, seqs, length, out_cols), BF16),
            pltpu.VMEM((tokens, width), F32),
            pltpu.VMEM((tokens, width), BF16),
            pltpu.VMEM((tokens, width), F32),
            pltpu.VMEM((4, 8, tokens), F32),
            sem((4 + 6 * seqs,)),
            sem((5,)),
            sem((2,)),
        ]
        + ring + [sem((2, 1, n - 1))] * 2 + ring + ring
        + [sem((3, 2 * seqs))] * 2 + [sem((n,))] * 2 + [sem((3,))] * 2,
        compiler_params=pltpu.CompilerParams(
            collective_id=0, has_side_effects=True, vmem_limit_bytes=63 * 2**20
        ),
        name="forward_all",
    )(hidden, g, w_zx, w_bc, w_out, pre_gain, gate_gain, marks, *shared)


class RingScatter:
    def __init__(self, n, terms, slots, sems, ways=2, sign=1):
        self.n, self.terms, self.slots, self.ways, self.sign = n, terms, slots, ways, sign
        self.send_sem, self.recv_sem = sems
        self.place, self.at = ring_place(n)

    def turn(self, way):
        return self.sign * (1 - 2 * way)

    def owner(self, way, k):
        return self.at(self.place - self.turn(way) * (1 + k))

    def copy(self, way, k):
        return remote(
            self.slots.at[way, k],
            self.slots.at[way, k + 1],
            self.send_sem.at[way, k],
            self.recv_sem.at[way, k],
            {"dp": self.at(self.place + self.turn(way))},
        )

    def step(self, way, k):
        @pl.when(k == 0)
        def _():
            self.slots[way, 0] = self.terms[way].astype(BF16)

        @pl.when(k > 0)
        def _():
            self.copy(way, k - 1).wait_recv()

            @pl.when(k < self.n - 1)
            def _():
                self.slots[way, k] = (self.terms[way].astype(F32) + self.slots[way, k].astype(F32)).astype(BF16)

        @pl.when(k < self.n - 1)
        def _():
            self.copy(way, k).start()

    def last(self, way):
        return self.terms[way].astype(F32) + self.slots[way, self.n - 1].astype(F32)

    def finish(self):
        for k in range(self.n - 1):
            for way in range(self.ways):
                self.copy(way, k).wait_send()


class RowScatter:
    def __init__(self, parts, value, hold, sems):
        self.parts, self.value, self.hold = parts, value, hold
        self.send_sem, self.recv_sem = sems
        self.me, self.other, self.across = tensor_place()

    def copy(self, kind, part):
        src, dst = ((0, 1), (1, 2), (0, 3))[kind]
        return remote(
            self.hold.at[src, part],
            self.hold.at[dst, part],
            self.send_sem.at[kind, part],
            self.recv_sem.at[kind, part],
            {"tensor": self.across if kind == 1 else self.other},
        )

    def stage(self, j):
        late = j // (2 * self.parts)
        near = j - 2 * self.parts
        stage = (1 - late) * (j % 2) + late * (2 + near // self.parts)
        return stage, (1 - late) * (j // 2) + late * (near % self.parts)

    def owner(self, j):
        stage, part = self.stage(j)
        x, core = self.me // 2, self.me % 2
        return 2 * ((x + 1 - stage // 2) % 2) + (core + 1 - stage % 2) % 2, part

    def step(self, j, store, wait=True):
        stage, part = self.stage(j)

        @pl.when(stage == 0)
        def _():
            self.hold[0, part] = self.value[...].astype(BF16)
            self.copy(0, part).start()

        @pl.when(stage == 1)
        def _():
            self.copy(0, part).wait_recv()
            self.hold[1, part] = (self.value[...].astype(F32) + self.hold[1, part].astype(F32)).astype(BF16)
            self.copy(1, part).start()

        @pl.when(stage == 2)
        def _():
            self.copy(0, part).wait_send()
            self.hold[0, part] = self.value[...].astype(BF16)
            self.copy(2, part).start()

        @pl.when(stage == 3)
        def _():
            value = self.value[...].astype(F32)
            store(part, value + self.arrived(part) if wait else value)

    def arrived(self, part):
        self.copy(2, part).wait_recv()
        self.copy(1, part).wait_recv()
        return self.hold[3, part].astype(F32) + self.hold[2, part].astype(F32)

    def finish(self):
        for part in range(self.parts):
            for kind in (1, 2):
                self.copy(kind, part).wait_send()


def back_kernel(n, *refs):
    (normed_ref, g_ref, u_ref, dz_ref, wo_ref), refs = refs[:5], refs[5:]
    ins, refs = refs[:15], refs[15:]
    (out_ref, gout_ref, gz_ref), refs = refs[:3], refs[3:]
    outs, refs = refs[:5], refs[5:]
    scratch, refs = refs[:7], refs[7:]
    normed, dz, wo, g_cols, u_cols, out_slots, z_slots, hold, terms, mixed, load_sem, stream_sem, out_sem = refs[:13]
    sems = refs[13:]

    k = pl.program_id(0)
    blocks = 4
    piece = out_ref.shape[1]
    length = blocks * BLOCK
    count = g_ref.shape[1] // n
    half = gz_ref.shape[1] // 2
    place, at = ring_place(n)

    loads = [
        pltpu.make_async_copy(src, dst, load_sem.at[i])
        for i, (src, dst) in enumerate(((normed_ref, normed), (dz_ref, dz), (wo_ref, wo)))
    ]

    def streams(k):
        copies = []
        for way in (0, 1):
            d = at(place - (1 - 2 * way) * (1 + k))
            for i, (src, dst) in enumerate(((g_ref, g_cols), (u_ref, u_cols))):
                copies.append(
                    pltpu.make_async_copy(
                        src.at[:, span(d * count, count, 128)], dst.at[way], stream_sem.at[i, way]
                    )
                )
        return copies

    @pl.when(k == 0)
    def _():
        for copy in loads + streams(0):
            copy.start()
        greet(n)
        for copy in loads:
            copy.wait()

    for copy in streams(k):
        copy.wait()

    rows = RowScatter(2, mixed, hold, sems[4:6])
    owner = rows.owner(k)
    own_rows = span(owner[1] * length + owner[0] * piece, piece, 16)

    for ring, (from_cols, to_cols) in enumerate(((g_cols, normed), (u_cols, dz))):
        for way in (0, 1):
            value = dot_tn(from_cols[way], to_cols[:, pl.ds(way * half, half)])
            terms[ring, way] = value.astype(BF16)
    mixed[...] = dot(normed[own_rows, :], wo[...]).astype(BF16)

    out_ring = RingScatter(n, terms.at[0], out_slots, sems[0:2])
    z_ring = RingScatter(n, terms.at[1], z_slots, sems[2:4])
    for way in (0, 1):
        out_ring.step(way, k)
        z_ring.step(way, k)

    @pl.when(k < n - 1)
    def _():
        for copy in streams(k + 1):
            copy.start()

    def out_copy(part):
        return pltpu.make_async_copy(hold.at[2, part], out_ref.at[part], out_sem.at[part])

    def store(part, value):
        hold[2, part] = value.astype(BF16)
        out_copy(part).start()

    rows.step(k, store)
    backward_block(k // blocks, k % blocks, *ins, *outs, *scratch)

    @pl.when(k == n - 1)
    def _():
        for way in (0, 1):
            at = pl.ds(way * half, half)
            gout_ref[at, :] = out_ring.last(way).T
            gz_ref[:, at] = z_ring.last(way)

    @pl.when(k == n - 1)
    def _():
        rows.finish()
        out_ring.finish()
        z_ring.finish()
        for part in range(2):
            out_copy(part).wait()


def backward_all(n, small, piece, normed, g, u, dz, w_out, dy, x, cx, bc, cbc, dt, marks, states, shared):
    seqs, length, channels = x.shape
    n2, heads = bc.shape[2], dt.shape[1]
    tokens, model = g.shape
    count = model // n
    blocks = length // BLOCK
    sem = pltpu.SemaphoreType.DMA
    anywhere = pl.BlockSpec(memory_space=pl.ANY)
    ins, outs = backward_specs(channels, n2, heads, small, lambda k: (k // blocks, blocks - 1 - k % blocks))
    whole = lambda *shape: pl.BlockSpec(shape, lambda k: (0,) * len(shape))
    return pl.pallas_call(
        functools.partial(back_kernel, n),
        grid=(n,),
        in_specs=[anywhere] * 5 + ins,
        out_specs=[anywhere, whole(channels, count), whole(count, channels)] + outs,
        out_shape=[
            jax.ShapeDtypeStruct((seqs, piece, model), BF16),
            jax.ShapeDtypeStruct((channels, count), F32),
            jax.ShapeDtypeStruct((count, channels), F32),
        ]
        + backward_outs(seqs, length, channels, n2, heads, small),
        scratch_shapes=backward_scratch(channels, n2, heads)
        + [
            pltpu.VMEM((tokens, channels), BF16),
            pltpu.VMEM((tokens, channels), BF16),
            pltpu.VMEM((channels, model), BF16),
            pltpu.VMEM((2, tokens, count), BF16),
            pltpu.VMEM((2, tokens, count), BF16),
            pltpu.VMEM((2, n, count, channels // 2), BF16),
            pltpu.VMEM((2, n, count, channels // 2), BF16),
            pltpu.VMEM((4, seqs, piece, model), BF16),
            pltpu.VMEM((2, 2, count, channels // 2), BF16),
            pltpu.VMEM((piece, model), BF16),
            sem((3,)),
            sem((2, 2)),
            sem((seqs,)),
        ]
        + [sem((2, n - 1))] * 4
        + [sem((3, seqs))] * 2,
        compiler_params=pltpu.CompilerParams(
            collective_id=1, has_side_effects=True, vmem_limit_bytes=127 * 2**19
        ),
        name="backward_all",
    )(normed, g, u, dz, w_out, dy, x, cx, bc, cbc, dt, marks, states, *shared)


class Fold:
    def __init__(self, n, total, came, sems):
        self.total, self.came = total, came
        self.send_sem, self.recv_sem = sems
        dp = lax.axis_index("dp")
        _, other, across = tensor_place()
        partners, ahead = [], 1
        while ahead < n:
            partners.append({"dp": dp + ahead * (1 - 2 * ((dp // ahead) % 2))})
            ahead *= 2
        self.over_dp = partners
        self.partners = partners + [{"tensor": other}, {"tensor": across}]

    def copy(self, r):
        return remote(
            self.total.at[r], self.came.at[r], self.send_sem.at[r], self.recv_sem.at[r], self.partners[r]
        )

    def start(self, r):
        self.copy(r).start()

    def take(self, r):
        self.copy(r).wait_recv()
        self.total[r + 1] = self.total[r] + self.came[r]

    def finish(self):
        for r in range(len(self.partners)):
            self.copy(r).wait_send()


def in_kernel(
    n, u_hbm, dz_hbm, dx_hbm, wz_hbm, wx_hbm, wb_hbm, dbc_hbm, gz_hbm, gx_in, gbc_in, gh_in, gate_in, gain_ref,
    din_ref, gx_ref, gb_ref, sums_ref, dots_ref, pre_ref,
    u_ref, dz_ref, dx_ref, wz_ref, wx_ref, wb_ref, dbc_ref,
    x_slots, b_slots, hold, bc_hold, x_terms, b_terms, in_value, bc_value, low, swap, pre, pre_dp, pre_tensor, total, came, load_sem, u_sem, *sems,
):
    seqs, piece = din_ref.shape[:2]
    tokens, model = u_ref.shape
    length = tokens // seqs
    count = model // n
    half = gx_ref.shape[2] // 2
    me, other, across = tensor_place()
    core = me % 2

    moves = (
        (dbc_hbm, dbc_ref),
        (dx_hbm, dx_ref),
        (dz_hbm, dz_ref),
        (wz_hbm, wz_ref),
        (wx_hbm, wx_ref),
        (wb_hbm, wb_ref),
        (gz_hbm, gx_ref.at[0]),
    )
    loads = [pltpu.make_async_copy(src, dst, load_sem.at[i]) for i, (src, dst) in enumerate(moves)]
    place, at_place = ring_place(n)
    u_copies = []
    for ahead in (-1, 1, -2, 2, -3, 3, 4, 0):
        cols = span(at_place(place + ahead) * count, count, 128)
        u_copies.append(pltpu.make_async_copy(u_hbm.at[:, cols], u_ref.at[:, cols], u_sem.at[ahead + 3]))
    for load in loads[:2] + u_copies[:2] + loads[2:] + u_copies[2:]:
        load.start()

    bc_rows = RowScatter(seqs, bc_value, bc_hold, sems[0:2])
    in_rows = RowScatter(seqs, in_value, hold, sems[2:4])
    x_ring = RingScatter(n, x_terms, x_slots, sems[4:6])
    b_ring = RingScatter(n, b_terms, b_slots, sems[6:8], 1, 1 - 2 * core)
    pair_send, pair_recv, swap_send, swap_recv = sems[8:12]
    dp_send, dp_recv, tensor_send, tensor_recv = sems[14:18]
    fold = Fold(n, total, came, sems[12:14])
    rounds = len(fold.partners)
    pair = remote(low.at[0], low.at[1], pair_send, pair_recv, {"tensor": other})

    total[0] = jnp.zeros_like(total[0])
    total[0, 0:6, :] = gx_in[0:6, :]
    total[0, 6:7, :] = gate_in[...]
    steps = gh_in[...].T
    total[0, 7:8, 0 : steps.shape[1]] = steps[0:1, :]
    total[0, 7:8, 128 : 128 + steps.shape[1]] = steps[1:2, :]
    total[0, 8:13, 0 : gbc_in.shape[1]] = gbc_in[0:5, :]
    pre[...] = jnp.zeros_like(pre)
    dp_now = lax.axis_index("dp")
    greet(
        n,
        fold.over_dp
        + [{"dp": (dp_now + o) % n} for o in range(1, n)]
        + [{"tensor": (me + o) % 4} for o in range(1, 4)],
    )
    def rows_at(t, part):
        return span(part * length + t * piece, piece, 16)

    def bc_store(part, value):
        low[0, part] = value.astype(BF16)

    def bc_step(j):
        t, part = bc_rows.owner(j)
        bc_value[...] = dbc_ref[rows_at(t, part), :].astype(F32)
        bc_rows.step(j, bc_store)

    def add_pre(at):
        pre[...] += jnp.sum(in_value[...] * u_ref[at, :].astype(F32), axis=0, keepdims=True)

    def store(part, value):
        in_value[...] = value + dot_nt(low[0, part], wb_ref[...])
        din_ref[part] = in_value[...]
        add_pre(rows_at(me, part))

    def row_term(j):
        at = rows_at(*in_rows.owner(j))
        in_value[...] = dot_nt(dz_ref[at, :], wz_ref[...]) + dot_nt(dx_ref[at, :], wx_ref[...])

    def row_step(j):
        in_rows.step(j, store, wait=False)

        @pl.when(j < 3 * seqs)
        def _():
            add_pre(rows_at(*in_rows.owner(j)))

    def x_term(k):
        for way in (0, 1):
            cols = span(x_ring.owner(way, k) * count, count, 128)
            x_terms[way] = dot_tn(u_ref[:, cols], dx_ref[:, pl.ds(way * half, half)])

    def x_step(k):
        for way in (0, 1):
            x_ring.step(way, k)

    def b_step(k):
        cols = span(b_ring.owner(0, k) * count + core * count // 2, count // 2, 128)
        value = 0.0
        for t, which in ((me, 0), (other, 1)):
            for part in range(seqs):
                value = value + dot_tn(u_ref[rows_at(t, part), cols], low[which, part])
        b_terms[0] = value
        b_ring.step(0, k)

    loads[0].wait()
    for part in range(seqs):
        bc_step(2 * part)
        bc_step(2 * seqs + part)
    loads[1].wait()
    for copy in u_copies[:2]:
        copy.wait()
    x_term(0)
    x_step(0)
    for load in loads[2:] + u_copies[2:]:
        load.wait()
    row_term(0)
    row_step(0)
    for part in range(seqs):
        bc_step(2 * part + 1)

    wide = model // 8
    gain = gain_ref[...]

    def dp_copy(o):
        ref = pre_dp.at[dp_now]
        return remote(ref, ref, dp_send.at[o], dp_recv.at[o], {"dp": (dp_now + o) % n})

    def tensor_copy(o):
        ref = pre_tensor.at[me]
        return remote(ref, ref, tensor_send.at[o], tensor_recv.at[o], {"tensor": (me + o) % 4})

    cross = remote(swap.at[0], swap.at[1], swap_send.at[0], swap_recv.at[0], {"tensor": across})
    back = remote(swap.at[2], swap.at[3], swap_send.at[1], swap_recv.at[1], {"tensor": other})

    def at_step(k, when, what):
        pl.when(k == when)(what)

    def own_bc():
        for part in range(seqs):
            bc_step(3 * seqs + part)
        pair.start()

    def send_pre():
        for i in range(8):
            at = slice(i * wide, (i + 1) * wide)
            pre_dp[dp_now, i : i + 1, :] = pre[:, at] / gain[:, at]
        for o in range(1, n):
            dp_copy(o).start()

    def pass_pre():
        for o in range(1, n):
            dp_copy(o).wait_recv()
        pre_tensor[me] = sum(pre_dp[d] for d in range(n))
        for o in range(1, 4):
            tensor_copy(o).start()

    def take_pre():
        for o in range(1, 4):
            tensor_copy(o).wait_recv()
        pre_ref[...] = (pre_tensor[0] + pre_tensor[1]) + (pre_tensor[2] + pre_tensor[3])

    def send_bc():
        swap[0] = b_ring.last(0)
        cross.start()

    def pass_bc():
        cross.wait_recv()
        swap[2] = swap[0] + swap[1]
        back.start()
        gb_ref[span(core * count // 2, count // 2, 16), :] = swap[2]

    def step(k, _):
        at_step(k, 5, send_pre)
        at_step(k, n - 1, send_bc)

        @pl.when(2 * k - 1 < 4 * seqs)
        def _():
            row_term(2 * k - 1)
            row_step(2 * k - 1)

        x_term(k)
        x_step(k)
        at_step(k, 2, pair.wait_recv)

        @pl.when((k >= 2) & (k <= 6))
        def _():
            b_step(jnp.maximum(k - 2, 2 * (k - 3)))

        @pl.when(2 * k < 4 * seqs)
        def _():
            row_term(2 * k)
            row_step(2 * k)

        at_step(k, 1, own_bc)

        @pl.when((k >= 4) & (k <= 6))
        def _():
            b_step(2 * (k - 3) + 1)

        at_step(k, 6, pass_pre)
        at_step(k, n - 1, pass_bc)
        at_step(k, n - 1, take_pre)
        for r in range(rounds + 1):

            @pl.when(k == r + 1)
            def _():
                if r > 0:
                    fold.take(r - 1)
                if r < rounds:
                    fold.start(r)

        return 0

    lax.fori_loop(1, n, step, 0)
    for way in (0, 1):
        gx_ref[1, :, pl.ds(way * half, half)] = x_ring.last(way)
    sums_ref[0:8, :] = total[rounds - 2, 0:8, :]
    sums_ref[8:16, :] = total[rounds, 8:16, :]
    for part in range(seqs):
        value = din_ref[part] + in_rows.arrived(part)
        din_ref[part] = value
        inner = jnp.sum(value * u_ref[rows_at(me, part), :].astype(F32), axis=1, keepdims=True)
        dots_ref[part] = jnp.broadcast_to(inner, (piece, 128))
    back.wait_recv()
    gb_ref[span((1 - core) * count // 2, count // 2, 16), :] = swap[3]
    for o in range(1, n):
        dp_copy(o).wait_send()
    for o in range(1, 4):
        tensor_copy(o).wait_send()
    for copy in (pair, cross, back):
        copy.wait_send()
    for part in (bc_rows, in_rows, x_ring, b_ring, fold):
        part.finish()


def scatter_in(n, piece, u, dz, dx, w_z, w_x, w_bc, dbc, grad_z, gx, gbc, gh, grad_gate, gain):
    tokens, model = u.shape
    width = dz.shape[1]
    small = dbc.shape[1]
    seqs = tokens // (4 * piece)
    count = model // n
    rounds = 5
    sem = pltpu.SemaphoreType.DMA
    vmem = pl.BlockSpec(memory_space=pltpu.VMEM)
    anywhere = pl.BlockSpec(memory_space=pl.ANY)
    big = (u, dz, dx, w_z, w_x, w_bc, dbc)
    return pl.pallas_call(
        functools.partial(in_kernel, n),
        in_specs=[anywhere] * 8 + [vmem] * 5,
        out_specs=[vmem] * 6,
        out_shape=[
            jax.ShapeDtypeStruct((seqs, piece, model), F32),
            jax.ShapeDtypeStruct((2, count, width), F32),
            jax.ShapeDtypeStruct((count, small), F32),
            jax.ShapeDtypeStruct((16, width), F32),
            jax.ShapeDtypeStruct((seqs, piece, 128), F32),
            jax.ShapeDtypeStruct((8, model // 8), F32),
        ],
        scratch_shapes=[pltpu.VMEM(a.shape, BF16) for a in big]
        + [
            pltpu.VMEM((2, n, count, width // 2), BF16),
            pltpu.VMEM((1, n, count // 2, small), BF16),
            pltpu.VMEM((4, seqs, piece, model), BF16),
            pltpu.VMEM((4, seqs, piece, small), BF16),
            pltpu.VMEM((2, count, width // 2), F32),
            pltpu.VMEM((1, count // 2, small), F32),
            pltpu.VMEM((piece, model), F32),
            pltpu.VMEM((piece, small), F32),
            pltpu.VMEM((2, seqs, piece, small), BF16),
            pltpu.VMEM((4, count // 2, small), F32),
            pltpu.VMEM((1, model), F32),
            pltpu.VMEM((n, 8, model // 8), F32),
            pltpu.VMEM((4, 8, model // 8), F32),
            pltpu.VMEM((rounds + 1, 16, width), F32),
            pltpu.VMEM((rounds, 16, width), F32),
            sem((len(big),)),
            sem((n,)),
        ]
        + [sem((3, seqs))] * 4 + [sem((2, n - 1))] * 2 + [sem((1, n - 1))] * 2 + [sem(())] * 2 + [sem((2,))] * 2
        + [sem((rounds,))] * 2 + [sem((n,))] * 2 + [sem((4,))] * 2,
        compiler_params=pltpu.CompilerParams(
            collective_id=2, has_side_effects=True, vmem_limit_bytes=63 * 2**20
        ),
        name="scatter_in",
    )(*big, grad_z, gx, gbc, gh, grad_gate, gain)


def rms_scale(values):
    return lax.rsqrt(jnp.mean(values * values, axis=-1, keepdims=True) + EPS)


def gather_plain(u, g, w_zx, w_bc, w_out):
    w_zx = lax.all_gather(w_zx, "dp", axis=1, tiled=True)
    return (
        lax.all_gather(u, "tensor", axis=1, tiled=True),
        lax.all_gather(g, "tensor", axis=1, tiled=True),
        w_zx[1],
        w_zx[0],
        lax.all_gather(w_bc, "dp", axis=0, tiled=True),
        lax.all_gather(w_out, "dp", axis=1, tiled=True),
    )


def rows_of(values, piece):
    by_seq = values.reshape(-1, 4 * piece, values.shape[-1])
    return lax.psum_scatter(by_seq, "tensor", scatter_dimension=1, tiled=True)


def scatter_out_plain(piece, normed, g, u, dz, w_out):
    return (
        rows_of(dot(normed, w_out), piece),
        lax.psum_scatter(dot_tn(normed, g), "dp", scatter_dimension=1, tiled=True),
        lax.psum_scatter(dot_tn(u, dz), "dp", scatter_dimension=0, tiled=True),
    )


def scatter_in_plain(piece, u, dz, dx, w_z, w_x, w_bc, dbc):
    low = lax.psum(dbc.astype(F32), "tensor").astype(BF16)
    d_in = rows_of(dot_nt(dz, w_z) + dot_nt(dx, w_x), piece)
    first = lax.axis_index("tensor") * piece
    own = lax.dynamic_slice_in_dim(low.reshape(-1, 4 * piece, low.shape[1]), first, piece, 1)
    d_in = d_in + jnp.einsum("slc,dc->sld", own, w_bc, preferred_element_type=F32)
    return (
        d_in,
        lax.psum_scatter(dot_tn(u, dx), "dp", scatter_dimension=0, tiled=True),
        lax.psum_scatter(dot_tn(u, low), "dp", scatter_dimension=0, tiled=True),
    )


def local(
    n_dp,
    n_tensor,
    hidden,
    pre_gain,
    w_zx,
    w_bcdt,
    conv_x,
    conv_bc,
    dt_bias,
    a_log,
    d_skip,
    gate_gain,
    w_out,
    cotangent,
    segments,
):
    seqs, piece, model = hidden.shape
    length = segments.shape[1]
    tokens = seqs * length
    heads = dt_bias.shape[0]
    channels = conv_x.shape[1]
    n2 = conv_bc.shape[1]
    columns = w_bcdt.shape[1]
    tensor = lax.axis_index("tensor")
    kernels = n_dp == 8 and n_tensor == 4 and seqs == 2 and length == 4 * BLOCK

    x_piece = hidden.astype(F32)
    w_bc_piece = jnp.pad(w_bcdt, ((0, 0), (0, -columns % 128)))
    marks = row_marks(segments)
    spread = jnp.asarray(spread_matrix(heads, channels), BF16)
    skip = jnp.repeat(d_skip, channels // heads)[None]
    pick = jnp.asarray(pick_matrix(heads, channels), BF16)
    shared = (conv_x, conv_bc, dt_bias[:, None], a_log[:, None], skip, spread, pick)
    if kernels:
        u, g, w_x, w_z, w_bc, w_o, cx, x, cbc, bc, dt, states, normed, dz, dy, grad_gate, scale_in = forward_all(
            n_dp, hidden, cotangent, w_zx, w_bc_piece, w_out, pre_gain[None], gate_gain[None], marks, shared
        )
        g = g.reshape(tokens, model)
        scale_in = scale_in[:, :, :1]
    else:
        scale_in = rms_scale(x_piece)
        u_piece = (x_piece * scale_in * pre_gain).astype(BF16)
        u, g, w_x, w_z, w_bc, w_o = gather_plain(u_piece, cotangent, w_zx, w_bc_piece, w_out)
        u = u.reshape(tokens, model)
        g = g.reshape(tokens, model)
        x = dot(u, w_x).reshape(seqs, length, channels)
        z = dot(u, w_z)
        bc_dt = dot(u, w_bc).reshape(seqs, length, -1)
        bc = bc_dt[:, :, :n2]
        dt = jnp.swapaxes(lax.dynamic_slice_in_dim(bc_dt, n2 + tensor * heads, heads, 2), 1, 2)
        y, cx, cbc, states = ssd_forward(x, bc, dt, marks, shared)
        d_normed = dot_nt(g, w_o)
        sig_z = sigmoid(z)
        silu_z = z * sig_z
        y_flat = y.reshape(tokens, channels)
        gated = y_flat * silu_z
        scaled = d_normed * gate_gain
        sums = jnp.stack([jnp.sum(gated * gated, axis=1), jnp.sum(scaled * gated, axis=1)])
        sums = lax.psum(sums, "tensor") / (channels * n_tensor)
        inverse = lax.rsqrt(sums[0] + EPS)[:, None]
        normed = (gated * inverse * gate_gain).astype(BF16)
        grad_gate = jnp.sum(d_normed * gated * inverse, axis=0)[None]
        d_gated = inverse * scaled - gated * inverse**3 * sums[1][:, None]
        dy = (d_gated * silu_z).astype(BF16)
        dz = (d_gated * y_flat * (sig_z * (1.0 + z * (1.0 - sig_z)))).astype(BF16)
        x, bc = x.astype(BF16), bc.astype(BF16)

    back_args = (dy.reshape(seqs, length, channels), x, cx, bc, cbc, dt, marks, states, shared)
    if kernels:
        mixed, grad_out, grad_z, *rest = backward_all(n_dp, w_bc.shape[1], piece, normed, g, u, dz, w_o, *back_args)
    else:
        mixed, grad_out, grad_z = scatter_out_plain(piece, normed, g, u, dz, w_o)
        rest = ssd_backward(w_bc.shape[1], *back_args)
    dx, dbc, gx, gbc, gh = rest
    out_hidden = (x_piece + mixed).astype(BF16)
    in_args = (piece, u, dz, dx.reshape(tokens, channels), w_z, w_x, w_bc, dbc.reshape(tokens, -1))
    if kernels:
        d_in, grad_zx, grad_bc, sums, dots, grad_pre = scatter_in(
            n_dp, *in_args, grad_z, gx, gbc, gh, grad_gate, pre_gain[None]
        )
        dots = dots[:, :, :1]
        grad_pre = grad_pre.reshape(model)
        grad_conv_bc = sums[8:13, :n2]
    else:
        d_in, grad_x, grad_bc = scatter_in_plain(*in_args)
        grad_zx = jnp.stack([grad_z, grad_x])
        grad_pre = jnp.sum(d_in * x_piece * scale_in, axis=(0, 1))
        dots = scale_in * jnp.sum(d_in * pre_gain * x_piece, axis=-1, keepdims=True)
        steps = jnp.pad(gh[:, :2].T, ((0, 0), (0, channels - heads)))
        sums = lax.psum(jnp.concatenate([gx[:6], grad_gate, steps]), "dp")
        sums = jnp.concatenate([sums[:7], jnp.concatenate([sums[7, :128], sums[8, : channels - 128]])[None]])
        grad_conv_bc, grad_pre = lax.psum((gbc[:5], grad_pre), ("dp", "tensor"))

    d_hidden = cotangent.astype(F32) + scale_in * (pre_gain * d_in) - x_piece * (scale_in**2 * dots / model)
    return (
        out_hidden,
        d_hidden,
        grad_pre,
        grad_zx,
        grad_bc[:, :columns],
        sums[:5],
        grad_conv_bc,
        sums[7, :heads],
        sums[7, 128 : 128 + heads],
        sums[5].reshape(heads, -1).sum(axis=1),
        sums[6],
        grad_out,
    )


def solution(mesh):
    placed = (
        P("dp", "tensor", None),
        P(),
        P(None, "dp", "tensor"),
        P("dp", None),
        P(None, "tensor"),
        P(),
        P("tensor"),
        P("tensor"),
        P("tensor"),
        P("tensor"),
        P("tensor", "dp"),
        P("dp", "tensor", None),
        P("dp", None),
    )
    return jax.shard_map(
        functools.partial(local, mesh.shape["dp"], mesh.shape["tensor"]),
        mesh=mesh,
        in_specs=placed,
        out_specs=(
            P("dp", "tensor", None),
            P("dp", "tensor", None),
            P(),
            P(None, "dp", "tensor"),
            P("dp", None),
            P(None, "tensor"),
            P(),
            P("tensor"),
            P("tensor"),
            P("tensor"),
            P("tensor"),
            P("tensor", "dp"),
        ),
        check_vma=False,
    )
```

```python
import functools

import jax
import jax.numpy as jnp
import numpy as np
from jax import lax
from jax.experimental import pallas as pl
from jax.experimental.pallas import tpu as pltpu
from jax.sharding import PartitionSpec as P

MESH = pl.DeviceIdType.MESH
EPS = 1e-05
BLOCK = 256
F32 = jnp.float32
BF16 = jnp.bfloat16
EXACT = lax.Precision.HIGHEST
LOG2E = 1.4426950408889634
NEG = -1e30


def sigmoid(v):
    return 0.5 * jnp.tanh(0.5 * v) + 0.5


def split3(v):
    hi = v.astype(BF16)
    rest = v - hi.astype(F32)
    mid = rest.astype(BF16)
    low = (rest - mid.astype(F32)).astype(BF16)
    return hi, mid, low


def dot(a, b):
    return jnp.dot(a, b, preferred_element_type=F32)


def dot_nt(a, b):
    return lax.dot_general(a, b, (((1,), (1,)), ((), ())), preferred_element_type=F32)


def dot_tn(a, b):
    return lax.dot_general(a, b, (((0,), (0,)), ((), ())), preferred_element_type=F32)


def softplus(v):
    return jnp.maximum(v, 0.0) + jnp.log1p(jnp.exp(-jnp.abs(v)))


def head_rows(raw, dt_bias, a_log):
    q = raw.shape[1]
    upto = (
        lax.broadcasted_iota(jnp.int32, (q, q), 0) <= lax.broadcasted_iota(jnp.int32, (q, q), 1)
    ).astype(F32)
    biased = raw + dt_bias
    step = softplus(biased)
    rate = -jnp.exp(a_log) * step
    cum = jnp.dot(rate, upto, precision=EXACT, preferred_element_type=F32) * LOG2E
    return biased, step, rate, cum


def exact_nt(a, b):
    a_hi, a_mid, _ = split3(a)
    b_hi, b_mid, _ = split3(b)
    return dot_nt(a_hi, b_hi) + dot_nt(a_hi, b_mid) + dot_nt(a_mid, b_hi)


def turned(row):
    k = row.shape[1]
    own = lax.broadcasted_iota(jnp.int32, (k, k), 0) == lax.broadcasted_iota(jnp.int32, (k, k), 1)
    return jnp.sum(jnp.where(own, row, 0.0), axis=1, keepdims=True)


def to_columns(rows):
    return jnp.concatenate([rows, jnp.zeros((128 - rows.shape[0], rows.shape[1]), F32)], axis=0).T


def head_columns(reads, last, step, cum, third):
    cum_end = cum[:, BLOCK - 1 : BLOCK]
    rows = []
    for factor in (reads * jnp.exp2(cum), last * jnp.exp2(cum_end - cum) * step):
        hi, mid, _ = split3(factor)
        rows += [hi.astype(F32), mid.astype(F32)]
    cols = to_columns(jnp.concatenate(rows + [third], axis=0))
    return cols[:, 4 * cum.shape[0] :], cols.astype(BF16), jnp.exp2(cum_end)


def log2_step(step):
    return jnp.log(jnp.maximum(step, 1e-37)) * LOG2E


def forward_block(
    block, x, bc, dt, marks_ref, taps_x_ref, taps_bc_ref, bias_ref, alog_ref, skip_ref, spread_ref, pick_ref,
    y_ref, cx_ref, cbc_ref, states_ref,
    xs, bs, state, mask_bias,
):
    q = BLOCK
    heads = dt.shape[0]
    channels = x.shape[-1]
    width = channels // heads

    @pl.when(block == 0)
    def _():
        xs[0:8, :] = jnp.zeros((8, xs.shape[1]), F32)
        bs[0:8, :] = jnp.zeros((8, bs.shape[1]), F32)
        state[...] = jnp.zeros_like(state)

    marks = to_columns(marks_ref[0])
    lag_masks = [marks[:, k : k + 1] for k in range(3)]

    def conv(hold, at, taps_ref):
        out = taps_ref[4:5, at] + taps_ref[3:4, at] * hold[8 : 8 + q, at]
        for lag in (1, 2, 3):
            out = out + (lag_masks[lag - 1] * hold[8 - lag : 8 - lag + q, at]) * taps_ref[3 - lag : 4 - lag, at]
        return out

    bs[8 : 8 + q, :] = bc
    xs[8 : 8 + q, :] = x
    cbc = conv(bs, slice(None), taps_bc_ref)
    cbc_ref[0] = cbc
    bc = cbc * sigmoid(cbc)
    n = bc.shape[1] // 2
    scores = exact_nt(bc[:, n:], bc[:, :n])
    b_mat, c_mat = bc[:, :n].astype(BF16), bc[:, n:].astype(BF16)
    b_turned = b_mat.T

    _, step, _, cum = head_rows(dt, turned(bias_ref[...]), turned(alog_ref[...]))
    cols, factors, carry = head_columns(marks_ref[0, 3:4, :], marks_ref[0, 4:5, :], step, cum, cum)
    source = cum - log2_step(step)
    carry_e = jnp.sum(carry * spread_ref[...].astype(F32), axis=0, keepdims=True)

    rows = lax.broadcasted_iota(jnp.int32, (q, q), 0)
    places = lax.broadcasted_iota(jnp.int32, (q, q), 1)
    mask_bias[...] = jnp.where((marks[:, 5:6] == marks_ref[0, 5:6, :]) & (rows >= places), 0.0, NEG)

    half = q // 2
    pair_width = 2 * width
    lane = lax.broadcasted_iota(jnp.int32, (1, pair_width), 1)
    every = slice(0, channels)
    cx = conv(xs, every, taps_x_ref)
    cx_ref[0] = cx
    xb = (cx * sigmoid(cx)).astype(BF16)
    xf = xb.astype(F32)
    stb = state[...].astype(BF16)
    states_ref[0, 0] = stb
    y_ref[...] = dot(c_mat, stb) * dot(factors, pick_ref[:, :channels]) + skip_ref[...] * xf
    scaled = (xf * dot(factors, pick_ref[:, channels:])).astype(BF16)
    state[...] = carry_e * state[...] + dot(b_turned, scaled)
    for pair in range(heads // 2):
        at = slice(pair * pair_width, (pair + 1) * pair_width)
        xp = xb[:, at]
        tops, lows = [], []
        for h in (2 * pair, 2 * pair + 1):
            col = cols[:, h : h + 1]
            row = source[h : h + 1, :]
            top = jnp.exp2((col[:half] - row[:, :half]) + mask_bias[:half, :half]) * scores[:half, :half]
            low = jnp.exp2((col[half:] - row) + mask_bias[half:, :]) * scores[half:, :]
            tops.append(top.astype(BF16))
            lows.append(low.astype(BF16))
        top = dot(jnp.concatenate(tops, axis=0), xp[:half])
        low = dot(jnp.concatenate(lows, axis=0), xp)
        first = lane < width
        y_ref[:half, at] += jnp.where(first, top[:half], top[half:])
        y_ref[half:, at] += jnp.where(first, low[:half], low[half:])

    xs[0:8, :] = xs[q : q + 8, :]
    bs[0:8, :] = bs[q : q + 8, :]


def backward_block(
    seq, step_id, dy_ref, x_ref, cx_ref, bc_ref, cbc_ref, dt_ref, marks_ref, states_ref,
    taps_x_ref, taps_bc_ref, bias_ref, alog_ref, skip_ref, spread_ref, pick_ref,
    dx_ref, dbc_ref, gx_ref, gbc_ref, gh_ref,
    ds_x, ds_bc, d_state, mask_bias, d_scores, d_in, row_sums,
):
    q = BLOCK
    heads = dt_ref.shape[1]
    channels = x_ref.shape[-1]
    width = channels // heads

    @pl.when(step_id == 0)
    def _():
        ds_x[:, q : q + 8, :] = jnp.zeros((3, 8, channels), F32)
        ds_bc[:, q : q + 8, :] = jnp.zeros((3, 8, ds_bc.shape[2]), F32)
        d_state[...] = jnp.zeros_like(d_state)

    @pl.when((step_id == 0) & (seq == 0))
    def _():
        gx_ref[...] = jnp.zeros_like(gx_ref)
        gbc_ref[...] = jnp.zeros_like(gbc_ref)
        gh_ref[...] = jnp.zeros_like(gh_ref)

    marks = to_columns(marks_ref[0])
    lag_masks = [marks[:, k : k + 1] for k in range(3)]

    def conv_back(d_out, value, hold, at, taps_ref, grad_ref):
        value = value.astype(F32)
        d_value = d_out * taps_ref[3:4, at]
        grad_ref[3:4, at] += jnp.sum(value * d_out, axis=0, keepdims=True)
        grad_ref[4:5, at] += jnp.sum(d_out, axis=0, keepdims=True)
        for lag in (1, 2, 3):
            hold[lag - 1, 0:q, at] = lag_masks[lag - 1] * d_out
            moved = hold[lag - 1, lag : lag + q, at]
            d_value = d_value + moved * taps_ref[3 - lag : 4 - lag, at]
            grad_ref[3 - lag : 4 - lag, at] += jnp.sum(value * moved, axis=0, keepdims=True)
            hold[lag - 1, q : q + 8, at] = hold[lag - 1, 0:8, at]
        return d_value

    cbc = cbc_ref[0]
    bc = cbc * sigmoid(cbc)
    n = bc.shape[1] // 2
    scores = exact_nt(bc[:, :n], bc[:, n:])
    b_mat, c_mat = bc[:, :n].astype(BF16), bc[:, n:].astype(BF16)
    c_turned = c_mat.T

    a_log = turned(alog_ref[...])
    biased, step, rate, cum = head_rows(dt_ref[0], turned(bias_ref[...]), a_log)
    source = cum - log2_step(step)
    cols, factors, carry = head_columns(marks_ref[0, 3:4, :], marks_ref[0, 4:5, :], step, cum, source)
    carry_e = jnp.sum(carry * spread_ref[...].astype(F32), axis=0, keepdims=True)

    rows = lax.broadcasted_iota(jnp.int32, (q, q), 0)
    places = lax.broadcasted_iota(jnp.int32, (q, q), 1)
    mask_bias[...] = jnp.where((marks[:, 5:6] == marks_ref[0, 5:6, :]) & (rows <= places), 0.0, NEG)

    half = q // 2
    pair_width = 2 * width
    lane = lax.broadcasted_iota(jnp.int32, (1, pair_width), 1)
    first = lane < width
    d_scores[...] = jnp.zeros_like(d_scores)
    col_h = jnp.zeros((heads, q), F32)
    head_row = lax.broadcasted_iota(jnp.int32, (heads, 3 * half), 0)
    spread = spread_ref[...]
    cx = cx_ref[0]
    xb = (cx * sigmoid(cx)).astype(BF16)
    dyb = dy_ref[0]
    st = states_ref[0, 0]
    dye = dyb.astype(F32) * dot(factors, pick_ref[:, :channels])
    out_h = dot_nt(spread, (dye * dot(c_mat, st)).astype(BF16))
    dye = dye.astype(BF16)
    d_c = dot_nt(dye, st)
    dst = d_state[...].astype(BF16)
    kept = jnp.sum(d_state[...] * st.astype(F32), axis=0, keepdims=True) * carry_e
    carried = jnp.sum(spread.astype(F32) * kept, axis=1, keepdims=True)
    d_state[...] = carry_e * d_state[...] + dot(c_turned, dye)
    xf = xb.astype(F32)
    to_end = dot(factors, pick_ref[:, channels:])
    d_b = dot_nt((xf * to_end).astype(BF16), dst)
    dx_st = dot(b_mat, dst) * to_end
    state_h = dot_nt(spread, (xf * dx_st).astype(BF16))
    d_in[...] = dx_st
    for pair in range(heads // 2):
        at = slice(pair * pair_width, (pair + 1) * pair_width)
        xp, dyp = xb[:, at], dyb[:, at]
        none = jnp.zeros_like(xp)
        x_first, x_second = jnp.where(first, xp, none), jnp.where(first, none, xp)
        g_top = dot_nt(jnp.concatenate([x_first[:half], x_second[:half]], axis=0), dyp)
        g_low = dot_nt(jnp.concatenate([x_first[half:], x_second[half:]], axis=0), dyp[half:])
        tops, lows, d_top, d_low = [], [], 0.0, 0.0
        for which in (0, 1):
            h = 2 * pair + which
            own = slice(which * half, (which + 1) * half)
            col = cols[:, h : h + 1]
            row = cum[h : h + 1, :]
            top = jnp.exp2((row - col[:half]) + mask_bias[:half, :])
            low = jnp.exp2((row[:, half:] - col[half:]) + mask_bias[half:, half:])
            p_top = top * g_top[own]
            p_low = low * g_low[own]
            d_top = d_top + p_top
            d_low = d_low + p_low
            m_top = p_top * scores[:half, :]
            m_low = p_low * scores[half:, half:]
            late = jnp.sum(m_top[:, half:], axis=0, keepdims=True) + jnp.sum(m_low, axis=0, keepdims=True)
            row_sums[h : h + 1, :half] = jnp.sum(m_top[:, :half], axis=0, keepdims=True)
            row_sums[h : h + 1, half:] = late
            parts = split3(jnp.concatenate([m_top[:, :half] + m_top[:, half:], m_low], axis=0))
            col_h = col_h + dot_nt((head_row == h).astype(BF16), jnp.concatenate(parts, axis=1))
            tops.append((top * scores[:half, :]).astype(BF16))
            lows.append((low * scores[half:, half:]).astype(BF16))
        d_scores[:half, :] += d_top
        d_scores[half:, half:] += d_low
        top = dot(jnp.concatenate(tops, axis=0), dyp)
        low = dot(jnp.concatenate(lows, axis=0), dyp[half:])
        d_in[:half, at] += jnp.where(first, top[:half], top[half:])
        d_in[half:, at] += jnp.where(first, low[:half], low[half:])

    everywhere = slice(0, channels)
    dyf = dy_ref[0].astype(F32)
    cx = cx_ref[0]
    sig = sigmoid(cx)
    gx_ref[5:6, :] += jnp.sum(dyf * (cx * sig).astype(BF16).astype(F32), axis=0, keepdims=True)
    d_cx = (d_in[...] + skip_ref[...] * dyf) * (sig * (1.0 + cx * (1.0 - sig)))
    dx_ref[0] = conv_back(d_cx, x_ref[0], ds_x, everywhere, taps_x_ref, gx_ref).astype(BF16)

    dsb = d_scores[...].astype(BF16)
    d_b = d_b + dot(dsb, c_mat)
    d_c = d_c + dot_tn(dsb, b_mat)
    sig = sigmoid(cbc)
    d_cbc = jnp.concatenate([d_b, d_c], axis=1) * (sig * (1.0 + cbc * (1.0 - sig)))
    every = slice(0, 2 * n)
    dbc_ref[0, :, every] = conv_back(d_cbc, bc_ref[0], ds_bc, every, taps_bc_ref, gbc_ref).astype(BF16)

    used_h = col_h + state_h
    diff_h = row_sums[...] - col_h + out_h
    since = (rows >= places).astype(F32)
    before = (rows < places).astype(F32)
    d_rate = (
        jnp.dot(diff_h, since, precision=EXACT, preferred_element_type=F32)
        + jnp.dot(state_h, before, precision=EXACT, preferred_element_type=F32)
        + carried
    )
    sig_dt = sigmoid(biased)
    ratio = jnp.where(step < 1e-30, 1.0, sig_dt / jnp.maximum(step, 1e-30))
    d_raw = used_h * ratio - jnp.exp(a_log) * sig_dt * d_rate
    lanes = dbc_ref.shape[2] - 2 * n
    mine = lax.broadcasted_iota(jnp.int32, (heads, lanes), 0) + lax.axis_index("tensor") * heads
    own = (lax.broadcasted_iota(jnp.int32, (heads, lanes), 1) == mine).astype(BF16)
    dbc_ref[0, :, 2 * n :] = dot_tn(d_raw.astype(BF16), own).astype(BF16)
    gh_ref[:, 0:1] += jnp.sum(d_raw, axis=1, keepdims=True)
    gh_ref[:, 1:2] += jnp.sum(d_rate * rate, axis=1, keepdims=True)


def row_marks(segments):
    seqs, length = segments.shape
    blocks = length // BLOCK
    lags = []
    for lag in (1, 2, 3):
        earlier = jnp.pad(segments, ((0, 0), (lag, 0)), constant_values=-1)[:, :length]
        lags.append(earlier == segments)
    grouped = segments.reshape(seqs, blocks, BLOCK)
    before = jnp.pad(segments, ((0, 0), (1, 0)), constant_values=-1)[:, :length].reshape(seqs, blocks, BLOCK)
    reads = (grouped == before[:, :, :1]).reshape(seqs, length)
    last = (grouped == grouped[:, :, -1:]).reshape(seqs, length)
    rows = [m.astype(F32) for m in (*lags, reads, last, segments)]
    return jnp.stack(rows + [jnp.zeros_like(rows[0])] * 2, axis=1)


def spread_matrix(heads, channels):
    width = channels // heads
    return (np.arange(heads)[:, None] == np.arange(channels)[None, :] // width).astype(np.float32)


def pick_matrix(heads, channels):
    spread = spread_matrix(heads, channels)
    out = np.zeros((128, 2 * channels), np.float32)
    for part in range(4):
        at = slice(part // 2 * channels, (part // 2 + 1) * channels)
        out[part * heads : (part + 1) * heads, at] = spread
    return out


def shared_specs(channels, n2, heads):
    full = lambda *shape: pl.BlockSpec(shape, lambda *i: (0,) * len(shape))
    return [
        full(5, channels),
        full(5, n2),
        full(1, heads),
        full(1, heads),
        full(1, channels),
        full(heads, channels),
        full(128, 2 * channels),
    ]


def forward_scratch(channels, n2):
    return [
        pltpu.VMEM((BLOCK + 8, channels), F32),
        pltpu.VMEM((BLOCK + 8, n2), F32),
        pltpu.VMEM((n2 // 2, channels), F32),
        pltpu.VMEM((BLOCK, BLOCK), F32),
    ]


def forward_kernel(x_ref, bc_ref, dt_ref, *refs):
    y_ref = refs[8]
    forward_block(pl.program_id(1), x_ref[0], bc_ref[0], dt_ref[0], *refs[:8], y_ref.at[0], *refs[9:])


def ssd_forward(x, bc, dt, marks, shared):
    seqs, length, channels = x.shape
    n2, heads = bc.shape[2], dt.shape[1]
    blocks = length // BLOCK
    tok = lambda w: pl.BlockSpec((1, BLOCK, w), lambda s, c: (s, c, 0))
    head = lambda w: pl.BlockSpec((1, w, BLOCK), lambda s, c: (s, 0, c))
    return pl.pallas_call(
        forward_kernel,
        grid=(seqs, blocks),
        in_specs=[tok(channels), tok(n2), head(heads), head(8)] + shared_specs(channels, n2, heads),
        out_specs=[
            tok(channels),
            tok(channels),
            tok(n2),
            pl.BlockSpec((1, 1, n2 // 2, channels), lambda s, c: (s, c, 0, 0)),
        ],
        out_shape=[
            jax.ShapeDtypeStruct((seqs, length, channels), F32),
            jax.ShapeDtypeStruct((seqs, length, channels), F32),
            jax.ShapeDtypeStruct((seqs, length, n2), F32),
            jax.ShapeDtypeStruct((seqs, blocks, n2 // 2, channels), BF16),
        ],
        scratch_shapes=forward_scratch(channels, n2),
        compiler_params=pltpu.CompilerParams(vmem_limit_bytes=48 * 2**20),
        name="ssd_forward",
    )(x, bc, dt, marks, *shared)


def backward_kernel(*refs):
    backward_block(pl.program_id(0), pl.program_id(1), *refs)


def backward_scratch(channels, n2, heads):
    return [
        pltpu.VMEM((3, BLOCK + 8, channels), F32),
        pltpu.VMEM((3, BLOCK + 8, n2), F32),
        pltpu.VMEM((n2 // 2, channels), F32),
        pltpu.VMEM((BLOCK, BLOCK), F32),
        pltpu.VMEM((BLOCK, BLOCK), F32),
        pltpu.VMEM((BLOCK, channels), F32),
        pltpu.VMEM((heads, BLOCK), F32),
    ]


def backward_specs(channels, n2, heads, small, place):
    tok = lambda w: pl.BlockSpec((1, BLOCK, w), lambda *i: (*place(*i), 0))
    full = lambda *shape: pl.BlockSpec(shape, lambda *i: (0,) * len(shape))
    ins = [tok(channels)] * 3 + [tok(n2)] * 2 + [
        pl.BlockSpec((1, heads, BLOCK), lambda *i: (place(*i)[0], 0, place(*i)[1])),
        pl.BlockSpec((1, 8, BLOCK), lambda *i: (place(*i)[0], 0, place(*i)[1])),
        pl.BlockSpec((1, 1, n2 // 2, channels), lambda *i: (*place(*i), 0, 0)),
    ]
    ins += shared_specs(channels, n2, heads)
    return ins, [tok(channels), tok(small), full(8, channels), full(8, n2), full(heads, 128)]


def backward_outs(seqs, length, channels, n2, heads, small):
    return [
        jax.ShapeDtypeStruct((seqs, length, channels), BF16),
        jax.ShapeDtypeStruct((seqs, length, small), BF16),
        jax.ShapeDtypeStruct((8, channels), F32),
        jax.ShapeDtypeStruct((8, n2), F32),
        jax.ShapeDtypeStruct((heads, 128), F32),
    ]


def ssd_backward(small, dy, x, cx, bc, cbc, dt, marks, states, shared):
    seqs, length, channels = x.shape
    n2, heads = bc.shape[2], dt.shape[1]
    blocks = length // BLOCK
    ins, outs = backward_specs(channels, n2, heads, small, lambda s, c: (s, blocks - 1 - c))
    return pl.pallas_call(
        backward_kernel,
        grid=(seqs, blocks),
        in_specs=ins,
        out_specs=outs,
        out_shape=backward_outs(seqs, length, channels, n2, heads, small),
        scratch_shapes=backward_scratch(channels, n2, heads),
        compiler_params=pltpu.CompilerParams(vmem_limit_bytes=56 * 2**20),
        name="ssd_backward",
    )(dy, x, cx, bc, cbc, dt, marks, states, *shared)


def ring_place(n):
    dp = lax.axis_index("dp")
    z, y = dp // 2, dp % 2

    def at(place):
        q = (place + 4 * n) % n
        return 2 * q + (q // (n // 2)) * (2 * n - 1 - 4 * q)

    return z + y * (n - 1 - 2 * z), at


def tensor_place():
    t = lax.axis_index("tensor")
    return t, t + 1 - 2 * (t % 2), (t + 2) % 4


def greet(n, more=()):
    place, at = ring_place(n)
    _, other, across = tensor_place()
    sem = pltpu.get_barrier_semaphore()
    targets = [{"dp": at(place + 1)}, {"dp": at(place - 1)}, {"tensor": other}, {"tensor": across}, *more]
    for target in targets:
        pl.semaphore_signal(sem, inc=1, device_id=target, device_id_type=MESH)
    pl.semaphore_wait(sem, len(targets))


def remote(src, dst, send_sem, recv_sem, target):
    return pltpu.make_async_remote_copy(
        src_ref=src, dst_ref=dst, send_sem=send_sem, recv_sem=recv_sem, device_id=target, device_id_type=MESH
    )


def span(first, count, unit):
    return pl.ds(pl.multiple_of(first, unit), count)


class RingGather:
    def __init__(self, n, parts, keep, sems):
        self.n, self.parts, self.keep = n, parts, keep
        self.send_sem, self.recv_sem = sems
        self.place, self.at = ring_place(n)

    def copy(self, way, part, step):
        sign = 1 - 2 * way
        ref = self.keep(way, part, self.at(self.place - sign * step))
        return remote(
            ref,
            ref,
            self.send_sem.at[way, part, step],
            self.recv_sem.at[way, part, step],
            {"dp": self.at(self.place + sign)},
        )

    def step(self, k):
        for part in range(self.parts):
            for way in (0, 1):
                if k > 0:
                    self.copy(way, part, k - 1).wait_recv()
                if k < self.n - 1:
                    self.copy(way, part, k).start()

    def later(self, k):
        for part in range(self.parts):
            for way in (0, 1):
                self.copy(way, part, k - 1).wait_recv()

                @pl.when(k < self.n - 1)
                def _():
                    self.copy(way, part, k).start()

    def finish(self):
        for k in range(self.n - 1):
            for part in range(self.parts):
                for way in (0, 1):
                    self.copy(way, part, k).wait_send()


class RowGather:
    def __init__(self, keep, sems):
        self.keep = keep
        self.send_sem, self.recv_sem = sems
        self.me, self.other, self.across = tensor_place()

    def copy(self, kind, part):
        ref = self.keep(part, self.across if kind == 2 else self.me)
        target = self.across if kind == 0 else self.other
        return remote(
            ref, ref, self.send_sem.at[kind, part], self.recv_sem.at[kind, part], {"tensor": target}
        )

    def start(self, part):
        self.copy(0, part).start()
        self.copy(1, part).start()

    def forward(self, part):
        self.copy(0, part).wait_recv()
        self.copy(2, part).start()

    def wait(self, part):
        self.copy(1, part).wait_recv()
        self.copy(2, part).wait_recv()

    def finish(self, parts):
        for part in range(parts):
            for kind in range(3):
                self.copy(kind, part).wait_send()


def all_kernel(n, *refs):
    (hidden_ref, g_ref, wzx_ref, wbc_ref, wout_ref, gain_ref, gate_ref, marks_ref), refs = refs[:8], refs[8:]
    shared, refs = refs[:7], refs[7:]
    (u_out, gf_out, wx_out, wz_out, wb_out, wo_out), refs = refs[:6], refs[6:]
    (cx_ref, x_ref, cbc_ref, bc_ref, dt_ref, states_ref), refs = refs[:6], refs[6:]
    (normed_ref, dz_ref, dy_ref, grad_ref, scale_ref), refs = refs[:5], refs[5:]
    scratch, refs = refs[:4], refs[4:]
    (u, wx, wz, wo, wb, wb_own, wdt, g_cols, y, z, dn, sums), refs = refs[:12], refs[12:]
    (load_sem, keep_sem, stream_sem), sems = refs[:3], refs[3:]

    i = pl.program_id(0)
    rows, width = wzx_ref.shape[1:]
    out_rows, out_cols = wout_ref.shape
    seqs, piece, model = hidden_ref.shape
    length = 4 * piece
    blocks = length // BLOCK
    heads = dt_ref.shape[1]
    n2 = bc_ref.shape[2]
    small_cols = wb.shape[1]
    dp = lax.axis_index("dp")
    place, at = ring_place(n)
    me, other, across = tensor_place()
    core = me % 2
    facing = (other + 2) % 4

    def keep_wide(ref):
        def keep(way, part, d):
            return ref.at[span(d * rows, rows, 16), pl.ds(way * width // 2 + part * width // 4, width // 4)]

        return keep

    def keep_out(way, part, d):
        first = way * out_rows // 2 + part * out_rows // 4
        return wo.at[pl.ds(first, out_rows // 4), span(d * out_cols, out_cols, 128)]

    def keep_small(way, part, d):
        return wb.at[span(d * rows + core * rows // 2 + way * rows // 4, rows // 4, 16), :]

    def keep_rows(part, t):
        if part < seqs:
            return u.at[span(part * length + t * piece, piece, 16), :]
        return gf_out.at[part - seqs, span(t * piece, piece, 16), :]

    x_ring = RingGather(n, 2, keep_wide(wx), sems[0:2])
    small = RingGather(n, 1, keep_small, sems[2:4])
    z_ring = RingGather(n, 2, keep_wide(wz), sems[4:6])
    out_ring = RingGather(n, 2, keep_out, sems[6:8])
    token_rows = RowGather(keep_rows, sems[8:10])
    halves_send, halves_recv, sums_send, sums_recv = sems[10:14]

    def half(ahead, whose):
        d = (dp + ahead) % n
        ref = wb.at[span(d * rows + whose * rows // 2, rows // 2, 16), :]
        return remote(ref, ref, halves_send.at[ahead], halves_recv.at[ahead], {"tensor": other})

    def sums_copy(kind):
        ref = sums.at[me]
        target = {"tensor": (other, across, facing)[kind]}
        return remote(ref, ref, sums_send.at[kind], sums_recv.at[kind], target)

    keeps = [
        pltpu.make_async_copy(src, dst, keep_sem.at[j])
        for j, (src, dst) in enumerate(((wx, wx_out), (wb, wb_out), (wz, wz_out), (u, u_out), (wo, wo_out)))
    ]

    def streams(k):
        return [
            pltpu.make_async_copy(
                gf_out.at[:, :, span(at(place - (1 - 2 * way) * k) * out_cols, out_cols, 128)],
                g_cols.at[way],
                stream_sem.at[way],
            )
            for way in (0, 1)
        ]

    def start(copies):
        for copy in copies:
            copy.start()

    def wait(copies):
        for copy in copies:
            copy.wait()

    @pl.when(i == 0)
    def _():
        def held(s, h):
            return z.at[pl.ds((2 * s + h) * piece, piece), :]

        halves = [(s, h) for s in range(seqs) for h in (0, 1)]
        cut = lambda h: pl.ds(h * (model // 2), model // 2)
        own = [
            (wzx_ref.at[1], wx.at[span(dp * rows, rows, 16), :]),
            (wbc_ref, wb_own),
            (wzx_ref.at[0], wz.at[span(dp * rows, rows, 16), :]),
            (wout_ref, wo.at[:, span(dp * out_cols, out_cols, 128)]),
        ]
        own += [(hidden_ref.at[s, :, cut(h)], held(seqs + s, h)) for s, h in halves]
        own += [(g_ref.at[s, :, cut(h)], held(s, h)) for s, h in halves]
        loads = [pltpu.make_async_copy(a, b, load_sem.at[j]) for j, (a, b) in enumerate(own)]
        first = 4 + 2 * seqs
        stores = [
            pltpu.make_async_copy(
                held(s, h), gf_out.at[s, span(me * piece, piece, 16), cut(h)], load_sem.at[first + 2 * seqs + j]
            )
            for j, (s, h) in enumerate(halves)
        ]
        start(loads)
        greet(n, [{"tensor": facing}])
        loads[0].wait()
        x_ring.step(0)
        loads[1].wait()
        columns = wb_own.shape[1]
        tail = columns // 128 * 128
        mine = span(dp * rows, rows, 16)
        wb[mine, :tail] = wb_own[:, :tail]
        wb[mine, tail:] = jnp.zeros((rows, small_cols - tail), BF16)
        wb[mine, tail:columns] = wb_own[:, tail:]
        small.step(0)
        wait(loads[4:first])
        for s in range(seqs):
            left = z[pl.ds((2 * (seqs + s)) * piece, piece), :].astype(F32)
            right = z[pl.ds((2 * (seqs + s) + 1) * piece, piece), :].astype(F32)
            squares = jnp.sum(left * left + right * right, axis=1, keepdims=True)
            scale = lax.rsqrt(squares / model + EPS)
            scale_ref[s] = jnp.broadcast_to(scale, (piece, 128))
            to = span(s * length + me * piece, piece, 16)
            u[to, cut(0)] = (left * scale * gain_ref[:, cut(0)]).astype(BF16)
            u[to, cut(1)] = (right * scale * gain_ref[:, cut(1)]).astype(BF16)
            token_rows.start(s)
        wait(loads[first:])
        start(stores)
        wait(loads[2:4])
        wait(stores)
        for k in range(1, n):
            x_ring.step(k)
            small.step(k)
            if k == n - 1:
                z_ring.step(0)
            if k == n // 2:
                token_rows.forward(0)
                token_rows.start(seqs)
        for ahead in range(1, n):
            half(ahead, core).start()
        for ahead in range(1, n):
            half(ahead, 1 - core).wait_recv()
        token_rows.wait(0)
        start(keeps[:2])
        lanes = small_cols - n2
        pick = lax.broadcasted_iota(jnp.int32, (heads, lanes), 1) == (
            lax.broadcasted_iota(jnp.int32, (heads, lanes), 0) + me * heads
        )
        wdt[...] = dot_nt(pick.astype(BF16), wb[:, n2:]).astype(BF16)

    b = i - 1

    @pl.when((b >= 0) & (b < n))
    def _():
        @pl.when(b < n - 1)
        def _():
            z_ring.later(b + 1)

        @pl.when(b == n - 2)
        def _():
            out_ring.step(0)

        @pl.when(b == n - 1)
        def _():
            keeps[2].start()
            out_ring.step(1)

        @pl.when(b == 0)
        def _():
            token_rows.forward(1)
            token_rows.start(seqs + 1)

        @pl.when(b == blocks)
        def _():
            token_rows.wait(1)
            keeps[3].start()

        at_block = span(b * BLOCK, BLOCK, BLOCK)
        tokens = u[at_block, :]
        x = dot(tokens, wx[...])
        bc = dot(tokens, wb[:, :n2])
        dt = dot_nt(wdt[...], tokens)
        x_ref[0] = x.astype(BF16)
        bc_ref[0] = bc.astype(BF16)
        dt_ref[0] = dt
        forward_block(
            b % blocks, x, bc, dt, marks_ref, *shared, y.at[at_block, :], cx_ref, cbc_ref, states_ref, *scratch
        )

    c = i - (n + 1)

    def add_shard(k):
        wait(streams(k))
        for way in (0, 1):
            e = pl.ds(way * (out_rows // 2), out_rows // 2)
            d = at(place - (1 - 2 * way) * k)
            cols = g_cols[way].reshape(seqs * length, out_cols)
            value = dot_nt(cols, wo[e, span(d * out_cols, out_cols, 128)])

            @pl.when(k == 0)
            def _():
                dn[:, e] = value

            @pl.when(k > 0)
            def _():
                dn[:, e] += value

    @pl.when((c >= 0) & (c < n - 2))
    def _():
        @pl.when(c == 0)
        def _():
            token_rows.forward(seqs)
            token_rows.forward(seqs + 1)
            token_rows.wait(seqs)
            token_rows.wait(seqs + 1)
            start(streams(0))
            add_shard(0)
            start(streams(1))

        @pl.when((c >= 1) & (c <= 4))
        def _():
            part = span((c - 1) * (seqs * length // 4), seqs * length // 4, 16)
            z[part, :] = dot(u[part, :], wz[...]).astype(BF16)

        add_shard(c + 1)
        start(streams(c + 2))
        out_ring.later(c + 2)

        @pl.when(c == n - 3)
        def _():
            add_shard(n - 1)
            keeps[4].start()

            def block_sums(e, _):
                part = span(e * BLOCK, BLOCK, BLOCK)
                zf = z[part, :].astype(F32)
                gated = y[part, :] * (zf * sigmoid(zf))
                squares = jnp.sum(gated * gated, axis=1, keepdims=True)
                inner = jnp.sum(gate_ref[...] * dn[part, :] * gated, axis=1, keepdims=True)
                lane = lax.broadcasted_iota(jnp.int32, (1, 128), 1)
                both = jnp.where(lane == 0, squares, jnp.where(lane == 1, inner, 0.0))
                sums[me, :, part] = both.T[0:8, :]
                return 0

            lax.fori_loop(0, n, block_sums, 0)
            for kind in range(3):
                sums_copy(kind).start()

    e = i - (2 * n - 1)

    @pl.when(e >= 0)
    def _():
        @pl.when(e == 0)
        def _():
            for kind in range(3):
                sums_copy(kind).wait_recv()
            grad_ref[...] = jnp.zeros_like(grad_ref)

        part = span(e * BLOCK, BLOCK, BLOCK)
        whole = (sums[0, :, part] + sums[1, :, part]) + (sums[2, :, part] + sums[3, :, part])
        cols = jnp.concatenate([whole, jnp.zeros((120, BLOCK), F32)], axis=0).T / (4 * width)
        inverse = lax.rsqrt(cols[:, 0:1] + EPS)
        zf = z[part, :].astype(F32)
        sig = sigmoid(zf)
        silu = zf * sig
        yf = y[part, :]
        dnf = dn[part, :]
        gain = gate_ref[...]
        gated = yf * silu
        scaled_gated = gated * inverse
        normed_ref[...] = (scaled_gated * gain).astype(BF16)
        grad_ref[...] += jnp.sum(dnf * scaled_gated, axis=0, keepdims=True)
        d_gated = inverse * (dnf * gain) - gated * (inverse * inverse * inverse * cols[:, 1:2])
        dy_ref[...] = (d_gated * silu).astype(BF16)
        dz_ref[...] = (d_gated * yf * (sig * (1.0 + zf * (1.0 - sig)))).astype(BF16)

        @pl.when(e == n - 1)
        def _():
            wait(keeps)
            for ring in (x_ring, small, z_ring, out_ring):
                ring.finish()
            token_rows.finish(2 * seqs)
            for ahead in range(1, n):
                half(ahead, core).wait_send()
            for kind in range(3):
                sums_copy(kind).wait_send()


def forward_all(n, hidden, g, w_zx, w_bc, w_out, pre_gain, gate_gain, marks, shared):
    seqs, piece, model = hidden.shape
    rows, width = w_zx.shape[1:]
    out_rows, out_cols = w_out.shape
    length = 4 * piece
    tokens = seqs * length
    blocks = length // BLOCK
    n2 = shared[1].shape[1]
    heads = shared[2].shape[1]
    columns = w_bc.shape[1]
    small = columns + -columns % 128
    sem = pltpu.SemaphoreType.DMA
    ring = [sem((2, 2, n - 1))] * 2
    anywhere = pl.BlockSpec(memory_space=pl.ANY)
    whole = lambda *shape: pl.BlockSpec(shape, lambda i: (0,) * len(shape))
    b = lambda i: jnp.minimum(jnp.maximum(i - 1, 0), n - 1)
    e = lambda i: jnp.maximum(i - (2 * n - 1), 0)
    tok = lambda w: pl.BlockSpec((1, BLOCK, w), lambda i: (b(i) // blocks, b(i) % blocks, 0))
    gate = pl.BlockSpec((BLOCK, width), lambda i: (e(i), 0))
    out_shape = [
        ((tokens, model), BF16),
        ((seqs, length, model), BF16),
        ((rows * n, width), BF16),
        ((rows * n, width), BF16),
        ((rows * n, small), BF16),
        ((out_rows, out_cols * n), BF16),
        ((seqs, length, width), F32),
        ((seqs, length, width), BF16),
        ((seqs, length, n2), F32),
        ((seqs, length, n2), BF16),
        ((seqs, heads, length), F32),
        ((seqs, blocks, n2 // 2, width), BF16),
        ((tokens, width), BF16),
        ((tokens, width), BF16),
        ((tokens, width), BF16),
        ((1, width), F32),
        ((seqs, piece, 128), F32),
    ]
    return pl.pallas_call(
        functools.partial(all_kernel, n),
        grid=(3 * n - 1,),
        in_specs=[anywhere] * 5
        + [
            whole(1, model),
            whole(1, width),
            pl.BlockSpec((1, 8, BLOCK), lambda i: (b(i) // blocks, 0, b(i) % blocks)),
        ]
        + shared_specs(width, n2, heads),
        out_specs=[anywhere] * 6
        + [tok(width), tok(width), tok(n2), tok(n2)]
        + [pl.BlockSpec((1, heads, BLOCK), lambda i: (b(i) // blocks, 0, b(i) % blocks))]
        + [pl.BlockSpec((1, 1, n2 // 2, width), lambda i: (b(i) // blocks, b(i) % blocks, 0, 0))]
        + [gate] * 3
        + [whole(1, width), whole(seqs, piece, 128)],
        out_shape=[jax.ShapeDtypeStruct(*s) for s in out_shape],
        scratch_shapes=forward_scratch(width, n2)
        + [
            pltpu.VMEM((tokens, model), BF16),
            pltpu.VMEM((rows * n, width), BF16),
            pltpu.VMEM((rows * n, width), BF16),
            pltpu.VMEM((out_rows, out_cols * n), BF16),
            pltpu.VMEM((rows * n, small), BF16),
            pltpu.VMEM(w_bc.shape, BF16),
            pltpu.VMEM((heads, rows * n), BF16),
            pltpu.VMEM((2, seqs, length, out_cols), BF16),
            pltpu.VMEM((tokens, width), F32),
            pltpu.VMEM((tokens, width), BF16),
            pltpu.VMEM((tokens, width), F32),
            pltpu.VMEM((4, 8, tokens), F32),
            sem((4 + 6 * seqs,)),
            sem((5,)),
            sem((2,)),
        ]
        + ring + [sem((2, 1, n - 1))] * 2 + ring + ring
        + [sem((3, 2 * seqs))] * 2 + [sem((n,))] * 2 + [sem((3,))] * 2,
        compiler_params=pltpu.CompilerParams(
            collective_id=0, has_side_effects=True, vmem_limit_bytes=63 * 2**20
        ),
        name="forward_all",
    )(hidden, g, w_zx, w_bc, w_out, pre_gain, gate_gain, marks, *shared)


class RingScatter:
    def __init__(self, n, terms, slots, sems, ways=2, sign=1):
        self.n, self.terms, self.slots, self.ways, self.sign = n, terms, slots, ways, sign
        self.send_sem, self.recv_sem = sems
        self.place, self.at = ring_place(n)

    def turn(self, way):
        return self.sign * (1 - 2 * way)

    def owner(self, way, k):
        return self.at(self.place - self.turn(way) * (1 + k))

    def copy(self, way, k):
        return remote(
            self.slots.at[way, k],
            self.slots.at[way, k + 1],
            self.send_sem.at[way, k],
            self.recv_sem.at[way, k],
            {"dp": self.at(self.place + self.turn(way))},
        )

    def step(self, way, k):
        @pl.when(k == 0)
        def _():
            self.slots[way, 0] = self.terms[way].astype(BF16)

        @pl.when(k > 0)
        def _():
            self.copy(way, k - 1).wait_recv()

            @pl.when(k < self.n - 1)
            def _():
                self.slots[way, k] = (self.terms[way].astype(F32) + self.slots[way, k].astype(F32)).astype(BF16)

        @pl.when(k < self.n - 1)
        def _():
            self.copy(way, k).start()

    def last(self, way):
        return self.terms[way].astype(F32) + self.slots[way, self.n - 1].astype(F32)

    def finish(self):
        for k in range(self.n - 1):
            for way in range(self.ways):
                self.copy(way, k).wait_send()


class RowScatter:
    def __init__(self, parts, value, hold, sems):
        self.parts, self.value, self.hold = parts, value, hold
        self.send_sem, self.recv_sem = sems
        self.me, self.other, self.across = tensor_place()

    def copy(self, kind, part):
        src, dst = ((0, 1), (1, 2), (0, 3))[kind]
        return remote(
            self.hold.at[src, part],
            self.hold.at[dst, part],
            self.send_sem.at[kind, part],
            self.recv_sem.at[kind, part],
            {"tensor": self.across if kind == 1 else self.other},
        )

    def stage(self, j):
        late = j // (2 * self.parts)
        near = j - 2 * self.parts
        stage = (1 - late) * (j % 2) + late * (2 + near // self.parts)
        return stage, (1 - late) * (j // 2) + late * (near % self.parts)

    def owner(self, j):
        stage, part = self.stage(j)
        x, core = self.me // 2, self.me % 2
        return 2 * ((x + 1 - stage // 2) % 2) + (core + 1 - stage % 2) % 2, part

    def step(self, j, store, wait=True):
        stage, part = self.stage(j)

        @pl.when(stage == 0)
        def _():
            self.hold[0, part] = self.value[...].astype(BF16)
            self.copy(0, part).start()

        @pl.when(stage == 1)
        def _():
            self.copy(0, part).wait_recv()
            self.hold[1, part] = (self.value[...].astype(F32) + self.hold[1, part].astype(F32)).astype(BF16)
            self.copy(1, part).start()

        @pl.when(stage == 2)
        def _():
            self.copy(0, part).wait_send()
            self.hold[0, part] = self.value[...].astype(BF16)
            self.copy(2, part).start()

        @pl.when(stage == 3)
        def _():
            value = self.value[...].astype(F32)
            store(part, value + self.arrived(part) if wait else value)

    def arrived(self, part):
        self.copy(2, part).wait_recv()
        self.copy(1, part).wait_recv()
        return self.hold[3, part].astype(F32) + self.hold[2, part].astype(F32)

    def finish(self):
        for part in range(self.parts):
            for kind in (1, 2):
                self.copy(kind, part).wait_send()


def back_kernel(n, *refs):
    (normed_ref, g_ref, u_ref, dz_ref, wo_ref), refs = refs[:5], refs[5:]
    ins, refs = refs[:15], refs[15:]
    (out_ref, gout_ref, gz_ref), refs = refs[:3], refs[3:]
    outs, refs = refs[:5], refs[5:]
    scratch, refs = refs[:7], refs[7:]
    normed, dz, wo, g_cols, u_cols, out_slots, z_slots, hold, terms, mixed, load_sem, stream_sem, out_sem = refs[:13]
    sems = refs[13:]

    k = pl.program_id(0)
    blocks = 4
    piece = out_ref.shape[1]
    length = blocks * BLOCK
    count = g_ref.shape[1] // n
    half = gz_ref.shape[1] // 2
    place, at = ring_place(n)

    loads = [
        pltpu.make_async_copy(src, dst, load_sem.at[i])
        for i, (src, dst) in enumerate(((normed_ref, normed), (dz_ref, dz), (wo_ref, wo)))
    ]

    def streams(k):
        copies = []
        for way in (0, 1):
            d = at(place - (1 - 2 * way) * (1 + k))
            for i, (src, dst) in enumerate(((g_ref, g_cols), (u_ref, u_cols))):
                copies.append(
                    pltpu.make_async_copy(
                        src.at[:, span(d * count, count, 128)], dst.at[way], stream_sem.at[i, way]
                    )
                )
        return copies

    @pl.when(k == 0)
    def _():
        for copy in streams(0) + loads:
            copy.start()
        greet(n)

    backward_block(k // blocks, k % blocks, *ins, *outs, *scratch)

    @pl.when(k == 0)
    def _():
        for copy in loads:
            copy.wait()

    for copy in streams(k):
        copy.wait()

    rows = RowScatter(2, mixed, hold, sems[4:6])
    owner = rows.owner(k)
    own_rows = span(owner[1] * length + owner[0] * piece, piece, 16)

    for ring, (from_cols, to_cols) in enumerate(((g_cols, normed), (u_cols, dz))):
        for way in (0, 1):
            value = dot_tn(from_cols[way], to_cols[:, pl.ds(way * half, half)])
            terms[ring, way] = value.astype(BF16)
    mixed[...] = dot(normed[own_rows, :], wo[...]).astype(BF16)

    out_ring = RingScatter(n, terms.at[0], out_slots, sems[0:2])
    z_ring = RingScatter(n, terms.at[1], z_slots, sems[2:4])
    for way in (0, 1):
        out_ring.step(way, k)
        z_ring.step(way, k)

    @pl.when(k < n - 1)
    def _():
        for copy in streams(k + 1):
            copy.start()

    def out_copy(part):
        return pltpu.make_async_copy(hold.at[2, part], out_ref.at[part], out_sem.at[part])

    def store(part, value):
        hold[2, part] = value.astype(BF16)
        out_copy(part).start()

    rows.step(k, store)

    @pl.when(k == n - 1)
    def _():
        for way in (0, 1):
            at = pl.ds(way * half, half)
            gout_ref[at, :] = out_ring.last(way).T
            gz_ref[:, at] = z_ring.last(way)

    @pl.when(k == n - 1)
    def _():
        rows.finish()
        out_ring.finish()
        z_ring.finish()
        for part in range(2):
            out_copy(part).wait()


def backward_all(n, small, piece, normed, g, u, dz, w_out, dy, x, cx, bc, cbc, dt, marks, states, shared):
    seqs, length, channels = x.shape
    n2, heads = bc.shape[2], dt.shape[1]
    tokens, model = g.shape
    count = model // n
    blocks = length // BLOCK
    sem = pltpu.SemaphoreType.DMA
    anywhere = pl.BlockSpec(memory_space=pl.ANY)
    ins, outs = backward_specs(channels, n2, heads, small, lambda k: (k // blocks, blocks - 1 - k % blocks))
    whole = lambda *shape: pl.BlockSpec(shape, lambda k: (0,) * len(shape))
    return pl.pallas_call(
        functools.partial(back_kernel, n),
        grid=(n,),
        in_specs=[anywhere] * 5 + ins,
        out_specs=[anywhere, whole(channels, count), whole(count, channels)] + outs,
        out_shape=[
            jax.ShapeDtypeStruct((seqs, piece, model), BF16),
            jax.ShapeDtypeStruct((channels, count), F32),
            jax.ShapeDtypeStruct((count, channels), F32),
        ]
        + backward_outs(seqs, length, channels, n2, heads, small),
        scratch_shapes=backward_scratch(channels, n2, heads)
        + [
            pltpu.VMEM((tokens, channels), BF16),
            pltpu.VMEM((tokens, channels), BF16),
            pltpu.VMEM((channels, model), BF16),
            pltpu.VMEM((2, tokens, count), BF16),
            pltpu.VMEM((2, tokens, count), BF16),
            pltpu.VMEM((2, n, count, channels // 2), BF16),
            pltpu.VMEM((2, n, count, channels // 2), BF16),
            pltpu.VMEM((4, seqs, piece, model), BF16),
            pltpu.VMEM((2, 2, count, channels // 2), BF16),
            pltpu.VMEM((piece, model), BF16),
            sem((3,)),
            sem((2, 2)),
            sem((seqs,)),
        ]
        + [sem((2, n - 1))] * 4
        + [sem((3, seqs))] * 2,
        compiler_params=pltpu.CompilerParams(
            collective_id=1, has_side_effects=True, vmem_limit_bytes=127 * 2**19
        ),
        name="backward_all",
    )(normed, g, u, dz, w_out, dy, x, cx, bc, cbc, dt, marks, states, *shared)


class Fold:
    def __init__(self, n, total, came, sems):
        self.total, self.came = total, came
        self.send_sem, self.recv_sem = sems
        dp = lax.axis_index("dp")
        _, other, across = tensor_place()
        partners, ahead = [], 1
        while ahead < n:
            partners.append({"dp": dp + ahead * (1 - 2 * ((dp // ahead) % 2))})
            ahead *= 2
        self.over_dp = partners
        self.partners = partners + [{"tensor": other}, {"tensor": across}]

    def copy(self, r):
        return remote(
            self.total.at[r], self.came.at[r], self.send_sem.at[r], self.recv_sem.at[r], self.partners[r]
        )

    def start(self, r):
        self.copy(r).start()

    def take(self, r):
        self.copy(r).wait_recv()
        self.total[r + 1] = self.total[r] + self.came[r]

    def finish(self):
        for r in range(len(self.partners)):
            self.copy(r).wait_send()


def in_kernel(
    n, u_hbm, dz_hbm, dx_hbm, wz_hbm, wx_hbm, wb_hbm, dbc_hbm, gz_hbm, gx_in, gbc_in, gh_in, gate_in, gain_ref,
    din_ref, gx_ref, gb_ref, sums_ref, dots_ref, pre_ref,
    u_ref, dz_ref, dx_ref, wz_ref, wx_ref, wb_ref, dbc_ref,
    x_slots, b_slots, hold, bc_hold, x_terms, b_terms, in_value, bc_value, low, swap, own_in, pre, pre_dp, pre_tensor, total, came, load_sem, u_sem, *sems,
):
    seqs, piece = din_ref.shape[:2]
    tokens, model = u_ref.shape
    length = tokens // seqs
    count = model // n
    half = gx_ref.shape[2] // 2
    me, other, across = tensor_place()
    core = me % 2

    moves = (
        (dbc_hbm, dbc_ref),
        (dx_hbm, dx_ref),
        (dz_hbm, dz_ref),
        (wz_hbm, wz_ref),
        (wx_hbm, wx_ref),
        (wb_hbm, wb_ref),
        (gz_hbm, gx_ref.at[0]),
    )
    loads = [pltpu.make_async_copy(src, dst, load_sem.at[i]) for i, (src, dst) in enumerate(moves)]
    place, at_place = ring_place(n)
    u_copies = []
    for ahead in (-1, 1, -2, 2, -3, 3, 4, 0):
        cols = span(at_place(place + ahead) * count, count, 128)
        u_copies.append(pltpu.make_async_copy(u_hbm.at[:, cols], u_ref.at[:, cols], u_sem.at[ahead + 3]))
    for load in loads[:2] + u_copies[:2] + loads[2:] + u_copies[2:]:
        load.start()

    bc_rows = RowScatter(seqs, bc_value, bc_hold, sems[0:2])
    in_rows = RowScatter(seqs, in_value, hold, sems[2:4])
    x_ring = RingScatter(n, x_terms, x_slots, sems[4:6])
    b_ring = RingScatter(n, b_terms, b_slots, sems[6:8], 1, 1 - 2 * core)
    pair_send, pair_recv, swap_send, swap_recv = sems[8:12]
    dp_send, dp_recv, tensor_send, tensor_recv = sems[14:18]
    fold = Fold(n, total, came, sems[12:14])
    rounds = len(fold.partners)
    pair = remote(low.at[0], low.at[1], pair_send, pair_recv, {"tensor": other})

    total[0] = jnp.zeros_like(total[0])
    total[0, 0:6, :] = gx_in[0:6, :]
    total[0, 6:7, :] = gate_in[...]
    steps = gh_in[...].T
    total[0, 7:8, 0 : steps.shape[1]] = steps[0:1, :]
    total[0, 7:8, 128 : 128 + steps.shape[1]] = steps[1:2, :]
    total[0, 8:13, 0 : gbc_in.shape[1]] = gbc_in[0:5, :]
    pre[...] = jnp.zeros_like(pre)
    dp_now = lax.axis_index("dp")
    greet(
        n,
        fold.over_dp
        + [{"dp": (dp_now + o) % n} for o in range(1, n)]
        + [{"tensor": (me + o) % 4} for o in range(1, 4)],
    )
    def rows_at(t, part):
        return span(part * length + t * piece, piece, 16)

    def bc_store(part, value):
        low[0, part] = value.astype(BF16)

    def bc_step(j):
        t, part = bc_rows.owner(j)
        bc_value[...] = dbc_ref[rows_at(t, part), :].astype(F32)
        bc_rows.step(j, bc_store)

    def add_pre(at):
        pre[...] += jnp.sum(in_value[...] * u_ref[at, :].astype(F32), axis=0, keepdims=True)

    def store(part, value):
        in_value[...] = value + dot_nt(low[0, part], wb_ref[...])
        own_in[part] = in_value[...]
        add_pre(rows_at(me, part))

    def row_term(j):
        at = rows_at(*in_rows.owner(j))
        in_value[...] = dot_nt(dz_ref[at, :], wz_ref[...]) + dot_nt(dx_ref[at, :], wx_ref[...])

    def row_step(j):
        in_rows.step(j, store, wait=False)

        @pl.when(j < 3 * seqs)
        def _():
            add_pre(rows_at(*in_rows.owner(j)))

    def x_term(k):
        for way in (0, 1):
            cols = span(x_ring.owner(way, k) * count, count, 128)
            x_terms[way] = dot_tn(u_ref[:, cols], dx_ref[:, pl.ds(way * half, half)])

    def x_step(k):
        for way in (0, 1):
            x_ring.step(way, k)

    def b_step(k):
        cols = span(b_ring.owner(0, k) * count + core * count // 2, count // 2, 128)
        value = 0.0
        for t, which in ((me, 0), (other, 1)):
            for part in range(seqs):
                value = value + dot_tn(u_ref[rows_at(t, part), cols], low[which, part])
        b_terms[0] = value
        b_ring.step(0, k)

    loads[0].wait()
    for part in range(seqs):
        bc_step(2 * part)
        bc_step(2 * seqs + part)
    loads[1].wait()
    for copy in u_copies[:2]:
        copy.wait()
    x_term(0)
    x_step(0)
    for load in loads[2:] + u_copies[2:]:
        load.wait()
    row_term(0)
    row_step(0)
    for part in range(seqs):
        bc_step(2 * part + 1)

    wide = model // 8
    gain = gain_ref[...]

    def dp_copy(o):
        ref = pre_dp.at[dp_now]
        return remote(ref, ref, dp_send.at[o], dp_recv.at[o], {"dp": (dp_now + o) % n})

    def tensor_copy(o):
        ref = pre_tensor.at[me]
        return remote(ref, ref, tensor_send.at[o], tensor_recv.at[o], {"tensor": (me + o) % 4})

    cross = remote(swap.at[0], swap.at[1], swap_send.at[0], swap_recv.at[0], {"tensor": across})
    back = remote(swap.at[2], swap.at[3], swap_send.at[1], swap_recv.at[1], {"tensor": other})

    def at_step(k, when, what):
        pl.when(k == when)(what)

    def own_bc():
        for part in range(seqs):
            bc_step(3 * seqs + part)
        pair.start()

    def send_pre():
        for i in range(8):
            at = slice(i * wide, (i + 1) * wide)
            pre_dp[dp_now, i : i + 1, :] = pre[:, at] / gain[:, at]
        for o in range(1, n):
            dp_copy(o).start()

    def pass_pre():
        for o in range(1, n):
            dp_copy(o).wait_recv()
        pre_tensor[me] = sum(pre_dp[d] for d in range(n))
        for o in range(1, 4):
            tensor_copy(o).start()

    def take_pre():
        for o in range(1, 4):
            tensor_copy(o).wait_recv()
        pre_ref[...] = (pre_tensor[0] + pre_tensor[1]) + (pre_tensor[2] + pre_tensor[3])

    def send_bc():
        swap[0] = b_ring.last(0)
        cross.start()

    def pass_bc():
        cross.wait_recv()
        swap[2] = swap[0] + swap[1]
        back.start()
        gb_ref[span(core * count // 2, count // 2, 16), :] = swap[2]

    def step(k, _):
        at_step(k, 5, send_pre)
        at_step(k, n - 1, send_bc)

        @pl.when(2 * k - 1 < 4 * seqs)
        def _():
            row_term(2 * k - 1)
            row_step(2 * k - 1)

        x_term(k)
        x_step(k)
        at_step(k, 2, pair.wait_recv)

        @pl.when((k >= 2) & (k <= 6))
        def _():
            b_step(jnp.maximum(k - 2, 2 * (k - 3)))

        @pl.when(2 * k < 4 * seqs)
        def _():
            row_term(2 * k)
            row_step(2 * k)

        at_step(k, 1, own_bc)

        @pl.when((k >= 4) & (k <= 6))
        def _():
            b_step(2 * (k - 3) + 1)

        at_step(k, 6, pass_pre)
        at_step(k, n - 1, pass_bc)
        at_step(k, n - 1, take_pre)
        for r in range(rounds + 1):

            @pl.when(k == r + 1)
            def _():
                if r > 0:
                    fold.take(r - 1)
                if r < rounds:
                    fold.start(r)

        return 0

    lax.fori_loop(1, n, step, 0)
    for way in (0, 1):
        gx_ref[1, :, pl.ds(way * half, half)] = x_ring.last(way)
    sums_ref[0:8, :] = total[rounds - 2, 0:8, :]
    sums_ref[8:16, :] = total[rounds, 8:16, :]
    for part in range(seqs):
        value = own_in[part] + in_rows.arrived(part)
        din_ref[part] = value.astype(BF16)
        inner = jnp.sum(value * u_ref[rows_at(me, part), :].astype(F32), axis=1, keepdims=True)
        dots_ref[part] = jnp.broadcast_to(inner, (piece, 128))
    back.wait_recv()
    gb_ref[span((1 - core) * count // 2, count // 2, 16), :] = swap[3]
    for o in range(1, n):
        dp_copy(o).wait_send()
    for o in range(1, 4):
        tensor_copy(o).wait_send()
    for copy in (pair, cross, back):
        copy.wait_send()
    for part in (bc_rows, in_rows, x_ring, b_ring, fold):
        part.finish()


def scatter_in(n, piece, u, dz, dx, w_z, w_x, w_bc, dbc, grad_z, gx, gbc, gh, grad_gate, gain):
    tokens, model = u.shape
    width = dz.shape[1]
    small = dbc.shape[1]
    seqs = tokens // (4 * piece)
    count = model // n
    rounds = 5
    sem = pltpu.SemaphoreType.DMA
    vmem = pl.BlockSpec(memory_space=pltpu.VMEM)
    anywhere = pl.BlockSpec(memory_space=pl.ANY)
    big = (u, dz, dx, w_z, w_x, w_bc, dbc)
    return pl.pallas_call(
        functools.partial(in_kernel, n),
        in_specs=[anywhere] * 8 + [vmem] * 5,
        out_specs=[vmem] * 6,
        out_shape=[
            jax.ShapeDtypeStruct((seqs, piece, model), BF16),
            jax.ShapeDtypeStruct((2, count, width), F32),
            jax.ShapeDtypeStruct((count, small), F32),
            jax.ShapeDtypeStruct((16, width), F32),
            jax.ShapeDtypeStruct((seqs, piece, 128), F32),
            jax.ShapeDtypeStruct((8, model // 8), F32),
        ],
        scratch_shapes=[pltpu.VMEM(a.shape, BF16) for a in big]
        + [
            pltpu.VMEM((2, n, count, width // 2), BF16),
            pltpu.VMEM((1, n, count // 2, small), BF16),
            pltpu.VMEM((4, seqs, piece, model), BF16),
            pltpu.VMEM((4, seqs, piece, small), BF16),
            pltpu.VMEM((2, count, width // 2), F32),
            pltpu.VMEM((1, count // 2, small), F32),
            pltpu.VMEM((piece, model), F32),
            pltpu.VMEM((piece, small), F32),
            pltpu.VMEM((2, seqs, piece, small), BF16),
            pltpu.VMEM((4, count // 2, small), F32),
            pltpu.VMEM((seqs, piece, model), F32),
            pltpu.VMEM((1, model), F32),
            pltpu.VMEM((n, 8, model // 8), F32),
            pltpu.VMEM((4, 8, model // 8), F32),
            pltpu.VMEM((rounds + 1, 16, width), F32),
            pltpu.VMEM((rounds, 16, width), F32),
            sem((len(big),)),
            sem((n,)),
        ]
        + [sem((3, seqs))] * 4 + [sem((2, n - 1))] * 2 + [sem((1, n - 1))] * 2 + [sem(())] * 2 + [sem((2,))] * 2
        + [sem((rounds,))] * 2 + [sem((n,))] * 2 + [sem((4,))] * 2,
        compiler_params=pltpu.CompilerParams(
            collective_id=2, has_side_effects=True, vmem_limit_bytes=63 * 2**20
        ),
        name="scatter_in",
    )(*big, grad_z, gx, gbc, gh, grad_gate, gain)


def finish_kernel(
    d_in_ref, hidden_ref, cot_ref, mixed_ref, scale_ref, dots_ref, gain_ref, gzx_in, gout_in, gb_in, sums_ref,
    out_ref, d_hidden_ref, gzx_ref, gout_ref, gb_ref, taps_ref, taps_bc_ref,
):
    model = gain_ref.shape[1]
    x = hidden_ref[0].astype(F32)
    scale = scale_ref[0][:, 0:1]
    factor = scale * scale * dots_ref[0][:, 0:1] / model
    d_hidden_ref[0] = cot_ref[0].astype(F32) + scale * (gain_ref[...] * d_in_ref[0].astype(F32)) - x * factor
    out_ref[0] = (x + mixed_ref[0].astype(F32)).astype(BF16)
    gzx_ref[...] = gzx_in[...]
    gout_ref[...] = gout_in[...]
    gb_ref[...] = gb_in[:, : gb_ref.shape[1]]
    taps_ref[...] = sums_ref[0 : taps_ref.shape[0], :]
    taps_bc_ref[...] = sums_ref[8 : 8 + taps_bc_ref.shape[0], : taps_bc_ref.shape[1]]


def finish(d_in, hidden, cotangent, mixed, scale, dots, gain, grad_zx, grad_out, grad_bc, sums, columns, n2):
    seqs, piece, model = hidden.shape
    count, width = grad_zx.shape[1:]
    steps = 4
    rows = piece // steps
    grid = seqs * steps
    piece_rows = lambda w: pl.BlockSpec((1, rows, w), lambda i: (i // steps, i % steps, 0))
    whole = lambda *shape: pl.BlockSpec(shape, lambda i: (0,) * len(shape))
    zx = pl.BlockSpec((1, 2 * count // grid, width), lambda i: (i // (grid // 2), i % (grid // 2), 0))
    down = lambda a, w: pl.BlockSpec((a.shape[0] // grid, w), lambda i: (i, 0))
    return pl.pallas_call(
        finish_kernel,
        grid=(grid,),
        in_specs=[piece_rows(model)] * 4
        + [piece_rows(128)] * 2
        + [whole(1, model), zx, down(grad_out, grad_out.shape[1]), down(grad_bc, grad_bc.shape[1])]
        + [whole(*sums.shape)],
        out_specs=[piece_rows(model)] * 2
        + [zx, down(grad_out, grad_out.shape[1]), down(grad_bc, columns), whole(5, width), whole(5, n2)],
        out_shape=[
            jax.ShapeDtypeStruct(hidden.shape, BF16),
            jax.ShapeDtypeStruct(hidden.shape, F32),
            jax.ShapeDtypeStruct(grad_zx.shape, F32),
            jax.ShapeDtypeStruct(grad_out.shape, F32),
            jax.ShapeDtypeStruct((grad_bc.shape[0], columns), F32),
            jax.ShapeDtypeStruct((5, width), F32),
            jax.ShapeDtypeStruct((5, n2), F32),
        ],
        compiler_params=pltpu.CompilerParams(vmem_limit_bytes=62 * 2**20),
        name="finish",
    )(d_in, hidden, cotangent, mixed, scale, dots, gain, grad_zx, grad_out, grad_bc, sums)


def rms_scale(values):
    return lax.rsqrt(jnp.mean(values * values, axis=-1, keepdims=True) + EPS)


def gather_plain(u, g, w_zx, w_bc, w_out):
    w_zx = lax.all_gather(w_zx, "dp", axis=1, tiled=True)
    return (
        lax.all_gather(u, "tensor", axis=1, tiled=True),
        lax.all_gather(g, "tensor", axis=1, tiled=True),
        w_zx[1],
        w_zx[0],
        lax.all_gather(w_bc, "dp", axis=0, tiled=True),
        lax.all_gather(w_out, "dp", axis=1, tiled=True),
    )


def rows_of(values, piece):
    by_seq = values.reshape(-1, 4 * piece, values.shape[-1])
    return lax.psum_scatter(by_seq, "tensor", scatter_dimension=1, tiled=True)


def scatter_out_plain(piece, normed, g, u, dz, w_out):
    return (
        rows_of(dot(normed, w_out), piece),
        lax.psum_scatter(dot_tn(normed, g), "dp", scatter_dimension=1, tiled=True),
        lax.psum_scatter(dot_tn(u, dz), "dp", scatter_dimension=0, tiled=True),
    )


def scatter_in_plain(piece, u, dz, dx, w_z, w_x, w_bc, dbc):
    low = lax.psum(dbc.astype(F32), "tensor").astype(BF16)
    d_in = rows_of(dot_nt(dz, w_z) + dot_nt(dx, w_x), piece)
    first = lax.axis_index("tensor") * piece
    own = lax.dynamic_slice_in_dim(low.reshape(-1, 4 * piece, low.shape[1]), first, piece, 1)
    d_in = d_in + jnp.einsum("slc,dc->sld", own, w_bc, preferred_element_type=F32)
    return (
        d_in,
        lax.psum_scatter(dot_tn(u, dx), "dp", scatter_dimension=0, tiled=True),
        lax.psum_scatter(dot_tn(u, low), "dp", scatter_dimension=0, tiled=True),
    )


def local(
    n_dp,
    n_tensor,
    hidden,
    pre_gain,
    w_zx,
    w_bcdt,
    conv_x,
    conv_bc,
    dt_bias,
    a_log,
    d_skip,
    gate_gain,
    w_out,
    cotangent,
    segments,
):
    seqs, piece, model = hidden.shape
    length = segments.shape[1]
    tokens = seqs * length
    heads = dt_bias.shape[0]
    channels = conv_x.shape[1]
    n2 = conv_bc.shape[1]
    columns = w_bcdt.shape[1]
    tensor = lax.axis_index("tensor")
    kernels = n_dp == 8 and n_tensor == 4 and seqs == 2 and length == 4 * BLOCK

    x_piece = hidden.astype(F32)
    marks = row_marks(segments)
    spread = jnp.asarray(spread_matrix(heads, channels), BF16)
    skip = jnp.repeat(d_skip, channels // heads)[None]
    pick = jnp.asarray(pick_matrix(heads, channels), BF16)
    shared = (conv_x, conv_bc, dt_bias[None], a_log[None], skip, spread, pick)
    if kernels:
        u, g, w_x, w_z, w_bc, w_o, cx, x, cbc, bc, dt, states, normed, dz, dy, grad_gate, scale_in = forward_all(
            n_dp, hidden, cotangent, w_zx, w_bcdt, w_out, pre_gain[None], gate_gain[None], marks, shared
        )
        g = g.reshape(tokens, model)
    else:
        scale_in = rms_scale(x_piece)
        u_piece = (x_piece * scale_in * pre_gain).astype(BF16)
        w_bc_piece = jnp.pad(w_bcdt, ((0, 0), (0, -columns % 128)))
        u, g, w_x, w_z, w_bc, w_o = gather_plain(u_piece, cotangent, w_zx, w_bc_piece, w_out)
        u = u.reshape(tokens, model)
        g = g.reshape(tokens, model)
        x = dot(u, w_x).reshape(seqs, length, channels)
        z = dot(u, w_z)
        bc_dt = dot(u, w_bc).reshape(seqs, length, -1)
        bc = bc_dt[:, :, :n2]
        dt = jnp.swapaxes(lax.dynamic_slice_in_dim(bc_dt, n2 + tensor * heads, heads, 2), 1, 2)
        y, cx, cbc, states = ssd_forward(x, bc, dt, marks, shared)
        d_normed = dot_nt(g, w_o)
        sig_z = sigmoid(z)
        silu_z = z * sig_z
        y_flat = y.reshape(tokens, channels)
        gated = y_flat * silu_z
        scaled = d_normed * gate_gain
        sums = jnp.stack([jnp.sum(gated * gated, axis=1), jnp.sum(scaled * gated, axis=1)])
        sums = lax.psum(sums, "tensor") / (channels * n_tensor)
        inverse = lax.rsqrt(sums[0] + EPS)[:, None]
        normed = (gated * inverse * gate_gain).astype(BF16)
        grad_gate = jnp.sum(d_normed * gated * inverse, axis=0)[None]
        d_gated = inverse * scaled - gated * inverse**3 * sums[1][:, None]
        dy = (d_gated * silu_z).astype(BF16)
        dz = (d_gated * y_flat * (sig_z * (1.0 + z * (1.0 - sig_z)))).astype(BF16)
        x, bc = x.astype(BF16), bc.astype(BF16)

    back_args = (dy.reshape(seqs, length, channels), x, cx, bc, cbc, dt, marks, states, shared)
    if kernels:
        mixed, grad_out, grad_z, *rest = backward_all(n_dp, w_bc.shape[1], piece, normed, g, u, dz, w_o, *back_args)
    else:
        mixed, grad_out, grad_z = scatter_out_plain(piece, normed, g, u, dz, w_o)
        rest = ssd_backward(w_bc.shape[1], *back_args)
    dx, dbc, gx, gbc, gh = rest
    in_args = (piece, u, dz, dx.reshape(tokens, channels), w_z, w_x, w_bc, dbc.reshape(tokens, -1))
    if kernels:
        d_in, grad_zx, grad_bc, sums, dots, grad_pre = scatter_in(
            n_dp, *in_args, grad_z, gx, gbc, gh, grad_gate, pre_gain[None]
        )
        grad_pre = grad_pre.reshape(model)
        out_hidden, d_hidden, grad_zx, grad_out, grad_bc, grad_conv_x, grad_conv_bc = finish(
            d_in, hidden, cotangent, mixed, scale_in, dots, pre_gain[None], grad_zx, grad_out, grad_bc, sums, columns, n2
        )
    else:
        d_in, grad_x, grad_bc = scatter_in_plain(*in_args)
        grad_zx = jnp.stack([grad_z, grad_x])
        grad_pre = jnp.sum(d_in * x_piece * scale_in, axis=(0, 1))
        dots = scale_in * jnp.sum(d_in * pre_gain * x_piece, axis=-1, keepdims=True)
        steps = jnp.pad(gh[:, :2].T, ((0, 0), (0, channels - heads)))
        sums = lax.psum(jnp.concatenate([gx[:6], grad_gate, steps]), "dp")
        sums = jnp.concatenate([sums[:7], jnp.concatenate([sums[7, :128], sums[8, : channels - 128]])[None]])
        grad_conv_bc, grad_pre = lax.psum((gbc[:5], grad_pre), ("dp", "tensor"))
        grad_conv_x = sums[:5]
        grad_bc = grad_bc[:, :columns]
        out_hidden = (x_piece + mixed).astype(BF16)
        d_hidden = cotangent.astype(F32) + scale_in * (pre_gain * d_in) - x_piece * (scale_in**2 * dots / model)

    return (
        out_hidden,
        d_hidden,
        grad_pre,
        grad_zx,
        grad_bc,
        grad_conv_x,
        grad_conv_bc,
        sums[7, :heads],
        sums[7, 128 : 128 + heads],
        sums[5].reshape(heads, -1).sum(axis=1),
        sums[6],
        grad_out,
    )


def solution(mesh):
    placed = (
        P("dp", "tensor", None),
        P(),
        P(None, "dp", "tensor"),
        P("dp", None),
        P(None, "tensor"),
        P(),
        P("tensor"),
        P("tensor"),
        P("tensor"),
        P("tensor"),
        P("tensor", "dp"),
        P("dp", "tensor", None),
        P("dp", None),
    )
    return jax.shard_map(
        functools.partial(local, mesh.shape["dp"], mesh.shape["tensor"]),
        mesh=mesh,
        in_specs=placed,
        out_specs=(
            P("dp", "tensor", None),
            P("dp", "tensor", None),
            P(),
            P(None, "dp", "tensor"),
            P("dp", None),
            P(None, "tensor"),
            P(),
            P("tensor"),
            P("tensor"),
            P("tensor"),
            P("tensor"),
            P("tensor", "dp"),
        ),
        check_vma=False,
    )
```

```python
import functools

import jax
import jax.numpy as jnp
import numpy as np
from jax import lax
from jax.experimental import pallas as pl
from jax.experimental.pallas import tpu as pltpu
from jax.sharding import PartitionSpec as P

MESH = pl.DeviceIdType.MESH
EPS = 1e-05
BLOCK = 256
F32 = jnp.float32
BF16 = jnp.bfloat16
EXACT = lax.Precision.HIGHEST
LOG2E = 1.4426950408889634
NEG = -1e30


def sigmoid(v):
    return 0.5 * jnp.tanh(0.5 * v) + 0.5


def split3(v):
    hi = v.astype(BF16)
    rest = v - hi.astype(F32)
    mid = rest.astype(BF16)
    low = (rest - mid.astype(F32)).astype(BF16)
    return hi, mid, low


def dot(a, b):
    return jnp.dot(a, b, preferred_element_type=F32)


def dot_nt(a, b):
    return lax.dot_general(a, b, (((1,), (1,)), ((), ())), preferred_element_type=F32)


def dot_tn(a, b):
    return lax.dot_general(a, b, (((0,), (0,)), ((), ())), preferred_element_type=F32)


def softplus(v):
    return jnp.maximum(v, 0.0) + jnp.log1p(jnp.exp(-jnp.abs(v)))


def head_rows(raw, dt_bias, a_log):
    q = raw.shape[1]
    upto = (
        lax.broadcasted_iota(jnp.int32, (q, q), 0) <= lax.broadcasted_iota(jnp.int32, (q, q), 1)
    ).astype(F32)
    biased = raw + dt_bias
    step = softplus(biased)
    rate = -jnp.exp(a_log) * step
    cum = jnp.dot(rate, upto, precision=EXACT, preferred_element_type=F32) * LOG2E
    return biased, step, rate, cum


def exact_nt(a, b):
    a_hi, a_mid, _ = split3(a)
    b_hi, b_mid, _ = split3(b)
    return dot_nt(a_hi, b_hi) + dot_nt(a_hi, b_mid) + dot_nt(a_mid, b_hi)


def turned(row):
    k = row.shape[1]
    own = lax.broadcasted_iota(jnp.int32, (k, k), 0) == lax.broadcasted_iota(jnp.int32, (k, k), 1)
    return jnp.sum(jnp.where(own, row, 0.0), axis=1, keepdims=True)


def to_columns(rows):
    return jnp.concatenate([rows, jnp.zeros((128 - rows.shape[0], rows.shape[1]), F32)], axis=0).T


def head_columns(reads, last, step, cum, third):
    cum_end = cum[:, BLOCK - 1 : BLOCK]
    rows = []
    for factor in (reads * jnp.exp2(cum), last * jnp.exp2(cum_end - cum) * step):
        hi, mid, _ = split3(factor)
        rows += [hi.astype(F32), mid.astype(F32)]
    cols = to_columns(jnp.concatenate(rows + [third], axis=0))
    return cols[:, 4 * cum.shape[0] :], cols.astype(BF16), jnp.exp2(cum_end)


def log2_step(step):
    return jnp.log(jnp.maximum(step, 1e-37)) * LOG2E


def forward_block(
    block, x, bc, dt, marks_ref, taps_x_ref, taps_bc_ref, bias_ref, alog_ref, skip_ref, spread_ref, pick_ref,
    y_ref, cx_ref, cbc_ref, states_ref,
    xs, bs, state, mask_bias,
):
    q = BLOCK
    heads = dt.shape[0]
    channels = x.shape[-1]
    width = channels // heads

    @pl.when(block == 0)
    def _():
        xs[0:8, :] = jnp.zeros((8, xs.shape[1]), F32)
        bs[0:8, :] = jnp.zeros((8, bs.shape[1]), F32)
        state[...] = jnp.zeros_like(state)

    marks = to_columns(marks_ref[0])
    lag_masks = [marks[:, k : k + 1] for k in range(3)]

    def conv(hold, at, taps_ref):
        out = taps_ref[4:5, at] + taps_ref[3:4, at] * hold[8 : 8 + q, at]
        for lag in (1, 2, 3):
            out = out + (lag_masks[lag - 1] * hold[8 - lag : 8 - lag + q, at]) * taps_ref[3 - lag : 4 - lag, at]
        return out

    bs[8 : 8 + q, :] = bc
    xs[8 : 8 + q, :] = x
    cbc = conv(bs, slice(None), taps_bc_ref)
    cbc_ref[0] = cbc
    bc = cbc * sigmoid(cbc)
    n = bc.shape[1] // 2
    scores = exact_nt(bc[:, n:], bc[:, :n])
    b_mat, c_mat = bc[:, :n].astype(BF16), bc[:, n:].astype(BF16)
    b_turned = b_mat.T

    _, step, _, cum = head_rows(dt, turned(bias_ref[...]), turned(alog_ref[...]))
    cols, factors, carry = head_columns(marks_ref[0, 3:4, :], marks_ref[0, 4:5, :], step, cum, cum)
    source = cum - log2_step(step)
    carry_e = jnp.sum(carry * spread_ref[...].astype(F32), axis=0, keepdims=True)
    skip_e = jnp.sum(turned(skip_ref[...]) * spread_ref[...].astype(F32), axis=0, keepdims=True)

    rows = lax.broadcasted_iota(jnp.int32, (q, q), 0)
    places = lax.broadcasted_iota(jnp.int32, (q, q), 1)
    mask_bias[...] = jnp.where((marks[:, 5:6] == marks_ref[0, 5:6, :]) & (rows >= places), 0.0, NEG)

    half = q // 2
    pair_width = 2 * width
    lane = lax.broadcasted_iota(jnp.int32, (1, pair_width), 1)
    every = slice(0, channels)
    cx = conv(xs, every, taps_x_ref)
    cx_ref[0] = cx
    xb = (cx * sigmoid(cx)).astype(BF16)
    xf = xb.astype(F32)
    stb = state[...].astype(BF16)
    states_ref[0, 0] = stb
    y_ref[...] = dot(c_mat, stb) * dot(factors, pick_ref[:, :channels]) + skip_e * xf
    scaled = (xf * dot(factors, pick_ref[:, channels:])).astype(BF16)
    state[...] = carry_e * state[...] + dot(b_turned, scaled)
    for pair in range(heads // 2):
        at = slice(pair * pair_width, (pair + 1) * pair_width)
        xp = xb[:, at]
        tops, lows = [], []
        for h in (2 * pair, 2 * pair + 1):
            col = cols[:, h : h + 1]
            row = source[h : h + 1, :]
            top = jnp.exp2((col[:half] - row[:, :half]) + mask_bias[:half, :half]) * scores[:half, :half]
            low = jnp.exp2((col[half:] - row) + mask_bias[half:, :]) * scores[half:, :]
            tops.append(top.astype(BF16))
            lows.append(low.astype(BF16))
        top = dot(jnp.concatenate(tops, axis=0), xp[:half])
        low = dot(jnp.concatenate(lows, axis=0), xp)
        first = lane < width
        y_ref[:half, at] += jnp.where(first, top[:half], top[half:])
        y_ref[half:, at] += jnp.where(first, low[:half], low[half:])

    xs[0:8, :] = xs[q : q + 8, :]
    bs[0:8, :] = bs[q : q + 8, :]


def backward_block(
    seq, step_id, dy_ref, x_ref, cx_ref, bc_ref, cbc_ref, dt_ref, marks_ref, states_ref,
    taps_x_ref, taps_bc_ref, bias_ref, alog_ref, skip_ref, spread_ref, pick_ref,
    dx_ref, dbc_ref, gx_ref, gbc_ref, gh_ref,
    ds_x, ds_bc, d_state, mask_bias, d_scores, d_in, row_sums,
):
    q = BLOCK
    heads = dt_ref.shape[1]
    channels = x_ref.shape[-1]
    width = channels // heads

    @pl.when(step_id == 0)
    def _():
        ds_x[:, q : q + 8, :] = jnp.zeros((3, 8, channels), F32)
        ds_bc[:, q : q + 8, :] = jnp.zeros((3, 8, ds_bc.shape[2]), F32)
        d_state[...] = jnp.zeros_like(d_state)

    @pl.when((step_id == 0) & (seq == 0))
    def _():
        gx_ref[...] = jnp.zeros_like(gx_ref)
        gbc_ref[...] = jnp.zeros_like(gbc_ref)
        gh_ref[...] = jnp.zeros_like(gh_ref)

    marks = to_columns(marks_ref[0])
    lag_masks = [marks[:, k : k + 1] for k in range(3)]

    def conv_back(d_out, value, hold, at, taps_ref, grad_ref):
        value = value.astype(F32)
        d_value = d_out * taps_ref[3:4, at]
        grad_ref[3:4, at] += jnp.sum(value * d_out, axis=0, keepdims=True)
        grad_ref[4:5, at] += jnp.sum(d_out, axis=0, keepdims=True)
        for lag in (1, 2, 3):
            hold[lag - 1, 0:q, at] = lag_masks[lag - 1] * d_out
            moved = hold[lag - 1, lag : lag + q, at]
            d_value = d_value + moved * taps_ref[3 - lag : 4 - lag, at]
            grad_ref[3 - lag : 4 - lag, at] += jnp.sum(value * moved, axis=0, keepdims=True)
            hold[lag - 1, q : q + 8, at] = hold[lag - 1, 0:8, at]
        return d_value

    cbc = cbc_ref[0]
    bc = cbc * sigmoid(cbc)
    n = bc.shape[1] // 2
    scores = exact_nt(bc[:, :n], bc[:, n:])
    b_mat, c_mat = bc[:, :n].astype(BF16), bc[:, n:].astype(BF16)
    c_turned = c_mat.T

    a_log = turned(alog_ref[...])
    biased, step, rate, cum = head_rows(dt_ref[0], turned(bias_ref[...]), a_log)
    source = cum - log2_step(step)
    cols, factors, carry = head_columns(marks_ref[0, 3:4, :], marks_ref[0, 4:5, :], step, cum, source)
    carry_e = jnp.sum(carry * spread_ref[...].astype(F32), axis=0, keepdims=True)
    skip_e = jnp.sum(turned(skip_ref[...]) * spread_ref[...].astype(F32), axis=0, keepdims=True)

    rows = lax.broadcasted_iota(jnp.int32, (q, q), 0)
    places = lax.broadcasted_iota(jnp.int32, (q, q), 1)
    mask_bias[...] = jnp.where((marks[:, 5:6] == marks_ref[0, 5:6, :]) & (rows <= places), 0.0, NEG)

    half = q // 2
    pair_width = 2 * width
    lane = lax.broadcasted_iota(jnp.int32, (1, pair_width), 1)
    first = lane < width
    d_scores[...] = jnp.zeros_like(d_scores)
    col_h = jnp.zeros((heads, q), F32)
    head_row = lax.broadcasted_iota(jnp.int32, (heads, 3 * half), 0)
    spread = spread_ref[...]
    cx = cx_ref[0]
    xb = (cx * sigmoid(cx)).astype(BF16)
    dyb = dy_ref[0]
    st = states_ref[0, 0]
    dye = dyb.astype(F32) * dot(factors, pick_ref[:, :channels])
    out_h = dot_nt(spread, (dye * dot(c_mat, st)).astype(BF16))
    dye = dye.astype(BF16)
    d_c = dot_nt(dye, st)
    dst = d_state[...].astype(BF16)
    kept = jnp.sum(d_state[...] * st.astype(F32), axis=0, keepdims=True) * carry_e
    carried = jnp.sum(spread.astype(F32) * kept, axis=1, keepdims=True)
    d_state[...] = carry_e * d_state[...] + dot(c_turned, dye)
    xf = xb.astype(F32)
    to_end = dot(factors, pick_ref[:, channels:])
    d_b = dot_nt((xf * to_end).astype(BF16), dst)
    dx_st = dot(b_mat, dst) * to_end
    state_h = dot_nt(spread, (xf * dx_st).astype(BF16))
    d_in[...] = dx_st
    for pair in range(heads // 2):
        at = slice(pair * pair_width, (pair + 1) * pair_width)
        xp, dyp = xb[:, at], dyb[:, at]
        none = jnp.zeros_like(xp)
        x_first, x_second = jnp.where(first, xp, none), jnp.where(first, none, xp)
        g_top = dot_nt(jnp.concatenate([x_first[:half], x_second[:half]], axis=0), dyp)
        g_low = dot_nt(jnp.concatenate([x_first[half:], x_second[half:]], axis=0), dyp[half:])
        tops, lows, d_top, d_low = [], [], 0.0, 0.0
        for which in (0, 1):
            h = 2 * pair + which
            own = slice(which * half, (which + 1) * half)
            col = cols[:, h : h + 1]
            row = cum[h : h + 1, :]
            top = jnp.exp2((row - col[:half]) + mask_bias[:half, :])
            low = jnp.exp2((row[:, half:] - col[half:]) + mask_bias[half:, half:])
            p_top = top * g_top[own]
            p_low = low * g_low[own]
            d_top = d_top + p_top
            d_low = d_low + p_low
            m_top = p_top * scores[:half, :]
            m_low = p_low * scores[half:, half:]
            late = jnp.sum(m_top[:, half:], axis=0, keepdims=True) + jnp.sum(m_low, axis=0, keepdims=True)
            row_sums[h : h + 1, :half] = jnp.sum(m_top[:, :half], axis=0, keepdims=True)
            row_sums[h : h + 1, half:] = late
            parts = split3(jnp.concatenate([m_top[:, :half] + m_top[:, half:], m_low], axis=0))
            col_h = col_h + dot_nt((head_row == h).astype(BF16), jnp.concatenate(parts, axis=1))
            tops.append((top * scores[:half, :]).astype(BF16))
            lows.append((low * scores[half:, half:]).astype(BF16))
        d_scores[:half, :] += d_top
        d_scores[half:, half:] += d_low
        top = dot(jnp.concatenate(tops, axis=0), dyp)
        low = dot(jnp.concatenate(lows, axis=0), dyp[half:])
        d_in[:half, at] += jnp.where(first, top[:half], top[half:])
        d_in[half:, at] += jnp.where(first, low[:half], low[half:])

    everywhere = slice(0, channels)
    dyf = dy_ref[0].astype(F32)
    cx = cx_ref[0]
    sig = sigmoid(cx)
    gx_ref[5:6, :] += jnp.sum(dyf * (cx * sig).astype(BF16).astype(F32), axis=0, keepdims=True)
    d_cx = (d_in[...] + skip_e * dyf) * (sig * (1.0 + cx * (1.0 - sig)))
    dx_ref[0] = conv_back(d_cx, x_ref[0], ds_x, everywhere, taps_x_ref, gx_ref).astype(BF16)

    dsb = d_scores[...].astype(BF16)
    d_b = d_b + dot(dsb, c_mat)
    d_c = d_c + dot_tn(dsb, b_mat)
    sig = sigmoid(cbc)
    d_cbc = jnp.concatenate([d_b, d_c], axis=1) * (sig * (1.0 + cbc * (1.0 - sig)))
    every = slice(0, 2 * n)
    dbc_ref[0, :, every] = conv_back(d_cbc, bc_ref[0], ds_bc, every, taps_bc_ref, gbc_ref).astype(BF16)

    used_h = col_h + state_h
    diff_h = row_sums[...] - col_h + out_h
    since = (rows >= places).astype(F32)
    before = (rows < places).astype(F32)
    d_rate = (
        jnp.dot(diff_h, since, precision=EXACT, preferred_element_type=F32)
        + jnp.dot(state_h, before, precision=EXACT, preferred_element_type=F32)
        + carried
    )
    sig_dt = sigmoid(biased)
    ratio = jnp.where(step < 1e-30, 1.0, sig_dt / jnp.maximum(step, 1e-30))
    d_raw = used_h * ratio - jnp.exp(a_log) * sig_dt * d_rate
    lanes = dbc_ref.shape[2] - 2 * n
    mine = lax.broadcasted_iota(jnp.int32, (heads, lanes), 0) + lax.axis_index("tensor") * heads
    own = (lax.broadcasted_iota(jnp.int32, (heads, lanes), 1) == mine).astype(BF16)
    dbc_ref[0, :, 2 * n :] = dot_tn(d_raw.astype(BF16), own).astype(BF16)
    gh_ref[:, 0:1] += jnp.sum(d_raw, axis=1, keepdims=True)
    gh_ref[:, 1:2] += jnp.sum(d_rate * rate, axis=1, keepdims=True)


def row_marks(segments):
    seqs, length = segments.shape
    blocks = length // BLOCK
    lags = []
    for lag in (1, 2, 3):
        earlier = jnp.pad(segments, ((0, 0), (lag, 0)), constant_values=-1)[:, :length]
        lags.append(earlier == segments)
    grouped = segments.reshape(seqs, blocks, BLOCK)
    before = jnp.pad(segments, ((0, 0), (1, 0)), constant_values=-1)[:, :length].reshape(seqs, blocks, BLOCK)
    reads = (grouped == before[:, :, :1]).reshape(seqs, length)
    last = (grouped == grouped[:, :, -1:]).reshape(seqs, length)
    rows = [m.astype(F32) for m in (*lags, reads, last, segments)]
    return jnp.stack(rows + [jnp.zeros_like(rows[0])] * 2, axis=1)


def spread_matrix(heads, channels):
    width = channels // heads
    return (np.arange(heads)[:, None] == np.arange(channels)[None, :] // width).astype(np.float32)


def pick_matrix(heads, channels):
    spread = spread_matrix(heads, channels)
    out = np.zeros((128, 2 * channels), np.float32)
    for part in range(4):
        at = slice(part // 2 * channels, (part // 2 + 1) * channels)
        out[part * heads : (part + 1) * heads, at] = spread
    return out


def shared_specs(channels, n2, heads):
    full = lambda *shape: pl.BlockSpec(shape, lambda *i: (0,) * len(shape))
    return [
        full(5, channels),
        full(5, n2),
        full(1, heads),
        full(1, heads),
        full(1, heads),
        full(heads, channels),
        full(128, 2 * channels),
    ]


def forward_scratch(channels, n2):
    return [
        pltpu.VMEM((BLOCK + 8, channels), F32),
        pltpu.VMEM((BLOCK + 8, n2), F32),
        pltpu.VMEM((n2 // 2, channels), F32),
        pltpu.VMEM((BLOCK, BLOCK), F32),
    ]


def forward_kernel(x_ref, bc_ref, dt_ref, *refs):
    y_ref = refs[8]
    forward_block(pl.program_id(1), x_ref[0], bc_ref[0], dt_ref[0], *refs[:8], y_ref.at[0], *refs[9:])


def ssd_forward(x, bc, dt, marks, shared):
    seqs, length, channels = x.shape
    n2, heads = bc.shape[2], dt.shape[1]
    blocks = length // BLOCK
    tok = lambda w: pl.BlockSpec((1, BLOCK, w), lambda s, c: (s, c, 0))
    head = lambda w: pl.BlockSpec((1, w, BLOCK), lambda s, c: (s, 0, c))
    return pl.pallas_call(
        forward_kernel,
        grid=(seqs, blocks),
        in_specs=[tok(channels), tok(n2), head(heads), head(8)] + shared_specs(channels, n2, heads),
        out_specs=[
            tok(channels),
            tok(channels),
            tok(n2),
            pl.BlockSpec((1, 1, n2 // 2, channels), lambda s, c: (s, c, 0, 0)),
        ],
        out_shape=[
            jax.ShapeDtypeStruct((seqs, length, channels), F32),
            jax.ShapeDtypeStruct((seqs, length, channels), F32),
            jax.ShapeDtypeStruct((seqs, length, n2), F32),
            jax.ShapeDtypeStruct((seqs, blocks, n2 // 2, channels), BF16),
        ],
        scratch_shapes=forward_scratch(channels, n2),
        compiler_params=pltpu.CompilerParams(vmem_limit_bytes=48 * 2**20),
        name="ssd_forward",
    )(x, bc, dt, marks, *shared)


def backward_kernel(*refs):
    backward_block(pl.program_id(0), pl.program_id(1), *refs)


def backward_scratch(channels, n2, heads):
    return [
        pltpu.VMEM((3, BLOCK + 8, channels), F32),
        pltpu.VMEM((3, BLOCK + 8, n2), F32),
        pltpu.VMEM((n2 // 2, channels), F32),
        pltpu.VMEM((BLOCK, BLOCK), F32),
        pltpu.VMEM((BLOCK, BLOCK), F32),
        pltpu.VMEM((BLOCK, channels), F32),
        pltpu.VMEM((heads, BLOCK), F32),
    ]


def backward_specs(channels, n2, heads, small, place):
    tok = lambda w: pl.BlockSpec((1, BLOCK, w), lambda *i: (*place(*i), 0))
    full = lambda *shape: pl.BlockSpec(shape, lambda *i: (0,) * len(shape))
    ins = [tok(channels)] * 3 + [tok(n2)] * 2 + [
        pl.BlockSpec((1, heads, BLOCK), lambda *i: (place(*i)[0], 0, place(*i)[1])),
        pl.BlockSpec((1, 8, BLOCK), lambda *i: (place(*i)[0], 0, place(*i)[1])),
        pl.BlockSpec((1, 1, n2 // 2, channels), lambda *i: (*place(*i), 0, 0)),
    ]
    ins += shared_specs(channels, n2, heads)
    return ins, [tok(channels), tok(small), full(8, channels), full(8, n2), full(heads, 128)]


def backward_outs(seqs, length, channels, n2, heads, small):
    return [
        jax.ShapeDtypeStruct((seqs, length, channels), BF16),
        jax.ShapeDtypeStruct((seqs, length, small), BF16),
        jax.ShapeDtypeStruct((8, channels), F32),
        jax.ShapeDtypeStruct((8, n2), F32),
        jax.ShapeDtypeStruct((heads, 128), F32),
    ]


def ssd_backward(small, dy, x, cx, bc, cbc, dt, marks, states, shared):
    seqs, length, channels = x.shape
    n2, heads = bc.shape[2], dt.shape[1]
    blocks = length // BLOCK
    ins, outs = backward_specs(channels, n2, heads, small, lambda s, c: (s, blocks - 1 - c))
    return pl.pallas_call(
        backward_kernel,
        grid=(seqs, blocks),
        in_specs=ins,
        out_specs=outs,
        out_shape=backward_outs(seqs, length, channels, n2, heads, small),
        scratch_shapes=backward_scratch(channels, n2, heads),
        compiler_params=pltpu.CompilerParams(vmem_limit_bytes=56 * 2**20),
        name="ssd_backward",
    )(dy, x, cx, bc, cbc, dt, marks, states, *shared)


def ring_place(n):
    dp = lax.axis_index("dp")
    z, y = dp // 2, dp % 2

    def at(place):
        q = (place + 4 * n) % n
        return 2 * q + (q // (n // 2)) * (2 * n - 1 - 4 * q)

    return z + y * (n - 1 - 2 * z), at


def tensor_place():
    t = lax.axis_index("tensor")
    return t, t + 1 - 2 * (t % 2), (t + 2) % 4


def greet(n, more=()):
    place, at = ring_place(n)
    _, other, across = tensor_place()
    sem = pltpu.get_barrier_semaphore()
    targets = [{"dp": at(place + 1)}, {"dp": at(place - 1)}, {"tensor": other}, {"tensor": across}, *more]
    for target in targets:
        pl.semaphore_signal(sem, inc=1, device_id=target, device_id_type=MESH)
    pl.semaphore_wait(sem, len(targets))


def remote(src, dst, send_sem, recv_sem, target):
    return pltpu.make_async_remote_copy(
        src_ref=src, dst_ref=dst, send_sem=send_sem, recv_sem=recv_sem, device_id=target, device_id_type=MESH
    )


def span(first, count, unit):
    return pl.ds(pl.multiple_of(first, unit), count)


class RingGather:
    def __init__(self, n, parts, keep, sems):
        self.n, self.parts, self.keep = n, parts, keep
        self.send_sem, self.recv_sem = sems
        self.place, self.at = ring_place(n)

    def copy(self, way, part, step):
        sign = 1 - 2 * way
        ref = self.keep(way, part, self.at(self.place - sign * step))
        return remote(
            ref,
            ref,
            self.send_sem.at[way, part, step],
            self.recv_sem.at[way, part, step],
            {"dp": self.at(self.place + sign)},
        )

    def step(self, k):
        for part in range(self.parts):
            for way in (0, 1):
                if k > 0:
                    self.copy(way, part, k - 1).wait_recv()
                if k < self.n - 1:
                    self.copy(way, part, k).start()

    def later(self, k):
        for part in range(self.parts):
            for way in (0, 1):
                self.copy(way, part, k - 1).wait_recv()

                @pl.when(k < self.n - 1)
                def _():
                    self.copy(way, part, k).start()

    def finish(self):
        for k in range(self.n - 1):
            for part in range(self.parts):
                for way in (0, 1):
                    self.copy(way, part, k).wait_send()


class RowGather:
    def __init__(self, keep, sems):
        self.keep = keep
        self.send_sem, self.recv_sem = sems
        self.me, self.other, self.across = tensor_place()

    def copy(self, kind, part):
        ref = self.keep(part, self.across if kind == 2 else self.me)
        target = self.across if kind == 0 else self.other
        return remote(
            ref, ref, self.send_sem.at[kind, part], self.recv_sem.at[kind, part], {"tensor": target}
        )

    def start(self, part):
        self.copy(0, part).start()
        self.copy(1, part).start()

    def forward(self, part):
        self.copy(0, part).wait_recv()
        self.copy(2, part).start()

    def wait(self, part):
        self.copy(1, part).wait_recv()
        self.copy(2, part).wait_recv()

    def finish(self, parts):
        for part in range(parts):
            for kind in range(3):
                self.copy(kind, part).wait_send()


def all_kernel(n, *refs):
    (hidden_ref, g_ref, wzx_ref, wbc_ref, wout_ref, gain_ref, gate_ref, marks_ref), refs = refs[:8], refs[8:]
    shared, refs = refs[:7], refs[7:]
    (u_out, gf_out, wx_out, wz_out, wb_out, wo_out), refs = refs[:6], refs[6:]
    (cx_ref, x_ref, cbc_ref, bc_ref, dt_ref, states_ref), refs = refs[:6], refs[6:]
    (normed_ref, dz_ref, dy_ref, grad_ref, scale_ref), refs = refs[:5], refs[5:]
    scratch, refs = refs[:4], refs[4:]
    (u, wx, wz, wo, wb, wb_own, wdt, g_cols, y, z, dn, sums), refs = refs[:12], refs[12:]
    (load_sem, keep_sem, stream_sem), sems = refs[:3], refs[3:]

    i = pl.program_id(0)
    rows, width = wzx_ref.shape[1:]
    out_rows, out_cols = wout_ref.shape
    seqs, piece, model = hidden_ref.shape
    length = 4 * piece
    blocks = length // BLOCK
    heads = dt_ref.shape[1]
    n2 = bc_ref.shape[2]
    small_cols = wb.shape[1]
    dp = lax.axis_index("dp")
    place, at = ring_place(n)
    me, other, across = tensor_place()
    core = me % 2
    facing = (other + 2) % 4

    def keep_wide(ref):
        def keep(way, part, d):
            return ref.at[span(d * rows, rows, 16), pl.ds(way * width // 2 + part * width // 4, width // 4)]

        return keep

    def keep_out(way, part, d):
        first = way * out_rows // 2 + part * out_rows // 4
        return wo.at[pl.ds(first, out_rows // 4), span(d * out_cols, out_cols, 128)]

    def keep_small(way, part, d):
        return wb.at[span(d * rows + core * rows // 2 + way * rows // 4, rows // 4, 16), :]

    def keep_rows(part, t):
        if part < seqs:
            return u.at[span(part * length + t * piece, piece, 16), :]
        return gf_out.at[part - seqs, span(t * piece, piece, 16), :]

    x_ring = RingGather(n, 2, keep_wide(wx), sems[0:2])
    small = RingGather(n, 1, keep_small, sems[2:4])
    z_ring = RingGather(n, 2, keep_wide(wz), sems[4:6])
    out_ring = RingGather(n, 2, keep_out, sems[6:8])
    token_rows = RowGather(keep_rows, sems[8:10])
    halves_send, halves_recv, sums_send, sums_recv = sems[10:14]

    def half(ahead, whose):
        d = (dp + ahead) % n
        ref = wb.at[span(d * rows + whose * rows // 2, rows // 2, 16), :]
        return remote(ref, ref, halves_send.at[ahead], halves_recv.at[ahead], {"tensor": other})

    def sums_copy(kind):
        ref = sums.at[me]
        target = {"tensor": (other, across, facing)[kind]}
        return remote(ref, ref, sums_send.at[kind], sums_recv.at[kind], target)

    keeps = [
        pltpu.make_async_copy(src, dst, keep_sem.at[j])
        for j, (src, dst) in enumerate(((wx, wx_out), (wb, wb_out), (wz, wz_out), (u, u_out), (wo, wo_out)))
    ]

    def streams(k):
        return [
            pltpu.make_async_copy(
                gf_out.at[:, :, span(at(place - (1 - 2 * way) * k) * out_cols, out_cols, 128)],
                g_cols.at[way],
                stream_sem.at[way],
            )
            for way in (0, 1)
        ]

    def start(copies):
        for copy in copies:
            copy.start()

    def wait(copies):
        for copy in copies:
            copy.wait()

    @pl.when(i == 0)
    def _():
        def held(s, h):
            return z.at[pl.ds((2 * s + h) * piece, piece), :]

        halves = [(s, h) for s in range(seqs) for h in (0, 1)]
        cut = lambda h: pl.ds(h * (model // 2), model // 2)
        own = [
            (wzx_ref.at[1], wx.at[span(dp * rows, rows, 16), :]),
            (wbc_ref, wb_own),
            (wzx_ref.at[0], wz.at[span(dp * rows, rows, 16), :]),
            (wout_ref, wo.at[:, span(dp * out_cols, out_cols, 128)]),
        ]
        own += [(hidden_ref.at[s, :, cut(h)], held(seqs + s, h)) for s, h in halves]
        own += [(g_ref.at[s, :, cut(h)], held(s, h)) for s, h in halves]
        loads = [pltpu.make_async_copy(a, b, load_sem.at[j]) for j, (a, b) in enumerate(own)]
        first = 4 + 2 * seqs
        stores = [
            pltpu.make_async_copy(
                held(s, h), gf_out.at[s, span(me * piece, piece, 16), cut(h)], load_sem.at[first + 2 * seqs + j]
            )
            for j, (s, h) in enumerate(halves)
        ]
        start(loads)
        greet(n, [{"tensor": facing}])
        loads[0].wait()
        x_ring.step(0)
        loads[1].wait()
        mine = span(dp * rows, rows, 16)
        short = jnp.zeros((small_cols - wb_own.shape[0], rows), BF16)
        wb[mine, :] = jnp.concatenate([wb_own[...], short], axis=0).T
        small.step(0)
        wait(loads[4:first])
        for s in range(seqs):
            left = z[pl.ds((2 * (seqs + s)) * piece, piece), :].astype(F32)
            right = z[pl.ds((2 * (seqs + s) + 1) * piece, piece), :].astype(F32)
            squares = jnp.sum(left * left + right * right, axis=1, keepdims=True)
            scale = lax.rsqrt(squares / model + EPS)
            scale_ref[s] = jnp.broadcast_to(scale, (piece, 128))
            to = span(s * length + me * piece, piece, 16)
            u[to, cut(0)] = (left * scale * gain_ref[:, cut(0)]).astype(BF16)
            u[to, cut(1)] = (right * scale * gain_ref[:, cut(1)]).astype(BF16)
            token_rows.start(s)
        wait(loads[first:])
        start(stores)
        wait(loads[2:4])
        wait(stores)
        for k in range(1, n):
            x_ring.step(k)
            small.step(k)
            if k == n - 1:
                z_ring.step(0)
            if k == n // 2:
                token_rows.forward(0)
                token_rows.start(seqs)
        for ahead in range(1, n):
            half(ahead, core).start()
        for ahead in range(1, n):
            half(ahead, 1 - core).wait_recv()
        token_rows.wait(0)
        start(keeps[:2])
        lanes = small_cols - n2
        pick = lax.broadcasted_iota(jnp.int32, (heads, lanes), 1) == (
            lax.broadcasted_iota(jnp.int32, (heads, lanes), 0) + me * heads
        )
        wdt[...] = dot_nt(pick.astype(BF16), wb[:, n2:]).astype(BF16)

    b = i - 1

    @pl.when((b >= 0) & (b < n))
    def _():
        @pl.when(b < n - 1)
        def _():
            z_ring.later(b + 1)

        @pl.when(b == n - 2)
        def _():
            out_ring.step(0)

        @pl.when(b == n - 1)
        def _():
            keeps[2].start()
            out_ring.step(1)

        @pl.when(b == 0)
        def _():
            token_rows.forward(1)
            token_rows.start(seqs + 1)

        @pl.when(b == blocks)
        def _():
            token_rows.wait(1)
            keeps[3].start()

        at_block = span(b * BLOCK, BLOCK, BLOCK)
        tokens = u[at_block, :]
        x = dot(tokens, wx[...])
        bc = dot(tokens, wb[:, :n2])
        dt = dot_nt(wdt[...], tokens)
        x_ref[0] = x.astype(BF16)
        bc_ref[0] = bc.astype(BF16)
        dt_ref[0] = dt
        forward_block(
            b % blocks, x, bc, dt, marks_ref, *shared, y.at[at_block, :], cx_ref, cbc_ref, states_ref, *scratch
        )

    slope = wx

    def add_shard(k):
        wait(streams(k))
        for way in (0, 1):
            e = pl.ds(way * (out_rows // 2), out_rows // 2)
            d = at(place - (1 - 2 * way) * k)
            cols = g_cols[way].reshape(seqs * length, out_cols)
            value = dot_nt(cols, wo[e, span(d * out_cols, out_cols, 128)])

            @pl.when(k == 0)
            def _():
                dn[:, e] = value

            @pl.when(k > 0)
            def _():
                dn[:, e] += value

    def gate_block(e, _):
        part = span(e * BLOCK, BLOCK, BLOCK)
        zf = dot(u[part, :], wz[...])
        sig = sigmoid(zf)
        silu = zf * sig
        yf = y[part, :]
        y[part, :] = yf * silu
        z[part, :] = silu.astype(BF16)
        slope[part, :] = (yf * (sig + silu * (1.0 - sig))).astype(BF16)
        return 0

    def shard_step(c, _):
        @pl.when(c == 0)
        def _():
            token_rows.forward(seqs)
            token_rows.forward(seqs + 1)
            token_rows.wait(seqs)
            token_rows.wait(seqs + 1)
            start(streams(0))
            add_shard(0)
            start(streams(1))
            keeps[0].wait()
            x_ring.finish()

        @pl.when((c >= 1) & (c <= 4))
        def _():
            lax.fori_loop(2 * (c - 1), 2 * c, gate_block, 0)

        add_shard(c + 1)
        start(streams(c + 2))
        out_ring.later(c + 2)
        return 0

    @pl.when(i == n + 1)
    def _():
        lax.fori_loop(0, n - 2, shard_step, 0)
        add_shard(n - 1)
        keeps[4].start()

        def block_sums(e, _):
            part = span(e * BLOCK, BLOCK, BLOCK)
            gated = y[part, :]
            squares = jnp.sum(gated * gated, axis=1, keepdims=True)
            inner = jnp.sum(gate_ref[...] * dn[part, :] * gated, axis=1, keepdims=True)
            lane = lax.broadcasted_iota(jnp.int32, (1, 128), 1)
            both = jnp.where(lane == 0, squares, jnp.where(lane == 1, inner, 0.0))
            sums[me, :, part] = both.T[0:8, :]
            return 0

        lax.fori_loop(0, n, block_sums, 0)
        for kind in range(3):
            sums_copy(kind).start()

    e = i - (n + 2)

    @pl.when(e >= 0)
    def _():
        @pl.when(e == 0)
        def _():
            for kind in range(3):
                sums_copy(kind).wait_recv()
            grad_ref[...] = jnp.zeros_like(grad_ref)

        part = span(e * BLOCK, BLOCK, BLOCK)
        whole = (sums[0, :, part] + sums[1, :, part]) + (sums[2, :, part] + sums[3, :, part])
        cols = jnp.concatenate([whole, jnp.zeros((120, BLOCK), F32)], axis=0).T / (4 * width)
        inverse = lax.rsqrt(cols[:, 0:1] + EPS)
        dnf = dn[part, :]
        gain = gate_ref[...]
        gated = y[part, :]
        scaled_gated = gated * inverse
        normed_ref[...] = (scaled_gated * gain).astype(BF16)
        grad_ref[...] += jnp.sum(dnf * scaled_gated, axis=0, keepdims=True)
        d_gated = inverse * (dnf * gain) - gated * (inverse * inverse * inverse * cols[:, 1:2])
        dy_ref[...] = (d_gated * z[part, :].astype(F32)).astype(BF16)
        dz_ref[...] = (d_gated * slope[part, :].astype(F32)).astype(BF16)

        @pl.when(e == n - 1)
        def _():
            wait(keeps[1:])
            for ring in (small, z_ring, out_ring):
                ring.finish()
            token_rows.finish(2 * seqs)
            for ahead in range(1, n):
                half(ahead, core).wait_send()
            for kind in range(3):
                sums_copy(kind).wait_send()


def forward_all(n, hidden, g, w_zx, w_bc, w_out, pre_gain, gate_gain, marks, shared):
    seqs, piece, model = hidden.shape
    rows, width = w_zx.shape[1:]
    out_rows, out_cols = w_out.shape
    length = 4 * piece
    tokens = seqs * length
    blocks = length // BLOCK
    n2 = shared[1].shape[1]
    heads = shared[2].shape[1]
    columns = w_bc.shape[0]
    small = columns + -columns % 128
    sem = pltpu.SemaphoreType.DMA
    ring = [sem((2, 2, n - 1))] * 2
    anywhere = pl.BlockSpec(memory_space=pl.ANY)
    whole = lambda *shape: pl.BlockSpec(shape, lambda i: (0,) * len(shape))
    b = lambda i: jnp.minimum(jnp.maximum(i - 1, 0), n - 1)
    e = lambda i: jnp.maximum(i - (n + 2), 0)
    tok = lambda w: pl.BlockSpec((1, BLOCK, w), lambda i: (b(i) // blocks, b(i) % blocks, 0))
    gate = pl.BlockSpec((BLOCK, width), lambda i: (e(i), 0))
    out_shape = [
        ((tokens, model), BF16),
        ((seqs, length, model), BF16),
        ((rows * n, width), BF16),
        ((rows * n, width), BF16),
        ((rows * n, small), BF16),
        ((out_rows, out_cols * n), BF16),
        ((seqs, length, width), F32),
        ((seqs, length, width), BF16),
        ((seqs, length, n2), F32),
        ((seqs, length, n2), BF16),
        ((seqs, heads, length), F32),
        ((seqs, blocks, n2 // 2, width), BF16),
        ((tokens, width), BF16),
        ((tokens, width), BF16),
        ((tokens, width), BF16),
        ((1, width), F32),
        ((seqs, piece, 128), F32),
    ]
    return pl.pallas_call(
        functools.partial(all_kernel, n),
        grid=(2 * n + 2,),
        in_specs=[anywhere] * 5
        + [
            whole(1, model),
            whole(1, width),
            pl.BlockSpec((1, 8, BLOCK), lambda i: (b(i) // blocks, 0, b(i) % blocks)),
        ]
        + shared_specs(width, n2, heads),
        out_specs=[anywhere] * 6
        + [tok(width), tok(width), tok(n2), tok(n2)]
        + [pl.BlockSpec((1, heads, BLOCK), lambda i: (b(i) // blocks, 0, b(i) % blocks))]
        + [pl.BlockSpec((1, 1, n2 // 2, width), lambda i: (b(i) // blocks, b(i) % blocks, 0, 0))]
        + [gate] * 3
        + [whole(1, width), whole(seqs, piece, 128)],
        out_shape=[jax.ShapeDtypeStruct(*s) for s in out_shape],
        scratch_shapes=forward_scratch(width, n2)
        + [
            pltpu.VMEM((tokens, model), BF16),
            pltpu.VMEM((rows * n, width), BF16),
            pltpu.VMEM((rows * n, width), BF16),
            pltpu.VMEM((out_rows, out_cols * n), BF16),
            pltpu.VMEM((rows * n, small), BF16),
            pltpu.VMEM(w_bc.shape, BF16),
            pltpu.VMEM((heads, rows * n), BF16),
            pltpu.VMEM((2, seqs, length, out_cols), BF16),
            pltpu.VMEM((tokens, width), F32),
            pltpu.VMEM((tokens, width), BF16),
            pltpu.VMEM((tokens, width), F32),
            pltpu.VMEM((4, 8, tokens), F32),
            sem((4 + 6 * seqs,)),
            sem((5,)),
            sem((2,)),
        ]
        + ring + [sem((2, 1, n - 1))] * 2 + ring + ring
        + [sem((3, 2 * seqs))] * 2 + [sem((n,))] * 2 + [sem((3,))] * 2,
        compiler_params=pltpu.CompilerParams(
            collective_id=0, has_side_effects=True, vmem_limit_bytes=63 * 2**20
        ),
        name="forward_all",
    )(hidden, g, w_zx, w_bc, w_out, pre_gain, gate_gain, marks, *shared)


class RingScatter:
    def __init__(self, n, terms, slots, sems, ways=2, sign=1):
        self.n, self.terms, self.slots, self.ways, self.sign = n, terms, slots, ways, sign
        self.send_sem, self.recv_sem = sems
        self.place, self.at = ring_place(n)

    def turn(self, way):
        return self.sign * (1 - 2 * way)

    def owner(self, way, k):
        return self.at(self.place - self.turn(way) * (1 + k))

    def copy(self, way, k):
        return remote(
            self.slots.at[way, k],
            self.slots.at[way, k + 1],
            self.send_sem.at[way, k],
            self.recv_sem.at[way, k],
            {"dp": self.at(self.place + self.turn(way))},
        )

    def step(self, way, k):
        @pl.when(k == 0)
        def _():
            self.slots[way, 0] = self.terms[way].astype(BF16)

        @pl.when(k > 0)
        def _():
            self.copy(way, k - 1).wait_recv()

            @pl.when(k < self.n - 1)
            def _():
                self.slots[way, k] = (self.terms[way].astype(F32) + self.slots[way, k].astype(F32)).astype(BF16)

        @pl.when(k < self.n - 1)
        def _():
            self.copy(way, k).start()

    def last(self, way):
        return self.terms[way].astype(F32) + self.slots[way, self.n - 1].astype(F32)

    def finish(self):
        for k in range(self.n - 1):
            for way in range(self.ways):
                self.copy(way, k).wait_send()


class RowScatter:
    def __init__(self, parts, value, hold, sems):
        self.parts, self.value, self.hold = parts, value, hold
        self.send_sem, self.recv_sem = sems
        self.me, self.other, self.across = tensor_place()

    def copy(self, kind, part):
        src, dst = ((0, 1), (1, 2), (0, 3))[kind]
        return remote(
            self.hold.at[src, part],
            self.hold.at[dst, part],
            self.send_sem.at[kind, part],
            self.recv_sem.at[kind, part],
            {"tensor": self.across if kind == 1 else self.other},
        )

    def stage(self, j):
        late = j // (2 * self.parts)
        near = j - 2 * self.parts
        stage = (1 - late) * (j % 2) + late * (2 + near // self.parts)
        return stage, (1 - late) * (j // 2) + late * (near % self.parts)

    def owner(self, j):
        stage, part = self.stage(j)
        x, core = self.me // 2, self.me % 2
        return 2 * ((x + 1 - stage // 2) % 2) + (core + 1 - stage % 2) % 2, part

    def step(self, j, store, wait=True):
        stage, part = self.stage(j)

        @pl.when(stage == 0)
        def _():
            self.hold[0, part] = self.value[...].astype(BF16)
            self.copy(0, part).start()

        @pl.when(stage == 1)
        def _():
            self.copy(0, part).wait_recv()
            self.hold[1, part] = (self.value[...].astype(F32) + self.hold[1, part].astype(F32)).astype(BF16)
            self.copy(1, part).start()

        @pl.when(stage == 2)
        def _():
            self.copy(0, part).wait_send()
            self.hold[0, part] = self.value[...].astype(BF16)
            self.copy(2, part).start()

        @pl.when(stage == 3)
        def _():
            value = self.value[...].astype(F32)
            store(part, value + self.arrived(part) if wait else value)

    def arrived(self, part):
        self.copy(2, part).wait_recv()
        self.copy(1, part).wait_recv()
        return self.hold[3, part].astype(F32) + self.hold[2, part].astype(F32)

    def finish(self):
        for part in range(self.parts):
            for kind in (1, 2):
                self.copy(kind, part).wait_send()


def back_kernel(n, *refs):
    (normed_ref, g_ref, u_ref, dz_ref, wo_ref), refs = refs[:5], refs[5:]
    ins, refs = refs[:15], refs[15:]
    (out_ref, gout_ref, gz_ref), refs = refs[:3], refs[3:]
    outs, refs = refs[:5], refs[5:]
    scratch, refs = refs[:7], refs[7:]
    normed, dz, wo, g_cols, u_cols, out_slots, z_slots, hold, terms, mixed, load_sem, stream_sem, out_sem = refs[:13]
    sems = refs[13:]

    k = pl.program_id(0)
    blocks = 4
    piece = out_ref.shape[1]
    length = blocks * BLOCK
    count = g_ref.shape[1] // n
    half = gz_ref.shape[1] // 2
    place, at = ring_place(n)

    loads = [
        pltpu.make_async_copy(src, dst, load_sem.at[i])
        for i, (src, dst) in enumerate(((normed_ref, normed), (dz_ref, dz), (wo_ref, wo)))
    ]

    def streams(k):
        copies = []
        for way in (0, 1):
            d = at(place - (1 - 2 * way) * (1 + k))
            for i, (src, dst) in enumerate(((g_ref, g_cols), (u_ref, u_cols))):
                copies.append(
                    pltpu.make_async_copy(
                        src.at[:, span(d * count, count, 128)], dst.at[way], stream_sem.at[i, way]
                    )
                )
        return copies

    @pl.when(k == 0)
    def _():
        for copy in streams(0) + loads:
            copy.start()
        greet(n)

    backward_block(k // blocks, k % blocks, *ins, *outs, *scratch)

    @pl.when(k == 0)
    def _():
        for copy in loads:
            copy.wait()

    for copy in streams(k):
        copy.wait()

    rows = RowScatter(2, mixed, hold, sems[4:6])
    owner = rows.owner(k)
    own_rows = span(owner[1] * length + owner[0] * piece, piece, 16)

    for ring, (from_cols, to_cols) in enumerate(((g_cols, normed), (u_cols, dz))):
        for way in (0, 1):
            value = dot_tn(from_cols[way], to_cols[:, pl.ds(way * half, half)])
            terms[ring, way] = value.astype(BF16)
    mixed[...] = dot(normed[own_rows, :], wo[...]).astype(BF16)

    out_ring = RingScatter(n, terms.at[0], out_slots, sems[0:2])
    z_ring = RingScatter(n, terms.at[1], z_slots, sems[2:4])
    for way in (0, 1):
        out_ring.step(way, k)
        z_ring.step(way, k)

    @pl.when(k < n - 1)
    def _():
        for copy in streams(k + 1):
            copy.start()

    def out_copy(part):
        return pltpu.make_async_copy(hold.at[2, part], out_ref.at[part], out_sem.at[part])

    def store(part, value):
        hold[2, part] = value.astype(BF16)
        out_copy(part).start()

    rows.step(k, store)

    @pl.when(k == n - 1)
    def _():
        for way in (0, 1):
            at = pl.ds(way * half, half)
            gout_ref[at, :] = out_ring.last(way).T
            gz_ref[:, at] = z_ring.last(way)

    @pl.when(k == n - 1)
    def _():
        rows.finish()
        out_ring.finish()
        z_ring.finish()
        for part in range(2):
            out_copy(part).wait()


def backward_all(n, small, piece, normed, g, u, dz, w_out, dy, x, cx, bc, cbc, dt, marks, states, shared):
    seqs, length, channels = x.shape
    n2, heads = bc.shape[2], dt.shape[1]
    tokens, model = g.shape
    count = model // n
    blocks = length // BLOCK
    sem = pltpu.SemaphoreType.DMA
    anywhere = pl.BlockSpec(memory_space=pl.ANY)
    ins, outs = backward_specs(channels, n2, heads, small, lambda k: (k // blocks, blocks - 1 - k % blocks))
    whole = lambda *shape: pl.BlockSpec(shape, lambda k: (0,) * len(shape))
    return pl.pallas_call(
        functools.partial(back_kernel, n),
        grid=(n,),
        in_specs=[anywhere] * 5 + ins,
        out_specs=[anywhere, whole(channels, count), whole(count, channels)] + outs,
        out_shape=[
            jax.ShapeDtypeStruct((seqs, piece, model), BF16),
            jax.ShapeDtypeStruct((channels, count), F32),
            jax.ShapeDtypeStruct((count, channels), F32),
        ]
        + backward_outs(seqs, length, channels, n2, heads, small),
        scratch_shapes=backward_scratch(channels, n2, heads)
        + [
            pltpu.VMEM((tokens, channels), BF16),
            pltpu.VMEM((tokens, channels), BF16),
            pltpu.VMEM((channels, model), BF16),
            pltpu.VMEM((2, tokens, count), BF16),
            pltpu.VMEM((2, tokens, count), BF16),
            pltpu.VMEM((2, n, count, channels // 2), BF16),
            pltpu.VMEM((2, n, count, channels // 2), BF16),
            pltpu.VMEM((4, seqs, piece, model), BF16),
            pltpu.VMEM((2, 2, count, channels // 2), BF16),
            pltpu.VMEM((piece, model), BF16),
            sem((3,)),
            sem((2, 2)),
            sem((seqs,)),
        ]
        + [sem((2, n - 1))] * 4
        + [sem((3, seqs))] * 2,
        compiler_params=pltpu.CompilerParams(
            collective_id=1, has_side_effects=True, vmem_limit_bytes=127 * 2**19
        ),
        name="backward_all",
    )(normed, g, u, dz, w_out, dy, x, cx, bc, cbc, dt, marks, states, *shared)


class Fold:
    def __init__(self, n, total, came, sems):
        self.total, self.came = total, came
        self.send_sem, self.recv_sem = sems
        dp = lax.axis_index("dp")
        _, other, across = tensor_place()
        partners, ahead = [], 1
        while ahead < n:
            partners.append({"dp": dp + ahead * (1 - 2 * ((dp // ahead) % 2))})
            ahead *= 2
        self.over_dp = partners
        self.partners = partners + [{"tensor": other}, {"tensor": across}]

    def copy(self, r):
        return remote(
            self.total.at[r], self.came.at[r], self.send_sem.at[r], self.recv_sem.at[r], self.partners[r]
        )

    def start(self, r):
        self.copy(r).start()

    def take(self, r):
        self.copy(r).wait_recv()
        self.total[r + 1] = self.total[r] + self.came[r]

    def finish(self):
        for r in range(len(self.partners)):
            self.copy(r).wait_send()


def in_kernel(
    n, u_hbm, dz_hbm, dx_hbm, wz_hbm, wx_hbm, wb_hbm, dbc_hbm, gz_hbm, gx_in, gbc_in, gh_in, gate_in, gain_ref,
    din_ref, gx_ref, gb_ref, sums_ref, dots_ref, pre_ref,
    u_ref, dz_ref, dx_ref, wz_ref, wx_ref, wb_ref, dbc_ref,
    x_slots, b_slots, hold, bc_hold, x_terms, b_terms, in_value, bc_value, low, swap, own_in, pre, pre_dp, pre_tensor, total, came, load_sem, u_sem, *sems,
):
    seqs, piece = din_ref.shape[:2]
    tokens, model = u_ref.shape
    length = tokens // seqs
    count = model // n
    half = gx_ref.shape[2] // 2
    me, other, across = tensor_place()
    core = me % 2

    moves = (
        (dbc_hbm, dbc_ref),
        (dx_hbm, dx_ref),
        (dz_hbm, dz_ref),
        (wz_hbm, wz_ref),
        (wx_hbm, wx_ref),
        (wb_hbm, wb_ref),
        (gz_hbm, gx_ref.at[0]),
    )
    loads = [pltpu.make_async_copy(src, dst, load_sem.at[i]) for i, (src, dst) in enumerate(moves)]
    place, at_place = ring_place(n)
    u_copies = []
    for ahead in (-1, 1, -2, 2, -3, 3, 4, 0):
        cols = span(at_place(place + ahead) * count, count, 128)
        u_copies.append(pltpu.make_async_copy(u_hbm.at[:, cols], u_ref.at[:, cols], u_sem.at[ahead + 3]))
    for load in loads[:2] + u_copies[:2] + loads[2:] + u_copies[2:]:
        load.start()

    bc_rows = RowScatter(seqs, bc_value, bc_hold, sems[0:2])
    in_rows = RowScatter(seqs, in_value, hold, sems[2:4])
    x_ring = RingScatter(n, x_terms, x_slots, sems[4:6])
    b_ring = RingScatter(n, b_terms, b_slots, sems[6:8], 1, 1 - 2 * core)
    pair_send, pair_recv, swap_send, swap_recv = sems[8:12]
    dp_send, dp_recv, tensor_send, tensor_recv = sems[14:18]
    fold = Fold(n, total, came, sems[12:14])
    rounds = len(fold.partners)
    pair = remote(low.at[0], low.at[1], pair_send, pair_recv, {"tensor": other})

    total[0] = jnp.zeros_like(total[0])
    total[0, 0:6, :] = gx_in[0:6, :]
    total[0, 6:7, :] = gate_in[...]
    steps = gh_in[...].T
    total[0, 7:8, 0 : steps.shape[1]] = steps[0:1, :]
    total[0, 7:8, 128 : 128 + steps.shape[1]] = steps[1:2, :]
    total[0, 8:13, 0 : gbc_in.shape[1]] = gbc_in[0:5, :]
    pre[...] = jnp.zeros_like(pre)
    dp_now = lax.axis_index("dp")
    greet(
        n,
        fold.over_dp
        + [{"dp": (dp_now + o) % n} for o in range(1, n)]
        + [{"tensor": (me + o) % 4} for o in range(1, 4)],
    )
    def rows_at(t, part):
        return span(part * length + t * piece, piece, 16)

    def bc_store(part, value):
        low[0, part] = value.astype(BF16)

    def bc_step(j):
        t, part = bc_rows.owner(j)
        bc_value[...] = dbc_ref[rows_at(t, part), :].astype(F32)
        bc_rows.step(j, bc_store)

    def add_pre(at):
        pre[...] += jnp.sum(in_value[...] * u_ref[at, :].astype(F32), axis=0, keepdims=True)

    def store(part, value):
        in_value[...] = value + dot_nt(low[0, part], wb_ref[...])
        own_in[part] = in_value[...]
        add_pre(rows_at(me, part))

    def row_term(j):
        at = rows_at(*in_rows.owner(j))
        in_value[...] = dot_nt(dz_ref[at, :], wz_ref[...]) + dot_nt(dx_ref[at, :], wx_ref[...])

    def row_step(j):
        in_rows.step(j, store, wait=False)

        @pl.when(j < 3 * seqs)
        def _():
            add_pre(rows_at(*in_rows.owner(j)))

    def x_term(k):
        for way in (0, 1):
            cols = span(x_ring.owner(way, k) * count, count, 128)
            x_terms[way] = dot_tn(u_ref[:, cols], dx_ref[:, pl.ds(way * half, half)])

    def x_step(k):
        for way in (0, 1):
            x_ring.step(way, k)

    def b_step(k):
        cols = span(b_ring.owner(0, k) * count + core * count // 2, count // 2, 128)
        value = 0.0
        for t, which in ((me, 0), (other, 1)):
            for part in range(seqs):
                value = value + dot_tn(u_ref[rows_at(t, part), cols], low[which, part])
        b_terms[0] = value
        b_ring.step(0, k)

    loads[0].wait()
    for part in range(seqs):
        bc_step(2 * part)
        bc_step(2 * seqs + part)
    loads[1].wait()
    for copy in u_copies[:2]:
        copy.wait()
    x_term(0)
    x_step(0)
    for load in loads[2:] + u_copies[2:]:
        load.wait()
    row_term(0)
    row_step(0)
    for part in range(seqs):
        bc_step(2 * part + 1)

    wide = model // 8
    gain = gain_ref[...]

    def dp_copy(o):
        ref = pre_dp.at[dp_now]
        return remote(ref, ref, dp_send.at[o], dp_recv.at[o], {"dp": (dp_now + o) % n})

    def tensor_copy(o):
        ref = pre_tensor.at[me]
        return remote(ref, ref, tensor_send.at[o], tensor_recv.at[o], {"tensor": (me + o) % 4})

    cross = remote(swap.at[0], swap.at[1], swap_send.at[0], swap_recv.at[0], {"tensor": across})
    back = remote(swap.at[2], swap.at[3], swap_send.at[1], swap_recv.at[1], {"tensor": other})

    def at_step(k, when, what):
        pl.when(k == when)(what)

    def own_bc():
        for part in range(seqs):
            bc_step(3 * seqs + part)
        pair.start()

    def send_pre():
        for i in range(8):
            at = slice(i * wide, (i + 1) * wide)
            pre_dp[dp_now, i : i + 1, :] = pre[:, at] / gain[:, at]
        for o in range(1, n):
            dp_copy(o).start()

    def pass_pre():
        for o in range(1, n):
            dp_copy(o).wait_recv()
        pre_tensor[me] = sum(pre_dp[d] for d in range(n))
        for o in range(1, 4):
            tensor_copy(o).start()

    def take_pre():
        for o in range(1, 4):
            tensor_copy(o).wait_recv()
        pre_ref[...] = (pre_tensor[0] + pre_tensor[1]) + (pre_tensor[2] + pre_tensor[3])

    def send_bc():
        swap[0] = b_ring.last(0)
        cross.start()

    def pass_bc():
        cross.wait_recv()
        swap[2] = swap[0] + swap[1]
        back.start()
        gb_ref[span(core * count // 2, count // 2, 16), :] = swap[2]

    def step(k, _):
        at_step(k, 5, send_pre)
        at_step(k, n - 1, send_bc)

        @pl.when(2 * k - 1 < 4 * seqs)
        def _():
            row_term(2 * k - 1)
            row_step(2 * k - 1)

        x_term(k)
        x_step(k)
        at_step(k, 2, pair.wait_recv)

        @pl.when((k >= 2) & (k <= 6))
        def _():
            b_step(jnp.maximum(k - 2, 2 * (k - 3)))

        @pl.when(2 * k < 4 * seqs)
        def _():
            row_term(2 * k)
            row_step(2 * k)

        at_step(k, 1, own_bc)

        @pl.when((k >= 4) & (k <= 6))
        def _():
            b_step(2 * (k - 3) + 1)

        at_step(k, 6, pass_pre)
        at_step(k, n - 1, pass_bc)
        at_step(k, n - 1, take_pre)
        for r in range(rounds + 1):

            @pl.when(k == r + 1)
            def _():
                if r > 0:
                    fold.take(r - 1)
                if r < rounds:
                    fold.start(r)

        return 0

    lax.fori_loop(1, n, step, 0)
    for way in (0, 1):
        gx_ref[1, :, pl.ds(way * half, half)] = x_ring.last(way)
    sums_ref[0:8, :] = total[rounds - 2, 0:8, :]
    sums_ref[8:16, :] = total[rounds, 8:16, :]
    for part in range(seqs):
        value = own_in[part] + in_rows.arrived(part)
        din_ref[part] = value.astype(BF16)
        inner = jnp.sum(value * u_ref[rows_at(me, part), :].astype(F32), axis=1, keepdims=True)
        dots_ref[part] = jnp.broadcast_to(inner, (piece, 128))
    back.wait_recv()
    gb_ref[span((1 - core) * count // 2, count // 2, 16), :] = swap[3]
    for o in range(1, n):
        dp_copy(o).wait_send()
    for o in range(1, 4):
        tensor_copy(o).wait_send()
    for copy in (pair, cross, back):
        copy.wait_send()
    for part in (bc_rows, in_rows, x_ring, b_ring, fold):
        part.finish()


def scatter_in(n, piece, u, dz, dx, w_z, w_x, w_bc, dbc, grad_z, gx, gbc, gh, grad_gate, gain):
    tokens, model = u.shape
    width = dz.shape[1]
    small = dbc.shape[1]
    seqs = tokens // (4 * piece)
    count = model // n
    rounds = 5
    sem = pltpu.SemaphoreType.DMA
    vmem = pl.BlockSpec(memory_space=pltpu.VMEM)
    anywhere = pl.BlockSpec(memory_space=pl.ANY)
    big = (u, dz, dx, w_z, w_x, w_bc, dbc)
    return pl.pallas_call(
        functools.partial(in_kernel, n),
        in_specs=[anywhere] * 8 + [vmem] * 5,
        out_specs=[vmem] * 6,
        out_shape=[
            jax.ShapeDtypeStruct((seqs, piece, model), BF16),
            jax.ShapeDtypeStruct((2, count, width), F32),
            jax.ShapeDtypeStruct((count, small), F32),
            jax.ShapeDtypeStruct((16, width), F32),
            jax.ShapeDtypeStruct((seqs, piece, 128), F32),
            jax.ShapeDtypeStruct((8, model // 8), F32),
        ],
        scratch_shapes=[pltpu.VMEM(a.shape, BF16) for a in big]
        + [
            pltpu.VMEM((2, n, count, width // 2), BF16),
            pltpu.VMEM((1, n, count // 2, small), BF16),
            pltpu.VMEM((4, seqs, piece, model), BF16),
            pltpu.VMEM((4, seqs, piece, small), BF16),
            pltpu.VMEM((2, count, width // 2), F32),
            pltpu.VMEM((1, count // 2, small), F32),
            pltpu.VMEM((piece, model), F32),
            pltpu.VMEM((piece, small), F32),
            pltpu.VMEM((2, seqs, piece, small), BF16),
            pltpu.VMEM((4, count // 2, small), F32),
            pltpu.VMEM((seqs, piece, model), F32),
            pltpu.VMEM((1, model), F32),
            pltpu.VMEM((n, 8, model // 8), F32),
            pltpu.VMEM((4, 8, model // 8), F32),
            pltpu.VMEM((rounds + 1, 16, width), F32),
            pltpu.VMEM((rounds, 16, width), F32),
            sem((len(big),)),
            sem((n,)),
        ]
        + [sem((3, seqs))] * 4 + [sem((2, n - 1))] * 2 + [sem((1, n - 1))] * 2 + [sem(())] * 2 + [sem((2,))] * 2
        + [sem((rounds,))] * 2 + [sem((n,))] * 2 + [sem((4,))] * 2,
        compiler_params=pltpu.CompilerParams(
            collective_id=2, has_side_effects=True, vmem_limit_bytes=63 * 2**20
        ),
        name="scatter_in",
    )(*big, grad_z, gx, gbc, gh, grad_gate, gain)


def finish_kernel(
    d_in_ref, hidden_ref, cot_ref, mixed_ref, scale_ref, dots_ref, gain_ref, gzx_in, gout_in, gb_in, sums_ref,
    out_ref, d_hidden_ref, gzx_ref, gout_ref, gb_ref, taps_ref, taps_bc_ref,
):
    model = gain_ref.shape[1]
    x = hidden_ref[0].astype(F32)
    scale = scale_ref[0][:, 0:1]
    factor = scale * scale * dots_ref[0][:, 0:1] / model
    d_hidden_ref[0] = cot_ref[0].astype(F32) + scale * (gain_ref[...] * d_in_ref[0].astype(F32)) - x * factor
    out_ref[0] = (x + mixed_ref[0].astype(F32)).astype(BF16)
    gzx_ref[...] = gzx_in[...]
    gout_ref[...] = gout_in[...]
    gb_ref[...] = gb_in[...].T[: gb_ref.shape[0], :]
    taps_ref[...] = sums_ref[0 : taps_ref.shape[0], :]
    taps_bc_ref[...] = sums_ref[8 : 8 + taps_bc_ref.shape[0], : taps_bc_ref.shape[1]]


def finish(d_in, hidden, cotangent, mixed, scale, dots, gain, grad_zx, grad_out, grad_bc, sums, columns, n2):
    seqs, piece, model = hidden.shape
    count, width = grad_zx.shape[1:]
    steps = 2
    rows = piece // steps
    grid = seqs * steps
    piece_rows = lambda w: pl.BlockSpec((1, rows, w), lambda i: (i // steps, i % steps, 0))
    whole = lambda *shape: pl.BlockSpec(shape, lambda i: (0,) * len(shape))
    zx = pl.BlockSpec((1, 2 * count // grid, width), lambda i: (i // (grid // 2), i % (grid // 2), 0))
    down = lambda a, w: pl.BlockSpec((a.shape[0] // grid, w), lambda i: (i, 0))
    return pl.pallas_call(
        finish_kernel,
        grid=(grid,),
        in_specs=[piece_rows(model)] * 4
        + [piece_rows(128)] * 2
        + [whole(1, model), zx, down(grad_out, grad_out.shape[1]), whole(*grad_bc.shape)]
        + [whole(*sums.shape)],
        out_specs=[piece_rows(model)] * 2
        + [zx, down(grad_out, grad_out.shape[1]), whole(columns, count), whole(5, width), whole(5, n2)],
        out_shape=[
            jax.ShapeDtypeStruct(hidden.shape, BF16),
            jax.ShapeDtypeStruct(hidden.shape, F32),
            jax.ShapeDtypeStruct(grad_zx.shape, F32),
            jax.ShapeDtypeStruct(grad_out.shape, F32),
            jax.ShapeDtypeStruct((columns, count), F32),
            jax.ShapeDtypeStruct((5, width), F32),
            jax.ShapeDtypeStruct((5, n2), F32),
        ],
        compiler_params=pltpu.CompilerParams(vmem_limit_bytes=62 * 2**20),
        name="finish",
    )(d_in, hidden, cotangent, mixed, scale, dots, gain, grad_zx, grad_out, grad_bc, sums)


def rms_scale(values):
    return lax.rsqrt(jnp.mean(values * values, axis=-1, keepdims=True) + EPS)


def gather_plain(u, g, w_zx, w_bc, w_out):
    w_zx = lax.all_gather(w_zx, "dp", axis=1, tiled=True)
    return (
        lax.all_gather(u, "tensor", axis=1, tiled=True),
        lax.all_gather(g, "tensor", axis=1, tiled=True),
        w_zx[1],
        w_zx[0],
        lax.all_gather(w_bc, "dp", axis=0, tiled=True),
        lax.all_gather(w_out, "dp", axis=1, tiled=True),
    )


def rows_of(values, piece):
    by_seq = values.reshape(-1, 4 * piece, values.shape[-1])
    return lax.psum_scatter(by_seq, "tensor", scatter_dimension=1, tiled=True)


def scatter_out_plain(piece, normed, g, u, dz, w_out):
    return (
        rows_of(dot(normed, w_out), piece),
        lax.psum_scatter(dot_tn(normed, g), "dp", scatter_dimension=1, tiled=True),
        lax.psum_scatter(dot_tn(u, dz), "dp", scatter_dimension=0, tiled=True),
    )


def scatter_in_plain(piece, u, dz, dx, w_z, w_x, w_bc, dbc):
    low = lax.psum(dbc.astype(F32), "tensor").astype(BF16)
    d_in = rows_of(dot_nt(dz, w_z) + dot_nt(dx, w_x), piece)
    first = lax.axis_index("tensor") * piece
    own = lax.dynamic_slice_in_dim(low.reshape(-1, 4 * piece, low.shape[1]), first, piece, 1)
    d_in = d_in + jnp.einsum("slc,dc->sld", own, w_bc, preferred_element_type=F32)
    return (
        d_in,
        lax.psum_scatter(dot_tn(u, dx), "dp", scatter_dimension=0, tiled=True),
        lax.psum_scatter(dot_tn(u, low), "dp", scatter_dimension=0, tiled=True),
    )


def local(
    n_dp,
    n_tensor,
    hidden,
    pre_gain,
    w_zx,
    w_bcdt,
    conv_x,
    conv_bc,
    dt_bias,
    a_log,
    d_skip,
    gate_gain,
    w_out,
    cotangent,
    segments,
):
    seqs, piece, model = hidden.shape
    length = segments.shape[1]
    tokens = seqs * length
    heads = dt_bias.shape[0]
    channels = conv_x.shape[1]
    n2 = conv_bc.shape[1]
    columns = w_bcdt.shape[1]
    tensor = lax.axis_index("tensor")
    kernels = n_dp == 8 and n_tensor == 4 and seqs == 2 and length == 4 * BLOCK

    x_piece = hidden.astype(F32)
    marks = row_marks(segments)
    spread = jnp.asarray(spread_matrix(heads, channels), BF16)
    pick = jnp.asarray(pick_matrix(heads, channels), BF16)
    shared = (conv_x, conv_bc, dt_bias[None], a_log[None], d_skip[None], spread, pick)
    if kernels:
        u, g, w_x, w_z, w_bc, w_o, cx, x, cbc, bc, dt, states, normed, dz, dy, grad_gate, scale_in = forward_all(
            n_dp, hidden, cotangent, w_zx, w_bcdt.T, w_out, pre_gain[None], gate_gain[None], marks, shared
        )
        g = g.reshape(tokens, model)
    else:
        scale_in = rms_scale(x_piece)
        u_piece = (x_piece * scale_in * pre_gain).astype(BF16)
        w_bc_piece = jnp.pad(w_bcdt, ((0, 0), (0, -columns % 128)))
        u, g, w_x, w_z, w_bc, w_o = gather_plain(u_piece, cotangent, w_zx, w_bc_piece, w_out)
        u = u.reshape(tokens, model)
        g = g.reshape(tokens, model)
        x = dot(u, w_x).reshape(seqs, length, channels)
        z = dot(u, w_z)
        bc_dt = dot(u, w_bc).reshape(seqs, length, -1)
        bc = bc_dt[:, :, :n2]
        dt = jnp.swapaxes(lax.dynamic_slice_in_dim(bc_dt, n2 + tensor * heads, heads, 2), 1, 2)
        y, cx, cbc, states = ssd_forward(x, bc, dt, marks, shared)
        d_normed = dot_nt(g, w_o)
        sig_z = sigmoid(z)
        silu_z = z * sig_z
        y_flat = y.reshape(tokens, channels)
        gated = y_flat * silu_z
        scaled = d_normed * gate_gain
        sums = jnp.stack([jnp.sum(gated * gated, axis=1), jnp.sum(scaled * gated, axis=1)])
        sums = lax.psum(sums, "tensor") / (channels * n_tensor)
        inverse = lax.rsqrt(sums[0] + EPS)[:, None]
        normed = (gated * inverse * gate_gain).astype(BF16)
        grad_gate = jnp.sum(d_normed * gated * inverse, axis=0)[None]
        d_gated = inverse * scaled - gated * inverse**3 * sums[1][:, None]
        dy = (d_gated * silu_z).astype(BF16)
        dz = (d_gated * y_flat * (sig_z * (1.0 + z * (1.0 - sig_z)))).astype(BF16)
        x, bc = x.astype(BF16), bc.astype(BF16)

    back_args = (dy.reshape(seqs, length, channels), x, cx, bc, cbc, dt, marks, states, shared)
    if kernels:
        mixed, grad_out, grad_z, *rest = backward_all(n_dp, w_bc.shape[1], piece, normed, g, u, dz, w_o, *back_args)
    else:
        mixed, grad_out, grad_z = scatter_out_plain(piece, normed, g, u, dz, w_o)
        rest = ssd_backward(w_bc.shape[1], *back_args)
    dx, dbc, gx, gbc, gh = rest
    in_args = (piece, u, dz, dx.reshape(tokens, channels), w_z, w_x, w_bc, dbc.reshape(tokens, -1))
    if kernels:
        d_in, grad_zx, grad_bc, sums, dots, grad_pre = scatter_in(
            n_dp, *in_args, grad_z, gx, gbc, gh, grad_gate, pre_gain[None]
        )
        grad_pre = grad_pre.reshape(model)
        out_hidden, d_hidden, grad_zx, grad_out, grad_bc, grad_conv_x, grad_conv_bc = finish(
            d_in, hidden, cotangent, mixed, scale_in, dots, pre_gain[None], grad_zx, grad_out, grad_bc, sums, columns, n2
        )
        grad_bc = grad_bc.T
    else:
        d_in, grad_x, grad_bc = scatter_in_plain(*in_args)
        grad_zx = jnp.stack([grad_z, grad_x])
        grad_pre = jnp.sum(d_in * x_piece * scale_in, axis=(0, 1))
        dots = scale_in * jnp.sum(d_in * pre_gain * x_piece, axis=-1, keepdims=True)
        steps = jnp.pad(gh[:, :2].T, ((0, 0), (0, channels - heads)))
        sums = lax.psum(jnp.concatenate([gx[:6], grad_gate, steps]), "dp")
        sums = jnp.concatenate([sums[:7], jnp.concatenate([sums[7, :128], sums[8, : channels - 128]])[None]])
        grad_conv_bc, grad_pre = lax.psum((gbc[:5], grad_pre), ("dp", "tensor"))
        grad_conv_x = sums[:5]
        grad_bc = grad_bc[:, :columns]
        out_hidden = (x_piece + mixed).astype(BF16)
        d_hidden = cotangent.astype(F32) + scale_in * (pre_gain * d_in) - x_piece * (scale_in**2 * dots / model)

    return (
        out_hidden,
        d_hidden,
        grad_pre,
        grad_zx,
        grad_bc,
        grad_conv_x,
        grad_conv_bc,
        sums[7, :heads],
        sums[7, 128 : 128 + heads],
        sums[5].reshape(heads, -1).sum(axis=1),
        sums[6],
        grad_out,
    )


def solution(mesh):
    placed = (
        P("dp", "tensor", None),
        P(),
        P(None, "dp", "tensor"),
        P("dp", None),
        P(None, "tensor"),
        P(),
        P("tensor"),
        P("tensor"),
        P("tensor"),
        P("tensor"),
        P("tensor", "dp"),
        P("dp", "tensor", None),
        P("dp", None),
    )
    return jax.shard_map(
        functools.partial(local, mesh.shape["dp"], mesh.shape["tensor"]),
        mesh=mesh,
        in_specs=placed,
        out_specs=(
            P("dp", "tensor", None),
            P("dp", "tensor", None),
            P(),
            P(None, "dp", "tensor"),
            P("dp", None),
            P(None, "tensor"),
            P(),
            P("tensor"),
            P("tensor"),
            P("tensor"),
            P("tensor"),
            P("tensor", "dp"),
        ),
        check_vma=False,
    )
```

```python
import functools

import jax
import jax.numpy as jnp
import numpy as np
from jax import lax
from jax.experimental import pallas as pl
from jax.experimental.pallas import tpu as pltpu
from jax.sharding import PartitionSpec as P

MESH = pl.DeviceIdType.MESH
EPS = 1e-05
BLOCK = 256
F32 = jnp.float32
BF16 = jnp.bfloat16
EXACT = lax.Precision.HIGHEST
LOG2E = 1.4426950408889634
NEG = -1e30


def sigmoid(v):
    return 0.5 * jnp.tanh(0.5 * v) + 0.5


def split3(v):
    hi = v.astype(BF16)
    rest = v - hi.astype(F32)
    mid = rest.astype(BF16)
    low = (rest - mid.astype(F32)).astype(BF16)
    return hi, mid, low


def dot(a, b):
    return jnp.dot(a, b, preferred_element_type=F32)


def dot_nt(a, b):
    return lax.dot_general(a, b, (((1,), (1,)), ((), ())), preferred_element_type=F32)


def dot_tn(a, b):
    return lax.dot_general(a, b, (((0,), (0,)), ((), ())), preferred_element_type=F32)


def softplus(v):
    return jnp.maximum(v, 0.0) + jnp.log1p(jnp.exp(-jnp.abs(v)))


def head_rows(raw, dt_bias, a_log):
    q = raw.shape[1]
    upto = (
        lax.broadcasted_iota(jnp.int32, (q, q), 0) <= lax.broadcasted_iota(jnp.int32, (q, q), 1)
    ).astype(F32)
    biased = raw + dt_bias
    step = softplus(biased)
    rate = -jnp.exp(a_log) * step
    cum = jnp.dot(rate, upto, precision=EXACT, preferred_element_type=F32) * LOG2E
    return biased, step, rate, cum


def exact_nt(a, b):
    a_hi, a_mid, _ = split3(a)
    b_hi, b_mid, _ = split3(b)
    return dot_nt(a_hi, b_hi) + dot_nt(a_hi, b_mid) + dot_nt(a_mid, b_hi)


def turned(row):
    k = row.shape[1]
    own = lax.broadcasted_iota(jnp.int32, (k, k), 0) == lax.broadcasted_iota(jnp.int32, (k, k), 1)
    return jnp.sum(jnp.where(own, row, 0.0), axis=1, keepdims=True)


def to_columns(rows):
    return jnp.concatenate([rows, jnp.zeros((128 - rows.shape[0], rows.shape[1]), F32)], axis=0).T


def head_columns(reads, last, step, cum, third):
    cum_end = cum[:, BLOCK - 1 : BLOCK]
    rows = []
    for factor in (reads * jnp.exp2(cum), last * jnp.exp2(cum_end - cum) * step):
        hi, mid, _ = split3(factor)
        rows += [hi.astype(F32), mid.astype(F32)]
    cols = to_columns(jnp.concatenate(rows + [third], axis=0))
    return cols[:, 4 * cum.shape[0] :], cols.astype(BF16), jnp.exp2(cum_end)


def log2_step(step):
    return jnp.log(jnp.maximum(step, 1e-37)) * LOG2E


def forward_block(
    block, x, bc, dt, marks_ref, taps_x_ref, taps_bc_ref, bias_ref, alog_ref, skip_ref, spread_ref, pick_ref,
    y_ref, cx_ref, cbc_ref, states_ref,
    xs, bs, state, mask_bias,
):
    q = BLOCK
    heads = dt.shape[0]
    channels = x.shape[-1]
    width = channels // heads

    @pl.when(block == 0)
    def _():
        xs[0:8, :] = jnp.zeros((8, xs.shape[1]), F32)
        bs[0:8, :] = jnp.zeros((8, bs.shape[1]), F32)
        state[...] = jnp.zeros_like(state)

    marks = to_columns(marks_ref[0])
    lag_masks = [marks[:, k : k + 1] for k in range(3)]

    def conv(hold, at, taps_ref):
        out = taps_ref[4:5, at] + taps_ref[3:4, at] * hold[8 : 8 + q, at]
        for lag in (1, 2, 3):
            out = out + (lag_masks[lag - 1] * hold[8 - lag : 8 - lag + q, at]) * taps_ref[3 - lag : 4 - lag, at]
        return out

    bs[8 : 8 + q, :] = bc
    xs[8 : 8 + q, :] = x
    cbc = conv(bs, slice(None), taps_bc_ref)
    cbc_ref[0] = cbc
    bc = cbc * sigmoid(cbc)
    n = bc.shape[1] // 2
    scores = exact_nt(bc[:, n:], bc[:, :n])
    b_mat, c_mat = bc[:, :n].astype(BF16), bc[:, n:].astype(BF16)
    b_turned = b_mat.T

    _, step, _, cum = head_rows(dt, turned(bias_ref[...]), turned(alog_ref[...]))
    cols, factors, carry = head_columns(marks_ref[0, 3:4, :], marks_ref[0, 4:5, :], step, cum, cum)
    source = cum - log2_step(step)
    carry_e = jnp.sum(carry * spread_ref[...].astype(F32), axis=0, keepdims=True)
    skip_e = jnp.sum(turned(skip_ref[...]) * spread_ref[...].astype(F32), axis=0, keepdims=True)

    rows = lax.broadcasted_iota(jnp.int32, (q, q), 0)
    places = lax.broadcasted_iota(jnp.int32, (q, q), 1)
    mask_bias[...] = jnp.where((marks[:, 5:6] == marks_ref[0, 5:6, :]) & (rows >= places), 0.0, NEG)

    half = q // 2
    pair_width = 2 * width
    lane = lax.broadcasted_iota(jnp.int32, (1, pair_width), 1)
    every = slice(0, channels)
    cx = conv(xs, every, taps_x_ref)
    cx_ref[0] = cx
    xb = (cx * sigmoid(cx)).astype(BF16)
    xf = xb.astype(F32)
    stb = state[...].astype(BF16)
    states_ref[0, 0] = stb
    y_ref[...] = dot(c_mat, stb) * dot(factors, pick_ref[:, :channels]) + skip_e * xf
    scaled = (xf * dot(factors, pick_ref[:, channels:])).astype(BF16)
    state[...] = carry_e * state[...] + dot(b_turned, scaled)
    for pair in range(heads // 2):
        at = slice(pair * pair_width, (pair + 1) * pair_width)
        xp = xb[:, at]
        tops, lows = [], []
        for h in (2 * pair, 2 * pair + 1):
            col = cols[:, h : h + 1]
            row = source[h : h + 1, :]
            top = jnp.exp2((col[:half] - row[:, :half]) + mask_bias[:half, :half]) * scores[:half, :half]
            low = jnp.exp2((col[half:] - row) + mask_bias[half:, :]) * scores[half:, :]
            tops.append(top.astype(BF16))
            lows.append(low.astype(BF16))
        top = dot(jnp.concatenate(tops, axis=0), xp[:half])
        low = dot(jnp.concatenate(lows, axis=0), xp)
        first = lane < width
        y_ref[:half, at] += jnp.where(first, top[:half], top[half:])
        y_ref[half:, at] += jnp.where(first, low[:half], low[half:])

    xs[0:8, :] = xs[q : q + 8, :]
    bs[0:8, :] = bs[q : q + 8, :]


def backward_block(
    seq, step_id, dy_ref, x_ref, cx_ref, bc_ref, cbc_ref, dt_ref, marks_ref, states_ref,
    taps_x_ref, taps_bc_ref, bias_ref, alog_ref, skip_ref, spread_ref, pick_ref,
    dx_ref, dbc_ref, gx_ref, gbc_ref, gh_ref,
    ds_x, ds_bc, d_state, mask_bias, d_scores, d_in, row_sums,
):
    q = BLOCK
    heads = dt_ref.shape[1]
    channels = x_ref.shape[-1]
    width = channels // heads

    @pl.when(step_id == 0)
    def _():
        ds_x[:, q : q + 8, :] = jnp.zeros((3, 8, channels), F32)
        ds_bc[:, q : q + 8, :] = jnp.zeros((3, 8, ds_bc.shape[2]), F32)
        d_state[...] = jnp.zeros_like(d_state)

    @pl.when((step_id == 0) & (seq == 0))
    def _():
        gx_ref[...] = jnp.zeros_like(gx_ref)
        gbc_ref[...] = jnp.zeros_like(gbc_ref)
        gh_ref[...] = jnp.zeros_like(gh_ref)

    marks = to_columns(marks_ref[0])
    lag_masks = [marks[:, k : k + 1] for k in range(3)]

    def conv_back(d_out, value, hold, at, taps_ref, grad_ref):
        value = value.astype(F32)
        d_value = d_out * taps_ref[3:4, at]
        grad_ref[3:4, at] += jnp.sum(value * d_out, axis=0, keepdims=True)
        grad_ref[4:5, at] += jnp.sum(d_out, axis=0, keepdims=True)
        for lag in (1, 2, 3):
            hold[lag - 1, 0:q, at] = lag_masks[lag - 1] * d_out
            moved = hold[lag - 1, lag : lag + q, at]
            d_value = d_value + moved * taps_ref[3 - lag : 4 - lag, at]
            grad_ref[3 - lag : 4 - lag, at] += jnp.sum(value * moved, axis=0, keepdims=True)
            hold[lag - 1, q : q + 8, at] = hold[lag - 1, 0:8, at]
        return d_value

    cbc = cbc_ref[0]
    bc = cbc * sigmoid(cbc)
    n = bc.shape[1] // 2
    scores = exact_nt(bc[:, :n], bc[:, n:])
    b_mat, c_mat = bc[:, :n].astype(BF16), bc[:, n:].astype(BF16)
    c_turned = c_mat.T

    a_log = turned(alog_ref[...])
    biased, step, rate, cum = head_rows(dt_ref[0], turned(bias_ref[...]), a_log)
    source = cum - log2_step(step)
    cols, factors, carry = head_columns(marks_ref[0, 3:4, :], marks_ref[0, 4:5, :], step, cum, source)
    carry_e = jnp.sum(carry * spread_ref[...].astype(F32), axis=0, keepdims=True)
    skip_e = jnp.sum(turned(skip_ref[...]) * spread_ref[...].astype(F32), axis=0, keepdims=True)

    rows = lax.broadcasted_iota(jnp.int32, (q, q), 0)
    places = lax.broadcasted_iota(jnp.int32, (q, q), 1)
    mask_bias[...] = jnp.where((marks[:, 5:6] == marks_ref[0, 5:6, :]) & (rows <= places), 0.0, NEG)

    half = q // 2
    pair_width = 2 * width
    lane = lax.broadcasted_iota(jnp.int32, (1, pair_width), 1)
    first = lane < width
    d_scores[...] = jnp.zeros_like(d_scores)
    col_h = jnp.zeros((heads, q), F32)
    head_row = lax.broadcasted_iota(jnp.int32, (heads, 3 * half), 0)
    spread = spread_ref[...]
    cx = cx_ref[0]
    xb = (cx * sigmoid(cx)).astype(BF16)
    dyb = dy_ref[0]
    st = states_ref[0, 0]
    dye = dyb.astype(F32) * dot(factors, pick_ref[:, :channels])
    out_h = dot_nt(spread, (dye * dot(c_mat, st)).astype(BF16))
    dye = dye.astype(BF16)
    d_c = dot_nt(dye, st)
    dst = d_state[...].astype(BF16)
    kept = jnp.sum(d_state[...] * st.astype(F32), axis=0, keepdims=True) * carry_e
    carried = jnp.sum(spread.astype(F32) * kept, axis=1, keepdims=True)
    d_state[...] = carry_e * d_state[...] + dot(c_turned, dye)
    xf = xb.astype(F32)
    to_end = dot(factors, pick_ref[:, channels:])
    d_b = dot_nt((xf * to_end).astype(BF16), dst)
    dx_st = dot(b_mat, dst) * to_end
    state_h = dot_nt(spread, (xf * dx_st).astype(BF16))
    d_in[...] = dx_st
    for pair in range(heads // 2):
        at = slice(pair * pair_width, (pair + 1) * pair_width)
        xp, dyp = xb[:, at], dyb[:, at]
        none = jnp.zeros_like(xp)
        x_first, x_second = jnp.where(first, xp, none), jnp.where(first, none, xp)
        g_top = dot_nt(jnp.concatenate([x_first[:half], x_second[:half]], axis=0), dyp)
        g_low = dot_nt(jnp.concatenate([x_first[half:], x_second[half:]], axis=0), dyp[half:])
        tops, lows, d_top, d_low = [], [], 0.0, 0.0
        for which in (0, 1):
            h = 2 * pair + which
            own = slice(which * half, (which + 1) * half)
            col = cols[:, h : h + 1]
            row = cum[h : h + 1, :]
            top = jnp.exp2((row - col[:half]) + mask_bias[:half, :])
            low = jnp.exp2((row[:, half:] - col[half:]) + mask_bias[half:, half:])
            p_top = top * g_top[own]
            p_low = low * g_low[own]
            d_top = d_top + p_top
            d_low = d_low + p_low
            m_top = p_top * scores[:half, :]
            m_low = p_low * scores[half:, half:]
            late = jnp.sum(m_top[:, half:], axis=0, keepdims=True) + jnp.sum(m_low, axis=0, keepdims=True)
            row_sums[h : h + 1, :half] = jnp.sum(m_top[:, :half], axis=0, keepdims=True)
            row_sums[h : h + 1, half:] = late
            parts = split3(jnp.concatenate([m_top[:, :half] + m_top[:, half:], m_low], axis=0))
            col_h = col_h + dot_nt((head_row == h).astype(BF16), jnp.concatenate(parts, axis=1))
            tops.append((top * scores[:half, :]).astype(BF16))
            lows.append((low * scores[half:, half:]).astype(BF16))
        d_scores[:half, :] += d_top
        d_scores[half:, half:] += d_low
        top = dot(jnp.concatenate(tops, axis=0), dyp)
        low = dot(jnp.concatenate(lows, axis=0), dyp[half:])
        d_in[:half, at] += jnp.where(first, top[:half], top[half:])
        d_in[half:, at] += jnp.where(first, low[:half], low[half:])

    everywhere = slice(0, channels)
    dyf = dy_ref[0].astype(F32)
    cx = cx_ref[0]
    sig = sigmoid(cx)
    gx_ref[5:6, :] += jnp.sum(dyf * (cx * sig).astype(BF16).astype(F32), axis=0, keepdims=True)
    d_cx = (d_in[...] + skip_e * dyf) * (sig * (1.0 + cx * (1.0 - sig)))
    dx_ref[0] = conv_back(d_cx, x_ref[0], ds_x, everywhere, taps_x_ref, gx_ref).astype(BF16)

    dsb = d_scores[...].astype(BF16)
    d_b = d_b + dot(dsb, c_mat)
    d_c = d_c + dot_tn(dsb, b_mat)
    sig = sigmoid(cbc)
    d_cbc = jnp.concatenate([d_b, d_c], axis=1) * (sig * (1.0 + cbc * (1.0 - sig)))
    every = slice(0, 2 * n)
    dbc_ref[0, :, every] = conv_back(d_cbc, bc_ref[0], ds_bc, every, taps_bc_ref, gbc_ref).astype(BF16)

    used_h = col_h + state_h
    diff_h = row_sums[...] - col_h + out_h
    since = (rows >= places).astype(F32)
    before = (rows < places).astype(F32)
    d_rate = (
        jnp.dot(diff_h, since, precision=EXACT, preferred_element_type=F32)
        + jnp.dot(state_h, before, precision=EXACT, preferred_element_type=F32)
        + carried
    )
    sig_dt = sigmoid(biased)
    ratio = jnp.where(step < 1e-30, 1.0, sig_dt / jnp.maximum(step, 1e-30))
    d_raw = used_h * ratio - jnp.exp(a_log) * sig_dt * d_rate
    lanes = dbc_ref.shape[2] - 2 * n
    mine = lax.broadcasted_iota(jnp.int32, (heads, lanes), 0) + lax.axis_index("tensor") * heads
    own = (lax.broadcasted_iota(jnp.int32, (heads, lanes), 1) == mine).astype(BF16)
    dbc_ref[0, :, 2 * n :] = dot_tn(d_raw.astype(BF16), own).astype(BF16)
    gh_ref[:, 0:1] += jnp.sum(d_raw, axis=1, keepdims=True)
    gh_ref[:, 1:2] += jnp.sum(d_rate * rate, axis=1, keepdims=True)


def row_marks(segments):
    seqs, length = segments.shape
    blocks = length // BLOCK
    lags = []
    for lag in (1, 2, 3):
        earlier = jnp.pad(segments, ((0, 0), (lag, 0)), constant_values=-1)[:, :length]
        lags.append(earlier == segments)
    grouped = segments.reshape(seqs, blocks, BLOCK)
    before = jnp.pad(segments, ((0, 0), (1, 0)), constant_values=-1)[:, :length].reshape(seqs, blocks, BLOCK)
    reads = (grouped == before[:, :, :1]).reshape(seqs, length)
    last = (grouped == grouped[:, :, -1:]).reshape(seqs, length)
    rows = [m.astype(F32) for m in (*lags, reads, last, segments)]
    return jnp.stack(rows + [jnp.zeros_like(rows[0])] * 2, axis=1)


def spread_matrix(heads, channels):
    width = channels // heads
    return (np.arange(heads)[:, None] == np.arange(channels)[None, :] // width).astype(np.float32)


def pick_matrix(heads, channels):
    spread = spread_matrix(heads, channels)
    out = np.zeros((128, 2 * channels), np.float32)
    for part in range(4):
        at = slice(part // 2 * channels, (part // 2 + 1) * channels)
        out[part * heads : (part + 1) * heads, at] = spread
    return out


def shared_specs(channels, n2, heads):
    full = lambda *shape: pl.BlockSpec(shape, lambda *i: (0,) * len(shape))
    return [
        full(5, channels),
        full(5, n2),
        full(1, heads),
        full(1, heads),
        full(1, heads),
        full(heads, channels),
        full(128, 2 * channels),
    ]


def forward_scratch(channels, n2):
    return [
        pltpu.VMEM((BLOCK + 8, channels), F32),
        pltpu.VMEM((BLOCK + 8, n2), F32),
        pltpu.VMEM((n2 // 2, channels), F32),
        pltpu.VMEM((BLOCK, BLOCK), F32),
    ]


def forward_kernel(x_ref, bc_ref, dt_ref, *refs):
    y_ref = refs[8]
    forward_block(pl.program_id(1), x_ref[0], bc_ref[0], dt_ref[0], *refs[:8], y_ref.at[0], *refs[9:])


def ssd_forward(x, bc, dt, marks, shared):
    seqs, length, channels = x.shape
    n2, heads = bc.shape[2], dt.shape[1]
    blocks = length // BLOCK
    tok = lambda w: pl.BlockSpec((1, BLOCK, w), lambda s, c: (s, c, 0))
    head = lambda w: pl.BlockSpec((1, w, BLOCK), lambda s, c: (s, 0, c))
    return pl.pallas_call(
        forward_kernel,
        grid=(seqs, blocks),
        in_specs=[tok(channels), tok(n2), head(heads), head(8)] + shared_specs(channels, n2, heads),
        out_specs=[
            tok(channels),
            tok(channels),
            tok(n2),
            pl.BlockSpec((1, 1, n2 // 2, channels), lambda s, c: (s, c, 0, 0)),
        ],
        out_shape=[
            jax.ShapeDtypeStruct((seqs, length, channels), F32),
            jax.ShapeDtypeStruct((seqs, length, channels), F32),
            jax.ShapeDtypeStruct((seqs, length, n2), F32),
            jax.ShapeDtypeStruct((seqs, blocks, n2 // 2, channels), BF16),
        ],
        scratch_shapes=forward_scratch(channels, n2),
        compiler_params=pltpu.CompilerParams(vmem_limit_bytes=48 * 2**20),
        name="ssd_forward",
    )(x, bc, dt, marks, *shared)


def backward_kernel(*refs):
    backward_block(pl.program_id(0), pl.program_id(1), *refs)


def backward_scratch(channels, n2, heads):
    return [
        pltpu.VMEM((3, BLOCK + 8, channels), F32),
        pltpu.VMEM((3, BLOCK + 8, n2), F32),
        pltpu.VMEM((n2 // 2, channels), F32),
        pltpu.VMEM((BLOCK, BLOCK), F32),
        pltpu.VMEM((BLOCK, BLOCK), F32),
        pltpu.VMEM((BLOCK, channels), F32),
        pltpu.VMEM((heads, BLOCK), F32),
    ]


def backward_specs(channels, n2, heads, small, place):
    tok = lambda w: pl.BlockSpec((1, BLOCK, w), lambda *i: (*place(*i), 0))
    full = lambda *shape: pl.BlockSpec(shape, lambda *i: (0,) * len(shape))
    ins = [tok(channels)] * 3 + [tok(n2)] * 2 + [
        pl.BlockSpec((1, heads, BLOCK), lambda *i: (place(*i)[0], 0, place(*i)[1])),
        pl.BlockSpec((1, 8, BLOCK), lambda *i: (place(*i)[0], 0, place(*i)[1])),
        pl.BlockSpec((1, 1, n2 // 2, channels), lambda *i: (*place(*i), 0, 0)),
    ]
    ins += shared_specs(channels, n2, heads)
    return ins, [tok(channels), tok(small), full(8, channels), full(8, n2), full(heads, 128)]


def backward_outs(seqs, length, channels, n2, heads, small):
    return [
        jax.ShapeDtypeStruct((seqs, length, channels), BF16),
        jax.ShapeDtypeStruct((seqs, length, small), BF16),
        jax.ShapeDtypeStruct((8, channels), F32),
        jax.ShapeDtypeStruct((8, n2), F32),
        jax.ShapeDtypeStruct((heads, 128), F32),
    ]


def ssd_backward(small, dy, x, cx, bc, cbc, dt, marks, states, shared):
    seqs, length, channels = x.shape
    n2, heads = bc.shape[2], dt.shape[1]
    blocks = length // BLOCK
    ins, outs = backward_specs(channels, n2, heads, small, lambda s, c: (s, blocks - 1 - c))
    return pl.pallas_call(
        backward_kernel,
        grid=(seqs, blocks),
        in_specs=ins,
        out_specs=outs,
        out_shape=backward_outs(seqs, length, channels, n2, heads, small),
        scratch_shapes=backward_scratch(channels, n2, heads),
        compiler_params=pltpu.CompilerParams(vmem_limit_bytes=56 * 2**20),
        name="ssd_backward",
    )(dy, x, cx, bc, cbc, dt, marks, states, *shared)


def ring_place(n):
    dp = lax.axis_index("dp")
    z, y = dp // 2, dp % 2

    def at(place):
        q = (place + 4 * n) % n
        return 2 * q + (q // (n // 2)) * (2 * n - 1 - 4 * q)

    return z + y * (n - 1 - 2 * z), at


def tensor_place():
    t = lax.axis_index("tensor")
    return t, t + 1 - 2 * (t % 2), (t + 2) % 4


def greet(n, more=()):
    place, at = ring_place(n)
    _, other, across = tensor_place()
    sem = pltpu.get_barrier_semaphore()
    targets = [{"dp": at(place + 1)}, {"dp": at(place - 1)}, {"tensor": other}, {"tensor": across}, *more]
    for target in targets:
        pl.semaphore_signal(sem, inc=1, device_id=target, device_id_type=MESH)
    pl.semaphore_wait(sem, len(targets))


def remote(src, dst, send_sem, recv_sem, target):
    return pltpu.make_async_remote_copy(
        src_ref=src, dst_ref=dst, send_sem=send_sem, recv_sem=recv_sem, device_id=target, device_id_type=MESH
    )


def span(first, count, unit):
    return pl.ds(pl.multiple_of(first, unit), count)


class RingGather:
    def __init__(self, n, parts, keep, sems):
        self.n, self.parts, self.keep = n, parts, keep
        self.send_sem, self.recv_sem = sems
        self.place, self.at = ring_place(n)

    def copy(self, way, part, step):
        sign = 1 - 2 * way
        ref = self.keep(way, part, self.at(self.place - sign * step))
        return remote(
            ref,
            ref,
            self.send_sem.at[way, part, step],
            self.recv_sem.at[way, part, step],
            {"dp": self.at(self.place + sign)},
        )

    def step(self, k):
        for part in range(self.parts):
            for way in (0, 1):
                if k > 0:
                    self.copy(way, part, k - 1).wait_recv()
                if k < self.n - 1:
                    self.copy(way, part, k).start()

    def later(self, k):
        for part in range(self.parts):
            for way in (0, 1):
                self.copy(way, part, k - 1).wait_recv()

                @pl.when(k < self.n - 1)
                def _():
                    self.copy(way, part, k).start()

    def finish(self):
        for k in range(self.n - 1):
            for part in range(self.parts):
                for way in (0, 1):
                    self.copy(way, part, k).wait_send()


class RowGather:
    def __init__(self, keep, sems):
        self.keep = keep
        self.send_sem, self.recv_sem = sems
        self.me, self.other, self.across = tensor_place()

    def copy(self, kind, part):
        ref = self.keep(part, self.across if kind == 2 else self.me)
        target = self.across if kind == 0 else self.other
        return remote(
            ref, ref, self.send_sem.at[kind, part], self.recv_sem.at[kind, part], {"tensor": target}
        )

    def start(self, part):
        self.copy(0, part).start()
        self.copy(1, part).start()

    def forward(self, part):
        self.copy(0, part).wait_recv()
        self.copy(2, part).start()

    def wait(self, part):
        self.copy(1, part).wait_recv()
        self.copy(2, part).wait_recv()

    def finish(self, parts):
        for part in range(parts):
            for kind in range(3):
                self.copy(kind, part).wait_send()


def marks_of(seg):
    length = seg.shape[1]
    lane = lax.broadcasted_iota(jnp.int32, seg.shape, 1)
    row = lax.broadcasted_iota(jnp.int32, seg.shape, 0)
    earlier = [jnp.where(lane < lag, -1.0, pltpu.roll(seg, lag, 1)) for lag in (1, 2, 3)]
    starts = range(0, length, BLOCK)
    spread = lambda values, at: jnp.broadcast_to(values[:, at : at + 1], (seg.shape[0], BLOCK))
    before = jnp.concatenate([spread(earlier[0], at) for at in starts], axis=1)
    final = jnp.concatenate([spread(seg, at + BLOCK - 1) for at in starts], axis=1)
    out = jnp.where(row == 5, seg, 0.0)
    for k, other in enumerate((*earlier, before, final)):
        out = jnp.where((row == k) & (other == seg), 1.0, out)
    return out


def all_kernel(n, *refs):
    (hidden_ref, g_ref, wzx_ref, wbc_ref, wout_ref, gain_ref, gate_ref, seg_ref), refs = refs[:8], refs[8:]
    shared, refs = refs[:7], refs[7:]
    (u_out, gf_out, wx_out, wz_out, wb_out, wo_out), refs = refs[:6], refs[6:]
    (cx_ref, x_ref, cbc_ref, bc_ref, dt_ref, states_ref), refs = refs[:6], refs[6:]
    (normed_ref, dz_ref, dy_ref, grad_ref, scale_ref, marks_ref), refs = refs[:6], refs[6:]
    scratch, refs = refs[:4], refs[4:]
    (u, wx, wz, wo, wb, wb_own, wdt, g_cols, y, z, dn, sums), refs = refs[:12], refs[12:]
    (load_sem, keep_sem, stream_sem), sems = refs[:3], refs[3:]

    i = pl.program_id(0)
    rows, width = wzx_ref.shape[1:]
    out_rows, out_cols = wout_ref.shape
    seqs, piece, model = hidden_ref.shape
    length = 4 * piece
    blocks = length // BLOCK
    heads = dt_ref.shape[1]
    n2 = bc_ref.shape[2]
    small_cols = wb.shape[1]
    dp = lax.axis_index("dp")
    place, at = ring_place(n)
    me, other, across = tensor_place()
    core = me % 2
    facing = (other + 2) % 4

    def keep_wide(ref):
        def keep(way, part, d):
            return ref.at[span(d * rows, rows, 16), pl.ds(way * width // 2 + part * width // 4, width // 4)]

        return keep

    def keep_out(way, part, d):
        first = way * out_rows // 2 + part * out_rows // 4
        return wo.at[pl.ds(first, out_rows // 4), span(d * out_cols, out_cols, 128)]

    def keep_small(way, part, d):
        return wb.at[span(d * rows + core * rows // 2 + way * rows // 4, rows // 4, 16), :]

    def keep_rows(part, t):
        if part < seqs:
            return u.at[span(part * length + t * piece, piece, 16), :]
        return gf_out.at[part - seqs, span(t * piece, piece, 16), :]

    x_ring = RingGather(n, 2, keep_wide(wx), sems[0:2])
    small = RingGather(n, 1, keep_small, sems[2:4])
    z_ring = RingGather(n, 2, keep_wide(wz), sems[4:6])
    out_ring = RingGather(n, 2, keep_out, sems[6:8])
    token_rows = RowGather(keep_rows, sems[8:10])
    halves_send, halves_recv, sums_send, sums_recv = sems[10:14]

    def half(ahead, whose):
        d = (dp + ahead) % n
        ref = wb.at[span(d * rows + whose * rows // 2, rows // 2, 16), :]
        return remote(ref, ref, halves_send.at[ahead], halves_recv.at[ahead], {"tensor": other})

    def sums_copy(kind):
        ref = sums.at[me]
        target = {"tensor": (other, across, facing)[kind]}
        return remote(ref, ref, sums_send.at[kind], sums_recv.at[kind], target)

    keeps = [
        pltpu.make_async_copy(src, dst, keep_sem.at[j])
        for j, (src, dst) in enumerate(((wx, wx_out), (wb, wb_out), (wz, wz_out), (u, u_out), (wo, wo_out)))
    ]

    def streams(k):
        return [
            pltpu.make_async_copy(
                gf_out.at[:, :, span(at(place - (1 - 2 * way) * k) * out_cols, out_cols, 128)],
                g_cols.at[way],
                stream_sem.at[way],
            )
            for way in (0, 1)
        ]

    def start(copies):
        for copy in copies:
            copy.start()

    def wait(copies):
        for copy in copies:
            copy.wait()

    @pl.when(i == 0)
    def _():
        def held(s, h):
            return z.at[pl.ds((2 * s + h) * piece, piece), :]

        halves = [(s, h) for s in range(seqs) for h in (0, 1)]
        cut = lambda h: pl.ds(h * (model // 2), model // 2)
        own = [
            (wzx_ref.at[1], wx.at[span(dp * rows, rows, 16), :]),
            (wbc_ref, wb_own),
            (wzx_ref.at[0], wz.at[span(dp * rows, rows, 16), :]),
            (wout_ref, wo.at[:, span(dp * out_cols, out_cols, 128)]),
        ]
        own += [(hidden_ref.at[s, :, cut(h)], held(seqs + s, h)) for s, h in halves]
        own += [(g_ref.at[s, :, cut(h)], held(s, h)) for s, h in halves]
        loads = [pltpu.make_async_copy(a, b, load_sem.at[j]) for j, (a, b) in enumerate(own)]
        first = 4 + 2 * seqs
        stores = [
            pltpu.make_async_copy(
                held(s, h), gf_out.at[s, span(me * piece, piece, 16), cut(h)], load_sem.at[first + 2 * seqs + j]
            )
            for j, (s, h) in enumerate(halves)
        ]
        start(loads)
        greet(n, [{"tensor": facing}])
        loads[0].wait()
        x_ring.step(0)
        loads[1].wait()
        mine = span(dp * rows, rows, 16)
        short = jnp.zeros((small_cols - wb_own.shape[0], rows), BF16)
        wb[mine, :] = jnp.concatenate([wb_own[...], short], axis=0).T
        small.step(0)
        wait(loads[4:first])
        for s in range(seqs):
            left = z[pl.ds((2 * (seqs + s)) * piece, piece), :].astype(F32)
            right = z[pl.ds((2 * (seqs + s) + 1) * piece, piece), :].astype(F32)
            squares = jnp.sum(left * left + right * right, axis=1, keepdims=True)
            scale = lax.rsqrt(squares / model + EPS)
            scale_ref[s] = jnp.broadcast_to(scale, (piece, 128))
            to = span(s * length + me * piece, piece, 16)
            u[to, cut(0)] = (left * scale * gain_ref[:, cut(0)]).astype(BF16)
            u[to, cut(1)] = (right * scale * gain_ref[:, cut(1)]).astype(BF16)
            token_rows.start(s)
        for s in range(seqs):
            seg = seg_ref[s : s + 1, :].astype(F32)
            marks_ref[s] = marks_of(jnp.broadcast_to(seg, (8, seg.shape[1])))
        wait(loads[first:])
        start(stores)
        wait(loads[2:4])
        wait(stores)
        for k in range(1, n):
            x_ring.step(k)
            small.step(k)
            if k == n - 1:
                z_ring.step(0)
            if k == n // 2:
                token_rows.forward(0)
                token_rows.start(seqs)
        for ahead in range(1, n):
            half(ahead, core).start()
        for ahead in range(1, n):
            half(ahead, 1 - core).wait_recv()
        token_rows.wait(0)
        start(keeps[:2])
        lanes = small_cols - n2
        pick = lax.broadcasted_iota(jnp.int32, (heads, lanes), 1) == (
            lax.broadcasted_iota(jnp.int32, (heads, lanes), 0) + me * heads
        )
        wdt[...] = dot_nt(pick.astype(BF16), wb[:, n2:]).astype(BF16)

    b = i - 1

    @pl.when((b >= 0) & (b < n))
    def _():
        @pl.when(b < n - 1)
        def _():
            z_ring.later(b + 1)

        @pl.when(b == n - 2)
        def _():
            out_ring.step(0)

        @pl.when(b == n - 1)
        def _():
            keeps[2].start()
            out_ring.step(1)

        @pl.when(b == 0)
        def _():
            token_rows.forward(1)
            token_rows.start(seqs + 1)

        @pl.when(b == blocks)
        def _():
            token_rows.wait(1)
            keeps[3].start()

        at_block = span(b * BLOCK, BLOCK, BLOCK)
        tokens = u[at_block, :]
        marks = marks_ref.at[pl.ds(b // blocks, 1), :, span(b % blocks * BLOCK, BLOCK, BLOCK)]
        x = dot(tokens, wx[...])
        bc = dot(tokens, wb[:, :n2])
        dt = dot_nt(wdt[...], tokens)
        x_ref[0] = x.astype(BF16)
        bc_ref[0] = bc.astype(BF16)
        dt_ref[0] = dt
        forward_block(
            b % blocks, x, bc, dt, marks, *shared, y.at[at_block, :], cx_ref, cbc_ref, states_ref, *scratch
        )

    slope = wx

    def add_shard(k):
        wait(streams(k))
        for way in (0, 1):
            e = pl.ds(way * (out_rows // 2), out_rows // 2)
            d = at(place - (1 - 2 * way) * k)
            cols = g_cols[way].reshape(seqs * length, out_cols)
            value = dot_nt(cols, wo[e, span(d * out_cols, out_cols, 128)])

            @pl.when(k == 0)
            def _():
                dn[:, e] = value

            @pl.when(k > 0)
            def _():
                dn[:, e] += value

    def gate_block(e, _):
        part = span(e * BLOCK, BLOCK, BLOCK)
        zf = dot(u[part, :], wz[...])
        sig = sigmoid(zf)
        silu = zf * sig
        yf = y[part, :]
        y[part, :] = yf * silu
        z[part, :] = silu.astype(BF16)
        slope[part, :] = (yf * (sig + silu * (1.0 - sig))).astype(BF16)
        return 0

    def shard_step(c, _):
        @pl.when(c == 0)
        def _():
            token_rows.forward(seqs)
            token_rows.forward(seqs + 1)
            token_rows.wait(seqs)
            token_rows.wait(seqs + 1)
            start(streams(0))
            add_shard(0)
            start(streams(1))
            keeps[0].wait()
            x_ring.finish()

        @pl.when((c >= 1) & (c <= 4))
        def _():
            lax.fori_loop(2 * (c - 1), 2 * c, gate_block, 0)

        add_shard(c + 1)
        start(streams(c + 2))
        out_ring.later(c + 2)
        return 0

    @pl.when(i == n + 1)
    def _():
        lax.fori_loop(0, n - 2, shard_step, 0)
        add_shard(n - 1)
        keeps[4].start()

        def block_sums(e, _):
            part = span(e * BLOCK, BLOCK, BLOCK)
            gated = y[part, :]
            squares = jnp.sum(gated * gated, axis=1, keepdims=True)
            inner = jnp.sum(gate_ref[...] * dn[part, :] * gated, axis=1, keepdims=True)
            lane = lax.broadcasted_iota(jnp.int32, (1, 128), 1)
            both = jnp.where(lane == 0, squares, jnp.where(lane == 1, inner, 0.0))
            sums[me, :, part] = both.T[0:8, :]
            return 0

        lax.fori_loop(0, n, block_sums, 0)
        for kind in range(3):
            sums_copy(kind).start()

    e = i - (n + 2)

    @pl.when(e >= 0)
    def _():
        @pl.when(e == 0)
        def _():
            for kind in range(3):
                sums_copy(kind).wait_recv()
            grad_ref[...] = jnp.zeros_like(grad_ref)

        part = span(e * BLOCK, BLOCK, BLOCK)
        whole = (sums[0, :, part] + sums[1, :, part]) + (sums[2, :, part] + sums[3, :, part])
        cols = jnp.concatenate([whole, jnp.zeros((120, BLOCK), F32)], axis=0).T / (4 * width)
        inverse = lax.rsqrt(cols[:, 0:1] + EPS)
        dnf = dn[part, :]
        gain = gate_ref[...]
        gated = y[part, :]
        scaled_gated = gated * inverse
        normed_ref[...] = (scaled_gated * gain).astype(BF16)
        grad_ref[...] += jnp.sum(dnf * scaled_gated, axis=0, keepdims=True)
        d_gated = inverse * (dnf * gain) - gated * (inverse * inverse * inverse * cols[:, 1:2])
        dy_ref[...] = (d_gated * z[part, :].astype(F32)).astype(BF16)
        dz_ref[...] = (d_gated * slope[part, :].astype(F32)).astype(BF16)

        @pl.when(e == n - 1)
        def _():
            wait(keeps[1:])
            for ring in (small, z_ring, out_ring):
                ring.finish()
            token_rows.finish(2 * seqs)
            for ahead in range(1, n):
                half(ahead, core).wait_send()
            for kind in range(3):
                sums_copy(kind).wait_send()


def forward_all(n, hidden, g, w_zx, w_bc, w_out, pre_gain, gate_gain, segments, shared):
    seqs, piece, model = hidden.shape
    rows, width = w_zx.shape[1:]
    out_rows, out_cols = w_out.shape
    length = 4 * piece
    tokens = seqs * length
    blocks = length // BLOCK
    n2 = shared[1].shape[1]
    heads = shared[2].shape[1]
    columns = w_bc.shape[0]
    small = columns + -columns % 128
    sem = pltpu.SemaphoreType.DMA
    ring = [sem((2, 2, n - 1))] * 2
    anywhere = pl.BlockSpec(memory_space=pl.ANY)
    whole = lambda *shape: pl.BlockSpec(shape, lambda i: (0,) * len(shape))
    b = lambda i: jnp.minimum(jnp.maximum(i - 1, 0), n - 1)
    e = lambda i: jnp.maximum(i - (n + 2), 0)
    tok = lambda w: pl.BlockSpec((1, BLOCK, w), lambda i: (b(i) // blocks, b(i) % blocks, 0))
    gate = pl.BlockSpec((BLOCK, width), lambda i: (e(i), 0))
    out_shape = [
        ((tokens, model), BF16),
        ((seqs, length, model), BF16),
        ((rows * n, width), BF16),
        ((rows * n, width), BF16),
        ((rows * n, small), BF16),
        ((out_rows, out_cols * n), BF16),
        ((seqs, length, width), F32),
        ((seqs, length, width), BF16),
        ((seqs, length, n2), F32),
        ((seqs, length, n2), BF16),
        ((seqs, heads, length), F32),
        ((seqs, blocks, n2 // 2, width), BF16),
        ((tokens, width), BF16),
        ((tokens, width), BF16),
        ((tokens, width), BF16),
        ((1, width), F32),
        ((seqs, piece, 128), F32),
        ((seqs, 8, length), F32),
    ]
    return pl.pallas_call(
        functools.partial(all_kernel, n),
        grid=(2 * n + 2,),
        in_specs=[anywhere] * 5
        + [
            whole(1, model),
            whole(1, width),
            whole(*segments.shape),
        ]
        + shared_specs(width, n2, heads),
        out_specs=[anywhere] * 6
        + [tok(width), tok(width), tok(n2), tok(n2)]
        + [pl.BlockSpec((1, heads, BLOCK), lambda i: (b(i) // blocks, 0, b(i) % blocks))]
        + [pl.BlockSpec((1, 1, n2 // 2, width), lambda i: (b(i) // blocks, b(i) % blocks, 0, 0))]
        + [gate] * 3
        + [whole(1, width), whole(seqs, piece, 128), whole(seqs, 8, length)],
        out_shape=[jax.ShapeDtypeStruct(*s) for s in out_shape],
        scratch_shapes=forward_scratch(width, n2)
        + [
            pltpu.VMEM((tokens, model), BF16),
            pltpu.VMEM((rows * n, width), BF16),
            pltpu.VMEM((rows * n, width), BF16),
            pltpu.VMEM((out_rows, out_cols * n), BF16),
            pltpu.VMEM((rows * n, small), BF16),
            pltpu.VMEM(w_bc.shape, BF16),
            pltpu.VMEM((heads, rows * n), BF16),
            pltpu.VMEM((2, seqs, length, out_cols), BF16),
            pltpu.VMEM((tokens, width), F32),
            pltpu.VMEM((tokens, width), BF16),
            pltpu.VMEM((tokens, width), F32),
            pltpu.VMEM((4, 8, tokens), F32),
            sem((4 + 6 * seqs,)),
            sem((5,)),
            sem((2,)),
        ]
        + ring + [sem((2, 1, n - 1))] * 2 + ring + ring
        + [sem((3, 2 * seqs))] * 2 + [sem((n,))] * 2 + [sem((3,))] * 2,
        compiler_params=pltpu.CompilerParams(
            collective_id=0, has_side_effects=True, vmem_limit_bytes=63 * 2**20
        ),
        name="forward_all",
    )(hidden, g, w_zx, w_bc, w_out, pre_gain, gate_gain, segments, *shared)


class RingScatter:
    def __init__(self, n, terms, slots, sems, ways=2, sign=1):
        self.n, self.terms, self.slots, self.ways, self.sign = n, terms, slots, ways, sign
        self.send_sem, self.recv_sem = sems
        self.place, self.at = ring_place(n)

    def turn(self, way):
        return self.sign * (1 - 2 * way)

    def owner(self, way, k):
        return self.at(self.place - self.turn(way) * (1 + k))

    def copy(self, way, k):
        return remote(
            self.slots.at[way, k],
            self.slots.at[way, k + 1],
            self.send_sem.at[way, k],
            self.recv_sem.at[way, k],
            {"dp": self.at(self.place + self.turn(way))},
        )

    def step(self, way, k):
        @pl.when(k == 0)
        def _():
            self.slots[way, 0] = self.terms[way].astype(BF16)

        @pl.when(k > 0)
        def _():
            self.copy(way, k - 1).wait_recv()

            @pl.when(k < self.n - 1)
            def _():
                self.slots[way, k] = (self.terms[way].astype(F32) + self.slots[way, k].astype(F32)).astype(BF16)

        @pl.when(k < self.n - 1)
        def _():
            self.copy(way, k).start()

    def last(self, way):
        return self.terms[way].astype(F32) + self.slots[way, self.n - 1].astype(F32)

    def finish(self):
        for k in range(self.n - 1):
            for way in range(self.ways):
                self.copy(way, k).wait_send()


class RowScatter:
    def __init__(self, parts, value, hold, sems):
        self.parts, self.value, self.hold = parts, value, hold
        self.send_sem, self.recv_sem = sems
        self.me, self.other, self.across = tensor_place()

    def copy(self, kind, part):
        src, dst = ((0, 1), (1, 2), (0, 3))[kind]
        return remote(
            self.hold.at[src, part],
            self.hold.at[dst, part],
            self.send_sem.at[kind, part],
            self.recv_sem.at[kind, part],
            {"tensor": self.across if kind == 1 else self.other},
        )

    def stage(self, j):
        late = j // (2 * self.parts)
        near = j - 2 * self.parts
        stage = (1 - late) * (j % 2) + late * (2 + near // self.parts)
        return stage, (1 - late) * (j // 2) + late * (near % self.parts)

    def owner(self, j):
        stage, part = self.stage(j)
        x, core = self.me // 2, self.me % 2
        return 2 * ((x + 1 - stage // 2) % 2) + (core + 1 - stage % 2) % 2, part

    def step(self, j, store, wait=True):
        stage, part = self.stage(j)

        @pl.when(stage == 0)
        def _():
            self.hold[0, part] = self.value[...].astype(BF16)
            self.copy(0, part).start()

        @pl.when(stage == 1)
        def _():
            self.copy(0, part).wait_recv()
            self.hold[1, part] = (self.value[...].astype(F32) + self.hold[1, part].astype(F32)).astype(BF16)
            self.copy(1, part).start()

        @pl.when(stage == 2)
        def _():
            self.copy(0, part).wait_send()
            self.hold[0, part] = self.value[...].astype(BF16)
            self.copy(2, part).start()

        @pl.when(stage == 3)
        def _():
            value = self.value[...].astype(F32)
            store(part, value + self.arrived(part) if wait else value)

    def arrived(self, part):
        self.copy(2, part).wait_recv()
        self.copy(1, part).wait_recv()
        return self.hold[3, part].astype(F32) + self.hold[2, part].astype(F32)

    def finish(self):
        for part in range(self.parts):
            for kind in (1, 2):
                self.copy(kind, part).wait_send()


def back_kernel(n, *refs):
    (normed_ref, g_ref, u_ref, dz_ref, wo_ref), refs = refs[:5], refs[5:]
    ins, refs = refs[:15], refs[15:]
    (out_ref, gout_ref, gz_ref), refs = refs[:3], refs[3:]
    outs, refs = refs[:5], refs[5:]
    scratch, refs = refs[:7], refs[7:]
    normed, dz, wo, g_cols, u_cols, out_slots, z_slots, hold, terms, mixed, load_sem, stream_sem, out_sem = refs[:13]
    sems = refs[13:]

    k = pl.program_id(0)
    blocks = 4
    piece = out_ref.shape[1]
    length = blocks * BLOCK
    count = g_ref.shape[1] // n
    half = gz_ref.shape[1] // 2
    place, at = ring_place(n)

    loads = [
        pltpu.make_async_copy(src, dst, load_sem.at[i])
        for i, (src, dst) in enumerate(((normed_ref, normed), (dz_ref, dz), (wo_ref, wo)))
    ]

    def streams(k):
        copies = []
        for way in (0, 1):
            d = at(place - (1 - 2 * way) * (1 + k))
            for i, (src, dst) in enumerate(((g_ref, g_cols), (u_ref, u_cols))):
                copies.append(
                    pltpu.make_async_copy(
                        src.at[:, span(d * count, count, 128)], dst.at[way], stream_sem.at[i, way]
                    )
                )
        return copies

    @pl.when(k == 0)
    def _():
        for copy in streams(0) + loads:
            copy.start()
        greet(n)

    backward_block(k // blocks, k % blocks, *ins, *outs, *scratch)

    @pl.when(k == 0)
    def _():
        for copy in loads:
            copy.wait()

    for copy in streams(k):
        copy.wait()

    rows = RowScatter(2, mixed, hold, sems[4:6])
    owner = rows.owner(k)
    own_rows = span(owner[1] * length + owner[0] * piece, piece, 16)

    for ring, (from_cols, to_cols) in enumerate(((g_cols, normed), (u_cols, dz))):
        for way in (0, 1):
            value = dot_tn(from_cols[way], to_cols[:, pl.ds(way * half, half)])
            terms[ring, way] = value.astype(BF16)
    mixed[...] = dot(normed[own_rows, :], wo[...]).astype(BF16)

    out_ring = RingScatter(n, terms.at[0], out_slots, sems[0:2])
    z_ring = RingScatter(n, terms.at[1], z_slots, sems[2:4])
    for way in (0, 1):
        out_ring.step(way, k)
        z_ring.step(way, k)

    @pl.when(k < n - 1)
    def _():
        for copy in streams(k + 1):
            copy.start()

    def out_copy(part):
        return pltpu.make_async_copy(hold.at[2, part], out_ref.at[part], out_sem.at[part])

    def store(part, value):
        hold[2, part] = value.astype(BF16)
        out_copy(part).start()

    rows.step(k, store)

    @pl.when(k == n - 1)
    def _():
        for way in (0, 1):
            at = pl.ds(way * half, half)
            gout_ref[at, :] = out_ring.last(way).T
            gz_ref[:, at] = z_ring.last(way)

    @pl.when(k == n - 1)
    def _():
        rows.finish()
        out_ring.finish()
        z_ring.finish()
        for part in range(2):
            out_copy(part).wait()


def backward_all(n, small, piece, normed, g, u, dz, w_out, dy, x, cx, bc, cbc, dt, marks, states, shared):
    seqs, length, channels = x.shape
    n2, heads = bc.shape[2], dt.shape[1]
    tokens, model = g.shape
    count = model // n
    blocks = length // BLOCK
    sem = pltpu.SemaphoreType.DMA
    anywhere = pl.BlockSpec(memory_space=pl.ANY)
    ins, outs = backward_specs(channels, n2, heads, small, lambda k: (k // blocks, blocks - 1 - k % blocks))
    whole = lambda *shape: pl.BlockSpec(shape, lambda k: (0,) * len(shape))
    return pl.pallas_call(
        functools.partial(back_kernel, n),
        grid=(n,),
        in_specs=[anywhere] * 5 + ins,
        out_specs=[anywhere, whole(channels, count), whole(count, channels)] + outs,
        out_shape=[
            jax.ShapeDtypeStruct((seqs, piece, model), BF16),
            jax.ShapeDtypeStruct((channels, count), F32),
            jax.ShapeDtypeStruct((count, channels), F32),
        ]
        + backward_outs(seqs, length, channels, n2, heads, small),
        scratch_shapes=backward_scratch(channels, n2, heads)
        + [
            pltpu.VMEM((tokens, channels), BF16),
            pltpu.VMEM((tokens, channels), BF16),
            pltpu.VMEM((channels, model), BF16),
            pltpu.VMEM((2, tokens, count), BF16),
            pltpu.VMEM((2, tokens, count), BF16),
            pltpu.VMEM((2, n, count, channels // 2), BF16),
            pltpu.VMEM((2, n, count, channels // 2), BF16),
            pltpu.VMEM((4, seqs, piece, model), BF16),
            pltpu.VMEM((2, 2, count, channels // 2), BF16),
            pltpu.VMEM((piece, model), BF16),
            sem((3,)),
            sem((2, 2)),
            sem((seqs,)),
        ]
        + [sem((2, n - 1))] * 4
        + [sem((3, seqs))] * 2,
        compiler_params=pltpu.CompilerParams(
            collective_id=1, has_side_effects=True, vmem_limit_bytes=127 * 2**19
        ),
        name="backward_all",
    )(normed, g, u, dz, w_out, dy, x, cx, bc, cbc, dt, marks, states, *shared)


class Fold:
    def __init__(self, n, total, came, sems):
        self.total, self.came = total, came
        self.send_sem, self.recv_sem = sems
        dp = lax.axis_index("dp")
        _, other, across = tensor_place()
        partners, ahead = [], 1
        while ahead < n:
            partners.append({"dp": dp + ahead * (1 - 2 * ((dp // ahead) % 2))})
            ahead *= 2
        self.over_dp = partners
        self.partners = partners + [{"tensor": other}, {"tensor": across}]

    def copy(self, r):
        return remote(
            self.total.at[r], self.came.at[r], self.send_sem.at[r], self.recv_sem.at[r], self.partners[r]
        )

    def start(self, r):
        self.copy(r).start()

    def take(self, r):
        self.copy(r).wait_recv()
        self.total[r + 1] = self.total[r] + self.came[r]

    def finish(self):
        for r in range(len(self.partners)):
            self.copy(r).wait_send()


def in_kernel(
    n, u_hbm, dz_hbm, dx_hbm, wz_hbm, wx_hbm, wb_hbm, dbc_hbm, gz_hbm, gx_in, gbc_in, gh_in, gate_in, gain_ref,
    din_ref, gx_ref, gb_ref, sums_ref, dots_ref, pre_ref,
    u_ref, dz_ref, dx_ref, wz_ref, wx_ref, wb_ref, dbc_ref,
    x_slots, b_slots, hold, bc_hold, x_terms, b_terms, in_value, bc_value, low, swap, own_in, pre, pre_dp, pre_tensor, total, came, load_sem, u_sem, *sems,
):
    seqs, piece = din_ref.shape[:2]
    tokens, model = u_ref.shape
    length = tokens // seqs
    count = model // n
    half = gx_ref.shape[2] // 2
    me, other, across = tensor_place()
    core = me % 2

    moves = (
        (dbc_hbm, dbc_ref),
        (dx_hbm, dx_ref),
        (dz_hbm, dz_ref),
        (wz_hbm, wz_ref),
        (wx_hbm, wx_ref),
        (wb_hbm, wb_ref),
        (gz_hbm, gx_ref.at[0]),
    )
    loads = [pltpu.make_async_copy(src, dst, load_sem.at[i]) for i, (src, dst) in enumerate(moves)]
    place, at_place = ring_place(n)
    u_copies = []
    for ahead in (-1, 1, -2, 2, -3, 3, 4, 0):
        cols = span(at_place(place + ahead) * count, count, 128)
        u_copies.append(pltpu.make_async_copy(u_hbm.at[:, cols], u_ref.at[:, cols], u_sem.at[ahead + 3]))
    for load in loads[:2] + u_copies[:2] + loads[2:] + u_copies[2:]:
        load.start()

    bc_rows = RowScatter(seqs, bc_value, bc_hold, sems[0:2])
    in_rows = RowScatter(seqs, in_value, hold, sems[2:4])
    x_ring = RingScatter(n, x_terms, x_slots, sems[4:6])
    b_ring = RingScatter(n, b_terms, b_slots, sems[6:8], 1, 1 - 2 * core)
    pair_send, pair_recv, swap_send, swap_recv = sems[8:12]
    dp_send, dp_recv, tensor_send, tensor_recv = sems[14:18]
    fold = Fold(n, total, came, sems[12:14])
    rounds = len(fold.partners)
    pair = remote(low.at[0], low.at[1], pair_send, pair_recv, {"tensor": other})

    total[0] = jnp.zeros_like(total[0])
    total[0, 0:6, :] = gx_in[0:6, :]
    total[0, 6:7, :] = gate_in[...]
    steps = gh_in[...].T
    total[0, 7:8, 0 : steps.shape[1]] = steps[0:1, :]
    total[0, 7:8, 128 : 128 + steps.shape[1]] = steps[1:2, :]
    total[0, 8:13, 0 : gbc_in.shape[1]] = gbc_in[0:5, :]
    pre[...] = jnp.zeros_like(pre)
    dp_now = lax.axis_index("dp")
    greet(
        n,
        fold.over_dp
        + [{"dp": (dp_now + o) % n} for o in range(1, n)]
        + [{"tensor": (me + o) % 4} for o in range(1, 4)],
    )
    def rows_at(t, part):
        return span(part * length + t * piece, piece, 16)

    def bc_store(part, value):
        low[0, part] = value.astype(BF16)

    def bc_step(j):
        t, part = bc_rows.owner(j)
        bc_value[...] = dbc_ref[rows_at(t, part), :].astype(F32)
        bc_rows.step(j, bc_store)

    def add_pre(at):
        pre[...] += jnp.sum(in_value[...] * u_ref[at, :].astype(F32), axis=0, keepdims=True)

    def store(part, value):
        in_value[...] = value + dot_nt(low[0, part], wb_ref[...])
        own_in[part] = in_value[...]
        add_pre(rows_at(me, part))

    def row_term(j):
        at = rows_at(*in_rows.owner(j))
        in_value[...] = dot_nt(dz_ref[at, :], wz_ref[...]) + dot_nt(dx_ref[at, :], wx_ref[...])

    def row_step(j):
        in_rows.step(j, store, wait=False)

        @pl.when(j < 3 * seqs)
        def _():
            add_pre(rows_at(*in_rows.owner(j)))

    def x_term(k):
        for way in (0, 1):
            cols = span(x_ring.owner(way, k) * count, count, 128)
            x_terms[way] = dot_tn(u_ref[:, cols], dx_ref[:, pl.ds(way * half, half)])

    def x_step(k):
        for way in (0, 1):
            x_ring.step(way, k)

    def b_step(k):
        cols = span(b_ring.owner(0, k) * count + core * count // 2, count // 2, 128)
        value = 0.0
        for t, which in ((me, 0), (other, 1)):
            for part in range(seqs):
                value = value + dot_tn(u_ref[rows_at(t, part), cols], low[which, part])
        b_terms[0] = value
        b_ring.step(0, k)

    loads[0].wait()
    for part in range(seqs):
        bc_step(2 * part)
        bc_step(2 * seqs + part)
    loads[1].wait()
    for copy in u_copies[:2]:
        copy.wait()
    x_term(0)
    x_step(0)
    for load in loads[2:] + u_copies[2:]:
        load.wait()
    row_term(0)
    row_step(0)
    for part in range(seqs):
        bc_step(2 * part + 1)

    wide = model // 8
    gain = gain_ref[...]

    def dp_copy(o):
        ref = pre_dp.at[dp_now]
        return remote(ref, ref, dp_send.at[o], dp_recv.at[o], {"dp": (dp_now + o) % n})

    def tensor_copy(o):
        ref = pre_tensor.at[me]
        return remote(ref, ref, tensor_send.at[o], tensor_recv.at[o], {"tensor": (me + o) % 4})

    cross = remote(swap.at[0], swap.at[1], swap_send.at[0], swap_recv.at[0], {"tensor": across})
    back = remote(swap.at[2], swap.at[3], swap_send.at[1], swap_recv.at[1], {"tensor": other})

    def at_step(k, when, what):
        pl.when(k == when)(what)

    def own_bc():
        for part in range(seqs):
            bc_step(3 * seqs + part)
        pair.start()

    def send_pre():
        for i in range(8):
            at = slice(i * wide, (i + 1) * wide)
            pre_dp[dp_now, i : i + 1, :] = pre[:, at] / gain[:, at]
        for o in range(1, n):
            dp_copy(o).start()

    def pass_pre():
        for o in range(1, n):
            dp_copy(o).wait_recv()
        pre_tensor[me] = sum(pre_dp[d] for d in range(n))
        for o in range(1, 4):
            tensor_copy(o).start()

    def take_pre():
        for o in range(1, 4):
            tensor_copy(o).wait_recv()
        pre_ref[...] = (pre_tensor[0] + pre_tensor[1]) + (pre_tensor[2] + pre_tensor[3])

    def send_bc():
        swap[0] = b_ring.last(0)
        cross.start()

    def pass_bc():
        cross.wait_recv()
        swap[2] = swap[0] + swap[1]
        back.start()
        gb_ref[span(core * count // 2, count // 2, 16), :] = swap[2]

    def step(k, _):
        at_step(k, 5, send_pre)
        at_step(k, n - 1, send_bc)

        @pl.when(2 * k - 1 < 4 * seqs)
        def _():
            row_term(2 * k - 1)
            row_step(2 * k - 1)

        x_term(k)
        x_step(k)
        at_step(k, 2, pair.wait_recv)

        @pl.when((k >= 2) & (k <= 6))
        def _():
            b_step(jnp.maximum(k - 2, 2 * (k - 3)))

        @pl.when(2 * k < 4 * seqs)
        def _():
            row_term(2 * k)
            row_step(2 * k)

        at_step(k, 1, own_bc)

        @pl.when((k >= 4) & (k <= 6))
        def _():
            b_step(2 * (k - 3) + 1)

        at_step(k, 6, pass_pre)
        at_step(k, n - 1, pass_bc)
        at_step(k, n - 1, take_pre)
        for r in range(rounds + 1):

            @pl.when(k == r + 1)
            def _():
                if r > 0:
                    fold.take(r - 1)
                if r < rounds:
                    fold.start(r)

        return 0

    lax.fori_loop(1, n, step, 0)
    for way in (0, 1):
        gx_ref[1, :, pl.ds(way * half, half)] = x_ring.last(way)
    sums_ref[0:8, :] = total[rounds - 2, 0:8, :]
    sums_ref[8:16, :] = total[rounds, 8:16, :]
    for part in range(seqs):
        value = own_in[part] + in_rows.arrived(part)
        din_ref[part] = value.astype(BF16)
        inner = jnp.sum(value * u_ref[rows_at(me, part), :].astype(F32), axis=1, keepdims=True)
        dots_ref[part] = jnp.broadcast_to(inner, (piece, 128))
    back.wait_recv()
    gb_ref[span((1 - core) * count // 2, count // 2, 16), :] = swap[3]
    for o in range(1, n):
        dp_copy(o).wait_send()
    for o in range(1, 4):
        tensor_copy(o).wait_send()
    for copy in (pair, cross, back):
        copy.wait_send()
    for part in (bc_rows, in_rows, x_ring, b_ring, fold):
        part.finish()


def scatter_in(n, piece, u, dz, dx, w_z, w_x, w_bc, dbc, grad_z, gx, gbc, gh, grad_gate, gain):
    tokens, model = u.shape
    width = dz.shape[1]
    small = dbc.shape[1]
    seqs = tokens // (4 * piece)
    count = model // n
    rounds = 5
    sem = pltpu.SemaphoreType.DMA
    vmem = pl.BlockSpec(memory_space=pltpu.VMEM)
    anywhere = pl.BlockSpec(memory_space=pl.ANY)
    big = (u, dz, dx, w_z, w_x, w_bc, dbc)
    return pl.pallas_call(
        functools.partial(in_kernel, n),
        in_specs=[anywhere] * 8 + [vmem] * 5,
        out_specs=[vmem] * 6,
        out_shape=[
            jax.ShapeDtypeStruct((seqs, piece, model), BF16),
            jax.ShapeDtypeStruct((2, count, width), F32),
            jax.ShapeDtypeStruct((count, small), F32),
            jax.ShapeDtypeStruct((16, width), F32),
            jax.ShapeDtypeStruct((seqs, piece, 128), F32),
            jax.ShapeDtypeStruct((8, model // 8), F32),
        ],
        scratch_shapes=[pltpu.VMEM(a.shape, BF16) for a in big]
        + [
            pltpu.VMEM((2, n, count, width // 2), BF16),
            pltpu.VMEM((1, n, count // 2, small), BF16),
            pltpu.VMEM((4, seqs, piece, model), BF16),
            pltpu.VMEM((4, seqs, piece, small), BF16),
            pltpu.VMEM((2, count, width // 2), F32),
            pltpu.VMEM((1, count // 2, small), F32),
            pltpu.VMEM((piece, model), F32),
            pltpu.VMEM((piece, small), F32),
            pltpu.VMEM((2, seqs, piece, small), BF16),
            pltpu.VMEM((4, count // 2, small), F32),
            pltpu.VMEM((seqs, piece, model), F32),
            pltpu.VMEM((1, model), F32),
            pltpu.VMEM((n, 8, model // 8), F32),
            pltpu.VMEM((4, 8, model // 8), F32),
            pltpu.VMEM((rounds + 1, 16, width), F32),
            pltpu.VMEM((rounds, 16, width), F32),
            sem((len(big),)),
            sem((n,)),
        ]
        + [sem((3, seqs))] * 4 + [sem((2, n - 1))] * 2 + [sem((1, n - 1))] * 2 + [sem(())] * 2 + [sem((2,))] * 2
        + [sem((rounds,))] * 2 + [sem((n,))] * 2 + [sem((4,))] * 2,
        compiler_params=pltpu.CompilerParams(
            collective_id=2, has_side_effects=True, vmem_limit_bytes=63 * 2**20
        ),
        name="scatter_in",
    )(*big, grad_z, gx, gbc, gh, grad_gate, gain)


def finish_kernel(
    d_in_ref, hidden_ref, cot_ref, mixed_ref, scale_ref, dots_ref, gain_ref, gzx_in, gout_in, gb_in, sums_ref,
    out_ref, d_hidden_ref, gzx_ref, gout_ref, gb_ref, taps_ref, taps_bc_ref,
):
    model = gain_ref.shape[1]
    x = hidden_ref[0].astype(F32)
    scale = scale_ref[0][:, 0:1]
    factor = scale * scale * dots_ref[0][:, 0:1] / model
    d_hidden_ref[0] = cot_ref[0].astype(F32) + scale * (gain_ref[...] * d_in_ref[0].astype(F32)) - x * factor
    out_ref[0] = (x + mixed_ref[0].astype(F32)).astype(BF16)
    gzx_ref[...] = gzx_in[...]
    gout_ref[...] = gout_in[...]
    gb_ref[...] = gb_in[...].T[: gb_ref.shape[0], :]
    taps_ref[...] = sums_ref[0 : taps_ref.shape[0], :]
    taps_bc_ref[...] = sums_ref[8 : 8 + taps_bc_ref.shape[0], : taps_bc_ref.shape[1]]


def finish(d_in, hidden, cotangent, mixed, scale, dots, gain, grad_zx, grad_out, grad_bc, sums, columns, n2):
    seqs, piece, model = hidden.shape
    count, width = grad_zx.shape[1:]
    steps = 2
    rows = piece // steps
    grid = seqs * steps
    piece_rows = lambda w: pl.BlockSpec((1, rows, w), lambda i: (i // steps, i % steps, 0))
    whole = lambda *shape: pl.BlockSpec(shape, lambda i: (0,) * len(shape))
    zx = pl.BlockSpec((1, 2 * count // grid, width), lambda i: (i // (grid // 2), i % (grid // 2), 0))
    down = lambda a, w: pl.BlockSpec((a.shape[0] // grid, w), lambda i: (i, 0))
    return pl.pallas_call(
        finish_kernel,
        grid=(grid,),
        in_specs=[piece_rows(model)] * 4
        + [piece_rows(128)] * 2
        + [whole(1, model), zx, down(grad_out, grad_out.shape[1]), whole(*grad_bc.shape)]
        + [whole(*sums.shape)],
        out_specs=[piece_rows(model)] * 2
        + [zx, down(grad_out, grad_out.shape[1]), whole(columns, count), whole(5, width), whole(5, n2)],
        out_shape=[
            jax.ShapeDtypeStruct(hidden.shape, BF16),
            jax.ShapeDtypeStruct(hidden.shape, F32),
            jax.ShapeDtypeStruct(grad_zx.shape, F32),
            jax.ShapeDtypeStruct(grad_out.shape, F32),
            jax.ShapeDtypeStruct((columns, count), F32),
            jax.ShapeDtypeStruct((5, width), F32),
            jax.ShapeDtypeStruct((5, n2), F32),
        ],
        compiler_params=pltpu.CompilerParams(vmem_limit_bytes=62 * 2**20),
        name="finish",
    )(d_in, hidden, cotangent, mixed, scale, dots, gain, grad_zx, grad_out, grad_bc, sums)


def rms_scale(values):
    return lax.rsqrt(jnp.mean(values * values, axis=-1, keepdims=True) + EPS)


def gather_plain(u, g, w_zx, w_bc, w_out):
    w_zx = lax.all_gather(w_zx, "dp", axis=1, tiled=True)
    return (
        lax.all_gather(u, "tensor", axis=1, tiled=True),
        lax.all_gather(g, "tensor", axis=1, tiled=True),
        w_zx[1],
        w_zx[0],
        lax.all_gather(w_bc, "dp", axis=0, tiled=True),
        lax.all_gather(w_out, "dp", axis=1, tiled=True),
    )


def rows_of(values, piece):
    by_seq = values.reshape(-1, 4 * piece, values.shape[-1])
    return lax.psum_scatter(by_seq, "tensor", scatter_dimension=1, tiled=True)


def scatter_out_plain(piece, normed, g, u, dz, w_out):
    return (
        rows_of(dot(normed, w_out), piece),
        lax.psum_scatter(dot_tn(normed, g), "dp", scatter_dimension=1, tiled=True),
        lax.psum_scatter(dot_tn(u, dz), "dp", scatter_dimension=0, tiled=True),
    )


def scatter_in_plain(piece, u, dz, dx, w_z, w_x, w_bc, dbc):
    low = lax.psum(dbc.astype(F32), "tensor").astype(BF16)
    d_in = rows_of(dot_nt(dz, w_z) + dot_nt(dx, w_x), piece)
    first = lax.axis_index("tensor") * piece
    own = lax.dynamic_slice_in_dim(low.reshape(-1, 4 * piece, low.shape[1]), first, piece, 1)
    d_in = d_in + jnp.einsum("slc,dc->sld", own, w_bc, preferred_element_type=F32)
    return (
        d_in,
        lax.psum_scatter(dot_tn(u, dx), "dp", scatter_dimension=0, tiled=True),
        lax.psum_scatter(dot_tn(u, low), "dp", scatter_dimension=0, tiled=True),
    )


def local(
    n_dp,
    n_tensor,
    hidden,
    pre_gain,
    w_zx,
    w_bcdt,
    conv_x,
    conv_bc,
    dt_bias,
    a_log,
    d_skip,
    gate_gain,
    w_out,
    cotangent,
    segments,
):
    seqs, piece, model = hidden.shape
    length = segments.shape[1]
    tokens = seqs * length
    heads = dt_bias.shape[0]
    channels = conv_x.shape[1]
    n2 = conv_bc.shape[1]
    columns = w_bcdt.shape[1]
    tensor = lax.axis_index("tensor")
    kernels = n_dp == 8 and n_tensor == 4 and seqs == 2 and length == 4 * BLOCK

    x_piece = hidden.astype(F32)
    spread = jnp.asarray(spread_matrix(heads, channels), BF16)
    pick = jnp.asarray(pick_matrix(heads, channels), BF16)
    shared = (conv_x, conv_bc, dt_bias[None], a_log[None], d_skip[None], spread, pick)
    if kernels:
        u, g, w_x, w_z, w_bc, w_o, cx, x, cbc, bc, dt, states, normed, dz, dy, grad_gate, scale_in, marks = forward_all(
            n_dp, hidden, cotangent, w_zx, w_bcdt.T, w_out, pre_gain[None], gate_gain[None], segments, shared
        )
        g = g.reshape(tokens, model)
    else:
        scale_in = rms_scale(x_piece)
        u_piece = (x_piece * scale_in * pre_gain).astype(BF16)
        w_bc_piece = jnp.pad(w_bcdt, ((0, 0), (0, -columns % 128)))
        u, g, w_x, w_z, w_bc, w_o = gather_plain(u_piece, cotangent, w_zx, w_bc_piece, w_out)
        u = u.reshape(tokens, model)
        g = g.reshape(tokens, model)
        x = dot(u, w_x).reshape(seqs, length, channels)
        z = dot(u, w_z)
        bc_dt = dot(u, w_bc).reshape(seqs, length, -1)
        bc = bc_dt[:, :, :n2]
        dt = jnp.swapaxes(lax.dynamic_slice_in_dim(bc_dt, n2 + tensor * heads, heads, 2), 1, 2)
        marks = row_marks(segments)
        y, cx, cbc, states = ssd_forward(x, bc, dt, marks, shared)
        d_normed = dot_nt(g, w_o)
        sig_z = sigmoid(z)
        silu_z = z * sig_z
        y_flat = y.reshape(tokens, channels)
        gated = y_flat * silu_z
        scaled = d_normed * gate_gain
        sums = jnp.stack([jnp.sum(gated * gated, axis=1), jnp.sum(scaled * gated, axis=1)])
        sums = lax.psum(sums, "tensor") / (channels * n_tensor)
        inverse = lax.rsqrt(sums[0] + EPS)[:, None]
        normed = (gated * inverse * gate_gain).astype(BF16)
        grad_gate = jnp.sum(d_normed * gated * inverse, axis=0)[None]
        d_gated = inverse * scaled - gated * inverse**3 * sums[1][:, None]
        dy = (d_gated * silu_z).astype(BF16)
        dz = (d_gated * y_flat * (sig_z * (1.0 + z * (1.0 - sig_z)))).astype(BF16)
        x, bc = x.astype(BF16), bc.astype(BF16)

    back_args = (dy.reshape(seqs, length, channels), x, cx, bc, cbc, dt, marks, states, shared)
    if kernels:
        mixed, grad_out, grad_z, *rest = backward_all(n_dp, w_bc.shape[1], piece, normed, g, u, dz, w_o, *back_args)
    else:
        mixed, grad_out, grad_z = scatter_out_plain(piece, normed, g, u, dz, w_o)
        rest = ssd_backward(w_bc.shape[1], *back_args)
    dx, dbc, gx, gbc, gh = rest
    in_args = (piece, u, dz, dx.reshape(tokens, channels), w_z, w_x, w_bc, dbc.reshape(tokens, -1))
    if kernels:
        d_in, grad_zx, grad_bc, sums, dots, grad_pre = scatter_in(
            n_dp, *in_args, grad_z, gx, gbc, gh, grad_gate, pre_gain[None]
        )
        grad_pre = grad_pre.reshape(model)
        out_hidden, d_hidden, grad_zx, grad_out, grad_bc, grad_conv_x, grad_conv_bc = finish(
            d_in, hidden, cotangent, mixed, scale_in, dots, pre_gain[None], grad_zx, grad_out, grad_bc, sums, columns, n2
        )
        grad_bc = grad_bc.T
    else:
        d_in, grad_x, grad_bc = scatter_in_plain(*in_args)
        grad_zx = jnp.stack([grad_z, grad_x])
        grad_pre = jnp.sum(d_in * x_piece * scale_in, axis=(0, 1))
        dots = scale_in * jnp.sum(d_in * pre_gain * x_piece, axis=-1, keepdims=True)
        steps = jnp.pad(gh[:, :2].T, ((0, 0), (0, channels - heads)))
        sums = lax.psum(jnp.concatenate([gx[:6], grad_gate, steps]), "dp")
        sums = jnp.concatenate([sums[:7], jnp.concatenate([sums[7, :128], sums[8, : channels - 128]])[None]])
        grad_conv_bc, grad_pre = lax.psum((gbc[:5], grad_pre), ("dp", "tensor"))
        grad_conv_x = sums[:5]
        grad_bc = grad_bc[:, :columns]
        out_hidden = (x_piece + mixed).astype(BF16)
        d_hidden = cotangent.astype(F32) + scale_in * (pre_gain * d_in) - x_piece * (scale_in**2 * dots / model)

    return (
        out_hidden,
        d_hidden,
        grad_pre,
        grad_zx,
        grad_bc,
        grad_conv_x,
        grad_conv_bc,
        sums[7, :heads],
        sums[7, 128 : 128 + heads],
        sums[5].reshape(heads, -1).sum(axis=1),
        sums[6],
        grad_out,
    )


def solution(mesh):
    placed = (
        P("dp", "tensor", None),
        P(),
        P(None, "dp", "tensor"),
        P("dp", None),
        P(None, "tensor"),
        P(),
        P("tensor"),
        P("tensor"),
        P("tensor"),
        P("tensor"),
        P("tensor", "dp"),
        P("dp", "tensor", None),
        P("dp", None),
    )
    return jax.shard_map(
        functools.partial(local, mesh.shape["dp"], mesh.shape["tensor"]),
        mesh=mesh,
        in_specs=placed,
        out_specs=(
            P("dp", "tensor", None),
            P("dp", "tensor", None),
            P(),
            P(None, "dp", "tensor"),
            P("dp", None),
            P(None, "tensor"),
            P(),
            P("tensor"),
            P("tensor"),
            P("tensor"),
            P("tensor"),
            P("tensor", "dp"),
        ),
        check_vma=False,
    )
```

```python
import functools

import jax
import jax.numpy as jnp
import numpy as np
from jax import lax
from jax.experimental import pallas as pl
from jax.experimental.pallas import tpu as pltpu
from jax.sharding import PartitionSpec as P

MESH = pl.DeviceIdType.MESH
EPS = 1e-05
BLOCK = 256
F32 = jnp.float32
BF16 = jnp.bfloat16
EXACT = lax.Precision.HIGHEST
LOG2E = 1.4426950408889634
NEG = -1e30


def sigmoid(v):
    return 0.5 * jnp.tanh(0.5 * v) + 0.5


def split3(v):
    hi = v.astype(BF16)
    rest = v - hi.astype(F32)
    mid = rest.astype(BF16)
    low = (rest - mid.astype(F32)).astype(BF16)
    return hi, mid, low


def dot(a, b):
    return jnp.dot(a, b, preferred_element_type=F32)


def dot_nt(a, b):
    return lax.dot_general(a, b, (((1,), (1,)), ((), ())), preferred_element_type=F32)


def dot_tn(a, b):
    return lax.dot_general(a, b, (((0,), (0,)), ((), ())), preferred_element_type=F32)


def softplus(v):
    return jnp.maximum(v, 0.0) + jnp.log1p(jnp.exp(-jnp.abs(v)))


def head_rows(raw, dt_bias, a_log):
    q = raw.shape[1]
    upto = (
        lax.broadcasted_iota(jnp.int32, (q, q), 0) <= lax.broadcasted_iota(jnp.int32, (q, q), 1)
    ).astype(F32)
    biased = raw + dt_bias
    step = softplus(biased)
    rate = -jnp.exp(a_log) * step
    cum = jnp.dot(rate, upto, precision=EXACT, preferred_element_type=F32) * LOG2E
    return biased, step, rate, cum


def exact_nt(a, b):
    a_hi, a_mid, _ = split3(a)
    b_hi, b_mid, _ = split3(b)
    return dot_nt(a_hi, b_hi) + dot_nt(a_hi, b_mid) + dot_nt(a_mid, b_hi)


def turned(row):
    k = row.shape[1]
    own = lax.broadcasted_iota(jnp.int32, (k, k), 0) == lax.broadcasted_iota(jnp.int32, (k, k), 1)
    return jnp.sum(jnp.where(own, row, 0.0), axis=1, keepdims=True)


def to_columns(rows):
    return jnp.concatenate([rows, jnp.zeros((128 - rows.shape[0], rows.shape[1]), F32)], axis=0).T


def head_columns(reads, last, step, cum, third):
    cum_end = cum[:, BLOCK - 1 : BLOCK]
    rows = []
    for factor in (reads * jnp.exp2(cum), last * jnp.exp2(cum_end - cum) * step):
        hi, mid, _ = split3(factor)
        rows += [hi.astype(F32), mid.astype(F32)]
    cols = to_columns(jnp.concatenate(rows + [third], axis=0))
    return cols[:, 4 * cum.shape[0] :], cols.astype(BF16), jnp.exp2(cum_end)


def log2_step(step):
    return jnp.log(jnp.maximum(step, 1e-37)) * LOG2E


def forward_block(
    block, x, bc, dt, marks_ref, taps_x_ref, taps_bc_ref, bias_ref, alog_ref, skip_ref, spread_ref, pick_ref,
    y_ref, cx_ref, cbc_ref, states_ref,
    xs, bs, state, mask_bias,
):
    q = BLOCK
    heads = dt.shape[0]
    channels = x.shape[-1]
    width = channels // heads

    @pl.when(block == 0)
    def _():
        xs[0:8, :] = jnp.zeros((8, xs.shape[1]), F32)
        bs[0:8, :] = jnp.zeros((8, bs.shape[1]), F32)
        state[...] = jnp.zeros_like(state)

    marks = to_columns(marks_ref[0])
    lag_masks = [marks[:, k : k + 1] for k in range(3)]

    def conv(hold, at, taps_ref):
        out = taps_ref[4:5, at] + taps_ref[3:4, at] * hold[8 : 8 + q, at]
        for lag in (1, 2, 3):
            out = out + (lag_masks[lag - 1] * hold[8 - lag : 8 - lag + q, at]) * taps_ref[3 - lag : 4 - lag, at]
        return out

    bs[8 : 8 + q, :] = bc
    xs[8 : 8 + q, :] = x
    cbc = conv(bs, slice(None), taps_bc_ref)
    cbc_ref[0] = cbc
    bc = cbc * sigmoid(cbc)
    n = bc.shape[1] // 2
    scores = exact_nt(bc[:, n:], bc[:, :n])
    b_mat, c_mat = bc[:, :n].astype(BF16), bc[:, n:].astype(BF16)
    b_turned = b_mat.T

    _, step, _, cum = head_rows(dt, turned(bias_ref[...]), turned(alog_ref[...]))
    cols, factors, carry = head_columns(marks_ref[0, 3:4, :], marks_ref[0, 4:5, :], step, cum, cum)
    source = cum - log2_step(step)
    carry_e = jnp.sum(carry * spread_ref[...].astype(F32), axis=0, keepdims=True)
    skip_e = jnp.sum(turned(skip_ref[...]) * spread_ref[...].astype(F32), axis=0, keepdims=True)

    rows = lax.broadcasted_iota(jnp.int32, (q, q), 0)
    places = lax.broadcasted_iota(jnp.int32, (q, q), 1)
    mask_bias[...] = jnp.where((marks[:, 5:6] == marks_ref[0, 5:6, :]) & (rows >= places), 0.0, NEG)

    half = q // 2
    pair_width = 2 * width
    lane = lax.broadcasted_iota(jnp.int32, (1, pair_width), 1)
    every = slice(0, channels)
    cx = conv(xs, every, taps_x_ref)
    cx_ref[0] = cx
    xb = (cx * sigmoid(cx)).astype(BF16)
    xf = xb.astype(F32)
    stb = state[...].astype(BF16)
    states_ref[0, 0] = stb
    y_ref[...] = dot(c_mat, stb) * dot(factors, pick_ref[:, :channels]) + skip_e * xf
    scaled = (xf * dot(factors, pick_ref[:, channels:])).astype(BF16)
    state[...] = carry_e * state[...] + dot(b_turned, scaled)
    for pair in range(heads // 2):
        at = slice(pair * pair_width, (pair + 1) * pair_width)
        xp = xb[:, at]
        tops, lows = [], []
        for h in (2 * pair, 2 * pair + 1):
            col = cols[:, h : h + 1]
            row = source[h : h + 1, :]
            top = jnp.exp2((col[:half] - row[:, :half]) + mask_bias[:half, :half]) * scores[:half, :half]
            low = jnp.exp2((col[half:] - row) + mask_bias[half:, :]) * scores[half:, :]
            tops.append(top.astype(BF16))
            lows.append(low.astype(BF16))
        top = dot(jnp.concatenate(tops, axis=0), xp[:half])
        low = dot(jnp.concatenate(lows, axis=0), xp)
        first = lane < width
        y_ref[:half, at] += jnp.where(first, top[:half], top[half:])
        y_ref[half:, at] += jnp.where(first, low[:half], low[half:])

    xs[0:8, :] = xs[q : q + 8, :]
    bs[0:8, :] = bs[q : q + 8, :]


def backward_block(
    seq, step_id, dy_ref, x_ref, cx_ref, bc_ref, cbc_ref, dt_ref, marks_ref, states_ref,
    taps_x_ref, taps_bc_ref, bias_ref, alog_ref, skip_ref, spread_ref, pick_ref,
    dx_ref, dbc_ref, gx_ref, gbc_ref, gh_ref,
    ds_x, ds_bc, d_state, mask_bias, d_scores, d_in, row_sums,
):
    q = BLOCK
    heads = dt_ref.shape[1]
    channels = x_ref.shape[-1]
    width = channels // heads

    @pl.when(step_id == 0)
    def _():
        ds_x[:, q : q + 8, :] = jnp.zeros((3, 8, channels), F32)
        ds_bc[:, q : q + 8, :] = jnp.zeros((3, 8, ds_bc.shape[2]), F32)
        d_state[...] = jnp.zeros_like(d_state)

    @pl.when((step_id == 0) & (seq == 0))
    def _():
        gx_ref[...] = jnp.zeros_like(gx_ref)
        gbc_ref[...] = jnp.zeros_like(gbc_ref)
        gh_ref[...] = jnp.zeros_like(gh_ref)

    marks = to_columns(marks_ref[0])
    lag_masks = [marks[:, k : k + 1] for k in range(3)]

    def conv_back(d_out, value, hold, at, taps_ref, grad_ref):
        value = value.astype(F32)
        d_value = d_out * taps_ref[3:4, at]
        grad_ref[3:4, at] += jnp.sum(value * d_out, axis=0, keepdims=True)
        grad_ref[4:5, at] += jnp.sum(d_out, axis=0, keepdims=True)
        for lag in (1, 2, 3):
            hold[lag - 1, 0:q, at] = lag_masks[lag - 1] * d_out
            moved = hold[lag - 1, lag : lag + q, at]
            d_value = d_value + moved * taps_ref[3 - lag : 4 - lag, at]
            grad_ref[3 - lag : 4 - lag, at] += jnp.sum(value * moved, axis=0, keepdims=True)
            hold[lag - 1, q : q + 8, at] = hold[lag - 1, 0:8, at]
        return d_value

    cbc = cbc_ref[0]
    bc = cbc * sigmoid(cbc)
    n = bc.shape[1] // 2
    scores = exact_nt(bc[:, :n], bc[:, n:])
    b_mat, c_mat = bc[:, :n].astype(BF16), bc[:, n:].astype(BF16)
    c_turned = c_mat.T

    a_log = turned(alog_ref[...])
    biased, step, rate, cum = head_rows(dt_ref[0], turned(bias_ref[...]), a_log)
    source = cum - log2_step(step)
    cols, factors, carry = head_columns(marks_ref[0, 3:4, :], marks_ref[0, 4:5, :], step, cum, source)
    carry_e = jnp.sum(carry * spread_ref[...].astype(F32), axis=0, keepdims=True)
    skip_e = jnp.sum(turned(skip_ref[...]) * spread_ref[...].astype(F32), axis=0, keepdims=True)

    rows = lax.broadcasted_iota(jnp.int32, (q, q), 0)
    places = lax.broadcasted_iota(jnp.int32, (q, q), 1)
    mask_bias[...] = jnp.where((marks[:, 5:6] == marks_ref[0, 5:6, :]) & (rows <= places), 0.0, NEG)

    half = q // 2
    pair_width = 2 * width
    lane = lax.broadcasted_iota(jnp.int32, (1, pair_width), 1)
    first = lane < width
    d_scores[...] = jnp.zeros_like(d_scores)
    col_h = jnp.zeros((heads, q), F32)
    head_row = lax.broadcasted_iota(jnp.int32, (heads, 3 * half), 0)
    spread = spread_ref[...]
    cx = cx_ref[0]
    xb = (cx * sigmoid(cx)).astype(BF16)
    dyb = dy_ref[0]
    st = states_ref[0, 0]
    dye = dyb.astype(F32) * dot(factors, pick_ref[:, :channels])
    out_h = dot_nt(spread, (dye * dot(c_mat, st)).astype(BF16))
    dye = dye.astype(BF16)
    d_c = dot_nt(dye, st)
    dst = d_state[...].astype(BF16)
    kept = jnp.sum(d_state[...] * st.astype(F32), axis=0, keepdims=True) * carry_e
    carried = jnp.sum(spread.astype(F32) * kept, axis=1, keepdims=True)
    d_state[...] = carry_e * d_state[...] + dot(c_turned, dye)
    xf = xb.astype(F32)
    to_end = dot(factors, pick_ref[:, channels:])
    d_b = dot_nt((xf * to_end).astype(BF16), dst)
    dx_st = dot(b_mat, dst) * to_end
    state_h = dot_nt(spread, (xf * dx_st).astype(BF16))
    d_in[...] = dx_st
    for pair in range(heads // 2):
        at = slice(pair * pair_width, (pair + 1) * pair_width)
        xp, dyp = xb[:, at], dyb[:, at]
        none = jnp.zeros_like(xp)
        x_first, x_second = jnp.where(first, xp, none), jnp.where(first, none, xp)
        g_top = dot_nt(jnp.concatenate([x_first[:half], x_second[:half]], axis=0), dyp)
        g_low = dot_nt(jnp.concatenate([x_first[half:], x_second[half:]], axis=0), dyp[half:])
        tops, lows, d_top, d_low = [], [], 0.0, 0.0
        for which in (0, 1):
            h = 2 * pair + which
            own = slice(which * half, (which + 1) * half)
            col = cols[:, h : h + 1]
            row = cum[h : h + 1, :]
            top = jnp.exp2((row - col[:half]) + mask_bias[:half, :])
            low = jnp.exp2((row[:, half:] - col[half:]) + mask_bias[half:, half:])
            p_top = top * g_top[own]
            p_low = low * g_low[own]
            d_top = d_top + p_top
            d_low = d_low + p_low
            m_top = p_top * scores[:half, :]
            m_low = p_low * scores[half:, half:]
            late = jnp.sum(m_top[:, half:], axis=0, keepdims=True) + jnp.sum(m_low, axis=0, keepdims=True)
            row_sums[h : h + 1, :half] = jnp.sum(m_top[:, :half], axis=0, keepdims=True)
            row_sums[h : h + 1, half:] = late
            parts = split3(jnp.concatenate([m_top[:, :half] + m_top[:, half:], m_low], axis=0))
            col_h = col_h + dot_nt((head_row == h).astype(BF16), jnp.concatenate(parts, axis=1))
            tops.append((top * scores[:half, :]).astype(BF16))
            lows.append((low * scores[half:, half:]).astype(BF16))
        d_scores[:half, :] += d_top
        d_scores[half:, half:] += d_low
        top = dot(jnp.concatenate(tops, axis=0), dyp)
        low = dot(jnp.concatenate(lows, axis=0), dyp[half:])
        d_in[:half, at] += jnp.where(first, top[:half], top[half:])
        d_in[half:, at] += jnp.where(first, low[:half], low[half:])

    everywhere = slice(0, channels)
    dyf = dy_ref[0].astype(F32)
    cx = cx_ref[0]
    sig = sigmoid(cx)
    gx_ref[5:6, :] += jnp.sum(dyf * (cx * sig).astype(BF16).astype(F32), axis=0, keepdims=True)
    d_cx = (d_in[...] + skip_e * dyf) * (sig * (1.0 + cx * (1.0 - sig)))
    dx_ref[0] = conv_back(d_cx, x_ref[0], ds_x, everywhere, taps_x_ref, gx_ref).astype(BF16)

    dsb = d_scores[...].astype(BF16)
    d_b = d_b + dot(dsb, c_mat)
    d_c = d_c + dot_tn(dsb, b_mat)
    sig = sigmoid(cbc)
    d_cbc = jnp.concatenate([d_b, d_c], axis=1) * (sig * (1.0 + cbc * (1.0 - sig)))
    every = slice(0, 2 * n)
    dbc_ref[0, :, every] = conv_back(d_cbc, bc_ref[0], ds_bc, every, taps_bc_ref, gbc_ref).astype(BF16)

    used_h = col_h + state_h
    diff_h = row_sums[...] - col_h + out_h
    since = (rows >= places).astype(F32)
    before = (rows < places).astype(F32)
    d_rate = (
        jnp.dot(diff_h, since, precision=EXACT, preferred_element_type=F32)
        + jnp.dot(state_h, before, precision=EXACT, preferred_element_type=F32)
        + carried
    )
    sig_dt = sigmoid(biased)
    ratio = jnp.where(step < 1e-30, 1.0, sig_dt / jnp.maximum(step, 1e-30))
    d_raw = used_h * ratio - jnp.exp(a_log) * sig_dt * d_rate
    lanes = dbc_ref.shape[2] - 2 * n
    mine = lax.broadcasted_iota(jnp.int32, (heads, lanes), 0) + lax.axis_index("tensor") * heads
    own = (lax.broadcasted_iota(jnp.int32, (heads, lanes), 1) == mine).astype(BF16)
    dbc_ref[0, :, 2 * n :] = dot_tn(d_raw.astype(BF16), own).astype(BF16)
    gh_ref[:, 0:1] += jnp.sum(d_raw, axis=1, keepdims=True)
    gh_ref[:, 1:2] += jnp.sum(d_rate * rate, axis=1, keepdims=True)


def row_marks(segments):
    seqs, length = segments.shape
    blocks = length // BLOCK
    lags = []
    for lag in (1, 2, 3):
        earlier = jnp.pad(segments, ((0, 0), (lag, 0)), constant_values=-1)[:, :length]
        lags.append(earlier == segments)
    grouped = segments.reshape(seqs, blocks, BLOCK)
    before = jnp.pad(segments, ((0, 0), (1, 0)), constant_values=-1)[:, :length].reshape(seqs, blocks, BLOCK)
    reads = (grouped == before[:, :, :1]).reshape(seqs, length)
    last = (grouped == grouped[:, :, -1:]).reshape(seqs, length)
    rows = [m.astype(F32) for m in (*lags, reads, last, segments)]
    return jnp.stack(rows + [jnp.zeros_like(rows[0])] * 2, axis=1)


def spread_matrix(heads, channels):
    width = channels // heads
    return (np.arange(heads)[:, None] == np.arange(channels)[None, :] // width).astype(np.float32)


def pick_matrix(heads, channels):
    spread = spread_matrix(heads, channels)
    out = np.zeros((128, 2 * channels), np.float32)
    for part in range(4):
        at = slice(part // 2 * channels, (part // 2 + 1) * channels)
        out[part * heads : (part + 1) * heads, at] = spread
    return out


def shared_specs(channels, n2, heads):
    full = lambda *shape: pl.BlockSpec(shape, lambda *i: (0,) * len(shape))
    return [
        full(5, channels),
        full(5, n2),
        full(1, heads),
        full(1, heads),
        full(1, heads),
        full(heads, channels),
        full(128, 2 * channels),
    ]


def forward_scratch(channels, n2):
    return [
        pltpu.VMEM((BLOCK + 8, channels), F32),
        pltpu.VMEM((BLOCK + 8, n2), F32),
        pltpu.VMEM((n2 // 2, channels), F32),
        pltpu.VMEM((BLOCK, BLOCK), F32),
    ]


def forward_kernel(x_ref, bc_ref, dt_ref, *refs):
    y_ref = refs[8]
    forward_block(pl.program_id(1), x_ref[0], bc_ref[0], dt_ref[0], *refs[:8], y_ref.at[0], *refs[9:])


def ssd_forward(x, bc, dt, marks, shared):
    seqs, length, channels = x.shape
    n2, heads = bc.shape[2], dt.shape[1]
    blocks = length // BLOCK
    tok = lambda w: pl.BlockSpec((1, BLOCK, w), lambda s, c: (s, c, 0))
    head = lambda w: pl.BlockSpec((1, w, BLOCK), lambda s, c: (s, 0, c))
    return pl.pallas_call(
        forward_kernel,
        grid=(seqs, blocks),
        in_specs=[tok(channels), tok(n2), head(heads), head(8)] + shared_specs(channels, n2, heads),
        out_specs=[
            tok(channels),
            tok(channels),
            tok(n2),
            pl.BlockSpec((1, 1, n2 // 2, channels), lambda s, c: (s, c, 0, 0)),
        ],
        out_shape=[
            jax.ShapeDtypeStruct((seqs, length, channels), F32),
            jax.ShapeDtypeStruct((seqs, length, channels), F32),
            jax.ShapeDtypeStruct((seqs, length, n2), F32),
            jax.ShapeDtypeStruct((seqs, blocks, n2 // 2, channels), BF16),
        ],
        scratch_shapes=forward_scratch(channels, n2),
        compiler_params=pltpu.CompilerParams(vmem_limit_bytes=48 * 2**20),
        name="ssd_forward",
    )(x, bc, dt, marks, *shared)


def backward_kernel(*refs):
    backward_block(pl.program_id(0), pl.program_id(1), *refs)


def backward_scratch(channels, n2, heads):
    return [
        pltpu.VMEM((3, BLOCK + 8, channels), F32),
        pltpu.VMEM((3, BLOCK + 8, n2), F32),
        pltpu.VMEM((n2 // 2, channels), F32),
        pltpu.VMEM((BLOCK, BLOCK), F32),
        pltpu.VMEM((BLOCK, BLOCK), F32),
        pltpu.VMEM((BLOCK, channels), F32),
        pltpu.VMEM((heads, BLOCK), F32),
    ]


def backward_specs(channels, n2, heads, small, place):
    tok = lambda w: pl.BlockSpec((1, BLOCK, w), lambda *i: (*place(*i), 0))
    full = lambda *shape: pl.BlockSpec(shape, lambda *i: (0,) * len(shape))
    ins = [tok(channels)] * 3 + [tok(n2)] * 2 + [
        pl.BlockSpec((1, heads, BLOCK), lambda *i: (place(*i)[0], 0, place(*i)[1])),
        pl.BlockSpec((1, 8, BLOCK), lambda *i: (place(*i)[0], 0, place(*i)[1])),
        pl.BlockSpec((1, 1, n2 // 2, channels), lambda *i: (*place(*i), 0, 0)),
    ]
    ins += shared_specs(channels, n2, heads)
    return ins, [tok(channels), tok(small), full(8, channels), full(8, n2), full(heads, 128)]


def backward_outs(seqs, length, channels, n2, heads, small):
    return [
        jax.ShapeDtypeStruct((seqs, length, channels), BF16),
        jax.ShapeDtypeStruct((seqs, length, small), BF16),
        jax.ShapeDtypeStruct((8, channels), F32),
        jax.ShapeDtypeStruct((8, n2), F32),
        jax.ShapeDtypeStruct((heads, 128), F32),
    ]


def ssd_backward(small, dy, x, cx, bc, cbc, dt, marks, states, shared):
    seqs, length, channels = x.shape
    n2, heads = bc.shape[2], dt.shape[1]
    blocks = length // BLOCK
    ins, outs = backward_specs(channels, n2, heads, small, lambda s, c: (s, blocks - 1 - c))
    return pl.pallas_call(
        backward_kernel,
        grid=(seqs, blocks),
        in_specs=ins,
        out_specs=outs,
        out_shape=backward_outs(seqs, length, channels, n2, heads, small),
        scratch_shapes=backward_scratch(channels, n2, heads),
        compiler_params=pltpu.CompilerParams(vmem_limit_bytes=56 * 2**20),
        name="ssd_backward",
    )(dy, x, cx, bc, cbc, dt, marks, states, *shared)


def ring_place(n):
    dp = lax.axis_index("dp")
    z, y = dp // 2, dp % 2

    def at(place):
        q = (place + 4 * n) % n
        return 2 * q + (q // (n // 2)) * (2 * n - 1 - 4 * q)

    return z + y * (n - 1 - 2 * z), at


def tensor_place():
    t = lax.axis_index("tensor")
    return t, t + 1 - 2 * (t % 2), (t + 2) % 4


def greet(n, more=()):
    place, at = ring_place(n)
    _, other, across = tensor_place()
    sem = pltpu.get_barrier_semaphore()
    targets = [{"dp": at(place + 1)}, {"dp": at(place - 1)}, {"tensor": other}, {"tensor": across}, *more]
    for target in targets:
        pl.semaphore_signal(sem, inc=1, device_id=target, device_id_type=MESH)
    pl.semaphore_wait(sem, len(targets))


def remote(src, dst, send_sem, recv_sem, target):
    return pltpu.make_async_remote_copy(
        src_ref=src, dst_ref=dst, send_sem=send_sem, recv_sem=recv_sem, device_id=target, device_id_type=MESH
    )


def span(first, count, unit):
    return pl.ds(pl.multiple_of(first, unit), count)


class RingGather:
    def __init__(self, n, parts, keep, sems):
        self.n, self.parts, self.keep = n, parts, keep
        self.send_sem, self.recv_sem = sems
        self.place, self.at = ring_place(n)

    def copy(self, way, part, step):
        sign = 1 - 2 * way
        ref = self.keep(way, part, self.at(self.place - sign * step))
        return remote(
            ref,
            ref,
            self.send_sem.at[way, part, step],
            self.recv_sem.at[way, part, step],
            {"dp": self.at(self.place + sign)},
        )

    def step(self, k):
        for part in range(self.parts):
            for way in (0, 1):
                if k > 0:
                    self.copy(way, part, k - 1).wait_recv()
                if k < self.n - 1:
                    self.copy(way, part, k).start()

    def later(self, k):
        for part in range(self.parts):
            for way in (0, 1):
                self.copy(way, part, k - 1).wait_recv()

                @pl.when(k < self.n - 1)
                def _():
                    self.copy(way, part, k).start()

    def finish(self):
        for k in range(self.n - 1):
            for part in range(self.parts):
                for way in (0, 1):
                    self.copy(way, part, k).wait_send()


class RowGather:
    def __init__(self, keep, sems):
        self.keep = keep
        self.send_sem, self.recv_sem = sems
        self.me, self.other, self.across = tensor_place()

    def copy(self, kind, part):
        ref = self.keep(part, self.across if kind == 2 else self.me)
        target = self.across if kind == 0 else self.other
        return remote(
            ref, ref, self.send_sem.at[kind, part], self.recv_sem.at[kind, part], {"tensor": target}
        )

    def start(self, part):
        self.copy(0, part).start()
        self.copy(1, part).start()

    def forward(self, part):
        self.copy(0, part).wait_recv()
        self.copy(2, part).start()

    def wait(self, part):
        self.copy(1, part).wait_recv()
        self.copy(2, part).wait_recv()

    def finish(self, parts):
        for part in range(parts):
            for kind in range(3):
                self.copy(kind, part).wait_send()


def marks_of(seg):
    length = seg.shape[1]
    lane = lax.broadcasted_iota(jnp.int32, seg.shape, 1)
    row = lax.broadcasted_iota(jnp.int32, seg.shape, 0)
    earlier = [jnp.where(lane < lag, -1.0, pltpu.roll(seg, lag, 1)) for lag in (1, 2, 3)]
    starts = range(0, length, BLOCK)
    spread = lambda values, at: jnp.broadcast_to(values[:, at : at + 1], (seg.shape[0], BLOCK))
    before = jnp.concatenate([spread(earlier[0], at) for at in starts], axis=1)
    final = jnp.concatenate([spread(seg, at + BLOCK - 1) for at in starts], axis=1)
    out = jnp.where(row == 5, seg, 0.0)
    for k, other in enumerate((*earlier, before, final)):
        out = jnp.where((row == k) & (other == seg), 1.0, out)
    return out


def all_kernel(n, *refs):
    (hidden_ref, g_ref, wzx_ref, wbc_ref, wout_ref, gain_ref, gate_ref, seg_ref), refs = refs[:8], refs[8:]
    shared, refs = refs[:7], refs[7:]
    (u_out, gf_out, wx_out, wz_out, wb_out, wo_out), refs = refs[:6], refs[6:]
    (cx_ref, x_ref, cbc_ref, bc_ref, dt_ref, states_ref), refs = refs[:6], refs[6:]
    (normed_ref, dz_ref, dy_ref, grad_ref, scale_ref, marks_ref), refs = refs[:6], refs[6:]
    scratch, refs = refs[:4], refs[4:]
    (u, wx, wz, wo, wb, wb_own, wdt, g_cols, y, z, dn, sums), refs = refs[:12], refs[12:]
    (load_sem, keep_sem, stream_sem), sems = refs[:3], refs[3:]

    i = pl.program_id(0)
    rows, width = wzx_ref.shape[1:]
    out_rows, out_cols = wout_ref.shape
    seqs, piece, model = hidden_ref.shape
    length = 4 * piece
    blocks = length // BLOCK
    heads = dt_ref.shape[1]
    n2 = bc_ref.shape[2]
    small_cols = wb.shape[1]
    dp = lax.axis_index("dp")
    place, at = ring_place(n)
    me, other, across = tensor_place()
    core = me % 2
    facing = (other + 2) % 4

    def keep_wide(ref):
        def keep(way, part, d):
            return ref.at[span(d * rows, rows, 16), pl.ds(way * width // 2 + part * width // 4, width // 4)]

        return keep

    def keep_out(way, part, d):
        first = way * out_rows // 2 + part * out_rows // 4
        return wo.at[pl.ds(first, out_rows // 4), span(d * out_cols, out_cols, 128)]

    def keep_small(way, part, d):
        return wb.at[span(d * rows + core * rows // 2 + way * rows // 4, rows // 4, 16), :]

    def keep_rows(part, t):
        if part < seqs:
            return u.at[span(part * length + t * piece, piece, 16), :]
        return gf_out.at[part - seqs, span(t * piece, piece, 16), :]

    x_ring = RingGather(n, 2, keep_wide(wx), sems[0:2])
    small = RingGather(n, 1, keep_small, sems[2:4])
    z_ring = RingGather(n, 2, keep_wide(wz), sems[4:6])
    out_ring = RingGather(n, 2, keep_out, sems[6:8])
    token_rows = RowGather(keep_rows, sems[8:10])
    halves_send, halves_recv, sums_send, sums_recv = sems[10:14]

    def half(ahead, whose):
        d = (dp + ahead) % n
        ref = wb.at[span(d * rows + whose * rows // 2, rows // 2, 16), :]
        return remote(ref, ref, halves_send.at[ahead], halves_recv.at[ahead], {"tensor": other})

    def sums_copy(kind):
        ref = sums.at[me]
        target = {"tensor": (other, across, facing)[kind]}
        return remote(ref, ref, sums_send.at[kind], sums_recv.at[kind], target)

    keeps = [
        pltpu.make_async_copy(src, dst, keep_sem.at[j])
        for j, (src, dst) in enumerate(((wx, wx_out), (wb, wb_out), (wz, wz_out), (u, u_out), (wo, wo_out)))
    ]

    def streams(k):
        return [
            pltpu.make_async_copy(
                gf_out.at[:, :, span(at(place - (1 - 2 * way) * k) * out_cols, out_cols, 128)],
                g_cols.at[way],
                stream_sem.at[way],
            )
            for way in (0, 1)
        ]

    def start(copies):
        for copy in copies:
            copy.start()

    def wait(copies):
        for copy in copies:
            copy.wait()

    @pl.when(i == 0)
    def _():
        def held(s, h):
            return z.at[pl.ds((2 * s + h) * piece, piece), :]

        halves = [(s, h) for s in range(seqs) for h in (0, 1)]
        cut = lambda h: pl.ds(h * (model // 2), model // 2)
        own = [
            (wzx_ref.at[1], wx.at[span(dp * rows, rows, 16), :]),
            (wbc_ref, wb_own),
            (wzx_ref.at[0], wz.at[span(dp * rows, rows, 16), :]),
            (wout_ref, wo.at[:, span(dp * out_cols, out_cols, 128)]),
        ]
        own += [(hidden_ref.at[s, :, cut(h)], held(seqs + s, h)) for s, h in halves]
        own += [(g_ref.at[s, :, cut(h)], held(s, h)) for s, h in halves]
        loads = [pltpu.make_async_copy(a, b, load_sem.at[j]) for j, (a, b) in enumerate(own)]
        first = 4 + 2 * seqs
        stores = [
            pltpu.make_async_copy(
                held(s, h), gf_out.at[s, span(me * piece, piece, 16), cut(h)], load_sem.at[first + 2 * seqs + j]
            )
            for j, (s, h) in enumerate(halves)
        ]
        start(loads)
        greet(n, [{"tensor": facing}])
        loads[0].wait()
        x_ring.step(0)
        loads[1].wait()
        mine = span(dp * rows, rows, 16)
        short = jnp.zeros((small_cols - wb_own.shape[0], rows), BF16)
        wb[mine, :] = jnp.concatenate([wb_own[...], short], axis=0).T
        small.step(0)
        wait(loads[4:first])
        for s in range(seqs):
            left = z[pl.ds((2 * (seqs + s)) * piece, piece), :].astype(F32)
            right = z[pl.ds((2 * (seqs + s) + 1) * piece, piece), :].astype(F32)
            squares = jnp.sum(left * left + right * right, axis=1, keepdims=True)
            scale = lax.rsqrt(squares / model + EPS)
            scale_ref[s] = jnp.broadcast_to(scale, (piece, 128))
            to = span(s * length + me * piece, piece, 16)
            u[to, cut(0)] = (left * scale * gain_ref[:, cut(0)]).astype(BF16)
            u[to, cut(1)] = (right * scale * gain_ref[:, cut(1)]).astype(BF16)
            token_rows.start(s)
        for s in range(seqs):
            seg = seg_ref[s : s + 1, :].astype(F32)
            marks_ref[s] = marks_of(jnp.broadcast_to(seg, (8, seg.shape[1])))
        wait(loads[first:])
        start(stores)
        wait(loads[2:4])
        wait(stores)
        for k in range(1, n):
            x_ring.step(k)
            small.step(k)
            if k == n - 1:
                z_ring.step(0)
            if k == n // 2:
                token_rows.forward(0)
                token_rows.start(seqs)
        for ahead in range(1, n):
            half(ahead, core).start()
        for ahead in range(1, n):
            half(ahead, 1 - core).wait_recv()
        token_rows.wait(0)
        start(keeps[:2])
        lanes = small_cols - n2
        pick = lax.broadcasted_iota(jnp.int32, (heads, lanes), 1) == (
            lax.broadcasted_iota(jnp.int32, (heads, lanes), 0) + me * heads
        )
        wdt[...] = dot_nt(pick.astype(BF16), wb[:, n2:]).astype(BF16)

    b = i - 1

    @pl.when((b >= 0) & (b < n))
    def _():
        @pl.when(b < n - 1)
        def _():
            z_ring.later(b + 1)

        @pl.when(b == n - 2)
        def _():
            out_ring.step(0)

        @pl.when(b == n - 1)
        def _():
            keeps[2].start()
            out_ring.step(1)

        @pl.when(b == 0)
        def _():
            token_rows.forward(1)
            token_rows.start(seqs + 1)

        @pl.when(b == blocks)
        def _():
            token_rows.wait(1)
            keeps[3].start()

        at_block = span(b * BLOCK, BLOCK, BLOCK)
        tokens = u[at_block, :]
        marks = marks_ref.at[pl.ds(b // blocks, 1), :, span(b % blocks * BLOCK, BLOCK, BLOCK)]
        x = dot(tokens, wx[...])
        bc = dot(tokens, wb[:, :n2])
        dt = dot_nt(wdt[...], tokens)
        x_ref[0] = x.astype(BF16)
        bc_ref[0] = bc.astype(BF16)
        dt_ref[0] = dt
        forward_block(
            b % blocks, x, bc, dt, marks, *shared, y.at[at_block, :], cx_ref, cbc_ref, states_ref, *scratch
        )

    slope = wx

    def add_shard(k):
        wait(streams(k))
        for way in (0, 1):
            e = pl.ds(way * (out_rows // 2), out_rows // 2)
            d = at(place - (1 - 2 * way) * k)
            cols = g_cols[way].reshape(seqs * length, out_cols)
            value = dot_nt(cols, wo[e, span(d * out_cols, out_cols, 128)])

            @pl.when(k == 0)
            def _():
                dn[:, e] = value

            @pl.when(k > 0)
            def _():
                dn[:, e] += value

    def gate_block(e, _):
        part = span(e * BLOCK, BLOCK, BLOCK)
        zf = dot(u[part, :], wz[...])
        sig = sigmoid(zf)
        silu = zf * sig
        yf = y[part, :]
        y[part, :] = yf * silu
        z[part, :] = silu.astype(BF16)
        slope[part, :] = (yf * (sig + silu * (1.0 - sig))).astype(BF16)
        return 0

    def shard_step(c, _):
        @pl.when(c == 0)
        def _():
            token_rows.forward(seqs)
            token_rows.forward(seqs + 1)
            token_rows.wait(seqs)
            token_rows.wait(seqs + 1)
            start(streams(0))
            add_shard(0)
            start(streams(1))
            keeps[0].wait()
            x_ring.finish()

        @pl.when((c >= 1) & (c <= 4))
        def _():
            lax.fori_loop(2 * (c - 1), 2 * c, gate_block, 0)

        add_shard(c + 1)
        start(streams(c + 2))
        out_ring.later(c + 2)
        return 0

    @pl.when(i == n + 1)
    def _():
        lax.fori_loop(0, n - 2, shard_step, 0)
        add_shard(n - 1)
        keeps[4].start()

        def block_sums(e, _):
            part = span(e * BLOCK, BLOCK, BLOCK)
            gated = y[part, :]
            squares = jnp.sum(gated * gated, axis=1, keepdims=True)
            inner = jnp.sum(gate_ref[...] * dn[part, :] * gated, axis=1, keepdims=True)
            lane = lax.broadcasted_iota(jnp.int32, (1, 128), 1)
            both = jnp.where(lane == 0, squares, jnp.where(lane == 1, inner, 0.0))
            sums[me, :, part] = both.T[0:8, :]
            return 0

        lax.fori_loop(0, n, block_sums, 0)
        for kind in range(3):
            sums_copy(kind).start()

    e = i - (n + 2)

    @pl.when(e >= 0)
    def _():
        @pl.when(e == 0)
        def _():
            for kind in range(3):
                sums_copy(kind).wait_recv()
            grad_ref[...] = jnp.zeros_like(grad_ref)

        part = span(e * BLOCK, BLOCK, BLOCK)
        whole = (sums[0, :, part] + sums[1, :, part]) + (sums[2, :, part] + sums[3, :, part])
        cols = jnp.concatenate([whole, jnp.zeros((120, BLOCK), F32)], axis=0).T / (4 * width)
        inverse = lax.rsqrt(cols[:, 0:1] + EPS)
        dnf = dn[part, :]
        gain = gate_ref[...]
        gated = y[part, :]
        scaled_gated = gated * inverse
        normed_ref[...] = (scaled_gated * gain).astype(BF16)
        grad_ref[...] += jnp.sum(dnf * scaled_gated, axis=0, keepdims=True)
        d_gated = inverse * (dnf * gain) - gated * (inverse * inverse * inverse * cols[:, 1:2])
        dy_ref[...] = (d_gated * z[part, :].astype(F32)).astype(BF16)
        dz_ref[...] = (d_gated * slope[part, :].astype(F32)).astype(BF16)

        @pl.when(e == n - 1)
        def _():
            wait(keeps[1:])
            for ring in (small, z_ring, out_ring):
                ring.finish()
            token_rows.finish(2 * seqs)
            for ahead in range(1, n):
                half(ahead, core).wait_send()
            for kind in range(3):
                sums_copy(kind).wait_send()


def forward_all(n, hidden, g, w_zx, w_bc, w_out, pre_gain, gate_gain, segments, shared):
    seqs, piece, model = hidden.shape
    rows, width = w_zx.shape[1:]
    out_rows, out_cols = w_out.shape
    length = 4 * piece
    tokens = seqs * length
    blocks = length // BLOCK
    n2 = shared[1].shape[1]
    heads = shared[2].shape[1]
    columns = w_bc.shape[0]
    small = columns + -columns % 128
    sem = pltpu.SemaphoreType.DMA
    ring = [sem((2, 2, n - 1))] * 2
    anywhere = pl.BlockSpec(memory_space=pl.ANY)
    whole = lambda *shape: pl.BlockSpec(shape, lambda i: (0,) * len(shape))
    b = lambda i: jnp.minimum(jnp.maximum(i - 1, 0), n - 1)
    e = lambda i: jnp.maximum(i - (n + 2), 0)
    tok = lambda w: pl.BlockSpec((1, BLOCK, w), lambda i: (b(i) // blocks, b(i) % blocks, 0))
    gate = pl.BlockSpec((BLOCK, width), lambda i: (e(i), 0))
    out_shape = [
        ((tokens, model), BF16),
        ((seqs, length, model), BF16),
        ((rows * n, width), BF16),
        ((rows * n, width), BF16),
        ((rows * n, small), BF16),
        ((out_rows, out_cols * n), BF16),
        ((seqs, length, width), F32),
        ((seqs, length, width), BF16),
        ((seqs, length, n2), F32),
        ((seqs, length, n2), BF16),
        ((seqs, heads, length), F32),
        ((seqs, blocks, n2 // 2, width), BF16),
        ((tokens, width), BF16),
        ((tokens, width), BF16),
        ((tokens, width), BF16),
        ((1, width), F32),
        ((seqs, piece, 128), F32),
        ((seqs, 8, length), F32),
    ]
    return pl.pallas_call(
        functools.partial(all_kernel, n),
        grid=(2 * n + 2,),
        in_specs=[anywhere] * 5
        + [
            whole(1, model),
            whole(1, width),
            whole(*segments.shape),
        ]
        + shared_specs(width, n2, heads),
        out_specs=[anywhere] * 6
        + [tok(width), tok(width), tok(n2), tok(n2)]
        + [pl.BlockSpec((1, heads, BLOCK), lambda i: (b(i) // blocks, 0, b(i) % blocks))]
        + [pl.BlockSpec((1, 1, n2 // 2, width), lambda i: (b(i) // blocks, b(i) % blocks, 0, 0))]
        + [gate] * 3
        + [whole(1, width), whole(seqs, piece, 128), whole(seqs, 8, length)],
        out_shape=[jax.ShapeDtypeStruct(*s) for s in out_shape],
        scratch_shapes=forward_scratch(width, n2)
        + [
            pltpu.VMEM((tokens, model), BF16),
            pltpu.VMEM((rows * n, width), BF16),
            pltpu.VMEM((rows * n, width), BF16),
            pltpu.VMEM((out_rows, out_cols * n), BF16),
            pltpu.VMEM((rows * n, small), BF16),
            pltpu.VMEM(w_bc.shape, BF16),
            pltpu.VMEM((heads, rows * n), BF16),
            pltpu.VMEM((2, seqs, length, out_cols), BF16),
            pltpu.VMEM((tokens, width), F32),
            pltpu.VMEM((tokens, width), BF16),
            pltpu.VMEM((tokens, width), F32),
            pltpu.VMEM((4, 8, tokens), F32),
            sem((4 + 6 * seqs,)),
            sem((5,)),
            sem((2,)),
        ]
        + ring + [sem((2, 1, n - 1))] * 2 + ring + ring
        + [sem((3, 2 * seqs))] * 2 + [sem((n,))] * 2 + [sem((3,))] * 2,
        compiler_params=pltpu.CompilerParams(
            collective_id=0, has_side_effects=True, vmem_limit_bytes=63 * 2**20
        ),
        name="forward_all",
    )(hidden, g, w_zx, w_bc, w_out, pre_gain, gate_gain, segments, *shared)


class RingScatter:
    def __init__(self, n, terms, slots, sems, ways=2, sign=1):
        self.n, self.terms, self.slots, self.ways, self.sign = n, terms, slots, ways, sign
        self.send_sem, self.recv_sem = sems
        self.place, self.at = ring_place(n)

    def turn(self, way):
        return self.sign * (1 - 2 * way)

    def owner(self, way, k):
        return self.at(self.place - self.turn(way) * (1 + k))

    def copy(self, way, k):
        return remote(
            self.slots.at[way, k],
            self.slots.at[way, k + 1],
            self.send_sem.at[way, k],
            self.recv_sem.at[way, k],
            {"dp": self.at(self.place + self.turn(way))},
        )

    def step(self, way, k):
        @pl.when(k == 0)
        def _():
            self.slots[way, 0] = self.terms[way].astype(BF16)

        @pl.when(k > 0)
        def _():
            self.copy(way, k - 1).wait_recv()

            @pl.when(k < self.n - 1)
            def _():
                self.slots[way, k] = (self.terms[way].astype(F32) + self.slots[way, k].astype(F32)).astype(BF16)

        @pl.when(k < self.n - 1)
        def _():
            self.copy(way, k).start()

    def last(self, way):
        return self.terms[way].astype(F32) + self.slots[way, self.n - 1].astype(F32)

    def finish(self):
        for k in range(self.n - 1):
            for way in range(self.ways):
                self.copy(way, k).wait_send()


class RowScatter:
    def __init__(self, parts, value, hold, sems):
        self.parts, self.value, self.hold = parts, value, hold
        self.send_sem, self.recv_sem = sems
        self.me, self.other, self.across = tensor_place()

    def copy(self, kind, part):
        src, dst = ((0, 1), (1, 2), (0, 3))[kind]
        return remote(
            self.hold.at[src, part],
            self.hold.at[dst, part],
            self.send_sem.at[kind, part],
            self.recv_sem.at[kind, part],
            {"tensor": self.across if kind == 1 else self.other},
        )

    def stage(self, j):
        late = j // (2 * self.parts)
        near = j - 2 * self.parts
        stage = (1 - late) * (j % 2) + late * (2 + near // self.parts)
        return stage, (1 - late) * (j // 2) + late * (near % self.parts)

    def owner(self, j):
        stage, part = self.stage(j)
        x, core = self.me // 2, self.me % 2
        return 2 * ((x + 1 - stage // 2) % 2) + (core + 1 - stage % 2) % 2, part

    def step(self, j, store, wait=True):
        stage, part = self.stage(j)

        @pl.when(stage == 0)
        def _():
            self.hold[0, part] = self.value[...].astype(BF16)
            self.copy(0, part).start()

        @pl.when(stage == 1)
        def _():
            self.copy(0, part).wait_recv()
            self.hold[1, part] = (self.value[...].astype(F32) + self.hold[1, part].astype(F32)).astype(BF16)
            self.copy(1, part).start()

        @pl.when(stage == 2)
        def _():
            self.copy(0, part).wait_send()
            self.hold[0, part] = self.value[...].astype(BF16)
            self.copy(2, part).start()

        @pl.when(stage == 3)
        def _():
            value = self.value[...].astype(F32)
            store(part, value + self.arrived(part) if wait else value)

    def arrived(self, part):
        self.copy(2, part).wait_recv()
        self.copy(1, part).wait_recv()
        return self.hold[3, part].astype(F32) + self.hold[2, part].astype(F32)

    def finish(self):
        for part in range(self.parts):
            for kind in (1, 2):
                self.copy(kind, part).wait_send()


def back_kernel(n, *refs):
    (normed_ref, g_ref, u_ref, dz_ref, wo_ref), refs = refs[:5], refs[5:]
    ins, refs = refs[:15], refs[15:]
    (out_ref, gout_ref, gz_ref), refs = refs[:3], refs[3:]
    outs, refs = refs[:5], refs[5:]
    scratch, refs = refs[:7], refs[7:]
    normed, dz, wo, g_cols, u_cols, out_slots, z_slots, hold, terms, mixed, load_sem, stream_sem, out_sem = refs[:13]
    sems = refs[13:]

    k = pl.program_id(0)
    blocks = 4
    piece = out_ref.shape[1]
    length = blocks * BLOCK
    count = g_ref.shape[1] // n
    half = gz_ref.shape[1] // 2
    place, at = ring_place(n)

    loads = [
        pltpu.make_async_copy(src, dst, load_sem.at[i])
        for i, (src, dst) in enumerate(((normed_ref, normed), (dz_ref, dz), (wo_ref, wo)))
    ]

    def streams(k):
        copies = []
        for way in (0, 1):
            d = at(place - (1 - 2 * way) * (1 + k))
            for i, (src, dst) in enumerate(((g_ref, g_cols), (u_ref, u_cols))):
                copies.append(
                    pltpu.make_async_copy(
                        src.at[:, span(d * count, count, 128)], dst.at[way], stream_sem.at[i, way]
                    )
                )
        return copies

    @pl.when(k == 0)
    def _():
        for copy in streams(0) + loads:
            copy.start()
        greet(n)

    backward_block(k // blocks, k % blocks, *ins, *outs, *scratch)

    @pl.when(k == 0)
    def _():
        for copy in loads:
            copy.wait()

    for copy in streams(k):
        copy.wait()

    rows = RowScatter(2, mixed, hold, sems[4:6])
    owner = rows.owner(k)
    own_rows = span(owner[1] * length + owner[0] * piece, piece, 16)

    for ring, (from_cols, to_cols) in enumerate(((g_cols, normed), (u_cols, dz))):
        for way in (0, 1):
            value = dot_tn(from_cols[way], to_cols[:, pl.ds(way * half, half)])
            terms[ring, way] = value.astype(BF16)
    mixed[...] = dot(normed[own_rows, :], wo[...]).astype(BF16)

    out_ring = RingScatter(n, terms.at[0], out_slots, sems[0:2])
    z_ring = RingScatter(n, terms.at[1], z_slots, sems[2:4])
    for way in (0, 1):
        out_ring.step(way, k)
        z_ring.step(way, k)

    @pl.when(k < n - 1)
    def _():
        for copy in streams(k + 1):
            copy.start()

    def out_copy(part):
        return pltpu.make_async_copy(hold.at[2, part], out_ref.at[part], out_sem.at[part])

    def store(part, value):
        hold[2, part] = value.astype(BF16)
        out_copy(part).start()

    rows.step(k, store)

    @pl.when(k == n - 1)
    def _():
        for way in (0, 1):
            at = pl.ds(way * half, half)
            gout_ref[at, :] = out_ring.last(way).T
            gz_ref[:, at] = z_ring.last(way)

    @pl.when(k == n - 1)
    def _():
        rows.finish()
        out_ring.finish()
        z_ring.finish()
        for part in range(2):
            out_copy(part).wait()


def backward_all(n, small, piece, normed, g, u, dz, w_out, dy, x, cx, bc, cbc, dt, marks, states, shared):
    seqs, length, channels = x.shape
    n2, heads = bc.shape[2], dt.shape[1]
    tokens, model = g.shape
    count = model // n
    blocks = length // BLOCK
    sem = pltpu.SemaphoreType.DMA
    anywhere = pl.BlockSpec(memory_space=pl.ANY)
    ins, outs = backward_specs(channels, n2, heads, small, lambda k: (k // blocks, blocks - 1 - k % blocks))
    whole = lambda *shape: pl.BlockSpec(shape, lambda k: (0,) * len(shape))
    return pl.pallas_call(
        functools.partial(back_kernel, n),
        grid=(n,),
        in_specs=[anywhere] * 5 + ins,
        out_specs=[anywhere, whole(channels, count), whole(count, channels)] + outs,
        out_shape=[
            jax.ShapeDtypeStruct((seqs, piece, model), BF16),
            jax.ShapeDtypeStruct((channels, count), F32),
            jax.ShapeDtypeStruct((count, channels), F32),
        ]
        + backward_outs(seqs, length, channels, n2, heads, small),
        scratch_shapes=backward_scratch(channels, n2, heads)
        + [
            pltpu.VMEM((tokens, channels), BF16),
            pltpu.VMEM((tokens, channels), BF16),
            pltpu.VMEM((channels, model), BF16),
            pltpu.VMEM((2, tokens, count), BF16),
            pltpu.VMEM((2, tokens, count), BF16),
            pltpu.VMEM((2, n, count, channels // 2), BF16),
            pltpu.VMEM((2, n, count, channels // 2), BF16),
            pltpu.VMEM((4, seqs, piece, model), BF16),
            pltpu.VMEM((2, 2, count, channels // 2), BF16),
            pltpu.VMEM((piece, model), BF16),
            sem((3,)),
            sem((2, 2)),
            sem((seqs,)),
        ]
        + [sem((2, n - 1))] * 4
        + [sem((3, seqs))] * 2,
        compiler_params=pltpu.CompilerParams(
            collective_id=1, has_side_effects=True, vmem_limit_bytes=127 * 2**19
        ),
        name="backward_all",
    )(normed, g, u, dz, w_out, dy, x, cx, bc, cbc, dt, marks, states, *shared)


class Fold:
    def __init__(self, n, total, came, sems):
        self.total, self.came = total, came
        self.send_sem, self.recv_sem = sems
        dp = lax.axis_index("dp")
        _, other, across = tensor_place()
        partners, ahead = [], 1
        while ahead < n:
            partners.append({"dp": dp + ahead * (1 - 2 * ((dp // ahead) % 2))})
            ahead *= 2
        self.over_dp = partners
        self.partners = partners + [{"tensor": other}, {"tensor": across}]

    def copy(self, r):
        return remote(
            self.total.at[r], self.came.at[r], self.send_sem.at[r], self.recv_sem.at[r], self.partners[r]
        )

    def start(self, r):
        self.copy(r).start()

    def take(self, r):
        self.copy(r).wait_recv()
        self.total[r + 1] = self.total[r] + self.came[r]

    def finish(self):
        for r in range(len(self.partners)):
            self.copy(r).wait_send()


def in_kernel(
    n, u_hbm, dz_hbm, dx_hbm, wz_hbm, wx_hbm, wb_hbm, dbc_hbm, gz_hbm, gx_in, gbc_in, gh_in, gate_in, gain_ref,
    din_ref, gx_ref, gb_ref, sums_ref, dots_ref, pre_ref,
    u_ref, dz_ref, dx_ref, wz_ref, wx_ref, wb_ref, dbc_ref,
    x_slots, b_slots, hold, bc_hold, x_terms, b_terms, in_value, bc_value, low, swap, own_in, pre, pre_dp, pre_tensor, total, came, load_sem, u_sem, *sems,
):
    seqs, piece = din_ref.shape[:2]
    tokens, model = u_ref.shape
    length = tokens // seqs
    count = model // n
    half = gx_ref.shape[2] // 2
    me, other, across = tensor_place()
    core = me % 2

    moves = (
        (dbc_hbm, dbc_ref),
        (dx_hbm, dx_ref),
        (dz_hbm, dz_ref),
        (wz_hbm, wz_ref),
        (wx_hbm, wx_ref),
        (wb_hbm, wb_ref),
        (gz_hbm, gx_ref.at[0]),
    )
    loads = [pltpu.make_async_copy(src, dst, load_sem.at[i]) for i, (src, dst) in enumerate(moves)]
    place, at_place = ring_place(n)
    u_copies = []
    for ahead in (-1, 1, -2, 2, -3, 3, 4, 0):
        cols = span(at_place(place + ahead) * count, count, 128)
        u_copies.append(pltpu.make_async_copy(u_hbm.at[:, cols], u_ref.at[:, cols], u_sem.at[ahead + 3]))
    for load in loads[:2] + u_copies[:2] + loads[2:] + u_copies[2:]:
        load.start()

    bc_rows = RowScatter(seqs, bc_value, bc_hold, sems[0:2])
    in_rows = RowScatter(seqs, in_value, hold, sems[2:4])
    x_ring = RingScatter(n, x_terms, x_slots, sems[4:6])
    b_ring = RingScatter(n, b_terms, b_slots, sems[6:8], 1, 1 - 2 * core)
    pair_send, pair_recv, swap_send, swap_recv = sems[8:12]
    dp_send, dp_recv, tensor_send, tensor_recv = sems[14:18]
    fold = Fold(n, total, came, sems[12:14])
    rounds = len(fold.partners)
    pair = remote(low.at[0], low.at[1], pair_send, pair_recv, {"tensor": other})

    total[0] = jnp.zeros_like(total[0])
    total[0, 0:6, :] = gx_in[0:6, :]
    total[0, 6:7, :] = gate_in[...]
    steps = gh_in[...].T
    total[0, 7:8, 0 : steps.shape[1]] = steps[0:1, :]
    total[0, 7:8, 128 : 128 + steps.shape[1]] = steps[1:2, :]
    total[0, 8:13, 0 : gbc_in.shape[1]] = gbc_in[0:5, :]
    pre[...] = jnp.zeros_like(pre)
    dp_now = lax.axis_index("dp")
    greet(
        n,
        fold.over_dp
        + [{"dp": (dp_now + o) % n} for o in range(1, n)]
        + [{"tensor": (me + o) % 4} for o in range(1, 4)],
    )
    def rows_at(t, part):
        return span(part * length + t * piece, piece, 16)

    def bc_store(part, value):
        low[0, part] = value.astype(BF16)

    def bc_step(j):
        t, part = bc_rows.owner(j)
        bc_value[...] = dbc_ref[rows_at(t, part), :].astype(F32)
        bc_rows.step(j, bc_store)

    def add_pre(at):
        pre[...] += jnp.sum(in_value[...] * u_ref[at, :].astype(F32), axis=0, keepdims=True)

    def store(part, value):
        in_value[...] = value + dot_nt(low[0, part], wb_ref[...])
        own_in[part] = in_value[...]
        add_pre(rows_at(me, part))

    def row_term(j):
        at = rows_at(*in_rows.owner(j))
        in_value[...] = dot_nt(dz_ref[at, :], wz_ref[...]) + dot_nt(dx_ref[at, :], wx_ref[...])

    def row_step(j):
        in_rows.step(j, store, wait=False)

        @pl.when(j < 3 * seqs)
        def _():
            add_pre(rows_at(*in_rows.owner(j)))

    def x_term(k):
        for way in (0, 1):
            cols = span(x_ring.owner(way, k) * count, count, 128)
            x_terms[way] = dot_tn(u_ref[:, cols], dx_ref[:, pl.ds(way * half, half)])

    def x_step(k):
        for way in (0, 1):
            x_ring.step(way, k)

    def b_step(k):
        cols = span(b_ring.owner(0, k) * count + core * count // 2, count // 2, 128)
        value = 0.0
        for t, which in ((me, 0), (other, 1)):
            for part in range(seqs):
                value = value + dot_tn(u_ref[rows_at(t, part), cols], low[which, part])
        b_terms[0] = value
        b_ring.step(0, k)

    loads[0].wait()
    for part in range(seqs):
        bc_step(2 * part)
        bc_step(2 * seqs + part)
    loads[1].wait()
    for copy in u_copies[:2]:
        copy.wait()
    x_term(0)
    x_step(0)
    for load in loads[2:] + u_copies[2:]:
        load.wait()
    row_term(0)
    row_step(0)
    for part in range(seqs):
        bc_step(2 * part + 1)

    wide = model // 8
    gain = gain_ref[...]

    def dp_copy(o):
        ref = pre_dp.at[dp_now]
        return remote(ref, ref, dp_send.at[o], dp_recv.at[o], {"dp": (dp_now + o) % n})

    def tensor_copy(o):
        ref = pre_tensor.at[me]
        return remote(ref, ref, tensor_send.at[o], tensor_recv.at[o], {"tensor": (me + o) % 4})

    cross = remote(swap.at[0], swap.at[1], swap_send.at[0], swap_recv.at[0], {"tensor": across})
    back = remote(swap.at[2], swap.at[3], swap_send.at[1], swap_recv.at[1], {"tensor": other})

    def at_step(k, when, what):
        pl.when(k == when)(what)

    def own_bc():
        for part in range(seqs):
            bc_step(3 * seqs + part)
        pair.start()

    def send_pre():
        for i in range(8):
            at = slice(i * wide, (i + 1) * wide)
            pre_dp[dp_now, i : i + 1, :] = pre[:, at] / gain[:, at]
        for o in range(1, n):
            dp_copy(o).start()

    def pass_pre():
        for o in range(1, n):
            dp_copy(o).wait_recv()
        pre_tensor[me] = sum(pre_dp[d] for d in range(n))
        for o in range(1, 4):
            tensor_copy(o).start()

    def take_pre():
        for o in range(1, 4):
            tensor_copy(o).wait_recv()
        pre_ref[...] = (pre_tensor[0] + pre_tensor[1]) + (pre_tensor[2] + pre_tensor[3])

    def send_bc():
        swap[0] = b_ring.last(0)
        cross.start()

    def pass_bc():
        cross.wait_recv()
        swap[2] = swap[0] + swap[1]
        back.start()
        gb_ref[span(core * count // 2, count // 2, 16), :] = swap[2]

    def step(k, _):
        at_step(k, 5, send_pre)
        at_step(k, n - 1, send_bc)

        @pl.when(2 * k - 1 < 4 * seqs)
        def _():
            row_term(2 * k - 1)
            row_step(2 * k - 1)

        x_term(k)
        x_step(k)
        at_step(k, 2, pair.wait_recv)

        @pl.when((k >= 2) & (k <= 6))
        def _():
            b_step(jnp.maximum(k - 2, 2 * (k - 3)))

        @pl.when(2 * k < 4 * seqs)
        def _():
            row_term(2 * k)
            row_step(2 * k)

        at_step(k, 1, own_bc)

        @pl.when((k >= 4) & (k <= 6))
        def _():
            b_step(2 * (k - 3) + 1)

        at_step(k, 6, pass_pre)
        at_step(k, n - 1, pass_bc)
        at_step(k, n - 1, take_pre)
        for r in range(rounds + 1):

            @pl.when(k == r + 1)
            def _():
                if r > 0:
                    fold.take(r - 1)
                if r < rounds:
                    fold.start(r)

        return 0

    lax.fori_loop(1, n, step, 0)
    for way in (0, 1):
        gx_ref[1, :, pl.ds(way * half, half)] = x_ring.last(way)
    sums_ref[0:8, :] = total[rounds - 2, 0:8, :]
    sums_ref[8:16, :] = total[rounds, 8:16, :]
    for part in range(seqs):
        value = own_in[part] + in_rows.arrived(part)
        din_ref[part] = value.astype(BF16)
        inner = jnp.sum(value * u_ref[rows_at(me, part), :].astype(F32), axis=1, keepdims=True)
        dots_ref[part] = jnp.broadcast_to(inner, (piece, 128))
    back.wait_recv()
    gb_ref[span((1 - core) * count // 2, count // 2, 16), :] = swap[3]
    for o in range(1, n):
        dp_copy(o).wait_send()
    for o in range(1, 4):
        tensor_copy(o).wait_send()
    for copy in (pair, cross, back):
        copy.wait_send()
    for part in (bc_rows, in_rows, x_ring, b_ring, fold):
        part.finish()


def scatter_in(n, piece, u, dz, dx, w_z, w_x, w_bc, dbc, grad_z, gx, gbc, gh, grad_gate, gain):
    tokens, model = u.shape
    width = dz.shape[1]
    small = dbc.shape[1]
    seqs = tokens // (4 * piece)
    count = model // n
    rounds = 5
    sem = pltpu.SemaphoreType.DMA
    vmem = pl.BlockSpec(memory_space=pltpu.VMEM)
    anywhere = pl.BlockSpec(memory_space=pl.ANY)
    big = (u, dz, dx, w_z, w_x, w_bc, dbc)
    return pl.pallas_call(
        functools.partial(in_kernel, n),
        in_specs=[anywhere] * 8 + [vmem] * 5,
        out_specs=[vmem] * 6,
        out_shape=[
            jax.ShapeDtypeStruct((seqs, piece, model), BF16),
            jax.ShapeDtypeStruct((2, count, width), F32),
            jax.ShapeDtypeStruct((count, small), F32),
            jax.ShapeDtypeStruct((16, width), F32),
            jax.ShapeDtypeStruct((seqs, piece, 128), F32),
            jax.ShapeDtypeStruct((8, model // 8), F32),
        ],
        scratch_shapes=[pltpu.VMEM(a.shape, BF16) for a in big]
        + [
            pltpu.VMEM((2, n, count, width // 2), BF16),
            pltpu.VMEM((1, n, count // 2, small), BF16),
            pltpu.VMEM((4, seqs, piece, model), BF16),
            pltpu.VMEM((4, seqs, piece, small), BF16),
            pltpu.VMEM((2, count, width // 2), F32),
            pltpu.VMEM((1, count // 2, small), F32),
            pltpu.VMEM((piece, model), F32),
            pltpu.VMEM((piece, small), F32),
            pltpu.VMEM((2, seqs, piece, small), BF16),
            pltpu.VMEM((4, count // 2, small), F32),
            pltpu.VMEM((seqs, piece, model), F32),
            pltpu.VMEM((1, model), F32),
            pltpu.VMEM((n, 8, model // 8), F32),
            pltpu.VMEM((4, 8, model // 8), F32),
            pltpu.VMEM((rounds + 1, 16, width), F32),
            pltpu.VMEM((rounds, 16, width), F32),
            sem((len(big),)),
            sem((n,)),
        ]
        + [sem((3, seqs))] * 4 + [sem((2, n - 1))] * 2 + [sem((1, n - 1))] * 2 + [sem(())] * 2 + [sem((2,))] * 2
        + [sem((rounds,))] * 2 + [sem((n,))] * 2 + [sem((4,))] * 2,
        compiler_params=pltpu.CompilerParams(
            collective_id=2, has_side_effects=True, vmem_limit_bytes=63 * 2**20
        ),
        name="scatter_in",
    )(*big, grad_z, gx, gbc, gh, grad_gate, gain)


def finish_kernel(
    d_in_ref, hidden_ref, cot_ref, mixed_ref, scale_ref, dots_ref, gain_ref, gzx_in, gout_in, gb_in, sums_ref,
    spread_ref, pre_in,
    out_ref, d_hidden_ref, gzx_ref, gout_ref, gb_ref, taps_ref, taps_bc_ref,
    bias_ref, alog_ref, skip_ref, gate_ref, pre_ref,
):
    model = gain_ref.shape[1]
    x = hidden_ref[0].astype(F32)
    scale = scale_ref[0][:, 0:1]
    factor = scale * scale * dots_ref[0][:, 0:1] / model
    d_hidden_ref[0] = cot_ref[0].astype(F32) + scale * (gain_ref[...] * d_in_ref[0].astype(F32)) - x * factor
    out_ref[0] = (x + mixed_ref[0].astype(F32)).astype(BF16)
    gzx_ref[...] = gzx_in[...]
    gout_ref[...] = gout_in[...]
    gb_ref[...] = gb_in[...].T[: gb_ref.shape[0], :]
    taps_ref[...] = sums_ref[0 : taps_ref.shape[0], :]
    taps_bc_ref[...] = sums_ref[8 : 8 + taps_bc_ref.shape[0], : taps_bc_ref.shape[1]]
    heads = bias_ref.shape[0]
    bias_ref[...] = sums_ref[7, 0:heads]
    alog_ref[...] = sums_ref[7, 128 : 128 + heads]
    gate_ref[...] = sums_ref[6, :]
    by_head = lax.dot_general(
        sums_ref[0:8, :],
        spread_ref[...].astype(F32),
        (((1,), (1,)), ((), ())),
        precision=EXACT,
        preferred_element_type=F32,
    )
    skip_ref[...] = by_head[5, :]
    wide = pre_in.shape[1]
    for i in range(pre_in.shape[0]):
        pre_ref[pl.ds(i * wide, wide)] = pre_in[i, :]


def finish(
    d_in, hidden, cotangent, mixed, scale, dots, gain, grad_zx, grad_out, grad_bc, sums, spread, pre, columns, n2
):
    seqs, piece, model = hidden.shape
    count, width = grad_zx.shape[1:]
    heads = spread.shape[0]
    steps = 2
    rows = piece // steps
    grid = seqs * steps
    piece_rows = lambda w: pl.BlockSpec((1, rows, w), lambda i: (i // steps, i % steps, 0))
    whole = lambda *shape: pl.BlockSpec(shape, lambda i: (0,) * len(shape))
    zx = pl.BlockSpec((1, 2 * count // grid, width), lambda i: (i // (grid // 2), i % (grid // 2), 0))
    down = lambda a, w: pl.BlockSpec((a.shape[0] // grid, w), lambda i: (i, 0))
    return pl.pallas_call(
        finish_kernel,
        grid=(grid,),
        in_specs=[piece_rows(model)] * 4
        + [piece_rows(128)] * 2
        + [whole(1, model), zx, down(grad_out, grad_out.shape[1]), whole(*grad_bc.shape)]
        + [whole(*sums.shape), whole(*spread.shape), whole(*pre.shape)],
        out_specs=[piece_rows(model)] * 2
        + [zx, down(grad_out, grad_out.shape[1]), whole(columns, count), whole(5, width), whole(5, n2)]
        + [whole(heads), whole(heads), whole(heads), whole(width), whole(model)],
        out_shape=[
            jax.ShapeDtypeStruct(hidden.shape, BF16),
            jax.ShapeDtypeStruct(hidden.shape, F32),
            jax.ShapeDtypeStruct(grad_zx.shape, F32),
            jax.ShapeDtypeStruct(grad_out.shape, F32),
            jax.ShapeDtypeStruct((columns, count), F32),
            jax.ShapeDtypeStruct((5, width), F32),
            jax.ShapeDtypeStruct((5, n2), F32),
        ]
        + [jax.ShapeDtypeStruct((k,), F32) for k in (heads, heads, heads, width, model)],
        compiler_params=pltpu.CompilerParams(vmem_limit_bytes=62 * 2**20),
        name="finish",
    )(d_in, hidden, cotangent, mixed, scale, dots, gain, grad_zx, grad_out, grad_bc, sums, spread, pre)


def rms_scale(values):
    return lax.rsqrt(jnp.mean(values * values, axis=-1, keepdims=True) + EPS)


def gather_plain(u, g, w_zx, w_bc, w_out):
    w_zx = lax.all_gather(w_zx, "dp", axis=1, tiled=True)
    return (
        lax.all_gather(u, "tensor", axis=1, tiled=True),
        lax.all_gather(g, "tensor", axis=1, tiled=True),
        w_zx[1],
        w_zx[0],
        lax.all_gather(w_bc, "dp", axis=0, tiled=True),
        lax.all_gather(w_out, "dp", axis=1, tiled=True),
    )


def rows_of(values, piece):
    by_seq = values.reshape(-1, 4 * piece, values.shape[-1])
    return lax.psum_scatter(by_seq, "tensor", scatter_dimension=1, tiled=True)


def scatter_out_plain(piece, normed, g, u, dz, w_out):
    return (
        rows_of(dot(normed, w_out), piece),
        lax.psum_scatter(dot_tn(normed, g), "dp", scatter_dimension=1, tiled=True),
        lax.psum_scatter(dot_tn(u, dz), "dp", scatter_dimension=0, tiled=True),
    )


def scatter_in_plain(piece, u, dz, dx, w_z, w_x, w_bc, dbc):
    low = lax.psum(dbc.astype(F32), "tensor").astype(BF16)
    d_in = rows_of(dot_nt(dz, w_z) + dot_nt(dx, w_x), piece)
    first = lax.axis_index("tensor") * piece
    own = lax.dynamic_slice_in_dim(low.reshape(-1, 4 * piece, low.shape[1]), first, piece, 1)
    d_in = d_in + jnp.einsum("slc,dc->sld", own, w_bc, preferred_element_type=F32)
    return (
        d_in,
        lax.psum_scatter(dot_tn(u, dx), "dp", scatter_dimension=0, tiled=True),
        lax.psum_scatter(dot_tn(u, low), "dp", scatter_dimension=0, tiled=True),
    )


def local(
    n_dp,
    n_tensor,
    hidden,
    pre_gain,
    w_zx,
    w_bcdt,
    conv_x,
    conv_bc,
    dt_bias,
    a_log,
    d_skip,
    gate_gain,
    w_out,
    cotangent,
    segments,
):
    seqs, piece, model = hidden.shape
    length = segments.shape[1]
    tokens = seqs * length
    heads = dt_bias.shape[0]
    channels = conv_x.shape[1]
    n2 = conv_bc.shape[1]
    columns = w_bcdt.shape[1]
    tensor = lax.axis_index("tensor")
    kernels = n_dp == 8 and n_tensor == 4 and seqs == 2 and length == 4 * BLOCK

    x_piece = hidden.astype(F32)
    spread = jnp.asarray(spread_matrix(heads, channels), BF16)
    pick = jnp.asarray(pick_matrix(heads, channels), BF16)
    shared = (conv_x, conv_bc, dt_bias[None], a_log[None], d_skip[None], spread, pick)
    if kernels:
        u, g, w_x, w_z, w_bc, w_o, cx, x, cbc, bc, dt, states, normed, dz, dy, grad_gate, scale_in, marks = forward_all(
            n_dp, hidden, cotangent, w_zx, w_bcdt.T, w_out, pre_gain[None], gate_gain[None], segments, shared
        )
        g = g.reshape(tokens, model)
    else:
        scale_in = rms_scale(x_piece)
        u_piece = (x_piece * scale_in * pre_gain).astype(BF16)
        w_bc_piece = jnp.pad(w_bcdt, ((0, 0), (0, -columns % 128)))
        u, g, w_x, w_z, w_bc, w_o = gather_plain(u_piece, cotangent, w_zx, w_bc_piece, w_out)
        u = u.reshape(tokens, model)
        g = g.reshape(tokens, model)
        x = dot(u, w_x).reshape(seqs, length, channels)
        z = dot(u, w_z)
        bc_dt = dot(u, w_bc).reshape(seqs, length, -1)
        bc = bc_dt[:, :, :n2]
        dt = jnp.swapaxes(lax.dynamic_slice_in_dim(bc_dt, n2 + tensor * heads, heads, 2), 1, 2)
        marks = row_marks(segments)
        y, cx, cbc, states = ssd_forward(x, bc, dt, marks, shared)
        d_normed = dot_nt(g, w_o)
        sig_z = sigmoid(z)
        silu_z = z * sig_z
        y_flat = y.reshape(tokens, channels)
        gated = y_flat * silu_z
        scaled = d_normed * gate_gain
        sums = jnp.stack([jnp.sum(gated * gated, axis=1), jnp.sum(scaled * gated, axis=1)])
        sums = lax.psum(sums, "tensor") / (channels * n_tensor)
        inverse = lax.rsqrt(sums[0] + EPS)[:, None]
        normed = (gated * inverse * gate_gain).astype(BF16)
        grad_gate = jnp.sum(d_normed * gated * inverse, axis=0)[None]
        d_gated = inverse * scaled - gated * inverse**3 * sums[1][:, None]
        dy = (d_gated * silu_z).astype(BF16)
        dz = (d_gated * y_flat * (sig_z * (1.0 + z * (1.0 - sig_z)))).astype(BF16)
        x, bc = x.astype(BF16), bc.astype(BF16)

    back_args = (dy.reshape(seqs, length, channels), x, cx, bc, cbc, dt, marks, states, shared)
    if kernels:
        mixed, grad_out, grad_z, *rest = backward_all(n_dp, w_bc.shape[1], piece, normed, g, u, dz, w_o, *back_args)
    else:
        mixed, grad_out, grad_z = scatter_out_plain(piece, normed, g, u, dz, w_o)
        rest = ssd_backward(w_bc.shape[1], *back_args)
    dx, dbc, gx, gbc, gh = rest
    in_args = (piece, u, dz, dx.reshape(tokens, channels), w_z, w_x, w_bc, dbc.reshape(tokens, -1))
    if kernels:
        d_in, grad_zx, grad_bc, sums, dots, grad_pre = scatter_in(
            n_dp, *in_args, grad_z, gx, gbc, gh, grad_gate, pre_gain[None]
        )
        finished = finish(
            d_in, hidden, cotangent, mixed, scale_in, dots, pre_gain[None], grad_zx, grad_out, grad_bc, sums, spread,
            grad_pre, columns, n2
        )
        out_hidden, d_hidden, grad_zx, grad_out, grad_bc, grad_conv_x, grad_conv_bc, *small = finished
        grad_bias, grad_alog, grad_skip, grad_gate, grad_pre = small
        grad_bc = grad_bc.T
    else:
        d_in, grad_x, grad_bc = scatter_in_plain(*in_args)
        grad_zx = jnp.stack([grad_z, grad_x])
        grad_pre = jnp.sum(d_in * x_piece * scale_in, axis=(0, 1))
        dots = scale_in * jnp.sum(d_in * pre_gain * x_piece, axis=-1, keepdims=True)
        steps = jnp.pad(gh[:, :2].T, ((0, 0), (0, channels - heads)))
        sums = lax.psum(jnp.concatenate([gx[:6], grad_gate, steps]), "dp")
        sums = jnp.concatenate([sums[:7], jnp.concatenate([sums[7, :128], sums[8, : channels - 128]])[None]])
        grad_conv_bc, grad_pre = lax.psum((gbc[:5], grad_pre), ("dp", "tensor"))
        grad_conv_x = sums[:5]
        grad_bias, grad_alog = sums[7, :heads], sums[7, 128 : 128 + heads]
        grad_skip = sums[5].reshape(heads, -1).sum(axis=1)
        grad_gate = sums[6]
        grad_bc = grad_bc[:, :columns]
        out_hidden = (x_piece + mixed).astype(BF16)
        d_hidden = cotangent.astype(F32) + scale_in * (pre_gain * d_in) - x_piece * (scale_in**2 * dots / model)

    return (
        out_hidden,
        d_hidden,
        grad_pre,
        grad_zx,
        grad_bc,
        grad_conv_x,
        grad_conv_bc,
        grad_bias,
        grad_alog,
        grad_skip,
        grad_gate,
        grad_out,
    )


def solution(mesh):
    placed = (
        P("dp", "tensor", None),
        P(),
        P(None, "dp", "tensor"),
        P("dp", None),
        P(None, "tensor"),
        P(),
        P("tensor"),
        P("tensor"),
        P("tensor"),
        P("tensor"),
        P("tensor", "dp"),
        P("dp", "tensor", None),
        P("dp", None),
    )
    return jax.shard_map(
        functools.partial(local, mesh.shape["dp"], mesh.shape["tensor"]),
        mesh=mesh,
        in_specs=placed,
        out_specs=(
            P("dp", "tensor", None),
            P("dp", "tensor", None),
            P(),
            P(None, "dp", "tensor"),
            P("dp", None),
            P(None, "tensor"),
            P(),
            P("tensor"),
            P("tensor"),
            P("tensor"),
            P("tensor"),
            P("tensor", "dp"),
        ),
        check_vma=False,
    )
```

```python
import functools

import jax
import jax.numpy as jnp
import numpy as np
from jax import lax
from jax.experimental import pallas as pl
from jax.experimental.pallas import tpu as pltpu
from jax.sharding import PartitionSpec as P

MESH = pl.DeviceIdType.MESH
EPS = 1e-05
BLOCK = 256
F32 = jnp.float32
BF16 = jnp.bfloat16
EXACT = lax.Precision.HIGHEST
LOG2E = 1.4426950408889634
NEG = -1e30


def sigmoid(v):
    return 0.5 * jnp.tanh(0.5 * v) + 0.5


def split3(v):
    hi = v.astype(BF16)
    rest = v - hi.astype(F32)
    mid = rest.astype(BF16)
    low = (rest - mid.astype(F32)).astype(BF16)
    return hi, mid, low


def dot(a, b):
    return jnp.dot(a, b, preferred_element_type=F32)


def dot_nt(a, b):
    return lax.dot_general(a, b, (((1,), (1,)), ((), ())), preferred_element_type=F32)


def dot_tn(a, b):
    return lax.dot_general(a, b, (((0,), (0,)), ((), ())), preferred_element_type=F32)


def softplus(v):
    return jnp.maximum(v, 0.0) + jnp.log1p(jnp.exp(-jnp.abs(v)))


def head_rows(raw, dt_bias, a_log):
    q = raw.shape[1]
    upto = (
        lax.broadcasted_iota(jnp.int32, (q, q), 0) <= lax.broadcasted_iota(jnp.int32, (q, q), 1)
    ).astype(F32)
    biased = raw + dt_bias
    step = softplus(biased)
    rate = -jnp.exp(a_log) * step
    cum = jnp.dot(rate, upto, precision=EXACT, preferred_element_type=F32) * LOG2E
    return biased, step, rate, cum


def exact_nt(a, b):
    a_hi, a_mid, _ = split3(a)
    b_hi, b_mid, _ = split3(b)
    return dot_nt(a_hi, b_hi) + dot_nt(a_hi, b_mid) + dot_nt(a_mid, b_hi)


def turned(row):
    k = row.shape[1]
    own = lax.broadcasted_iota(jnp.int32, (k, k), 0) == lax.broadcasted_iota(jnp.int32, (k, k), 1)
    return jnp.sum(jnp.where(own, row, 0.0), axis=1, keepdims=True)


def to_columns(rows):
    return jnp.concatenate([rows, jnp.zeros((128 - rows.shape[0], rows.shape[1]), F32)], axis=0).T


def head_columns(reads, last, step, cum, third):
    cum_end = cum[:, BLOCK - 1 : BLOCK]
    rows = []
    for factor in (reads * jnp.exp2(cum), last * jnp.exp2(cum_end - cum) * step):
        hi, mid, _ = split3(factor)
        rows += [hi.astype(F32), mid.astype(F32)]
    cols = to_columns(jnp.concatenate(rows + [third], axis=0))
    return cols[:, 4 * cum.shape[0] :], cols.astype(BF16), jnp.exp2(cum_end)


def log2_step(step):
    return jnp.log(jnp.maximum(step, 1e-37)) * LOG2E


def forward_block(
    block, x, bc, dt, marks_ref, taps_x_ref, taps_bc_ref, bias_ref, alog_ref, skip_ref, spread_ref, pick_ref,
    y_ref, cx_ref, cbc_ref, states_ref,
    xs, bs, state, mask_bias,
):
    q = BLOCK
    heads = dt.shape[0]
    channels = x.shape[-1]
    width = channels // heads

    @pl.when(block == 0)
    def _():
        xs[0:8, :] = jnp.zeros((8, xs.shape[1]), F32)
        bs[0:8, :] = jnp.zeros((8, bs.shape[1]), F32)
        state[...] = jnp.zeros_like(state)

    marks = to_columns(marks_ref[0])
    lag_masks = [marks[:, k : k + 1] for k in range(3)]

    def conv(hold, at, taps_ref):
        out = taps_ref[4:5, at] + taps_ref[3:4, at] * hold[8 : 8 + q, at]
        for lag in (1, 2, 3):
            out = out + (lag_masks[lag - 1] * hold[8 - lag : 8 - lag + q, at]) * taps_ref[3 - lag : 4 - lag, at]
        return out

    bs[8 : 8 + q, :] = bc
    xs[8 : 8 + q, :] = x
    cbc = conv(bs, slice(None), taps_bc_ref)
    cbc_ref[0] = cbc
    bc = cbc * sigmoid(cbc)
    n = bc.shape[1] // 2
    scores = exact_nt(bc[:, n:], bc[:, :n])
    b_mat, c_mat = bc[:, :n].astype(BF16), bc[:, n:].astype(BF16)
    b_turned = b_mat.T

    _, step, _, cum = head_rows(dt, turned(bias_ref[...]), turned(alog_ref[...]))
    cols, factors, carry = head_columns(marks_ref[0, 3:4, :], marks_ref[0, 4:5, :], step, cum, cum)
    source = cum - log2_step(step)
    carry_e = jnp.sum(carry * spread_ref[...].astype(F32), axis=0, keepdims=True)
    skip_e = jnp.sum(turned(skip_ref[...]) * spread_ref[...].astype(F32), axis=0, keepdims=True)

    rows = lax.broadcasted_iota(jnp.int32, (q, q), 0)
    places = lax.broadcasted_iota(jnp.int32, (q, q), 1)
    mask_bias[...] = jnp.where((marks[:, 5:6] == marks_ref[0, 5:6, :]) & (rows >= places), 0.0, NEG)

    half = q // 2
    pair_width = 2 * width
    lane = lax.broadcasted_iota(jnp.int32, (1, pair_width), 1)
    every = slice(0, channels)
    cx = conv(xs, every, taps_x_ref)
    cx_ref[0] = cx
    xb = (cx * sigmoid(cx)).astype(BF16)
    xf = xb.astype(F32)
    stb = state[...].astype(BF16)
    states_ref[0, 0] = stb
    y_ref[...] = dot(c_mat, stb) * dot(factors, pick_ref[:, :channels]) + skip_e * xf
    scaled = (xf * dot(factors, pick_ref[:, channels:])).astype(BF16)
    state[...] = carry_e * state[...] + dot(b_turned, scaled)
    for pair in range(heads // 2):
        at = slice(pair * pair_width, (pair + 1) * pair_width)
        xp = xb[:, at]
        tops, lows = [], []
        for h in (2 * pair, 2 * pair + 1):
            col = cols[:, h : h + 1]
            row = source[h : h + 1, :]
            top = jnp.exp2((col[:half] - row[:, :half]) + mask_bias[:half, :half]) * scores[:half, :half]
            low = jnp.exp2((col[half:] - row) + mask_bias[half:, :]) * scores[half:, :]
            tops.append(top.astype(BF16))
            lows.append(low.astype(BF16))
        top = dot(jnp.concatenate(tops, axis=0), xp[:half])
        low = dot(jnp.concatenate(lows, axis=0), xp)
        first = lane < width
        y_ref[:half, at] += jnp.where(first, top[:half], top[half:])
        y_ref[half:, at] += jnp.where(first, low[:half], low[half:])

    xs[0:8, :] = xs[q : q + 8, :]
    bs[0:8, :] = bs[q : q + 8, :]


def backward_block(
    seq, step_id, dy_ref, x_ref, cx_ref, bc_ref, cbc_ref, dt_ref, marks_ref, states_ref,
    taps_x_ref, taps_bc_ref, bias_ref, alog_ref, skip_ref, spread_ref, pick_ref,
    dx_ref, dbc_ref, gx_ref, gbc_ref, gh_ref,
    ds_x, ds_bc, d_state, mask_bias, d_scores, d_in, row_sums,
):
    q = BLOCK
    heads = dt_ref.shape[1]
    channels = x_ref.shape[-1]
    width = channels // heads

    @pl.when(step_id == 0)
    def _():
        ds_x[:, q : q + 8, :] = jnp.zeros((3, 8, channels), F32)
        ds_bc[:, q : q + 8, :] = jnp.zeros((3, 8, ds_bc.shape[2]), F32)
        d_state[...] = jnp.zeros_like(d_state)

    @pl.when((step_id == 0) & (seq == 0))
    def _():
        gx_ref[...] = jnp.zeros_like(gx_ref)
        gbc_ref[...] = jnp.zeros_like(gbc_ref)
        gh_ref[...] = jnp.zeros_like(gh_ref)

    marks = to_columns(marks_ref[0])
    lag_masks = [marks[:, k : k + 1] for k in range(3)]

    def conv_back(d_out, value, hold, at, taps_ref, grad_ref):
        value = value.astype(F32)
        d_value = d_out * taps_ref[3:4, at]
        grad_ref[3:4, at] += jnp.sum(value * d_out, axis=0, keepdims=True)
        grad_ref[4:5, at] += jnp.sum(d_out, axis=0, keepdims=True)
        for lag in (1, 2, 3):
            hold[lag - 1, 0:q, at] = lag_masks[lag - 1] * d_out
            moved = hold[lag - 1, lag : lag + q, at]
            d_value = d_value + moved * taps_ref[3 - lag : 4 - lag, at]
            grad_ref[3 - lag : 4 - lag, at] += jnp.sum(value * moved, axis=0, keepdims=True)
            hold[lag - 1, q : q + 8, at] = hold[lag - 1, 0:8, at]
        return d_value

    cbc = cbc_ref[0]
    bc = cbc * sigmoid(cbc)
    n = bc.shape[1] // 2
    scores = exact_nt(bc[:, :n], bc[:, n:])
    b_mat, c_mat = bc[:, :n].astype(BF16), bc[:, n:].astype(BF16)
    c_turned = c_mat.T

    a_log = turned(alog_ref[...])
    biased, step, rate, cum = head_rows(dt_ref[0], turned(bias_ref[...]), a_log)
    source = cum - log2_step(step)
    cols, factors, carry = head_columns(marks_ref[0, 3:4, :], marks_ref[0, 4:5, :], step, cum, source)
    carry_e = jnp.sum(carry * spread_ref[...].astype(F32), axis=0, keepdims=True)
    skip_e = jnp.sum(turned(skip_ref[...]) * spread_ref[...].astype(F32), axis=0, keepdims=True)

    rows = lax.broadcasted_iota(jnp.int32, (q, q), 0)
    places = lax.broadcasted_iota(jnp.int32, (q, q), 1)
    mask_bias[...] = jnp.where((marks[:, 5:6] == marks_ref[0, 5:6, :]) & (rows <= places), 0.0, NEG)

    half = q // 2
    pair_width = 2 * width
    lane = lax.broadcasted_iota(jnp.int32, (1, pair_width), 1)
    first = lane < width
    d_scores[...] = jnp.zeros_like(d_scores)
    col_h = jnp.zeros((heads, q), F32)
    head_row = lax.broadcasted_iota(jnp.int32, (heads, 3 * half), 0)
    spread = spread_ref[...]
    cx = cx_ref[0]
    xb = (cx * sigmoid(cx)).astype(BF16)
    dyb = dy_ref[0]
    st = states_ref[0, 0]
    dye = dyb.astype(F32) * dot(factors, pick_ref[:, :channels])
    out_h = dot_nt(spread, (dye * dot(c_mat, st)).astype(BF16))
    dye = dye.astype(BF16)
    d_c = dot_nt(dye, st)
    dst = d_state[...].astype(BF16)
    kept = jnp.sum(d_state[...] * st.astype(F32), axis=0, keepdims=True) * carry_e
    carried = jnp.sum(spread.astype(F32) * kept, axis=1, keepdims=True)
    d_state[...] = carry_e * d_state[...] + dot(c_turned, dye)
    xf = xb.astype(F32)
    to_end = dot(factors, pick_ref[:, channels:])
    d_b = dot_nt((xf * to_end).astype(BF16), dst)
    dx_st = dot(b_mat, dst) * to_end
    state_h = dot_nt(spread, (xf * dx_st).astype(BF16))
    d_in[...] = dx_st
    for pair in range(heads // 2):
        at = slice(pair * pair_width, (pair + 1) * pair_width)
        xp, dyp = xb[:, at], dyb[:, at]
        none = jnp.zeros_like(xp)
        x_first, x_second = jnp.where(first, xp, none), jnp.where(first, none, xp)
        g_top = dot_nt(jnp.concatenate([x_first[:half], x_second[:half]], axis=0), dyp)
        g_low = dot_nt(jnp.concatenate([x_first[half:], x_second[half:]], axis=0), dyp[half:])
        tops, lows, d_top, d_low = [], [], 0.0, 0.0
        for which in (0, 1):
            h = 2 * pair + which
            own = slice(which * half, (which + 1) * half)
            col = cols[:, h : h + 1]
            row = cum[h : h + 1, :]
            top = jnp.exp2((row - col[:half]) + mask_bias[:half, :])
            low = jnp.exp2((row[:, half:] - col[half:]) + mask_bias[half:, half:])
            p_top = top * g_top[own]
            p_low = low * g_low[own]
            d_top = d_top + p_top
            d_low = d_low + p_low
            m_top = p_top * scores[:half, :]
            m_low = p_low * scores[half:, half:]
            late = jnp.sum(m_top[:, half:], axis=0, keepdims=True) + jnp.sum(m_low, axis=0, keepdims=True)
            row_sums[h : h + 1, :half] = jnp.sum(m_top[:, :half], axis=0, keepdims=True)
            row_sums[h : h + 1, half:] = late
            parts = split3(jnp.concatenate([m_top[:, :half] + m_top[:, half:], m_low], axis=0))
            col_h = col_h + dot_nt((head_row == h).astype(BF16), jnp.concatenate(parts, axis=1))
            tops.append((top * scores[:half, :]).astype(BF16))
            lows.append((low * scores[half:, half:]).astype(BF16))
        d_scores[:half, :] += d_top
        d_scores[half:, half:] += d_low
        top = dot(jnp.concatenate(tops, axis=0), dyp)
        low = dot(jnp.concatenate(lows, axis=0), dyp[half:])
        d_in[:half, at] += jnp.where(first, top[:half], top[half:])
        d_in[half:, at] += jnp.where(first, low[:half], low[half:])

    everywhere = slice(0, channels)
    dyf = dy_ref[0].astype(F32)
    cx = cx_ref[0]
    sig = sigmoid(cx)
    gx_ref[5:6, :] += jnp.sum(dyf * (cx * sig).astype(BF16).astype(F32), axis=0, keepdims=True)
    d_cx = (d_in[...] + skip_e * dyf) * (sig * (1.0 + cx * (1.0 - sig)))
    dx_ref[0] = conv_back(d_cx, x_ref[0], ds_x, everywhere, taps_x_ref, gx_ref).astype(BF16)

    dsb = d_scores[...].astype(BF16)
    d_b = d_b + dot(dsb, c_mat)
    d_c = d_c + dot_tn(dsb, b_mat)
    sig = sigmoid(cbc)
    d_cbc = jnp.concatenate([d_b, d_c], axis=1) * (sig * (1.0 + cbc * (1.0 - sig)))
    every = slice(0, 2 * n)
    dbc_ref[0, :, every] = conv_back(d_cbc, bc_ref[0], ds_bc, every, taps_bc_ref, gbc_ref).astype(BF16)

    used_h = col_h + state_h
    diff_h = row_sums[...] - col_h + out_h
    since = (rows >= places).astype(F32)
    before = (rows < places).astype(F32)
    d_rate = (
        jnp.dot(diff_h, since, precision=EXACT, preferred_element_type=F32)
        + jnp.dot(state_h, before, precision=EXACT, preferred_element_type=F32)
        + carried
    )
    sig_dt = sigmoid(biased)
    ratio = jnp.where(step < 1e-30, 1.0, sig_dt / jnp.maximum(step, 1e-30))
    d_raw = used_h * ratio - jnp.exp(a_log) * sig_dt * d_rate
    lanes = dbc_ref.shape[2] - 2 * n
    mine = lax.broadcasted_iota(jnp.int32, (heads, lanes), 0) + lax.axis_index("tensor") * heads
    own = (lax.broadcasted_iota(jnp.int32, (heads, lanes), 1) == mine).astype(BF16)
    dbc_ref[0, :, 2 * n :] = dot_tn(d_raw.astype(BF16), own).astype(BF16)
    gh_ref[:, 0:1] += jnp.sum(d_raw, axis=1, keepdims=True)
    gh_ref[:, 1:2] += jnp.sum(d_rate * rate, axis=1, keepdims=True)


def row_marks(segments):
    seqs, length = segments.shape
    blocks = length // BLOCK
    lags = []
    for lag in (1, 2, 3):
        earlier = jnp.pad(segments, ((0, 0), (lag, 0)), constant_values=-1)[:, :length]
        lags.append(earlier == segments)
    grouped = segments.reshape(seqs, blocks, BLOCK)
    before = jnp.pad(segments, ((0, 0), (1, 0)), constant_values=-1)[:, :length].reshape(seqs, blocks, BLOCK)
    reads = (grouped == before[:, :, :1]).reshape(seqs, length)
    last = (grouped == grouped[:, :, -1:]).reshape(seqs, length)
    rows = [m.astype(F32) for m in (*lags, reads, last, segments)]
    return jnp.stack(rows + [jnp.zeros_like(rows[0])] * 2, axis=1)


def spread_matrix(heads, channels):
    width = channels // heads
    return (np.arange(heads)[:, None] == np.arange(channels)[None, :] // width).astype(np.float32)


def pick_matrix(heads, channels):
    spread = spread_matrix(heads, channels)
    out = np.zeros((128, 2 * channels), np.float32)
    for part in range(4):
        at = slice(part // 2 * channels, (part // 2 + 1) * channels)
        out[part * heads : (part + 1) * heads, at] = spread
    return out


def shared_specs(channels, n2, heads):
    full = lambda *shape: pl.BlockSpec(shape, lambda *i: (0,) * len(shape))
    return [
        full(5, channels),
        full(5, n2),
        full(1, heads),
        full(1, heads),
        full(1, heads),
        full(heads, channels),
        full(128, 2 * channels),
    ]


def forward_scratch(channels, n2):
    return [
        pltpu.VMEM((BLOCK + 8, channels), F32),
        pltpu.VMEM((BLOCK + 8, n2), F32),
        pltpu.VMEM((n2 // 2, channels), F32),
        pltpu.VMEM((BLOCK, BLOCK), F32),
    ]


def forward_kernel(x_ref, bc_ref, dt_ref, *refs):
    y_ref = refs[8]
    forward_block(pl.program_id(1), x_ref[0], bc_ref[0], dt_ref[0], *refs[:8], y_ref.at[0], *refs[9:])


def ssd_forward(x, bc, dt, marks, shared):
    seqs, length, channels = x.shape
    n2, heads = bc.shape[2], dt.shape[1]
    blocks = length // BLOCK
    tok = lambda w: pl.BlockSpec((1, BLOCK, w), lambda s, c: (s, c, 0))
    head = lambda w: pl.BlockSpec((1, w, BLOCK), lambda s, c: (s, 0, c))
    return pl.pallas_call(
        forward_kernel,
        grid=(seqs, blocks),
        in_specs=[tok(channels), tok(n2), head(heads), head(8)] + shared_specs(channels, n2, heads),
        out_specs=[
            tok(channels),
            tok(channels),
            tok(n2),
            pl.BlockSpec((1, 1, n2 // 2, channels), lambda s, c: (s, c, 0, 0)),
        ],
        out_shape=[
            jax.ShapeDtypeStruct((seqs, length, channels), F32),
            jax.ShapeDtypeStruct((seqs, length, channels), F32),
            jax.ShapeDtypeStruct((seqs, length, n2), F32),
            jax.ShapeDtypeStruct((seqs, blocks, n2 // 2, channels), BF16),
        ],
        scratch_shapes=forward_scratch(channels, n2),
        compiler_params=pltpu.CompilerParams(vmem_limit_bytes=48 * 2**20),
        name="ssd_forward",
    )(x, bc, dt, marks, *shared)


def backward_kernel(*refs):
    backward_block(pl.program_id(0), pl.program_id(1), *refs)


def backward_scratch(channels, n2, heads):
    return [
        pltpu.VMEM((3, BLOCK + 8, channels), F32),
        pltpu.VMEM((3, BLOCK + 8, n2), F32),
        pltpu.VMEM((n2 // 2, channels), F32),
        pltpu.VMEM((BLOCK, BLOCK), F32),
        pltpu.VMEM((BLOCK, BLOCK), F32),
        pltpu.VMEM((BLOCK, channels), F32),
        pltpu.VMEM((heads, BLOCK), F32),
    ]


def backward_specs(channels, n2, heads, small, place):
    tok = lambda w: pl.BlockSpec((1, BLOCK, w), lambda *i: (*place(*i), 0))
    full = lambda *shape: pl.BlockSpec(shape, lambda *i: (0,) * len(shape))
    ins = [tok(channels)] * 3 + [tok(n2)] * 2 + [
        pl.BlockSpec((1, heads, BLOCK), lambda *i: (place(*i)[0], 0, place(*i)[1])),
        pl.BlockSpec((1, 8, BLOCK), lambda *i: (place(*i)[0], 0, place(*i)[1])),
        pl.BlockSpec((1, 1, n2 // 2, channels), lambda *i: (*place(*i), 0, 0)),
    ]
    ins += shared_specs(channels, n2, heads)
    return ins, [tok(channels), tok(small), full(8, channels), full(8, n2), full(heads, 128)]


def backward_outs(seqs, length, channels, n2, heads, small):
    return [
        jax.ShapeDtypeStruct((seqs, length, channels), BF16),
        jax.ShapeDtypeStruct((seqs, length, small), BF16),
        jax.ShapeDtypeStruct((8, channels), F32),
        jax.ShapeDtypeStruct((8, n2), F32),
        jax.ShapeDtypeStruct((heads, 128), F32),
    ]


def ssd_backward(small, dy, x, cx, bc, cbc, dt, marks, states, shared):
    seqs, length, channels = x.shape
    n2, heads = bc.shape[2], dt.shape[1]
    blocks = length // BLOCK
    ins, outs = backward_specs(channels, n2, heads, small, lambda s, c: (s, blocks - 1 - c))
    return pl.pallas_call(
        backward_kernel,
        grid=(seqs, blocks),
        in_specs=ins,
        out_specs=outs,
        out_shape=backward_outs(seqs, length, channels, n2, heads, small),
        scratch_shapes=backward_scratch(channels, n2, heads),
        compiler_params=pltpu.CompilerParams(vmem_limit_bytes=56 * 2**20),
        name="ssd_backward",
    )(dy, x, cx, bc, cbc, dt, marks, states, *shared)


def ring_place(n):
    dp = lax.axis_index("dp")
    z, y = dp // 2, dp % 2

    def at(place):
        q = (place + 4 * n) % n
        return 2 * q + (q // (n // 2)) * (2 * n - 1 - 4 * q)

    return z + y * (n - 1 - 2 * z), at


def tensor_place():
    t = lax.axis_index("tensor")
    return t, t + 1 - 2 * (t % 2), (t + 2) % 4


def greet(n, more=()):
    place, at = ring_place(n)
    _, other, across = tensor_place()
    sem = pltpu.get_barrier_semaphore()
    targets = [{"dp": at(place + 1)}, {"dp": at(place - 1)}, {"tensor": other}, {"tensor": across}, *more]
    for target in targets:
        pl.semaphore_signal(sem, inc=1, device_id=target, device_id_type=MESH)
    pl.semaphore_wait(sem, len(targets))


def remote(src, dst, send_sem, recv_sem, target):
    return pltpu.make_async_remote_copy(
        src_ref=src, dst_ref=dst, send_sem=send_sem, recv_sem=recv_sem, device_id=target, device_id_type=MESH
    )


def span(first, count, unit):
    return pl.ds(pl.multiple_of(first, unit), count)


class RingGather:
    def __init__(self, n, parts, keep, sems):
        self.n, self.parts, self.keep = n, parts, keep
        self.send_sem, self.recv_sem = sems
        self.place, self.at = ring_place(n)

    def copy(self, way, part, step):
        sign = 1 - 2 * way
        ref = self.keep(way, part, self.at(self.place - sign * step))
        return remote(
            ref,
            ref,
            self.send_sem.at[way, part, step],
            self.recv_sem.at[way, part, step],
            {"dp": self.at(self.place + sign)},
        )

    def step(self, k):
        for part in range(self.parts):
            for way in (0, 1):
                if k > 0:
                    self.copy(way, part, k - 1).wait_recv()
                if k < self.n - 1:
                    self.copy(way, part, k).start()

    def later(self, k):
        for part in range(self.parts):
            for way in (0, 1):
                self.copy(way, part, k - 1).wait_recv()

                @pl.when(k < self.n - 1)
                def _():
                    self.copy(way, part, k).start()

    def finish(self):
        for k in range(self.n - 1):
            for part in range(self.parts):
                for way in (0, 1):
                    self.copy(way, part, k).wait_send()


class RowGather:
    def __init__(self, keep, sems):
        self.keep = keep
        self.send_sem, self.recv_sem = sems
        self.me, self.other, self.across = tensor_place()

    def copy(self, kind, part):
        ref = self.keep(part, self.across if kind == 2 else self.me)
        target = self.across if kind == 0 else self.other
        return remote(
            ref, ref, self.send_sem.at[kind, part], self.recv_sem.at[kind, part], {"tensor": target}
        )

    def start(self, part):
        self.copy(0, part).start()
        self.copy(1, part).start()

    def forward(self, part):
        self.copy(0, part).wait_recv()
        self.copy(2, part).start()

    def wait(self, part):
        self.copy(1, part).wait_recv()
        self.copy(2, part).wait_recv()

    def finish(self, parts):
        for part in range(parts):
            for kind in range(3):
                self.copy(kind, part).wait_send()


def marks_of(seg):
    length = seg.shape[1]
    lane = lax.broadcasted_iota(jnp.int32, seg.shape, 1)
    row = lax.broadcasted_iota(jnp.int32, seg.shape, 0)
    earlier = [jnp.where(lane < lag, -1.0, pltpu.roll(seg, lag, 1)) for lag in (1, 2, 3)]
    starts = range(0, length, BLOCK)
    spread = lambda values, at: jnp.broadcast_to(values[:, at : at + 1], (seg.shape[0], BLOCK))
    before = jnp.concatenate([spread(earlier[0], at) for at in starts], axis=1)
    final = jnp.concatenate([spread(seg, at + BLOCK - 1) for at in starts], axis=1)
    out = jnp.where(row == 5, seg, 0.0)
    for k, other in enumerate((*earlier, before, final)):
        out = jnp.where((row == k) & (other == seg), 1.0, out)
    return out


def all_kernel(n, *refs):
    (hidden_ref, g_ref, wzx_ref, wbc_ref, wout_ref, gain_ref, gate_ref, seg_ref), refs = refs[:8], refs[8:]
    shared, refs = refs[:7], refs[7:]
    (u_out, gf_out, wx_out, wz_out, wb_out, wo_out), refs = refs[:6], refs[6:]
    (cx_ref, x_ref, cbc_ref, bc_ref, dt_ref, states_ref), refs = refs[:6], refs[6:]
    (normed_ref, dz_ref, dy_ref, grad_ref, scale_ref, marks_ref), refs = refs[:6], refs[6:]
    scratch, refs = refs[:4], refs[4:]
    (u, wx, wz, wo, wb, wb_own, wdt, g_cols, y, z, dn, sums), refs = refs[:12], refs[12:]
    (load_sem, keep_sem, stream_sem), sems = refs[:3], refs[3:]

    i = pl.program_id(0)
    rows, width = wzx_ref.shape[1:]
    out_rows, out_cols = wout_ref.shape
    seqs, piece, model = hidden_ref.shape
    length = 4 * piece
    blocks = length // BLOCK
    heads = dt_ref.shape[1]
    n2 = bc_ref.shape[2]
    small_cols = wb.shape[1]
    dp = lax.axis_index("dp")
    place, at = ring_place(n)
    me, other, across = tensor_place()
    core = me % 2
    facing = (other + 2) % 4

    def keep_wide(ref):
        def keep(way, part, d):
            return ref.at[span(d * rows, rows, 16), pl.ds(way * width // 2 + part * width // 4, width // 4)]

        return keep

    def keep_out(way, part, d):
        first = way * out_rows // 2 + part * out_rows // 4
        return wo.at[pl.ds(first, out_rows // 4), span(d * out_cols, out_cols, 128)]

    def keep_small(way, part, d):
        return wb.at[span(d * rows + core * rows // 2 + way * rows // 4, rows // 4, 16), :]

    def keep_rows(part, t):
        if part < seqs:
            return u.at[span(part * length + t * piece, piece, 16), :]
        return gf_out.at[part - seqs, span(t * piece, piece, 16), :]

    x_ring = RingGather(n, 2, keep_wide(wx), sems[0:2])
    small = RingGather(n, 1, keep_small, sems[2:4])
    z_ring = RingGather(n, 2, keep_wide(wz), sems[4:6])
    out_ring = RingGather(n, 2, keep_out, sems[6:8])
    token_rows = RowGather(keep_rows, sems[8:10])
    halves_send, halves_recv, sums_send, sums_recv = sems[10:14]

    def half(ahead, whose):
        d = (dp + ahead) % n
        ref = wb.at[span(d * rows + whose * rows // 2, rows // 2, 16), :]
        return remote(ref, ref, halves_send.at[ahead], halves_recv.at[ahead], {"tensor": other})

    def sums_copy(kind):
        ref = sums.at[me]
        target = {"tensor": (other, across, facing)[kind]}
        return remote(ref, ref, sums_send.at[kind], sums_recv.at[kind], target)

    keeps = [
        pltpu.make_async_copy(src, dst, keep_sem.at[j])
        for j, (src, dst) in enumerate(((wx, wx_out), (wb, wb_out), (wz, wz_out), (u, u_out), (wo, wo_out)))
    ]

    def streams(k):
        return [
            pltpu.make_async_copy(
                gf_out.at[:, :, span(at(place - (1 - 2 * way) * k) * out_cols, out_cols, 128)],
                g_cols.at[way],
                stream_sem.at[way],
            )
            for way in (0, 1)
        ]

    def start(copies):
        for copy in copies:
            copy.start()

    def wait(copies):
        for copy in copies:
            copy.wait()

    @pl.when(i == 0)
    def _():
        def held(s, h):
            return z.at[pl.ds((2 * s + h) * piece, piece), :]

        halves = [(s, h) for s in range(seqs) for h in (0, 1)]
        cut = lambda h: pl.ds(h * (model // 2), model // 2)
        own = [
            (wzx_ref.at[1], wx.at[span(dp * rows, rows, 16), :]),
            (wbc_ref, wb_own),
            (wzx_ref.at[0], wz.at[span(dp * rows, rows, 16), :]),
            (wout_ref, wo.at[:, span(dp * out_cols, out_cols, 128)]),
        ]
        own += [(hidden_ref.at[s, :, cut(h)], held(seqs + s, h)) for s, h in halves]
        own += [(g_ref.at[s, :, cut(h)], held(s, h)) for s, h in halves]
        loads = [pltpu.make_async_copy(a, b, load_sem.at[j]) for j, (a, b) in enumerate(own)]
        first = 4 + 2 * seqs
        stores = [
            pltpu.make_async_copy(
                held(s, h), gf_out.at[s, span(me * piece, piece, 16), cut(h)], load_sem.at[first + 2 * seqs + j]
            )
            for j, (s, h) in enumerate(halves)
        ]
        start(loads)
        greet(n, [{"tensor": facing}])
        loads[0].wait()
        x_ring.step(0)
        loads[1].wait()
        mine = span(dp * rows, rows, 16)
        short = jnp.zeros((small_cols - wb_own.shape[0], rows), BF16)
        wb[mine, :] = jnp.concatenate([wb_own[...], short], axis=0).T
        small.step(0)
        wait(loads[4:first])
        for s in range(seqs):
            left = z[pl.ds((2 * (seqs + s)) * piece, piece), :].astype(F32)
            right = z[pl.ds((2 * (seqs + s) + 1) * piece, piece), :].astype(F32)
            squares = jnp.sum(left * left + right * right, axis=1, keepdims=True)
            scale = lax.rsqrt(squares / model + EPS)
            scale_ref[s] = jnp.broadcast_to(scale, (piece, 128))
            to = span(s * length + me * piece, piece, 16)
            u[to, cut(0)] = (left * scale * gain_ref[:, cut(0)]).astype(BF16)
            u[to, cut(1)] = (right * scale * gain_ref[:, cut(1)]).astype(BF16)
            token_rows.start(s)
        for s in range(seqs):
            seg = seg_ref[s : s + 1, :].astype(F32)
            marks_ref[s] = marks_of(jnp.broadcast_to(seg, (8, seg.shape[1])))
        wait(loads[first:])
        start(stores)
        wait(loads[2:4])
        wait(stores)
        for k in range(1, n):
            x_ring.step(k)
            small.step(k)
            if k == n - 1:
                z_ring.step(0)
            if k == n // 2:
                token_rows.forward(0)
                token_rows.start(seqs)
        for ahead in range(1, n):
            half(ahead, core).start()
        for ahead in range(1, n):
            half(ahead, 1 - core).wait_recv()
        token_rows.wait(0)
        start(keeps[:2])
        lanes = small_cols - n2
        pick = lax.broadcasted_iota(jnp.int32, (heads, lanes), 1) == (
            lax.broadcasted_iota(jnp.int32, (heads, lanes), 0) + me * heads
        )
        wdt[...] = dot_nt(pick.astype(BF16), wb[:, n2:]).astype(BF16)

    b = i - 1

    @pl.when((b >= 0) & (b < n))
    def _():
        @pl.when(b < n - 1)
        def _():
            z_ring.later(b + 1)

        @pl.when(b == n - 2)
        def _():
            out_ring.step(0)
            token_rows.forward(seqs)

        @pl.when(b == n - 1)
        def _():
            keeps[2].start()
            out_ring.step(1)

        @pl.when(b == 0)
        def _():
            token_rows.forward(1)
            token_rows.start(seqs + 1)

        @pl.when(b == blocks)
        def _():
            token_rows.wait(1)
            keeps[3].start()

        at_block = span(b * BLOCK, BLOCK, BLOCK)
        tokens = u[at_block, :]
        marks = marks_ref.at[pl.ds(b // blocks, 1), :, span(b % blocks * BLOCK, BLOCK, BLOCK)]
        x = dot(tokens, wx[...])
        bc = dot(tokens, wb[:, :n2])
        dt = dot_nt(wdt[...], tokens)
        x_ref[0] = x.astype(BF16)
        bc_ref[0] = bc.astype(BF16)
        dt_ref[0] = dt
        forward_block(
            b % blocks, x, bc, dt, marks, *shared, y.at[at_block, :], cx_ref, cbc_ref, states_ref, *scratch
        )

        @pl.when(b == n - 1)
        def _():
            token_rows.forward(seqs + 1)

    slope = wx

    def add_shard(k):
        wait(streams(k))
        for way in (0, 1):
            e = pl.ds(way * (out_rows // 2), out_rows // 2)
            d = at(place - (1 - 2 * way) * k)
            cols = g_cols[way].reshape(seqs * length, out_cols)
            value = dot_nt(cols, wo[e, span(d * out_cols, out_cols, 128)])

            @pl.when(k == 0)
            def _():
                dn[:, e] = value

            @pl.when(k > 0)
            def _():
                dn[:, e] += value

    def gate_block(e, _):
        part = span(e * BLOCK, BLOCK, BLOCK)
        zf = dot(u[part, :], wz[...])
        sig = sigmoid(zf)
        silu = zf * sig
        yf = y[part, :]
        y[part, :] = yf * silu
        z[part, :] = silu.astype(BF16)
        slope[part, :] = (yf * (sig + silu * (1.0 - sig))).astype(BF16)
        return 0

    def shard_step(c, _):
        @pl.when(c == 0)
        def _():
            token_rows.wait(seqs)
            token_rows.wait(seqs + 1)
            start(streams(0))
            add_shard(0)
            start(streams(1))
            keeps[0].wait()
            x_ring.finish()

        @pl.when((c >= 1) & (c <= 4))
        def _():
            lax.fori_loop(2 * (c - 1), 2 * c, gate_block, 0)

        add_shard(c + 1)
        start(streams(c + 2))
        out_ring.later(c + 2)
        return 0

    @pl.when(i == n + 1)
    def _():
        lax.fori_loop(0, n - 2, shard_step, 0)
        add_shard(n - 1)
        keeps[4].start()

        def block_sums(e, _):
            part = span(e * BLOCK, BLOCK, BLOCK)
            gated = y[part, :]
            squares = jnp.sum(gated * gated, axis=1, keepdims=True)
            inner = jnp.sum(gate_ref[...] * dn[part, :] * gated, axis=1, keepdims=True)
            lane = lax.broadcasted_iota(jnp.int32, (1, 128), 1)
            both = jnp.where(lane == 0, squares, jnp.where(lane == 1, inner, 0.0))
            sums[me, :, part] = both.T[0:8, :]
            return 0

        lax.fori_loop(0, n, block_sums, 0)
        for kind in range(3):
            sums_copy(kind).start()

    e = i - (n + 2)

    @pl.when(e >= 0)
    def _():
        @pl.when(e == 0)
        def _():
            for kind in range(3):
                sums_copy(kind).wait_recv()
            grad_ref[...] = jnp.zeros_like(grad_ref)

        part = span(e * BLOCK, BLOCK, BLOCK)
        whole = (sums[0, :, part] + sums[1, :, part]) + (sums[2, :, part] + sums[3, :, part])
        cols = jnp.concatenate([whole, jnp.zeros((120, BLOCK), F32)], axis=0).T / (4 * width)
        inverse = lax.rsqrt(cols[:, 0:1] + EPS)
        dnf = dn[part, :]
        gain = gate_ref[...]
        gated = y[part, :]
        scaled_gated = gated * inverse
        normed_ref[...] = (scaled_gated * gain).astype(BF16)
        grad_ref[...] += jnp.sum(dnf * scaled_gated, axis=0, keepdims=True)
        d_gated = inverse * (dnf * gain) - gated * (inverse * inverse * inverse * cols[:, 1:2])
        dy_ref[...] = (d_gated * z[part, :].astype(F32)).astype(BF16)
        dz_ref[...] = (d_gated * slope[part, :].astype(F32)).astype(BF16)

        @pl.when(e == n - 1)
        def _():
            wait(keeps[1:])
            for ring in (small, z_ring, out_ring):
                ring.finish()
            token_rows.finish(2 * seqs)
            for ahead in range(1, n):
                half(ahead, core).wait_send()
            for kind in range(3):
                sums_copy(kind).wait_send()


def forward_all(n, hidden, g, w_zx, w_bc, w_out, pre_gain, gate_gain, segments, shared):
    seqs, piece, model = hidden.shape
    rows, width = w_zx.shape[1:]
    out_rows, out_cols = w_out.shape
    length = 4 * piece
    tokens = seqs * length
    blocks = length // BLOCK
    n2 = shared[1].shape[1]
    heads = shared[2].shape[1]
    columns = w_bc.shape[0]
    small = columns + -columns % 128
    sem = pltpu.SemaphoreType.DMA
    ring = [sem((2, 2, n - 1))] * 2
    anywhere = pl.BlockSpec(memory_space=pl.ANY)
    whole = lambda *shape: pl.BlockSpec(shape, lambda i: (0,) * len(shape))
    b = lambda i: jnp.minimum(jnp.maximum(i - 1, 0), n - 1)
    e = lambda i: jnp.maximum(i - (n + 2), 0)
    tok = lambda w: pl.BlockSpec((1, BLOCK, w), lambda i: (b(i) // blocks, b(i) % blocks, 0))
    gate = pl.BlockSpec((BLOCK, width), lambda i: (e(i), 0))
    out_shape = [
        ((tokens, model), BF16),
        ((seqs, length, model), BF16),
        ((rows * n, width), BF16),
        ((rows * n, width), BF16),
        ((rows * n, small), BF16),
        ((out_rows, out_cols * n), BF16),
        ((seqs, length, width), F32),
        ((seqs, length, width), BF16),
        ((seqs, length, n2), F32),
        ((seqs, length, n2), BF16),
        ((seqs, heads, length), F32),
        ((seqs, blocks, n2 // 2, width), BF16),
        ((tokens, width), BF16),
        ((tokens, width), BF16),
        ((tokens, width), BF16),
        ((1, width), F32),
        ((seqs, piece, 128), F32),
        ((seqs, 8, length), F32),
    ]
    return pl.pallas_call(
        functools.partial(all_kernel, n),
        grid=(2 * n + 2,),
        in_specs=[anywhere] * 5
        + [
            whole(1, model),
            whole(1, width),
            whole(*segments.shape),
        ]
        + shared_specs(width, n2, heads),
        out_specs=[anywhere] * 6
        + [tok(width), tok(width), tok(n2), tok(n2)]
        + [pl.BlockSpec((1, heads, BLOCK), lambda i: (b(i) // blocks, 0, b(i) % blocks))]
        + [pl.BlockSpec((1, 1, n2 // 2, width), lambda i: (b(i) // blocks, b(i) % blocks, 0, 0))]
        + [gate] * 3
        + [whole(1, width), whole(seqs, piece, 128), whole(seqs, 8, length)],
        out_shape=[jax.ShapeDtypeStruct(*s) for s in out_shape],
        scratch_shapes=forward_scratch(width, n2)
        + [
            pltpu.VMEM((tokens, model), BF16),
            pltpu.VMEM((rows * n, width), BF16),
            pltpu.VMEM((rows * n, width), BF16),
            pltpu.VMEM((out_rows, out_cols * n), BF16),
            pltpu.VMEM((rows * n, small), BF16),
            pltpu.VMEM(w_bc.shape, BF16),
            pltpu.VMEM((heads, rows * n), BF16),
            pltpu.VMEM((2, seqs, length, out_cols), BF16),
            pltpu.VMEM((tokens, width), F32),
            pltpu.VMEM((tokens, width), BF16),
            pltpu.VMEM((tokens, width), F32),
            pltpu.VMEM((4, 8, tokens), F32),
            sem((4 + 6 * seqs,)),
            sem((5,)),
            sem((2,)),
        ]
        + ring + [sem((2, 1, n - 1))] * 2 + ring + ring
        + [sem((3, 2 * seqs))] * 2 + [sem((n,))] * 2 + [sem((3,))] * 2,
        compiler_params=pltpu.CompilerParams(
            collective_id=0, has_side_effects=True, vmem_limit_bytes=63 * 2**20
        ),
        name="forward_all",
    )(hidden, g, w_zx, w_bc, w_out, pre_gain, gate_gain, segments, *shared)


class RingScatter:
    def __init__(self, n, terms, slots, sems, ways=2, sign=1):
        self.n, self.terms, self.slots, self.ways, self.sign = n, terms, slots, ways, sign
        self.send_sem, self.recv_sem = sems
        self.place, self.at = ring_place(n)

    def turn(self, way):
        return self.sign * (1 - 2 * way)

    def owner(self, way, k):
        return self.at(self.place - self.turn(way) * (1 + k))

    def copy(self, way, k):
        return remote(
            self.slots.at[way, k],
            self.slots.at[way, k + 1],
            self.send_sem.at[way, k],
            self.recv_sem.at[way, k],
            {"dp": self.at(self.place + self.turn(way))},
        )

    def step(self, way, k):
        @pl.when(k == 0)
        def _():
            self.slots[way, 0] = self.terms[way].astype(BF16)

        @pl.when(k > 0)
        def _():
            self.copy(way, k - 1).wait_recv()

            @pl.when(k < self.n - 1)
            def _():
                self.slots[way, k] = (self.terms[way].astype(F32) + self.slots[way, k].astype(F32)).astype(BF16)

        @pl.when(k < self.n - 1)
        def _():
            self.copy(way, k).start()

    def last(self, way):
        return self.terms[way].astype(F32) + self.slots[way, self.n - 1].astype(F32)

    def finish(self):
        for k in range(self.n - 1):
            for way in range(self.ways):
                self.copy(way, k).wait_send()


class RowScatter:
    def __init__(self, parts, value, hold, sems):
        self.parts, self.value, self.hold = parts, value, hold
        self.send_sem, self.recv_sem = sems
        self.me, self.other, self.across = tensor_place()

    def copy(self, kind, part):
        src, dst = ((0, 1), (1, 2), (0, 3))[kind]
        return remote(
            self.hold.at[src, part],
            self.hold.at[dst, part],
            self.send_sem.at[kind, part],
            self.recv_sem.at[kind, part],
            {"tensor": self.across if kind == 1 else self.other},
        )

    def stage(self, j):
        late = j // (2 * self.parts)
        near = j - 2 * self.parts
        stage = (1 - late) * (j % 2) + late * (2 + near // self.parts)
        return stage, (1 - late) * (j // 2) + late * (near % self.parts)

    def owner(self, j):
        stage, part = self.stage(j)
        x, core = self.me // 2, self.me % 2
        return 2 * ((x + 1 - stage // 2) % 2) + (core + 1 - stage % 2) % 2, part

    def step(self, j, store, wait=True):
        stage, part = self.stage(j)

        @pl.when(stage == 0)
        def _():
            self.hold[0, part] = self.value[...].astype(BF16)
            self.copy(0, part).start()

        @pl.when(stage == 1)
        def _():
            self.copy(0, part).wait_recv()
            self.hold[1, part] = (self.value[...].astype(F32) + self.hold[1, part].astype(F32)).astype(BF16)
            self.copy(1, part).start()

        @pl.when(stage == 2)
        def _():
            self.copy(0, part).wait_send()
            self.hold[0, part] = self.value[...].astype(BF16)
            self.copy(2, part).start()

        @pl.when(stage == 3)
        def _():
            value = self.value[...].astype(F32)
            store(part, value + self.arrived(part) if wait else value)

    def arrived(self, part):
        self.copy(2, part).wait_recv()
        self.copy(1, part).wait_recv()
        return self.hold[3, part].astype(F32) + self.hold[2, part].astype(F32)

    def finish(self):
        for part in range(self.parts):
            for kind in (1, 2):
                self.copy(kind, part).wait_send()


def back_kernel(n, *refs):
    (normed_ref, g_ref, u_ref, dz_ref, wo_ref), refs = refs[:5], refs[5:]
    ins, refs = refs[:15], refs[15:]
    (out_ref, gout_ref, gz_ref), refs = refs[:3], refs[3:]
    outs, refs = refs[:5], refs[5:]
    scratch, refs = refs[:7], refs[7:]
    normed, dz, wo, g_cols, u_cols, out_slots, z_slots, hold, terms, mixed, load_sem, stream_sem, out_sem = refs[:13]
    sems = refs[13:]

    k = pl.program_id(0)
    blocks = 4
    piece = out_ref.shape[1]
    length = blocks * BLOCK
    count = g_ref.shape[1] // n
    half = gz_ref.shape[1] // 2
    place, at = ring_place(n)

    loads = [
        pltpu.make_async_copy(src, dst, load_sem.at[i])
        for i, (src, dst) in enumerate(((normed_ref, normed), (dz_ref, dz), (wo_ref, wo)))
    ]

    def streams(k):
        copies = []
        for way in (0, 1):
            d = at(place - (1 - 2 * way) * (1 + k))
            for i, (src, dst) in enumerate(((g_ref, g_cols), (u_ref, u_cols))):
                copies.append(
                    pltpu.make_async_copy(
                        src.at[:, span(d * count, count, 128)], dst.at[way], stream_sem.at[i, way]
                    )
                )
        return copies

    @pl.when(k == 0)
    def _():
        for copy in streams(0) + loads:
            copy.start()
        greet(n)

    backward_block(k // blocks, k % blocks, *ins, *outs, *scratch)

    @pl.when(k == 0)
    def _():
        for copy in loads:
            copy.wait()

    for copy in streams(k):
        copy.wait()

    rows = RowScatter(2, mixed, hold, sems[4:6])
    owner = rows.owner(k)
    own_rows = span(owner[1] * length + owner[0] * piece, piece, 16)

    for ring, (from_cols, to_cols) in enumerate(((g_cols, normed), (u_cols, dz))):
        for way in (0, 1):
            value = dot_tn(from_cols[way], to_cols[:, pl.ds(way * half, half)])
            terms[ring, way] = value.astype(BF16)
    mixed[...] = dot(normed[own_rows, :], wo[...]).astype(BF16)

    out_ring = RingScatter(n, terms.at[0], out_slots, sems[0:2])
    z_ring = RingScatter(n, terms.at[1], z_slots, sems[2:4])
    for way in (0, 1):
        out_ring.step(way, k)
        z_ring.step(way, k)

    @pl.when(k < n - 1)
    def _():
        for copy in streams(k + 1):
            copy.start()

    def out_copy(part):
        return pltpu.make_async_copy(hold.at[2, part], out_ref.at[part], out_sem.at[part])

    def store(part, value):
        hold[2, part] = value.astype(BF16)
        out_copy(part).start()

    rows.step(k, store)

    @pl.when(k == n - 1)
    def _():
        for way in (0, 1):
            at = pl.ds(way * half, half)
            gout_ref[at, :] = out_ring.last(way).T
            gz_ref[:, at] = z_ring.last(way)

    @pl.when(k == n - 1)
    def _():
        rows.finish()
        out_ring.finish()
        z_ring.finish()
        for part in range(2):
            out_copy(part).wait()


def backward_all(n, small, piece, normed, g, u, dz, w_out, dy, x, cx, bc, cbc, dt, marks, states, shared):
    seqs, length, channels = x.shape
    n2, heads = bc.shape[2], dt.shape[1]
    tokens, model = g.shape
    count = model // n
    blocks = length // BLOCK
    sem = pltpu.SemaphoreType.DMA
    anywhere = pl.BlockSpec(memory_space=pl.ANY)
    ins, outs = backward_specs(channels, n2, heads, small, lambda k: (k // blocks, blocks - 1 - k % blocks))
    whole = lambda *shape: pl.BlockSpec(shape, lambda k: (0,) * len(shape))
    return pl.pallas_call(
        functools.partial(back_kernel, n),
        grid=(n,),
        in_specs=[anywhere] * 5 + ins,
        out_specs=[anywhere, whole(channels, count), whole(count, channels)] + outs,
        out_shape=[
            jax.ShapeDtypeStruct((seqs, piece, model), BF16),
            jax.ShapeDtypeStruct((channels, count), F32),
            jax.ShapeDtypeStruct((count, channels), F32),
        ]
        + backward_outs(seqs, length, channels, n2, heads, small),
        scratch_shapes=backward_scratch(channels, n2, heads)
        + [
            pltpu.VMEM((tokens, channels), BF16),
            pltpu.VMEM((tokens, channels), BF16),
            pltpu.VMEM((channels, model), BF16),
            pltpu.VMEM((2, tokens, count), BF16),
            pltpu.VMEM((2, tokens, count), BF16),
            pltpu.VMEM((2, n, count, channels // 2), BF16),
            pltpu.VMEM((2, n, count, channels // 2), BF16),
            pltpu.VMEM((4, seqs, piece, model), BF16),
            pltpu.VMEM((2, 2, count, channels // 2), BF16),
            pltpu.VMEM((piece, model), BF16),
            sem((3,)),
            sem((2, 2)),
            sem((seqs,)),
        ]
        + [sem((2, n - 1))] * 4
        + [sem((3, seqs))] * 2,
        compiler_params=pltpu.CompilerParams(
            collective_id=1, has_side_effects=True, vmem_limit_bytes=127 * 2**19
        ),
        name="backward_all",
    )(normed, g, u, dz, w_out, dy, x, cx, bc, cbc, dt, marks, states, *shared)


class Fold:
    def __init__(self, n, total, came, sems):
        self.total, self.came = total, came
        self.send_sem, self.recv_sem = sems
        dp = lax.axis_index("dp")
        _, other, across = tensor_place()
        partners, ahead = [], 1
        while ahead < n:
            partners.append({"dp": dp + ahead * (1 - 2 * ((dp // ahead) % 2))})
            ahead *= 2
        self.over_dp = partners
        self.partners = partners + [{"tensor": other}, {"tensor": across}]

    def copy(self, r):
        return remote(
            self.total.at[r], self.came.at[r], self.send_sem.at[r], self.recv_sem.at[r], self.partners[r]
        )

    def start(self, r):
        self.copy(r).start()

    def take(self, r):
        self.copy(r).wait_recv()
        self.total[r + 1] = self.total[r] + self.came[r]

    def finish(self):
        for r in range(len(self.partners)):
            self.copy(r).wait_send()


def in_kernel(
    n, u_hbm, dz_hbm, dx_hbm, wz_hbm, wx_hbm, wb_hbm, dbc_hbm, gz_hbm, gx_in, gbc_in, gh_in, gate_in, gain_ref,
    din_ref, gx_ref, gb_ref, sums_ref, dots_ref, pre_ref,
    u_ref, dz_ref, dx_ref, wz_ref, wx_ref, wb_ref, dbc_ref,
    x_slots, b_slots, hold, bc_hold, x_terms, b_terms, in_value, bc_value, low, swap, own_in, pre, pre_dp, pre_tensor, total, came, load_sem, u_sem, *sems,
):
    seqs, piece = din_ref.shape[:2]
    tokens, model = u_ref.shape
    length = tokens // seqs
    count = model // n
    half = gx_ref.shape[2] // 2
    me, other, across = tensor_place()
    core = me % 2

    moves = (
        (dbc_hbm, dbc_ref),
        (dx_hbm, dx_ref),
        (dz_hbm, dz_ref),
        (wz_hbm, wz_ref),
        (wx_hbm, wx_ref),
        (wb_hbm, wb_ref),
        (gz_hbm, gx_ref.at[0]),
    )
    loads = [pltpu.make_async_copy(src, dst, load_sem.at[i]) for i, (src, dst) in enumerate(moves)]
    place, at_place = ring_place(n)
    u_copies = []
    for ahead in (-1, 1, -2, 2, -3, 3, 4, 0):
        cols = span(at_place(place + ahead) * count, count, 128)
        u_copies.append(pltpu.make_async_copy(u_hbm.at[:, cols], u_ref.at[:, cols], u_sem.at[ahead + 3]))
    for load in loads[:2] + u_copies[:2] + loads[2:] + u_copies[2:]:
        load.start()

    bc_rows = RowScatter(seqs, bc_value, bc_hold, sems[0:2])
    in_rows = RowScatter(seqs, in_value, hold, sems[2:4])
    x_ring = RingScatter(n, x_terms, x_slots, sems[4:6])
    b_ring = RingScatter(n, b_terms, b_slots, sems[6:8], 1, 1 - 2 * core)
    pair_send, pair_recv, swap_send, swap_recv = sems[8:12]
    dp_send, dp_recv, tensor_send, tensor_recv = sems[14:18]
    fold = Fold(n, total, came, sems[12:14])
    rounds = len(fold.partners)
    pair = remote(low.at[0], low.at[1], pair_send, pair_recv, {"tensor": other})

    total[0] = jnp.zeros_like(total[0])
    total[0, 0:6, :] = gx_in[0:6, :]
    total[0, 6:7, :] = gate_in[...]
    steps = gh_in[...].T
    total[0, 7:8, 0 : steps.shape[1]] = steps[0:1, :]
    total[0, 7:8, 128 : 128 + steps.shape[1]] = steps[1:2, :]
    total[0, 8:13, 0 : gbc_in.shape[1]] = gbc_in[0:5, :]
    pre[...] = jnp.zeros_like(pre)
    dp_now = lax.axis_index("dp")
    greet(
        n,
        fold.over_dp
        + [{"dp": (dp_now + o) % n} for o in range(1, n)]
        + [{"tensor": (me + o) % 4} for o in range(1, 4)],
    )
    def rows_at(t, part):
        return span(part * length + t * piece, piece, 16)

    def bc_store(part, value):
        low[0, part] = value.astype(BF16)

    def bc_step(j):
        t, part = bc_rows.owner(j)
        bc_value[...] = dbc_ref[rows_at(t, part), :].astype(F32)
        bc_rows.step(j, bc_store)

    def add_pre(at):
        pre[...] += jnp.sum(in_value[...] * u_ref[at, :].astype(F32), axis=0, keepdims=True)

    def store(part, value):
        in_value[...] = value + dot_nt(low[0, part], wb_ref[...])
        own_in[part] = in_value[...]
        add_pre(rows_at(me, part))

    def row_term(j):
        at = rows_at(*in_rows.owner(j))
        in_value[...] = dot_nt(dz_ref[at, :], wz_ref[...]) + dot_nt(dx_ref[at, :], wx_ref[...])

    def row_step(j):
        in_rows.step(j, store, wait=False)

        @pl.when(j < 3 * seqs)
        def _():
            add_pre(rows_at(*in_rows.owner(j)))

    def x_term(k):
        for way in (0, 1):
            cols = span(x_ring.owner(way, k) * count, count, 128)
            x_terms[way] = dot_tn(u_ref[:, cols], dx_ref[:, pl.ds(way * half, half)])

    def x_step(k):
        for way in (0, 1):
            x_ring.step(way, k)

    def b_step(k):
        cols = span(b_ring.owner(0, k) * count + core * count // 2, count // 2, 128)
        value = 0.0
        for t, which in ((me, 0), (other, 1)):
            for part in range(seqs):
                value = value + dot_tn(u_ref[rows_at(t, part), cols], low[which, part])
        b_terms[0] = value
        b_ring.step(0, k)

    loads[0].wait()
    for part in range(seqs):
        bc_step(2 * part)
        bc_step(2 * seqs + part)
    loads[1].wait()
    for copy in u_copies[:2]:
        copy.wait()
    x_term(0)
    x_step(0)
    for load in loads[2:] + u_copies[2:]:
        load.wait()
    row_term(0)
    row_step(0)
    for part in range(seqs):
        bc_step(2 * part + 1)

    wide = model // 8
    gain = gain_ref[...]

    def dp_copy(o):
        ref = pre_dp.at[dp_now]
        return remote(ref, ref, dp_send.at[o], dp_recv.at[o], {"dp": (dp_now + o) % n})

    def tensor_copy(o):
        ref = pre_tensor.at[me]
        return remote(ref, ref, tensor_send.at[o], tensor_recv.at[o], {"tensor": (me + o) % 4})

    cross = remote(swap.at[0], swap.at[1], swap_send.at[0], swap_recv.at[0], {"tensor": across})
    back = remote(swap.at[2], swap.at[3], swap_send.at[1], swap_recv.at[1], {"tensor": other})

    def at_step(k, when, what):
        pl.when(k == when)(what)

    def own_bc():
        for part in range(seqs):
            bc_step(3 * seqs + part)
        pair.start()

    def send_pre():
        for i in range(8):
            at = slice(i * wide, (i + 1) * wide)
            pre_dp[dp_now, i : i + 1, :] = pre[:, at] / gain[:, at]
        for o in range(1, n):
            dp_copy(o).start()

    def pass_pre():
        for o in range(1, n):
            dp_copy(o).wait_recv()
        pre_tensor[me] = sum(pre_dp[d] for d in range(n))
        for o in range(1, 4):
            tensor_copy(o).start()

    def take_pre():
        for o in range(1, 4):
            tensor_copy(o).wait_recv()
        pre_ref[...] = (pre_tensor[0] + pre_tensor[1]) + (pre_tensor[2] + pre_tensor[3])

    def send_bc():
        swap[0] = b_ring.last(0)
        cross.start()

    def pass_bc():
        cross.wait_recv()
        swap[2] = swap[0] + swap[1]
        back.start()
        gb_ref[span(core * count // 2, count // 2, 16), :] = swap[2]

    def step(k, _):
        at_step(k, 5, send_pre)
        at_step(k, n - 1, send_bc)

        @pl.when(2 * k - 1 < 4 * seqs)
        def _():
            row_term(2 * k - 1)
            row_step(2 * k - 1)

        x_term(k)
        x_step(k)
        at_step(k, 2, pair.wait_recv)

        @pl.when((k >= 2) & (k <= 6))
        def _():
            b_step(jnp.maximum(k - 2, 2 * (k - 3)))

        @pl.when(2 * k < 4 * seqs)
        def _():
            row_term(2 * k)
            row_step(2 * k)

        at_step(k, 1, own_bc)

        @pl.when((k >= 4) & (k <= 6))
        def _():
            b_step(2 * (k - 3) + 1)

        at_step(k, 6, pass_pre)
        at_step(k, n - 1, pass_bc)
        at_step(k, n - 1, take_pre)
        for r in range(rounds + 1):

            @pl.when(k == r + 1)
            def _():
                if r > 0:
                    fold.take(r - 1)
                if r < rounds:
                    fold.start(r)

        return 0

    lax.fori_loop(1, n, step, 0)
    for way in (0, 1):
        gx_ref[1, :, pl.ds(way * half, half)] = x_ring.last(way)
    sums_ref[0:8, :] = total[rounds - 2, 0:8, :]
    sums_ref[8:16, :] = total[rounds, 8:16, :]
    for part in range(seqs):
        value = own_in[part] + in_rows.arrived(part)
        din_ref[part] = value.astype(BF16)
        inner = jnp.sum(value * u_ref[rows_at(me, part), :].astype(F32), axis=1, keepdims=True)
        dots_ref[part] = jnp.broadcast_to(inner, (piece, 128))
    back.wait_recv()
    gb_ref[span((1 - core) * count // 2, count // 2, 16), :] = swap[3]
    for o in range(1, n):
        dp_copy(o).wait_send()
    for o in range(1, 4):
        tensor_copy(o).wait_send()
    for copy in (pair, cross, back):
        copy.wait_send()
    for part in (bc_rows, in_rows, x_ring, b_ring, fold):
        part.finish()


def scatter_in(n, piece, u, dz, dx, w_z, w_x, w_bc, dbc, grad_z, gx, gbc, gh, grad_gate, gain):
    tokens, model = u.shape
    width = dz.shape[1]
    small = dbc.shape[1]
    seqs = tokens // (4 * piece)
    count = model // n
    rounds = 5
    sem = pltpu.SemaphoreType.DMA
    vmem = pl.BlockSpec(memory_space=pltpu.VMEM)
    anywhere = pl.BlockSpec(memory_space=pl.ANY)
    big = (u, dz, dx, w_z, w_x, w_bc, dbc)
    return pl.pallas_call(
        functools.partial(in_kernel, n),
        in_specs=[anywhere] * 8 + [vmem] * 5,
        out_specs=[vmem] * 6,
        out_shape=[
            jax.ShapeDtypeStruct((seqs, piece, model), BF16),
            jax.ShapeDtypeStruct((2, count, width), F32),
            jax.ShapeDtypeStruct((count, small), F32),
            jax.ShapeDtypeStruct((16, width), F32),
            jax.ShapeDtypeStruct((seqs, piece, 128), F32),
            jax.ShapeDtypeStruct((8, model // 8), F32),
        ],
        scratch_shapes=[pltpu.VMEM(a.shape, BF16) for a in big]
        + [
            pltpu.VMEM((2, n, count, width // 2), BF16),
            pltpu.VMEM((1, n, count // 2, small), BF16),
            pltpu.VMEM((4, seqs, piece, model), BF16),
            pltpu.VMEM((4, seqs, piece, small), BF16),
            pltpu.VMEM((2, count, width // 2), F32),
            pltpu.VMEM((1, count // 2, small), F32),
            pltpu.VMEM((piece, model), F32),
            pltpu.VMEM((piece, small), F32),
            pltpu.VMEM((2, seqs, piece, small), BF16),
            pltpu.VMEM((4, count // 2, small), F32),
            pltpu.VMEM((seqs, piece, model), F32),
            pltpu.VMEM((1, model), F32),
            pltpu.VMEM((n, 8, model // 8), F32),
            pltpu.VMEM((4, 8, model // 8), F32),
            pltpu.VMEM((rounds + 1, 16, width), F32),
            pltpu.VMEM((rounds, 16, width), F32),
            sem((len(big),)),
            sem((n,)),
        ]
        + [sem((3, seqs))] * 4 + [sem((2, n - 1))] * 2 + [sem((1, n - 1))] * 2 + [sem(())] * 2 + [sem((2,))] * 2
        + [sem((rounds,))] * 2 + [sem((n,))] * 2 + [sem((4,))] * 2,
        compiler_params=pltpu.CompilerParams(
            collective_id=2, has_side_effects=True, vmem_limit_bytes=63 * 2**20
        ),
        name="scatter_in",
    )(*big, grad_z, gx, gbc, gh, grad_gate, gain)


def finish_kernel(
    d_in_ref, hidden_ref, cot_ref, mixed_ref, scale_ref, dots_ref, gain_ref, gzx_in, gout_in, gb_in, sums_ref,
    spread_ref, pre_in,
    out_ref, d_hidden_ref, gzx_ref, gout_ref, gb_ref, taps_ref, taps_bc_ref,
    bias_ref, alog_ref, skip_ref, gate_ref, pre_ref,
):
    model = gain_ref.shape[1]
    x = hidden_ref[0].astype(F32)
    scale = scale_ref[0][:, 0:1]
    factor = scale * scale * dots_ref[0][:, 0:1] / model
    d_hidden_ref[0] = cot_ref[0].astype(F32) + scale * (gain_ref[...] * d_in_ref[0].astype(F32)) - x * factor
    out_ref[0] = (x + mixed_ref[0].astype(F32)).astype(BF16)
    gzx_ref[...] = gzx_in[...]
    gout_ref[...] = gout_in[...]
    gb_ref[...] = gb_in[...].T[: gb_ref.shape[0], :]
    taps_ref[...] = sums_ref[0 : taps_ref.shape[0], :]
    taps_bc_ref[...] = sums_ref[8 : 8 + taps_bc_ref.shape[0], : taps_bc_ref.shape[1]]
    heads = bias_ref.shape[0]
    bias_ref[...] = sums_ref[7, 0:heads]
    alog_ref[...] = sums_ref[7, 128 : 128 + heads]
    gate_ref[...] = sums_ref[6, :]
    by_head = lax.dot_general(
        sums_ref[0:8, :],
        spread_ref[...].astype(F32),
        (((1,), (1,)), ((), ())),
        precision=EXACT,
        preferred_element_type=F32,
    )
    skip_ref[...] = by_head[5, :]
    wide = pre_in.shape[1]
    for i in range(pre_in.shape[0]):
        pre_ref[pl.ds(i * wide, wide)] = pre_in[i, :]


def finish(
    d_in, hidden, cotangent, mixed, scale, dots, gain, grad_zx, grad_out, grad_bc, sums, spread, pre, columns, n2
):
    seqs, piece, model = hidden.shape
    count, width = grad_zx.shape[1:]
    heads = spread.shape[0]
    steps = 2
    rows = piece // steps
    grid = seqs * steps
    piece_rows = lambda w: pl.BlockSpec((1, rows, w), lambda i: (i // steps, i % steps, 0))
    whole = lambda *shape: pl.BlockSpec(shape, lambda i: (0,) * len(shape))
    zx = pl.BlockSpec((1, 2 * count // grid, width), lambda i: (i // (grid // 2), i % (grid // 2), 0))
    down = lambda a, w: pl.BlockSpec((a.shape[0] // grid, w), lambda i: (i, 0))
    return pl.pallas_call(
        finish_kernel,
        grid=(grid,),
        in_specs=[piece_rows(model)] * 4
        + [piece_rows(128)] * 2
        + [whole(1, model), zx, down(grad_out, grad_out.shape[1]), whole(*grad_bc.shape)]
        + [whole(*sums.shape), whole(*spread.shape), whole(*pre.shape)],
        out_specs=[piece_rows(model)] * 2
        + [zx, down(grad_out, grad_out.shape[1]), whole(columns, count), whole(5, width), whole(5, n2)]
        + [whole(heads), whole(heads), whole(heads), whole(width), whole(model)],
        out_shape=[
            jax.ShapeDtypeStruct(hidden.shape, BF16),
            jax.ShapeDtypeStruct(hidden.shape, F32),
            jax.ShapeDtypeStruct(grad_zx.shape, F32),
            jax.ShapeDtypeStruct(grad_out.shape, F32),
            jax.ShapeDtypeStruct((columns, count), F32),
            jax.ShapeDtypeStruct((5, width), F32),
            jax.ShapeDtypeStruct((5, n2), F32),
        ]
        + [jax.ShapeDtypeStruct((k,), F32) for k in (heads, heads, heads, width, model)],
        compiler_params=pltpu.CompilerParams(vmem_limit_bytes=62 * 2**20),
        name="finish",
    )(d_in, hidden, cotangent, mixed, scale, dots, gain, grad_zx, grad_out, grad_bc, sums, spread, pre)


def rms_scale(values):
    return lax.rsqrt(jnp.mean(values * values, axis=-1, keepdims=True) + EPS)


def gather_plain(u, g, w_zx, w_bc, w_out):
    w_zx = lax.all_gather(w_zx, "dp", axis=1, tiled=True)
    return (
        lax.all_gather(u, "tensor", axis=1, tiled=True),
        lax.all_gather(g, "tensor", axis=1, tiled=True),
        w_zx[1],
        w_zx[0],
        lax.all_gather(w_bc, "dp", axis=0, tiled=True),
        lax.all_gather(w_out, "dp", axis=1, tiled=True),
    )


def rows_of(values, piece):
    by_seq = values.reshape(-1, 4 * piece, values.shape[-1])
    return lax.psum_scatter(by_seq, "tensor", scatter_dimension=1, tiled=True)


def scatter_out_plain(piece, normed, g, u, dz, w_out):
    return (
        rows_of(dot(normed, w_out), piece),
        lax.psum_scatter(dot_tn(normed, g), "dp", scatter_dimension=1, tiled=True),
        lax.psum_scatter(dot_tn(u, dz), "dp", scatter_dimension=0, tiled=True),
    )


def scatter_in_plain(piece, u, dz, dx, w_z, w_x, w_bc, dbc):
    low = lax.psum(dbc.astype(F32), "tensor").astype(BF16)
    d_in = rows_of(dot_nt(dz, w_z) + dot_nt(dx, w_x), piece)
    first = lax.axis_index("tensor") * piece
    own = lax.dynamic_slice_in_dim(low.reshape(-1, 4 * piece, low.shape[1]), first, piece, 1)
    d_in = d_in + jnp.einsum("slc,dc->sld", own, w_bc, preferred_element_type=F32)
    return (
        d_in,
        lax.psum_scatter(dot_tn(u, dx), "dp", scatter_dimension=0, tiled=True),
        lax.psum_scatter(dot_tn(u, low), "dp", scatter_dimension=0, tiled=True),
    )


def local(
    n_dp,
    n_tensor,
    hidden,
    pre_gain,
    w_zx,
    w_bcdt,
    conv_x,
    conv_bc,
    dt_bias,
    a_log,
    d_skip,
    gate_gain,
    w_out,
    cotangent,
    segments,
):
    seqs, piece, model = hidden.shape
    length = segments.shape[1]
    tokens = seqs * length
    heads = dt_bias.shape[0]
    channels = conv_x.shape[1]
    n2 = conv_bc.shape[1]
    columns = w_bcdt.shape[1]
    tensor = lax.axis_index("tensor")
    kernels = n_dp == 8 and n_tensor == 4 and seqs == 2 and length == 4 * BLOCK

    x_piece = hidden.astype(F32)
    spread = jnp.asarray(spread_matrix(heads, channels), BF16)
    pick = jnp.asarray(pick_matrix(heads, channels), BF16)
    shared = (conv_x, conv_bc, dt_bias[None], a_log[None], d_skip[None], spread, pick)
    if kernels:
        u, g, w_x, w_z, w_bc, w_o, cx, x, cbc, bc, dt, states, normed, dz, dy, grad_gate, scale_in, marks = forward_all(
            n_dp, hidden, cotangent, w_zx, w_bcdt.T, w_out, pre_gain[None], gate_gain[None], segments, shared
        )
        g = g.reshape(tokens, model)
    else:
        scale_in = rms_scale(x_piece)
        u_piece = (x_piece * scale_in * pre_gain).astype(BF16)
        w_bc_piece = jnp.pad(w_bcdt, ((0, 0), (0, -columns % 128)))
        u, g, w_x, w_z, w_bc, w_o = gather_plain(u_piece, cotangent, w_zx, w_bc_piece, w_out)
        u = u.reshape(tokens, model)
        g = g.reshape(tokens, model)
        x = dot(u, w_x).reshape(seqs, length, channels)
        z = dot(u, w_z)
        bc_dt = dot(u, w_bc).reshape(seqs, length, -1)
        bc = bc_dt[:, :, :n2]
        dt = jnp.swapaxes(lax.dynamic_slice_in_dim(bc_dt, n2 + tensor * heads, heads, 2), 1, 2)
        marks = row_marks(segments)
        y, cx, cbc, states = ssd_forward(x, bc, dt, marks, shared)
        d_normed = dot_nt(g, w_o)
        sig_z = sigmoid(z)
        silu_z = z * sig_z
        y_flat = y.reshape(tokens, channels)
        gated = y_flat * silu_z
        scaled = d_normed * gate_gain
        sums = jnp.stack([jnp.sum(gated * gated, axis=1), jnp.sum(scaled * gated, axis=1)])
        sums = lax.psum(sums, "tensor") / (channels * n_tensor)
        inverse = lax.rsqrt(sums[0] + EPS)[:, None]
        normed = (gated * inverse * gate_gain).astype(BF16)
        grad_gate = jnp.sum(d_normed * gated * inverse, axis=0)[None]
        d_gated = inverse * scaled - gated * inverse**3 * sums[1][:, None]
        dy = (d_gated * silu_z).astype(BF16)
        dz = (d_gated * y_flat * (sig_z * (1.0 + z * (1.0 - sig_z)))).astype(BF16)
        x, bc = x.astype(BF16), bc.astype(BF16)

    back_args = (dy.reshape(seqs, length, channels), x, cx, bc, cbc, dt, marks, states, shared)
    if kernels:
        mixed, grad_out, grad_z, *rest = backward_all(n_dp, w_bc.shape[1], piece, normed, g, u, dz, w_o, *back_args)
    else:
        mixed, grad_out, grad_z = scatter_out_plain(piece, normed, g, u, dz, w_o)
        rest = ssd_backward(w_bc.shape[1], *back_args)
    dx, dbc, gx, gbc, gh = rest
    in_args = (piece, u, dz, dx.reshape(tokens, channels), w_z, w_x, w_bc, dbc.reshape(tokens, -1))
    if kernels:
        d_in, grad_zx, grad_bc, sums, dots, grad_pre = scatter_in(
            n_dp, *in_args, grad_z, gx, gbc, gh, grad_gate, pre_gain[None]
        )
        finished = finish(
            d_in, hidden, cotangent, mixed, scale_in, dots, pre_gain[None], grad_zx, grad_out, grad_bc, sums, spread,
            grad_pre, columns, n2
        )
        out_hidden, d_hidden, grad_zx, grad_out, grad_bc, grad_conv_x, grad_conv_bc, *small = finished
        grad_bias, grad_alog, grad_skip, grad_gate, grad_pre = small
        grad_bc = grad_bc.T
    else:
        d_in, grad_x, grad_bc = scatter_in_plain(*in_args)
        grad_zx = jnp.stack([grad_z, grad_x])
        grad_pre = jnp.sum(d_in * x_piece * scale_in, axis=(0, 1))
        dots = scale_in * jnp.sum(d_in * pre_gain * x_piece, axis=-1, keepdims=True)
        steps = jnp.pad(gh[:, :2].T, ((0, 0), (0, channels - heads)))
        sums = lax.psum(jnp.concatenate([gx[:6], grad_gate, steps]), "dp")
        sums = jnp.concatenate([sums[:7], jnp.concatenate([sums[7, :128], sums[8, : channels - 128]])[None]])
        grad_conv_bc, grad_pre = lax.psum((gbc[:5], grad_pre), ("dp", "tensor"))
        grad_conv_x = sums[:5]
        grad_bias, grad_alog = sums[7, :heads], sums[7, 128 : 128 + heads]
        grad_skip = sums[5].reshape(heads, -1).sum(axis=1)
        grad_gate = sums[6]
        grad_bc = grad_bc[:, :columns]
        out_hidden = (x_piece + mixed).astype(BF16)
        d_hidden = cotangent.astype(F32) + scale_in * (pre_gain * d_in) - x_piece * (scale_in**2 * dots / model)

    return (
        out_hidden,
        d_hidden,
        grad_pre,
        grad_zx,
        grad_bc,
        grad_conv_x,
        grad_conv_bc,
        grad_bias,
        grad_alog,
        grad_skip,
        grad_gate,
        grad_out,
    )


def solution(mesh):
    placed = (
        P("dp", "tensor", None),
        P(),
        P(None, "dp", "tensor"),
        P("dp", None),
        P(None, "tensor"),
        P(),
        P("tensor"),
        P("tensor"),
        P("tensor"),
        P("tensor"),
        P("tensor", "dp"),
        P("dp", "tensor", None),
        P("dp", None),
    )
    return jax.shard_map(
        functools.partial(local, mesh.shape["dp"], mesh.shape["tensor"]),
        mesh=mesh,
        in_specs=placed,
        out_specs=(
            P("dp", "tensor", None),
            P("dp", "tensor", None),
            P(),
            P(None, "dp", "tensor"),
            P("dp", None),
            P(None, "tensor"),
            P(),
            P("tensor"),
            P("tensor"),
            P("tensor"),
            P("tensor"),
            P("tensor", "dp"),
        ),
        check_vma=False,
    )
```
